32 devices in a mesh: gx: 4 (over z), gy: 2 (over x), gz: 4 (over y, core).
Axes of the slice: x: 2, y: 2, z: 4, core: 2. Of those that a mesh axis runs over, the one named last changes fastest.
Arguments:
- positions: float32 [3, 8, 2, 8, 8], P(None, 'gx', 'gy', 'gz'), as said below
- features: float32 [8, 2, 8, 8, 128], P('gx', 'gy', 'gz'), may hold values from -6 to 6
- species: int32 [8, 2, 8, 8], P('gx', 'gy', 'gz'), may hold values from 0 to 4
- centers: int32 [1024], P(('gx', 'gy', 'gz')), may hold values from 0 to 32, as said below
- neighbours: int32 [1024, 32], P(('gx', 'gy', 'gz')), may hold values from 0 to 384, as said below
- counts: int32 [32], P(('gx', 'gy', 'gz')), may hold values from 0 to 32, as said below
- species_scale: float32 [5], replicated, may hold values from 0.5 to 2
- species_shift: float32 [5], replicated, may hold values from -4 to 4
- center_weight: float32 [128, 128], replicated, may hold values from -0.5 to 0.5
- near_weight: float32 [128, 128], replicated, may hold values from -0.5 to 0.5
- basis_weight: float32 [8, 128], replicated, may hold values from -12 to 12
- path_weight: float32 [3, 128], replicated, may hold values from -6 to 6
- value_weight: float32 [128, 256], replicated, may hold values from -0.5 to 0.5
- latent_weight: float32 [256, 128], replicated, may hold values from -0.375 to 0.375
- out_weight: float32 [128], replicated, may hold values from -0.5 to 0.5
Outputs:
- site_energy: float32 [8, 2, 8, 8], P('gx', 'gy', 'gz')
- forces: float32 [3, 8, 2, 8, 8], P(None, 'gx', 'gy', 'gz')
- virial: float32 [9, 8, 2, 8, 8], P(None, 'gx', 'gy', 'gz')
The draws below stay inside these ranges and needn't reach their ends.
Inputs may be any that keep to these rules, and one draw needn't show every extreme that they name: `positions`: a listed neighbour lies within two lattice steps of its center, closer than 4.95 Angstrom; coordinates are the site's place in the cell plus a small jitter. `centers`: domain d's block of 32 entries lists its occupied own slots in increasing order, then 32 in the rest. `neighbours`: row k of domain d's block holds the frame rows of the occupied sites within two lattice steps of center k, in any order, and 384 in the other entries; rows of padding centers are all 384. counts[d] is the number of entries of domain d's block of centers that are not 32; some domain holds 32.
All inputs are finite; a program needn't handle non-finite values.
Results may differ from the reference program's by a relative error of at most 0.0003.
Values sent between devices are 32-bit elements; how exact they have to be, the bound alone decides.
No kernel may reach another device: no remote copies, remote signals or barrier semaphores. Data moves between devices by JAX's collectives and lax.ppermute only.
A program may use at most 64 MiB of HBM per device.

```python
import math
import jax
import jax.numpy as jnp
import numpy as np
from jax import lax

C = 128
NB = 8
NSPEC = 5
SLOT = 8
NBR = 32
CX = 2
CY = 1
CZ = 2
DOMS_X = 4
DOMS_Y = 2
DOMS_Z = 4
DOMAINS = 32
NCX = 8
NCY = 2
NCZ = 8
OWN = 32
FRAME = 384


def lattice_offsets():
    table = []
    for step_x in range(-2, 3):
        for step_y in range(-2, 3):
            for step_z in range(-2, 3):
                radius = step_x * step_x + step_y * step_y + step_z * step_z
                if 0 < radius <= 4:
                    table.append([step_x, step_y, step_z])
    return np.array(table, dtype=np.int32)


def lattice_layout(key):
    base = jax.random.fold_in(key, 811)
    doms_x = NCX // CX
    doms_y = NCY // CY
    doms_z = NCZ // CZ
    domains = doms_x * doms_y * doms_z
    owned = SLOT * CX * CY * CZ
    frame_count = SLOT * (CX + 2) * (CY + 2) * (CZ + 2)
    order = jnp.arange(domains)
    dense = jax.random.randint(jax.random.fold_in(base, 1), (domains,), 0, 4) == 0
    chosen = jax.random.randint(jax.random.fold_in(base, 2), (), 0, domains)
    dense = jnp.where(order == chosen, True, dense)
    dense = jnp.where(order == (chosen + 1) % domains, False, dense)
    keep = jax.random.randint(jax.random.fold_in(base, 3), (domains, owned), 0, 10) < 8
    keep = keep | dense[:, None]
    counts = jnp.sum(keep.astype(jnp.int32), axis=1)
    slot_ids = jnp.arange(owned)
    score = (1 - keep.astype(jnp.int32)) * owned + slot_ids[None, :]
    ordered = jnp.argsort(score, axis=1)
    centers = jnp.where(slot_ids[None, :] < counts[:, None], ordered, owned).astype(jnp.int32)
    lattice = keep.reshape(doms_x, doms_y, doms_z, CX, CY, CZ, 2, 2, 2)
    lattice = jnp.transpose(lattice, (0, 3, 6, 1, 4, 7, 2, 5, 8)).reshape(2 * NCX, 2 * NCY, 2 * NCZ)
    site = centers % SLOT
    cell = centers // SLOT
    cell_z = cell % CZ
    cell_y = cell // CZ % CY
    cell_x = cell // (CZ * CY)
    local_x = 2 * cell_x + site // 4
    local_y = 2 * cell_y + site // 2 % 2
    local_z = 2 * cell_z + site % 2
    offsets = jnp.asarray(lattice_offsets())
    near_x = local_x[..., None] + offsets[:, 0]
    near_y = local_y[..., None] + offsets[:, 1]
    near_z = local_z[..., None] + offsets[:, 2]
    domain_x = (order // (doms_y * doms_z))[:, None, None]
    domain_y = (order // doms_z % doms_y)[:, None, None]
    domain_z = (order % doms_z)[:, None, None]
    global_x = (domain_x * 2 * CX + near_x) % (2 * NCX)
    global_y = (domain_y * 2 * CY + near_y) % (2 * NCY)
    global_z = (domain_z * 2 * CZ + near_z) % (2 * NCZ)
    occupied = lattice[global_x, global_y, global_z]
    frame_x = near_x + 2
    frame_y = near_y + 2
    frame_z = near_z + 2
    rows = ((frame_x // 2 * (CY + 2) + frame_y // 2) * (CZ + 2) + frame_z // 2) * SLOT
    rows = rows + frame_x % 2 * 4 + frame_y % 2 * 2 + frame_z % 2
    live_center = (slot_ids[None, :] < counts[:, None])[..., None]
    rows = jnp.where(occupied & live_center, rows, frame_count)
    count_slots = offsets.shape[0]
    shuffle = jax.random.randint(jax.random.fold_in(base, 4), (domains, owned, count_slots), 0, 1 << 20) * count_slots + jnp.arange(count_slots)
    arrangement = jnp.argsort(shuffle, axis=-1)
    rows = jnp.take_along_axis(rows, arrangement, axis=-1)
    return (centers.reshape(-1), rows.reshape(domains * owned, count_slots).astype(jnp.int32), counts.astype(jnp.int32))


def draw_centers(key, part):
    return lattice_layout(key)[0]


def draw_neighbours(key, part):
    return lattice_layout(key)[1]


def draw_counts(key, part):
    return lattice_layout(key)[2]


def draw_positions(key, part):
    site = jnp.arange(SLOT)
    sub_cell = jnp.stack([site // 4, site // 2 % 2, site % 2]).astype(jnp.float32)
    centre = (sub_cell + 0.5) * 2.3
    extent = (3, NCX, NCY, NCZ, SLOT)
    jitter = jnp.clip(0.06 * jax.random.normal(key, extent, jnp.float32), -0.15, 0.15)
    return centre[:, None, None, None, :] + jitter


def set_ends(entries, own_key, least, high):
    longest = entries.shape.index(max(entries.shape))
    spots = []
    for shift in (0, 1):
        where = [jax.random.randint(jax.random.fold_in(own_key, axis), (), 0, length) for axis, length in enumerate(entries.shape)]
        where[longest] = (where[longest] + shift) % entries.shape[longest]
        spots.append(tuple(where))
    return entries.at[spots[0]].set(least).at[spots[1]].set(high)


def block_levels(key, shape, shards, least, high):
    level, own = 1.0, jax.random.fold_in(key, 6)
    for position, parts in shards:
        draws = jnp.exp(jax.random.uniform(jax.random.fold_in(own, position), (parts,), jnp.float32, least / len(shards), high / len(shards)))
        level = level * jnp.repeat(draws, shape[position] // parts).reshape([-1 if axis == position else 1 for axis in range(len(shape))])
    return level


def scatter_about(stream_key, shape, scale, bound, split=(), kind=jnp.bfloat16):
    entries = jax.random.normal(stream_key, shape, jnp.float32) * scale
    if len(split) > 0:
        entries = block_levels(stream_key, shape, split, -0.22, 0.18) * entries
    return jnp.clip(entries, min=-bound, max=bound).astype(kind)


def setup_inputs(seed: int = 0) -> dict:
    key_list = jax.random.split(jax.random.key(seed), 16)
    positions = draw_positions(jax.random.fold_in(key_list[15], 71), 0)
    features = scatter_about(key_list[1], (NCX, NCY, NCZ, SLOT, C), 1.0, 6.0, ((0, 4), (1, 2), (2, 4)), jnp.float32)
    species = set_ends(jax.random.randint(key_list[2], (NCX, NCY, NCZ, SLOT), 0, NSPEC), jax.random.fold_in(key_list[2], 1), 0, NSPEC - 1).astype(jnp.int32)
    centers = draw_centers(jax.random.fold_in(key_list[15], 71), 0)
    neighbours = draw_neighbours(jax.random.fold_in(key_list[15], 71), 0)
    counts = draw_counts(jax.random.fold_in(key_list[15], 71), 0)
    species_scale = jnp.clip(jnp.exp(jax.random.uniform(key_list[6], (NSPEC,), jnp.float32, math.log(0.5), math.log(2.0))), 0.5, 2.0)
    species_shift = scatter_about(key_list[7], (NSPEC,), 1.0, 4.0, (), jnp.float32)
    center_weight = scatter_about(key_list[8], (C, C), C ** -0.5, 0.5, (), jnp.float32)
    near_weight = scatter_about(key_list[9], (C, C), C ** -0.5, 0.5, (), jnp.float32)
    basis_weight = scatter_about(key_list[10], (NB, C), 2.0, 12.0, (), jnp.float32)
    path_weight = scatter_about(key_list[11], (3, C), 1.0, 6.0, (), jnp.float32)
    value_weight = scatter_about(key_list[12], (C, 2 * C), C ** -0.5, 0.5, (), jnp.float32)
    latent_weight = scatter_about(key_list[13], (2 * C, C), (2 * C) ** -0.5, 0.375, (), jnp.float32)
    out_weight = scatter_about(key_list[14], (C,), C ** -0.5, 0.5, (), jnp.float32)
    return dict(positions=positions, features=features, species=species, centers=centers, neighbours=neighbours, counts=counts, species_scale=species_scale, species_shift=species_shift, center_weight=center_weight, near_weight=near_weight, basis_weight=basis_weight, path_weight=path_weight, value_weight=value_weight, latent_weight=latent_weight, out_weight=out_weight)


EXACT_DOT = lax.Precision.HIGHEST
CUTOFF = 5.0
CELL_SIDE = 4.6
ROOT_HALF = 0.7071067811865476

def envelope(ratio):
    polynomial = 1.0 - 28.0 * ratio ** 6 + 48.0 * ratio ** 7 - 21.0 * ratio ** 8
    return jnp.where(ratio < 1.0, polynomial, 0.0)

def harmonics(unit):
    along_x = unit[..., 0]
    along_y = unit[..., 1]
    along_z = unit[..., 2]
    root_three = math.sqrt(3.0)
    root_fifteen = math.sqrt(15.0)
    root_five = math.sqrt(5.0)
    return jnp.stack([jnp.ones_like(along_x), root_three * along_x, root_three * along_y, root_three * along_z, root_fifteen * along_x * along_y, root_fifteen * along_y * along_z, 0.5 * root_five * (3.0 * along_z * along_z - 1.0), root_fifteen * along_x * along_z, 0.5 * root_fifteen * (along_x * along_x - along_y * along_y)], axis=-1)

def path_table(path_weight):
    width = path_weight.shape[1]
    return jnp.concatenate([path_weight[0:1], jnp.broadcast_to(path_weight[1:2], (3, width)), jnp.broadcast_to(path_weight[2:3], (5, width))], axis=0)

def center_energy(displace, live, center_proj, near_proj, scale, shift, active, basis_weight, paths, value_weight, latent_weight, out_weight):
    width = center_proj.shape[-1]
    neighbours_count = displace.shape[1]
    length = jnp.sqrt(lax.optimization_barrier(jnp.sum(displace * displace, axis=-1)))
    ratio = length / CUTOFF
    weight = envelope(ratio) * live
    frequency = jnp.arange(1, basis_weight.shape[0] + 1).astype(jnp.float32) * math.pi
    basis = math.sqrt(2.0 / CUTOFF) * jnp.sin(ratio[..., None] * frequency) / length[..., None]
    angular = harmonics(displace / length[..., None])
    radial = jnp.einsum('knb,bc->knc', basis, basis_weight, precision=EXACT_DOT)
    latent = weight[..., None] * jax.nn.silu(radial + center_proj[:, None, :] + near_proj)
    mixed = jnp.einsum('knc,cd->knd', latent, value_weight, precision=EXACT_DOT)
    values = mixed[..., :width]
    env_weight = mixed[..., width:]
    embed = jnp.einsum('knc,knm->kcm', env_weight, angular, precision=EXACT_DOT) / math.sqrt(neighbours_count)
    weighted = embed * jnp.transpose(paths)[None]
    inner = jnp.einsum('knm,kcm->knc', angular, weighted, precision=EXACT_DOT)
    scalars = values * inner
    joined = jnp.concatenate([latent, scalars], axis=-1)
    update = jax.nn.silu(jnp.einsum('knc,cd->knd', joined, latent_weight, precision=EXACT_DOT))
    final = (latent + weight[..., None] * update) * ROOT_HALF
    pair_energy = jnp.einsum('knc,c->kn', final, out_weight, precision=EXACT_DOT)
    return active * (scale * lax.optimization_barrier(jnp.sum(pair_energy, axis=1)) / math.sqrt(neighbours_count) + shift)

def own_to_frame(slots, cells_x, cells_y, cells_z, sites):
    owned = cells_x * cells_y * cells_z * sites
    frame_count = (cells_x + 2) * (cells_y + 2) * (cells_z + 2) * sites
    site = slots % sites
    cell = slots // sites
    cell_z = cell % cells_z
    cell_y = cell // cells_z % cells_y
    cell_x = cell // (cells_z * cells_y)
    frame = (((cell_x + 1) * (cells_y + 2) + cell_y + 1) * (cells_z + 2) + cell_z + 1) * sites + site
    return jnp.where(slots < owned, frame, frame_count).astype(jnp.int32)

def cell_corner(span_x, span_y, span_z):
    grid_x = jnp.broadcast_to(jnp.arange(span_x).astype(jnp.float32)[:, None, None], (span_x, span_y, span_z))
    grid_y = jnp.broadcast_to(jnp.arange(span_y).astype(jnp.float32)[None, :, None], (span_x, span_y, span_z))
    grid_z = jnp.broadcast_to(jnp.arange(span_z).astype(jnp.float32)[None, None, :], (span_x, span_y, span_z))
    return (jnp.stack([grid_x, grid_y, grid_z], axis=-1) * CELL_SIDE)[:, :, :, None, :]

def pair_return(totals, centre_rows, near_rows, displace, pair_grad):
    block = displace.shape[0]
    slots_count = displace.shape[1]
    pair_virial = -(displace[..., :, None] * pair_grad[..., None, :]).reshape(block, slots_count, 9)
    centre_part = jnp.concatenate([lax.optimization_barrier(jnp.sum(pair_grad, axis=1)), 0.5 * lax.optimization_barrier(jnp.sum(pair_virial, axis=1))], axis=-1)
    near_part = jnp.concatenate([-pair_grad, 0.5 * pair_virial], axis=-1).reshape(block * slots_count, 12)
    totals = totals.at[centre_rows].add(centre_part)
    return totals.at[near_rows.reshape(-1)].add(near_part)

def fold_axis(grid, axis, count):
    moved = jnp.moveaxis(grid, axis, 0)
    inner = moved[1:count + 1]
    inner = inner.at[0].add(moved[count + 1])
    inner = inner.at[count - 1].add(moved[0])
    return jnp.moveaxis(inner, 0, axis)

def reference(positions, features, species, centers, neighbours, counts, species_scale, species_shift, center_weight, near_weight, basis_weight, path_weight, value_weight, latent_weight, out_weight):
    width = features.shape[-1]
    flat = features.reshape(-1, width)
    center_all = jnp.dot(flat, center_weight, precision=EXACT_DOT, preferred_element_type=jnp.float32).reshape(NCX, NCY, NCZ, SLOT, width)
    near_all = jnp.dot(flat, near_weight, precision=EXACT_DOT, preferred_element_type=jnp.float32).reshape(NCX, NCY, NCZ, SLOT, width)
    near_pad = jnp.pad(near_all, ((1, 1), (1, 1), (1, 1), (0, 0), (0, 0)), mode='wrap')
    position_pad = jnp.pad(positions, ((0, 0), (1, 1), (1, 1), (1, 1), (0, 0)), mode='wrap')
    paths = path_table(path_weight)
    corner = cell_corner(CX + 2, CY + 2, CZ + 2)
    dead_shift = jnp.array([6.0, 0.0, 0.0], jnp.float32)
    zero_index = jnp.zeros((), jnp.int32)

    def domain(index):
        index = index.astype(jnp.int32)
        start_x = (index // (DOMS_Y * DOMS_Z) * CX).astype(jnp.int32)
        start_y = (index // DOMS_Z % DOMS_Y * CY).astype(jnp.int32)
        start_z = (index % DOMS_Z * CZ).astype(jnp.int32)
        in_cell = lax.dynamic_slice(position_pad, (zero_index, start_x, start_y, start_z, zero_index), (3, CX + 2, CY + 2, CZ + 2, SLOT))
        frame_position = (jnp.transpose(in_cell, (1, 2, 3, 4, 0)) + corner).reshape(FRAME, 3)
        frame_position = jnp.concatenate([frame_position, jnp.zeros((1, 3), jnp.float32)], axis=0)
        near = lax.dynamic_slice(near_pad, (start_x, start_y, start_z, zero_index, zero_index), (CX + 2, CY + 2, CZ + 2, SLOT, width)).reshape(FRAME, width)
        near = jnp.concatenate([near, jnp.zeros((1, width), jnp.float32)], axis=0)
        own_center = lax.dynamic_slice(center_all, (start_x, start_y, start_z, zero_index, zero_index), (CX, CY, CZ, SLOT, width)).reshape(OWN, width)
        own_center = jnp.concatenate([own_center, jnp.zeros((1, width), jnp.float32)], axis=0)
        own_species = lax.dynamic_slice(species, (start_x, start_y, start_z, zero_index), (CX, CY, CZ, SLOT)).reshape(OWN)
        own_species = jnp.concatenate([own_species, jnp.zeros((1,), jnp.int32)], axis=0)
        first = (index * OWN).astype(jnp.int32)
        slots = lax.dynamic_slice(centers, (first,), (OWN,)).astype(jnp.int32)
        rows = lax.dynamic_slice(neighbours, (first, zero_index), (OWN, NBR)).astype(jnp.int32)
        active = (jnp.arange(OWN).astype(jnp.int32) < counts[index]).astype(jnp.float32)
        kind = own_species[slots]
        scale = species_scale[kind]
        shift = species_shift[kind]
        centre_rows = own_to_frame(slots, CX, CY, CZ, SLOT)
        live = (rows != FRAME).astype(jnp.float32)
        separation = frame_position[rows] - frame_position[centre_rows][:, None, :]
        displace = jnp.where(live[..., None] > 0.0, separation, dead_shift)
        center_proj = own_center[slots]
        near_proj = near[rows]

        def energy_of(moved):
            return center_energy(moved, live, center_proj, near_proj, scale, shift, active, basis_weight, paths, value_weight, latent_weight, out_weight)
        energies, pull = jax.vjp(energy_of, displace)
        pair_grad = pull(jnp.ones_like(energies))[0]
        totals = pair_return(jnp.zeros((FRAME + 1, 12), jnp.float32), centre_rows, rows, displace, pair_grad)
        energy = jnp.zeros((OWN + 1,), jnp.float32).at[slots].add(energies)
        return (totals[:FRAME].reshape(CX + 2, CY + 2, CZ + 2, SLOT, 12), energy[:OWN].reshape(CX, CY, CZ, SLOT))
    frames, energies = lax.map(domain, jnp.arange(DOMAINS).astype(jnp.int32))

    def place(index, grid):
        index = jnp.asarray(index).astype(jnp.int32)
        start = ((index // (DOMS_Y * DOMS_Z) * CX).astype(jnp.int32), (index // DOMS_Z % DOMS_Y * CY).astype(jnp.int32), (index % DOMS_Z * CZ).astype(jnp.int32), zero_index, zero_index)
        current = lax.dynamic_slice(grid, start, (CX + 2, CY + 2, CZ + 2, SLOT, 12))
        return lax.dynamic_update_slice(grid, current + frames[index], start)
    grid = lax.fori_loop(0, DOMAINS, place, jnp.zeros((NCX + 2, NCY + 2, NCZ + 2, SLOT, 12), jnp.float32))
    grid = fold_axis(grid, 0, NCX)
    grid = fold_axis(grid, 1, NCY)
    grid = fold_axis(grid, 2, NCZ)
    forces = jnp.transpose(grid[..., 0:3], (4, 0, 1, 2, 3))
    virial = jnp.transpose(grid[..., 3:12], (4, 0, 1, 2, 3))
    site_energy = energies.reshape(DOMS_X, DOMS_Y, DOMS_Z, CX, CY, CZ, SLOT)
    site_energy = jnp.transpose(site_energy, (0, 3, 1, 4, 2, 5, 6)).reshape(NCX, NCY, NCZ, SLOT)
    return (site_energy, forces, virial)
```

```python
import math

import jax
import jax.numpy as jnp
import numpy as np
from jax import lax
from jax.experimental import pallas as pl
from jax.experimental.pallas import tpu as pltpu
from jax.sharding import PartitionSpec as P

EXACT_DOT = lax.Precision.HIGHEST
CUTOFF = 5.0
CELL_SIDE = 4.6
ROOT_HALF = 0.7071067811865476
GROUP = 8
ORDERS = 16
F32 = jnp.float32
BF16 = jnp.bfloat16


def padded(array, sides, width):
    for axis, dim in sides:
        size, length = (lax.axis_size(axis), array.shape[dim])
        up = [(i, (i + 1) % size) for i in range(size)]
        down = [(j, i) for i, j in up]
        last = lax.slice_in_dim(array, length - width, length, axis=dim)
        leading = lax.slice_in_dim(array, 0, width, axis=dim)
        before = lax.ppermute(last, axis, up)
        if size == 2 and length == width:
            after = before
        else:
            after = lax.ppermute(leading, axis, down)
        array = jnp.concatenate([before, array, after], axis=dim)
    return array


def cell_corner(span_x, span_y, span_z):
    grid = np.stack(
        np.meshgrid(np.arange(span_x), np.arange(span_y), np.arange(span_z), indexing="ij"),
        axis=-1,
    ).astype(np.float32)
    return grid * np.float32(CELL_SIDE)


def split(value):
    high = value.astype(BF16)
    low = (value - high.astype(F32)).astype(BF16)
    return high, low


def split3(value):
    high = value.astype(BF16)
    rest = value - high.astype(F32)
    middle = rest.astype(BF16)
    low = (rest - middle.astype(F32)).astype(BF16)
    return high, middle, low


def mm(a, b):
    return lax.dot_general(a, b, (((1,), (0,)), ((), ())), preferred_element_type=F32)


def mm_nt(a, b):
    return lax.dot_general(a, b, (((1,), (1,)), ((), ())), preferred_element_type=F32)


def stacked(high, low):
    top = jnp.concatenate([high, high], axis=1)
    bottom = jnp.concatenate([low, jnp.zeros_like(low)], axis=1)
    return jnp.concatenate([top, bottom], axis=0)


def folded(product):
    half = product.shape[0] // 2
    return product[:half] + product[half:]


def half_depth(weights, value):
    return folded(mm(weights, jnp.concatenate(split(value), axis=0)))


def full_depth(both, high, value_high, value_low):
    return folded(mm(both, value_high)) + mm(high, value_low)


def sin_cos_pi(turns):
    near = turns - 2.0 * jnp.round(turns * 0.5)
    quarter = jnp.round(near * 2.0)
    v = (near - 0.5 * quarter) * math.pi
    v2 = v * v
    s = v * (
        1.0
        + v2
        * (-1.0 / 6 + v2 * (1.0 / 120 + v2 * (-1.0 / 5040 + v2 * (1.0 / 362880 - v2 / 39916800))))
    )
    c = 1.0 + v2 * (
        -0.5
        + v2
        * (1.0 / 24 + v2 * (-1.0 / 720 + v2 * (1.0 / 40320 + v2 * (-1.0 / 3628800 + v2 / 479001600))))
    )
    odd = jnp.abs(quarter) == 1.0
    sine = jnp.where(odd, quarter * c, jnp.where(quarter == 0.0, s, -s))
    cosine = jnp.where(odd, -quarter * s, jnp.where(quarter == 0.0, c, -c))
    return sine, cosine


def force_kernel(
    feats_ref,
    coords_ref,
    own_ref,
    near_row_ref,
    center_row_ref,
    center_slot_ref,
    center_list_ref,
    species_ref,
    scale_ref,
    shift_ref,
    center_weight_ref,
    near_weight_ref,
    basis_weight_ref,
    path_weight_ref,
    value_weight_ref,
    latent_weight_ref,
    out_weight_ref,
    totals_ref,
    energy_ref,
):
    frame, width = feats_ref.shape
    owned = own_ref.shape[0]
    pairs = near_row_ref.shape[1]
    nbr = pairs // owned
    radial = basis_weight_ref.shape[0]
    sites = frame // coords_ref.shape[0]
    span = GROUP * nbr
    root_count = math.sqrt(nbr)
    root_three = math.sqrt(3.0)
    root_fifteen = math.sqrt(15.0)
    root_five = math.sqrt(5.0)

    value_t = jnp.transpose(value_weight_ref[...])
    latent_t = jnp.transpose(latent_weight_ref[...])
    value_rows = stacked(*split(value_t))
    latent_high_t, latent_low_t = split(latent_t)
    latent_both_t = jnp.concatenate([latent_high_t, latent_low_t], axis=0)
    latent_rows = stacked(*split(latent_weight_ref[...]))
    value_high, value_low = split(value_weight_ref[...])
    value_both = jnp.concatenate([value_high, value_low], axis=0)
    basis_t = jnp.transpose(basis_weight_ref[...])
    basis_high_t, basis_low_t = split(basis_t)
    basis_rows = stacked(*split(basis_weight_ref[...]))

    def project(weight, rows):
        weight_t = jnp.transpose(weight)
        high, low = split(rows)
        return folded(
            mm_nt(stacked(*split(weight_t)), jnp.concatenate([high, low], axis=1))
        )

    near_t = project(near_weight_ref[...], feats_ref[...])
    own_t = project(center_weight_ref[...], own_ref[...])
    near_high, near_low = split(near_t)
    own_high, own_low = split(own_t)
    lookup = jnp.concatenate(
        [
            jnp.concatenate([near_high, own_high, basis_high_t, basis_high_t], axis=1),
            jnp.concatenate([near_low, own_low, basis_low_t, jnp.zeros_like(basis_low_t)], axis=1),
        ],
        axis=0,
    )

    cells = frame // sites
    spread = jnp.broadcast_to(coords_ref[...][:, None, :], (cells, sites, 128)).reshape(frame, 128)
    lane = lax.broadcasted_iota(jnp.int32, (frame, 128), 1)
    row = lax.broadcasted_iota(jnp.int32, (frame, 128), 0)
    keep = (lane % sites == row % sites) & (lane < 3 * sites)
    spread = jnp.where(keep, spread, 0.0)
    place_t = jnp.concatenate(
        [jnp.transpose(spread)[: 3 * sites]], axis=0
    )
    place_parts = jnp.concatenate(split3(place_t), axis=0)

    species = species_ref[...]
    scale_slot = jnp.zeros(species.shape, F32)
    shift_slot = jnp.zeros(species.shape, F32)
    for s in range(scale_ref.shape[0]):
        scale_slot = jnp.where(species == s, scale_ref[s], scale_slot)
        shift_slot = jnp.where(species == s, shift_ref[s], shift_slot)
    scale_parts = jnp.concatenate(
        [*split3(scale_slot), jnp.zeros((13, owned), BF16)], axis=0
    )

    kind = lax.broadcasted_iota(jnp.int32, (ORDERS, width), 0)
    path_rows = jnp.where(
        kind == 0,
        path_weight_ref[0:1, :],
        jnp.where(
            kind < 4,
            path_weight_ref[1:2, :],
            jnp.where(kind < 9, path_weight_ref[2:3, :], 0.0),
        ),
    )
    paths_t = jnp.transpose(jnp.concatenate([path_rows] * GROUP, axis=0)) * (1.0 / root_count)
    out_column = jnp.transpose(jnp.broadcast_to(out_weight_ref[...], (width, width)))
    out_column = jnp.concatenate([out_column] * (span // width), axis=1)

    frame_ids = lax.broadcasted_iota(jnp.int32, (frame, span), 0)
    slot_ids = lax.broadcasted_iota(jnp.int32, (owned, span), 0)
    block_row = lax.broadcasted_iota(jnp.int32, (GROUP * ORDERS, span), 0) // ORDERS
    block_lane = lax.broadcasted_iota(jnp.int32, (GROUP * ORDERS, span), 1) // nbr
    block_mask = (block_row == block_lane).astype(F32)
    block_half = block_mask.astype(BF16)
    order = lax.broadcasted_iota(jnp.int32, (radial, span), 0).astype(F32) + 1.0

    totals = jnp.zeros((frame, 2 * ORDERS), F32)
    own_sums = jnp.zeros((4 * ORDERS, owned), F32)
    for g in range(owned // GROUP):
        lanes = slice(g * span, (g + 1) * span)
        near_row = near_row_ref[:, lanes]
        hit = frame_ids == near_row
        pick = jnp.where(hit, 1.0, 0.0)
        from_center = jnp.where(frame_ids == center_row_ref[:, lanes], 1.0, 0.0)
        pick_half = pick.astype(BF16)
        slot_half = jnp.where(slot_ids == center_slot_ref[:, lanes], 1.0, 0.0).astype(BF16)
        live = near_row != frame

        moved = mm(place_parts, (pick - from_center).astype(BF16))
        moved = moved[: 3 * sites] + moved[3 * sites : 6 * sites] + moved[6 * sites :]
        dx = jnp.sum(moved[:sites], axis=0, keepdims=True)
        dy = jnp.sum(moved[sites : 2 * sites], axis=0, keepdims=True)
        dz = jnp.sum(moved[2 * sites :], axis=0, keepdims=True)
        dx = jnp.where(live, dx, 6.0)
        dy = jnp.where(live, dy, 0.0)
        dz = jnp.where(live, dz, 0.0)
        length = jnp.sqrt(dx * dx + dy * dy + dz * dz)
        inverse = 1.0 / length
        ratio = length * (1.0 / CUTOFF)
        inside = live & (ratio < 1.0)
        r2 = ratio * ratio
        r5 = r2 * r2 * ratio
        r6 = r5 * ratio
        weight = jnp.where(inside, 1.0 - r6 * (28.0 - 48.0 * ratio + 21.0 * r2), 0.0)
        slope = jnp.where(inside, -168.0 * r5 * (1.0 - 2.0 * ratio + r2), 0.0)
        sine, cosine = sin_cos_pi(order * ratio)
        basis = (math.sqrt(2.0 / CUTOFF) * inverse) * sine
        basis_slope = (math.sqrt(2.0 / CUTOFF) * inverse) * (
            (math.pi / CUTOFF) * order * cosine - sine * inverse
        )
        ex = dx * inverse
        ey = dy * inverse
        ez = dz * inverse
        angular = jnp.concatenate(
            [
                jnp.ones_like(ex),
                root_three * ex,
                root_three * ey,
                root_three * ez,
                root_fifteen * ex * ey,
                root_fifteen * ey * ez,
                0.5 * root_five * (3.0 * ez * ez - 1.0),
                root_fifteen * ex * ez,
                0.5 * root_fifteen * (ex * ex - ey * ey),
                jnp.zeros((ORDERS - 9, span), F32),
            ],
            axis=0,
        )
        angular_high, angular_low = split(angular)
        block_high = jnp.concatenate([angular_high] * GROUP, axis=0) * block_half
        block_low = jnp.concatenate([angular_low] * GROUP, axis=0) * block_half
        block_pair = jnp.concatenate([block_high, block_low], axis=0)

        basis_high, basis_low = split(basis)
        before = folded(
            mm(lookup, jnp.concatenate([pick_half, slot_half, basis_high, basis_low], axis=0))
        )
        gate = 0.5 * jnp.tanh(0.5 * before) + 0.5
        active = before * gate
        latent = weight * active
        mixed = half_depth(value_rows, latent)
        values = mixed[:width]
        env = mixed[width:]
        env_high, env_low = split(env)
        env_pair = jnp.concatenate([env_high, env_low], axis=0)
        quad = mm_nt(env_pair, block_pair)
        wide = GROUP * ORDERS
        embed = quad[:width, :wide] + quad[:width, wide:] + quad[width:, :wide]
        weighted = embed * paths_t
        weighted_high, weighted_low = split(weighted)
        inner = folded(mm(stacked(weighted_high, weighted_low), block_pair))
        scalars = values * inner
        joined_high, joined_low = split(jnp.concatenate([latent, scalars], axis=0))
        z = full_depth(latent_both_t, latent_high_t, joined_high, joined_low)
        z_gate = 0.5 * jnp.tanh(0.5 * z) + 0.5
        update = z * z_gate
        update_out = update * out_column
        pair_energy = jnp.sum(latent * out_column + weight * update_out, axis=0, keepdims=True)

        scale = mm(scale_parts, slot_half)
        scale = (scale[0:1] + scale[1:2] + scale[2:3]) * (1.0 / root_count)
        pair_energy = pair_energy * (ROOT_HALF * scale)
        pull = ROOT_HALF * scale
        dz_full = (pull * weight) * out_column * (z_gate + update * (1.0 - z_gate))
        spread_back = half_depth(latent_rows, dz_full)
        d_scalars = spread_back[width:]
        d_values = d_scalars * inner
        d_inner = d_scalars * values
        dinner_high, dinner_low = split(d_inner)
        quad = mm_nt(jnp.concatenate([dinner_high, dinner_low], axis=0), block_pair)
        d_weighted = quad[:width, :wide] + quad[:width, wide:] + quad[width:, :wide]
        d_embed = d_weighted * paths_t
        dembed_high, dembed_low = split(d_embed)
        d_env = folded(mm(stacked(dembed_high, dembed_low), block_pair))

        sides = jnp.transpose(jnp.concatenate([weighted, d_embed], axis=0))
        sides_high, sides_low = split(sides)
        d_block = full_depth(
            jnp.concatenate([sides_high, sides_low], axis=0),
            sides_high,
            jnp.concatenate([dinner_high, env_high], axis=0),
            jnp.concatenate([dinner_low, env_low], axis=0),
        )
        d_block = d_block * block_mask
        d_angular = d_block[:ORDERS]
        for k in range(1, GROUP):
            d_angular = d_angular + d_block[k * ORDERS : (k + 1) * ORDERS]

        mixed_high, mixed_low = split(jnp.concatenate([d_values, d_env], axis=0))
        d_latent = (
            full_depth(value_both, value_high, mixed_high, mixed_low)
            + spread_back[:width]
            + pull * out_column
        )
        d_weight = jnp.sum(d_latent * active + pull * update_out, axis=0, keepdims=True)
        d_before = d_latent * weight * (gate + active * (1.0 - gate))
        d_basis = half_depth(basis_rows, d_before)

        d_length = (
            jnp.sum(d_basis * basis_slope, axis=0, keepdims=True)
            + d_weight * slope * (1.0 / CUTOFF)
        )
        a1 = d_angular[1:2]
        a2 = d_angular[2:3]
        a3 = d_angular[3:4]
        a4 = d_angular[4:5]
        a5 = d_angular[5:6]
        a6 = d_angular[6:7]
        a7 = d_angular[7:8]
        a8 = d_angular[8:9]
        ux = root_three * a1 + root_fifteen * (ey * a4 + ez * a7 + ex * a8)
        uy = root_three * a2 + root_fifteen * (ex * a4 + ez * a5 - ey * a8)
        uz = root_three * a3 + root_fifteen * (ey * a5 + ex * a7) + 3.0 * root_five * ez * a6
        along = ex * ux + ey * uy + ez * uz
        radial_part = d_length - along * inverse
        gx = ux * inverse + ex * radial_part
        gy = uy * inverse + ey * radial_part
        gz = uz * inverse + ez * radial_part
        hx = -0.5 * dx
        hy = -0.5 * dy
        hz = -0.5 * dz
        virial = [hx * gx, hx * gy, hx * gz, hy * gx, hy * gy, hy * gz, hz * gx, hz * gy, hz * gz]
        near_terms = jnp.concatenate(
            [-gx, -gy, -gz, *virial, pair_energy, jnp.ones_like(gx), jnp.zeros((2, span), F32)],
            axis=0,
        )
        near_high, near_low = split(near_terms)
        totals = totals + mm_nt(pick_half, jnp.concatenate([near_high, near_low], axis=0))
        own_sums = own_sums + mm_nt(
            jnp.concatenate([*split3(near_terms), jnp.zeros((ORDERS, span), BF16)], axis=0),
            slot_half,
        )

    sums = own_sums[:ORDERS] + own_sums[ORDERS : 2 * ORDERS] + own_sums[2 * ORDERS : 3 * ORDERS]
    energy_ref[...] = sums[12:13] + jnp.where(sums[13:14] > 0.5, shift_slot, 0.0)
    sign_row = lax.broadcasted_iota(jnp.int32, (ORDERS, owned), 0)
    center_terms = jnp.where(sign_row < 3, -sums, sums)
    center_high, center_low = split(center_terms)
    own_rows = jnp.where(
        lax.broadcasted_iota(jnp.int32, (frame, owned), 0) == center_list_ref[...], 1.0, 0.0
    ).astype(BF16)
    totals = totals + mm_nt(own_rows, jnp.concatenate([center_high, center_low], axis=0))
    both = totals[:, :ORDERS] + totals[:, ORDERS:]
    totals_ref[...] = jnp.concatenate([both, jnp.zeros((frame, 128 - ORDERS), F32)], axis=1)


def own_frame_rows(cells_x, cells_y, cells_z, sites):
    slots = np.arange(cells_x * cells_y * cells_z * sites)
    site = slots % sites
    cell = slots // sites
    cell_z = cell % cells_z
    cell_y = cell // cells_z % cells_y
    cell_x = cell // (cells_z * cells_y)
    return (
        ((cell_x + 1) * (cells_y + 2) + cell_y + 1) * (cells_z + 2) + cell_z + 1
    ) * sites + site


def own_to_frame(slots, cells_x, cells_y, cells_z, sites):
    owned = cells_x * cells_y * cells_z * sites
    frame_count = (cells_x + 2) * (cells_y + 2) * (cells_z + 2) * sites
    site = slots % sites
    cell = slots // sites
    cell_z = cell % cells_z
    cell_y = cell // cells_z % cells_y
    cell_x = cell // (cells_z * cells_y)
    frame = (
        ((cell_x + 1) * (cells_y + 2) + cell_y + 1) * (cells_z + 2) + cell_z + 1
    ) * sites + site
    return jnp.where(slots < owned, frame, frame_count)


def frame_terms(
    frame_feat,
    coords,
    features,
    species,
    centers,
    neighbours,
    species_scale,
    species_shift,
    center_weight,
    near_weight,
    basis_weight,
    path_weight,
    value_weight,
    latent_weight,
    out_weight,
):
    cells_x, cells_y, cells_z, sites, width = features.shape
    owned = cells_x * cells_y * cells_z * sites
    frame_count = frame_feat.shape[0]
    pairs = neighbours.size
    nbr = pairs // owned
    near_row = neighbours.reshape(1, pairs)
    rows = own_to_frame(centers, cells_x, cells_y, cells_z, sites)
    center_row = jnp.broadcast_to(rows[:, None], (owned, nbr)).reshape(1, pairs)
    center_slot = jnp.broadcast_to(centers[:, None], (owned, nbr)).reshape(1, pairs)
    own_rows = jnp.asarray(own_frame_rows(cells_x, cells_y, cells_z, sites), jnp.int32)
    vmem = pl.BlockSpec(memory_space=pltpu.VMEM)
    smem = pl.BlockSpec(memory_space=pltpu.SMEM)
    return pl.pallas_call(
        force_kernel,
        out_shape=(
            jax.ShapeDtypeStruct((frame_count, 128), F32),
            jax.ShapeDtypeStruct((1, owned), F32),
        ),
        in_specs=[vmem] * 8 + [smem] * 2 + [vmem] * 7,
        out_specs=(vmem, vmem),
        compiler_params=pltpu.CompilerParams(vmem_limit_bytes=32 * 1024 * 1024),
        name="pair_forces",
    )(
        frame_feat,
        coords,
        features.reshape(owned, width),
        near_row,
        center_row,
        center_slot,
        own_rows.reshape(1, owned),
        species.reshape(1, owned),
        species_scale,
        species_shift,
        center_weight,
        near_weight,
        basis_weight,
        path_weight,
        value_weight,
        latent_weight,
        out_weight.reshape(1, width),
    )


def local(
    positions,
    features,
    species,
    centers,
    neighbours,
    counts,
    species_scale,
    species_shift,
    center_weight,
    near_weight,
    basis_weight,
    path_weight,
    value_weight,
    latent_weight,
    out_weight,
):
    cells_x, cells_y, cells_z, sites, width = features.shape
    owned = cells_x * cells_y * cells_z * sites
    span_x = cells_x + 2
    span_y = cells_y + 2
    span_z = cells_z + 2
    frame_count = span_x * span_y * span_z * sites
    coords = jnp.transpose(positions, (1, 2, 3, 0, 4)).reshape(
        cells_x, cells_y, cells_z, 1, sites * 3
    )
    coords = jnp.pad(coords, ((0, 0), (0, 0), (0, 0), (0, 0), (0, width - sites * 3)))
    payload = jnp.concatenate([features, coords], axis=3)
    framed = padded(payload, (("gy", 1), ("gz", 2), ("gx", 0)), 1)
    frame_feat = framed[:, :, :, :sites, :].reshape(frame_count, width)
    corner = np.repeat(cell_corner(span_x, span_y, span_z), sites, axis=-1)
    corner = np.pad(corner, ((0, 0), (0, 0), (0, 0), (0, width - sites * 3)))
    frame_coords = (framed[:, :, :, sites, :] + jnp.asarray(corner)).reshape(-1, width)
    totals, energy = frame_terms(
        frame_feat,
        frame_coords,
        features,
        species,
        centers,
        neighbours,
        species_scale,
        species_shift,
        center_weight,
        near_weight,
        basis_weight,
        path_weight,
        value_weight,
        latent_weight,
        out_weight,
    )
    grid = totals.reshape(span_x, span_y, span_z, sites, totals.shape[-1])
    for axis, dim, cells in (("gx", 0, cells_x), ("gz", 2, cells_z), ("gy", 1, cells_y)):
        size = lax.axis_size(axis)
        up = [(i, (i + 1) % size) for i in range(size)]
        down = [(j, i) for i, j in up]
        first = lax.slice_in_dim(grid, 0, 1, axis=dim)
        last = lax.slice_in_dim(grid, cells + 1, cells + 2, axis=dim)
        inner = lax.slice_in_dim(grid, 1, cells + 1, axis=dim)
        if size == 2 and cells == 1:
            grid = inner + lax.ppermute(first + last, axis, up)
            continue
        to_last = lax.ppermute(first, axis, down)
        to_first = lax.ppermute(last, axis, up)
        low = lax.slice_in_dim(inner, 0, 1, axis=dim) + to_first
        if cells == 1:
            grid = low + to_last
            continue
        high = lax.slice_in_dim(inner, cells - 1, cells, axis=dim) + to_last
        middle = lax.slice_in_dim(inner, 1, cells - 1, axis=dim)
        grid = jnp.concatenate([low, middle, high], axis=dim)
    forces = jnp.transpose(grid[..., 0:3], (4, 0, 1, 2, 3))
    virial = jnp.transpose(grid[..., 3:12], (4, 0, 1, 2, 3))
    site_energy = energy.reshape(cells_x, cells_y, cells_z, sites)
    return (site_energy, forces, virial)


def solution(mesh):
    placed = (
        P(None, "gx", "gy", "gz", None),
        P("gx", "gy", "gz", None, None),
        P("gx", "gy", "gz", None),
        P(("gx", "gy", "gz")),
        P(("gx", "gy", "gz"), None),
        P(("gx", "gy", "gz")),
        P(),
        P(),
        P(),
        P(),
        P(),
        P(),
        P(),
        P(),
        P(),
    )
    return jax.shard_map(
        local,
        mesh=mesh,
        in_specs=placed,
        out_specs=(
            P("gx", "gy", "gz", None),
            P(None, "gx", "gy", "gz", None),
            P(None, "gx", "gy", "gz", None),
        ),
        check_vma=False,
    )
```

```python
import functools
import math

import jax
import jax.numpy as jnp
import numpy as np
from jax import lax
from jax.experimental import pallas as pl
from jax.experimental.pallas import tpu as pltpu
from jax.sharding import PartitionSpec as P

EXACT_DOT = lax.Precision.HIGHEST
CUTOFF = 5.0
CELL_SIDE = 4.6
ROOT_HALF = 0.7071067811865476
GROUP = 8
ORDERS = 16
F32 = jnp.float32
BF16 = jnp.bfloat16


def split(value):
    high = value.astype(BF16)
    low = (value - high.astype(F32)).astype(BF16)
    return high, low


def split3(value):
    high = value.astype(BF16)
    rest = value - high.astype(F32)
    middle = rest.astype(BF16)
    low = (rest - middle.astype(F32)).astype(BF16)
    return high, middle, low


def mm(a, b):
    return lax.dot_general(a, b, (((1,), (0,)), ((), ())), preferred_element_type=F32)


def mm_nt(a, b):
    return lax.dot_general(a, b, (((1,), (1,)), ((), ())), preferred_element_type=F32)


def stacked(high, low):
    top = jnp.concatenate([high, high], axis=1)
    bottom = jnp.concatenate([low, jnp.zeros_like(low)], axis=1)
    return jnp.concatenate([top, bottom], axis=0)


def folded(product):
    half = product.shape[0] // 2
    return product[:half] + product[half:]


def half_depth(weights, value):
    return folded(mm(weights, jnp.concatenate(split(value), axis=0)))


def full_depth(both, high, value_high, value_low):
    return folded(mm(both, value_high)) + mm(high, value_low)


def sin_cos_pi(turns):
    near = turns - 2.0 * jnp.round(turns * 0.5)
    quarter = jnp.round(near * 2.0)
    v = (near - 0.5 * quarter) * math.pi
    v2 = v * v
    s = v * (
        1.0
        + v2
        * (-1.0 / 6 + v2 * (1.0 / 120 + v2 * (-1.0 / 5040 + v2 * (1.0 / 362880 - v2 / 39916800))))
    )
    c = 1.0 + v2 * (
        -0.5
        + v2
        * (1.0 / 24 + v2 * (-1.0 / 720 + v2 * (1.0 / 40320 + v2 * (-1.0 / 3628800 + v2 / 479001600))))
    )
    odd = jnp.abs(quarter) == 1.0
    sine = jnp.where(odd, quarter * c, jnp.where(quarter == 0.0, s, -s))
    cosine = jnp.where(odd, -quarter * s, jnp.where(quarter == 0.0, c, -c))
    return sine, cosine


def center_rows(slots, cells, sites):
    cells_x, cells_y, cells_z = cells
    owned = cells_x * cells_y * cells_z * sites
    frame_count = (cells_x + 2) * (cells_y + 2) * (cells_z + 2) * sites
    site = slots % sites
    cell = slots // sites
    cell_z = cell % cells_z
    cell_y = cell // cells_z % cells_y
    cell_x = cell // (cells_z * cells_y)
    frame = (
        ((cell_x + 1) * (cells_y + 2) + cell_y + 1) * (cells_z + 2) + cell_z + 1
    ) * sites + site
    return jnp.where(slots < owned, frame, frame_count)


def target_rows(rows, cells, sites, kinds):
    spans = [count + 2 for count in cells]
    site = rows % sites
    cell = rows // sites
    places = (cell // (spans[1] * spans[2]), cell // spans[2] % spans[1], cell % spans[2])
    block = jnp.zeros_like(rows)
    slot = jnp.zeros_like(rows)
    for place, count, kind in zip(places, cells, kinds):
        above = place > count
        below = place < 1
        step = jnp.where(below, kind - 1, jnp.where(above, 1, 0))
        inside = jnp.where(below, count - 1, jnp.where(above, 0, place - 1))
        block = block * kind + step
        slot = slot * count + inside
    owned = cells[0] * cells[1] * cells[2] * sites
    target = block * owned + slot * sites + site
    return jnp.where(rows < spans[0] * spans[1] * spans[2] * sites, target, -1)


def force_kernel(
    cells,
    axes,
    kinds,
    gathered_ref,
    place_ref,
    own_ref,
    near_row_ref,
    target_row_ref,
    center_row_ref,
    center_slot_ref,
    species_ref,
    scale_ref,
    shift_ref,
    center_weight_ref,
    near_weight_ref,
    basis_weight_ref,
    path_weight_ref,
    value_weight_ref,
    latent_weight_ref,
    out_weight_ref,
    parts_ref,
    energy_ref,
    feats_ref,
    coords_ref,
):
    frame, width = feats_ref.shape
    owned = own_ref.shape[0]
    pairs = near_row_ref.shape[1]
    nbr = pairs // owned
    radial = basis_weight_ref.shape[0]
    spans = [count + 2 for count in cells]
    sites = frame // (spans[0] * spans[1] * spans[2])
    stride = gathered_ref.shape[0] // (axes[0] * axes[1] * axes[2])
    span = GROUP * nbr
    groups = owned // GROUP
    wide = GROUP * ORDERS
    root_count = math.sqrt(nbr)
    root_three = math.sqrt(3.0)
    root_fifteen = math.sqrt(15.0)
    root_five = math.sqrt(5.0)
    here = [place_ref[i] for i in range(3)]

    def shifted(axis, step):
        moved = here[axis] + step
        size = axes[axis]
        moved = jnp.where(moved >= size, moved - size, moved)
        return jnp.where(moved < 0, moved + size, moved)

    steps = [[shifted(axis, step) for step in (-1, 0, 1)] for axis in range(3)]

    def device(x, y, z):
        return (steps[0][x + 1] * axes[1] + steps[1][y + 1]) * axes[2] + steps[2][z + 1]

    tile_lane = lax.broadcasted_iota(jnp.int32, (sites, 128), 1)
    tile_row = lax.broadcasted_iota(jnp.int32, (sites, 128), 0)
    keep = (tile_lane % sites == tile_row) & (tile_lane < 3 * sites)
    component = tile_lane // sites
    for cell in range(spans[0] * spans[1] * spans[2]):
        place = (cell // (spans[1] * spans[2]), cell // spans[2] % spans[1], cell % spans[2])
        step = [(p > c) * 1 - (p < 1) * 1 for p, c in zip(place, cells)]
        inside = [(p - 1) % c for p, c in zip(place, cells)]
        local_cell = (inside[0] * cells[1] + inside[1]) * cells[2] + inside[2]
        base = device(*step) * stride
        start = pl.multiple_of(base + local_cell * sites, 8)
        feats_ref[cell * sites : (cell + 1) * sites, :] = gathered_ref[pl.ds(start, sites), :]
        row = gathered_ref[pl.ds(base + (owned + local_cell), 1), :]
        corner = [np.float32(p) * np.float32(CELL_SIDE) for p in place]
        offset = jnp.where(
            component == 0, corner[0], jnp.where(component == 1, corner[1], corner[2])
        )
        coords_ref[cell * sites : (cell + 1) * sites, :] = jnp.where(keep, row + offset, 0.0)

    value_t = jnp.transpose(value_weight_ref[...])
    latent_t = jnp.transpose(latent_weight_ref[...])
    value_rows = stacked(*split(value_t))
    latent_high_t, latent_low_t = split(latent_t)
    latent_both_t = jnp.concatenate([latent_high_t, latent_low_t], axis=0)
    latent_rows = stacked(*split(latent_weight_ref[...]))
    value_high, value_low = split(value_weight_ref[...])
    value_both = jnp.concatenate([value_high, value_low], axis=0)
    basis_t = jnp.transpose(basis_weight_ref[...])
    basis_high_t, basis_low_t = split(basis_t)
    basis_rows = stacked(*split(basis_weight_ref[...]))

    def project(weight, rows):
        high, low = split(rows)
        return folded(
            mm_nt(stacked(*split(jnp.transpose(weight))), jnp.concatenate([high, low], axis=1))
        )

    near_t = project(near_weight_ref[...], feats_ref[...])
    own_t = project(center_weight_ref[...], own_ref[...])
    near_high, near_low = split(near_t)
    own_high, own_low = split(own_t)
    lookup = jnp.concatenate(
        [
            jnp.concatenate([near_high, own_high, basis_high_t, basis_high_t], axis=1),
            jnp.concatenate([near_low, own_low, basis_low_t, jnp.zeros_like(basis_low_t)], axis=1),
        ],
        axis=0,
    )
    place_parts = jnp.concatenate(
        split3(jnp.transpose(coords_ref[...])[: 3 * sites]), axis=0
    )

    species = species_ref[...]
    scale_slot = jnp.zeros(species.shape, F32)
    shift_slot = jnp.zeros(species.shape, F32)
    for s in range(scale_ref.shape[0]):
        scale_slot = jnp.where(species == s, scale_ref[s], scale_slot)
        shift_slot = jnp.where(species == s, shift_ref[s], shift_slot)
    scale_parts = jnp.concatenate([*split3(scale_slot), jnp.zeros((13, owned), BF16)], axis=0)

    kind = lax.broadcasted_iota(jnp.int32, (ORDERS, width), 0)
    path_rows = jnp.where(
        kind == 0,
        path_weight_ref[0:1, :],
        jnp.where(
            kind < 4,
            path_weight_ref[1:2, :],
            jnp.where(kind < 9, path_weight_ref[2:3, :], 0.0),
        ),
    )
    paths_t = jnp.transpose(jnp.concatenate([path_rows] * GROUP, axis=0)) * (1.0 / root_count)
    out_column = jnp.transpose(jnp.broadcast_to(out_weight_ref[...], (width, width)))
    out_column = jnp.concatenate([out_column] * (pairs // width), axis=1)

    frame_ids = lax.broadcasted_iota(jnp.int32, (frame, pairs), 0)
    slot_ids = lax.broadcasted_iota(jnp.int32, (owned, pairs), 0)
    block_row = lax.broadcasted_iota(jnp.int32, (wide, span), 0) // ORDERS
    block_lane = lax.broadcasted_iota(jnp.int32, (wide, span), 1) // nbr
    block_mask = (block_row == block_lane).astype(F32)
    block_half = block_mask.astype(BF16)
    order = lax.broadcasted_iota(jnp.int32, (radial, pairs), 0).astype(F32) + 1.0
    lanes = [slice(g * span, (g + 1) * span) for g in range(groups)]

    near_row = near_row_ref[...]
    pick = jnp.where(frame_ids == near_row, 1.0, 0.0)
    from_center = jnp.where(frame_ids == center_row_ref[...], 1.0, 0.0)
    pick_half = pick.astype(BF16)
    slot_half = jnp.where(slot_ids == center_slot_ref[...], 1.0, 0.0).astype(BF16)
    live = near_row != frame

    moved = mm(place_parts, (pick - from_center).astype(BF16))
    moved = moved[: 3 * sites] + moved[3 * sites : 6 * sites] + moved[6 * sites :]
    dx = jnp.where(live, jnp.sum(moved[:sites], axis=0, keepdims=True), 6.0)
    dy = jnp.where(live, jnp.sum(moved[sites : 2 * sites], axis=0, keepdims=True), 0.0)
    dz = jnp.where(live, jnp.sum(moved[2 * sites :], axis=0, keepdims=True), 0.0)
    length = jnp.sqrt(dx * dx + dy * dy + dz * dz)
    inverse = 1.0 / length
    ratio = length * (1.0 / CUTOFF)
    inside = live & (ratio < 1.0)
    r2 = ratio * ratio
    r5 = r2 * r2 * ratio
    r6 = r5 * ratio
    weight = jnp.where(inside, 1.0 - r6 * (28.0 - 48.0 * ratio + 21.0 * r2), 0.0)
    slope = jnp.where(inside, -168.0 * r5 * (1.0 - 2.0 * ratio + r2), 0.0)
    sine, cosine = sin_cos_pi(order * ratio)
    basis = (math.sqrt(2.0 / CUTOFF) * inverse) * sine
    basis_slope = (math.sqrt(2.0 / CUTOFF) * inverse) * (
        (math.pi / CUTOFF) * order * cosine - sine * inverse
    )
    ex = dx * inverse
    ey = dy * inverse
    ez = dz * inverse
    angular = jnp.concatenate(
        [
            jnp.ones_like(ex),
            root_three * ex,
            root_three * ey,
            root_three * ez,
            root_fifteen * ex * ey,
            root_fifteen * ey * ez,
            0.5 * root_five * (3.0 * ez * ez - 1.0),
            root_fifteen * ex * ez,
            0.5 * root_fifteen * (ex * ex - ey * ey),
            jnp.zeros((ORDERS - 9, pairs), F32),
        ],
        axis=0,
    )
    angular_high, angular_low = split(angular)
    blocks = [
        jnp.concatenate(
            [
                jnp.concatenate([angular_high[:, cut]] * GROUP, axis=0) * block_half,
                jnp.concatenate([angular_low[:, cut]] * GROUP, axis=0) * block_half,
            ],
            axis=0,
        )
        for cut in lanes
    ]
    scale = mm(scale_parts, slot_half)
    scale = (scale[0:1] + scale[1:2] + scale[2:3]) * (1.0 / root_count)
    pull = ROOT_HALF * scale

    basis_high, basis_low = split(basis)
    before = folded(
        mm(lookup, jnp.concatenate([pick_half, slot_half, basis_high, basis_low], axis=0))
    )
    gate = 0.5 * jnp.tanh(0.5 * before) + 0.5
    active = before * gate
    latent = weight * active
    mixed = half_depth(value_rows, latent)
    values = mixed[:width]
    env_high, env_low = split(mixed[width:])

    def over_pairs(high, low):
        sums = []
        for cut, block in zip(lanes, blocks):
            quad = mm_nt(jnp.concatenate([high[:, cut], low[:, cut]], axis=0), block)
            sums.append((quad[:width, :wide] + quad[:width, wide:] + quad[width:, :wide]) * paths_t)
        return sums

    def over_orders(tables):
        parts = [folded(mm(stacked(*split(t)), block)) for t, block in zip(tables, blocks)]
        return jnp.concatenate(parts, axis=1)

    weighted = over_pairs(env_high, env_low)
    inner = over_orders(weighted)
    scalars = values * inner
    joined_high, joined_low = split(jnp.concatenate([latent, scalars], axis=0))
    z = full_depth(latent_both_t, latent_high_t, joined_high, joined_low)
    z_gate = 0.5 * jnp.tanh(0.5 * z) + 0.5
    update = z * z_gate
    update_out = update * out_column
    pair_energy = jnp.sum(latent * out_column + weight * update_out, axis=0, keepdims=True)
    pair_energy = pair_energy * pull
    d_z = (pull * weight) * out_column * (z_gate + update * (1.0 - z_gate))
    spread_back = half_depth(latent_rows, d_z)
    d_scalars = spread_back[width:]
    d_values = d_scalars * inner
    dinner_high, dinner_low = split(d_scalars * values)
    d_embed = over_pairs(dinner_high, dinner_low)
    d_env = over_orders(d_embed)

    d_angular = []
    for g, cut in enumerate(lanes):
        sides = jnp.transpose(jnp.concatenate([weighted[g], d_embed[g]], axis=0))
        sides_high, sides_low = split(sides)
        d_block = full_depth(
            jnp.concatenate([sides_high, sides_low], axis=0),
            sides_high,
            jnp.concatenate([dinner_high[:, cut], env_high[:, cut]], axis=0),
            jnp.concatenate([dinner_low[:, cut], env_low[:, cut]], axis=0),
        )
        d_block = d_block * block_mask
        total = d_block[:ORDERS]
        for k in range(1, GROUP):
            total = total + d_block[k * ORDERS : (k + 1) * ORDERS]
        d_angular.append(total)
    d_angular = jnp.concatenate(d_angular, axis=1)

    mixed_high, mixed_low = split(jnp.concatenate([d_values, d_env], axis=0))
    d_latent = (
        full_depth(value_both, value_high, mixed_high, mixed_low)
        + spread_back[:width]
        + pull * out_column
    )
    d_weight = jnp.sum(d_latent * active + pull * update_out, axis=0, keepdims=True)
    d_before = d_latent * weight * (gate + active * (1.0 - gate))
    d_basis = half_depth(basis_rows, d_before)

    d_length = jnp.sum(d_basis * basis_slope, axis=0, keepdims=True) + d_weight * slope * (
        1.0 / CUTOFF
    )
    a1, a2, a3, a4, a5, a6, a7, a8 = [d_angular[m : m + 1] for m in range(1, 9)]
    ux = root_three * a1 + root_fifteen * (ey * a4 + ez * a7 + ex * a8)
    uy = root_three * a2 + root_fifteen * (ex * a4 + ez * a5 - ey * a8)
    uz = root_three * a3 + root_fifteen * (ey * a5 + ex * a7) + 3.0 * root_five * ez * a6
    along = ex * ux + ey * uy + ez * uz
    radial_part = d_length - along * inverse
    gx = ux * inverse + ex * radial_part
    gy = uy * inverse + ey * radial_part
    gz = uz * inverse + ez * radial_part
    hx = -0.5 * dx
    hy = -0.5 * dy
    hz = -0.5 * dz
    virial = [hx * gx, hx * gy, hx * gz, hy * gx, hy * gy, hy * gz, hz * gx, hz * gy, hz * gz]
    near_terms = jnp.concatenate(
        [-gx, -gy, -gz, *virial, pair_energy, jnp.ones_like(gx), jnp.zeros((2, pairs), F32)],
        axis=0,
    )
    terms_high, terms_middle, terms_low = split3(near_terms)
    count = kinds[0] * kinds[1] * kinds[2]
    target_ids = lax.broadcasted_iota(jnp.int32, (count * owned, pairs), 0)
    reach = jnp.where(target_ids == target_row_ref[...], 1.0, 0.0).astype(BF16)
    totals = folded(mm_nt(jnp.concatenate([terms_high, terms_middle], axis=0), reach))
    own_sums = mm_nt(
        jnp.concatenate(
            [terms_high, terms_middle, terms_low, jnp.zeros((ORDERS, pairs), BF16)], axis=0
        ),
        slot_half,
    )
    sums = own_sums[:ORDERS] + own_sums[ORDERS : 2 * ORDERS] + own_sums[2 * ORDERS : 3 * ORDERS]
    energy_ref[...] = sums[12:13] + jnp.where(sums[13:14] > 0.5, shift_slot, 0.0)
    sign_row = lax.broadcasted_iota(jnp.int32, (ORDERS, owned), 0)
    center_terms = jnp.where(sign_row < 3, -sums, sums)
    center_terms = jnp.concatenate(
        [center_terms, jnp.zeros((ORDERS, 128 - owned), F32)], axis=1
    )

    parts_ref[...] = jnp.zeros(parts_ref.shape, F32)
    per_tile = 128 // owned
    half = ORDERS // 2
    padding = -count % per_tile * owned
    if padding:
        totals = jnp.concatenate([totals, jnp.zeros((ORDERS, padding), F32)], axis=1)
    lane = lax.broadcasted_iota(jnp.int32, (half, 128), 1)
    for block in range(count):
        choice = (block // (kinds[1] * kinds[2]), block // kinds[2] % kinds[1], block % kinds[2])
        step = [-1 if c == 2 else c for c in choice]
        column = block // per_tile * 128
        tile = totals[:, column : column + 128]
        if block == 0:
            tile = tile + center_terms
        turn = block % per_tile * owned
        first = tile[:half] if turn == 0 else pltpu.roll(tile[:half], 128 - turn, 1)
        back = (128 - turn + owned) % 128
        second = tile[half:] if back == 0 else pltpu.roll(tile[half:], back, 1)
        packed = jnp.where(lane < owned, first, jnp.where(lane < 2 * owned, second, 0.0))
        parts_ref[pl.ds(device(*step), 1)] = packed[None]


def local(
    positions,
    features,
    species,
    centers,
    neighbours,
    counts,
    species_scale,
    species_shift,
    center_weight,
    near_weight,
    basis_weight,
    path_weight,
    value_weight,
    latent_weight,
    out_weight,
):
    names = ("gx", "gy", "gz")
    cells_x, cells_y, cells_z, sites, width = features.shape
    cells = (cells_x, cells_y, cells_z)
    cell_count = cells_x * cells_y * cells_z
    owned = cell_count * sites
    frame_count = (cells_x + 2) * (cells_y + 2) * (cells_z + 2) * sites
    axes = tuple(lax.axis_size(name) for name in names)
    kinds = tuple(min(3, size) for size in axes)
    devices = axes[0] * axes[1] * axes[2]
    pairs = neighbours.size
    nbr = pairs // owned

    coords = jnp.transpose(positions, (1, 2, 3, 0, 4)).reshape(cell_count, 3 * sites)
    coords = jnp.pad(coords, ((0, -cell_count % 8), (0, width - 3 * sites)))
    payload = jnp.concatenate([features.reshape(owned, width), coords], axis=0)
    gathered = lax.all_gather(payload, names, tiled=True)

    near_row = neighbours.reshape(1, pairs)
    rows = center_rows(centers, cells, sites)
    center_row = jnp.broadcast_to(rows[:, None], (owned, nbr)).reshape(1, pairs)
    center_slot = jnp.broadcast_to(centers[:, None], (owned, nbr)).reshape(1, pairs)
    target_row = target_rows(near_row, cells, sites, kinds)
    place = jnp.stack([lax.axis_index(name) for name in names]).astype(jnp.int32)
    vmem = pl.BlockSpec(memory_space=pltpu.VMEM)
    smem = pl.BlockSpec(memory_space=pltpu.SMEM)
    parts, energy = pl.pallas_call(
        functools.partial(force_kernel, cells, axes, kinds),
        out_shape=(
            jax.ShapeDtypeStruct((devices, 8, 128), F32),
            jax.ShapeDtypeStruct((1, owned), F32),
        ),
        in_specs=[vmem, smem] + [vmem] * 6 + [smem] * 2 + [vmem] * 7,
        out_specs=(vmem, vmem),
        scratch_shapes=[
            pltpu.VMEM((frame_count, width), F32),
            pltpu.VMEM((frame_count, 128), F32),
        ],
        compiler_params=pltpu.CompilerParams(vmem_limit_bytes=40 * 1024 * 1024),
        name="pair_forces",
    )(
        gathered,
        place,
        features.reshape(owned, width),
        near_row,
        target_row,
        center_row,
        center_slot,
        species.reshape(1, owned),
        species_scale,
        species_shift,
        center_weight,
        near_weight,
        basis_weight,
        path_weight,
        value_weight,
        latent_weight,
        out_weight.reshape(1, width),
    )
    returned = lax.all_to_all(parts, names, split_axis=0, concat_axis=0, tiled=True)
    summed = jnp.sum(returned, axis=0)
    terms = jnp.concatenate([summed[:, :owned], summed[:, owned : 2 * owned]], axis=0)
    forces = terms[0:3].reshape(3, cells_x, cells_y, cells_z, sites)
    virial = terms[3:12].reshape(9, cells_x, cells_y, cells_z, sites)
    site_energy = energy.reshape(cells_x, cells_y, cells_z, sites)
    return (site_energy, forces, virial)


def solution(mesh):
    placed = (
        P(None, "gx", "gy", "gz", None),
        P("gx", "gy", "gz", None, None),
        P("gx", "gy", "gz", None),
        P(("gx", "gy", "gz")),
        P(("gx", "gy", "gz"), None),
        P(("gx", "gy", "gz")),
        P(),
        P(),
        P(),
        P(),
        P(),
        P(),
        P(),
        P(),
        P(),
    )
    return jax.shard_map(
        local,
        mesh=mesh,
        in_specs=placed,
        out_specs=(
            P("gx", "gy", "gz", None),
            P(None, "gx", "gy", "gz", None),
            P(None, "gx", "gy", "gz", None),
        ),
        check_vma=False,
    )
```

```python
import functools
import math

import jax
import jax.numpy as jnp
import numpy as np
from jax import lax
from jax.experimental import pallas as pl
from jax.experimental.pallas import tpu as pltpu
from jax.sharding import PartitionSpec as P

EXACT_DOT = lax.Precision.HIGHEST
CUTOFF = 5.0
CELL_SIDE = 4.6
ROOT_HALF = 0.7071067811865476
GROUP = 8
ORDERS = 16
F32 = jnp.float32
BF16 = jnp.bfloat16


def split(value):
    high = value.astype(BF16)
    low = (value - high.astype(F32)).astype(BF16)
    return high, low


def split3(value):
    high = value.astype(BF16)
    rest = value - high.astype(F32)
    middle = rest.astype(BF16)
    low = (rest - middle.astype(F32)).astype(BF16)
    return high, middle, low


def mm(a, b):
    return lax.dot_general(a, b, (((1,), (0,)), ((), ())), preferred_element_type=F32)


def mm_nt(a, b):
    return lax.dot_general(a, b, (((1,), (1,)), ((), ())), preferred_element_type=F32)


def stacked(high, low):
    top = jnp.concatenate([high, high], axis=1)
    bottom = jnp.concatenate([low, jnp.zeros_like(low)], axis=1)
    return jnp.concatenate([top, bottom], axis=0)


def folded(product):
    half = product.shape[0] // 2
    return product[:half] + product[half:]


def half_depth(weights, value):
    return folded(mm(weights, jnp.concatenate(split(value), axis=0)))


def full_depth(both, high, value_high, value_low):
    return folded(mm(both, value_high)) + mm(high, value_low)


def sin_cos_pi(turns):
    near = turns - 2.0 * jnp.round(turns * 0.5)
    quarter = jnp.round(near * 2.0)
    v = (near - 0.5 * quarter) * math.pi
    v2 = v * v
    s = v * (
        1.0
        + v2
        * (-1.0 / 6 + v2 * (1.0 / 120 + v2 * (-1.0 / 5040 + v2 * (1.0 / 362880 - v2 / 39916800))))
    )
    c = 1.0 + v2 * (
        -0.5
        + v2
        * (1.0 / 24 + v2 * (-1.0 / 720 + v2 * (1.0 / 40320 + v2 * (-1.0 / 3628800 + v2 / 479001600))))
    )
    odd = jnp.abs(quarter) == 1.0
    sine = jnp.where(odd, quarter * c, jnp.where(quarter == 0.0, s, -s))
    cosine = jnp.where(odd, -quarter * s, jnp.where(quarter == 0.0, c, -c))
    return sine, cosine


def center_rows(slots, cells, sites):
    cells_x, cells_y, cells_z = cells
    owned = cells_x * cells_y * cells_z * sites
    frame_count = (cells_x + 2) * (cells_y + 2) * (cells_z + 2) * sites
    site = slots % sites
    cell = slots // sites
    cell_z = cell % cells_z
    cell_y = cell // cells_z % cells_y
    cell_x = cell // (cells_z * cells_y)
    frame = (
        ((cell_x + 1) * (cells_y + 2) + cell_y + 1) * (cells_z + 2) + cell_z + 1
    ) * sites + site
    return jnp.where(slots < owned, frame, frame_count)


def target_rows(rows, cells, sites, kinds):
    spans = [count + 2 for count in cells]
    site = rows % sites
    cell = rows // sites
    places = (cell // (spans[1] * spans[2]), cell // spans[2] % spans[1], cell % spans[2])
    block = jnp.zeros_like(rows)
    slot = jnp.zeros_like(rows)
    for place, count, kind in zip(places, cells, kinds):
        above = place > count
        below = place < 1
        step = jnp.where(below, kind - 1, jnp.where(above, 1, 0))
        inside = jnp.where(below, count - 1, jnp.where(above, 0, place - 1))
        block = block * kind + step
        slot = slot * count + inside
    owned = cells[0] * cells[1] * cells[2] * sites
    target = block * owned + slot * sites + site
    return jnp.where(rows < spans[0] * spans[1] * spans[2] * sites, target, -1)


def force_kernel(
    cells,
    axes,
    kinds,
    *refs,
):
    pieces = refs[: kinds[0] * kinds[1] * kinds[2]]
    force_body(cells, axes, kinds, pieces, *refs[len(pieces) :])


def force_body(
    cells,
    axes,
    kinds,
    pieces,
    place_ref,
    own_ref,
    near_row_ref,
    target_row_ref,
    center_row_ref,
    center_slot_ref,
    species_ref,
    scale_ref,
    shift_ref,
    center_weight_ref,
    near_weight_ref,
    basis_weight_ref,
    path_weight_ref,
    value_weight_ref,
    latent_weight_ref,
    out_weight_ref,
    parts_ref,
    energy_ref,
    feats_ref,
    coords_ref,
):
    frame, width = feats_ref.shape
    owned = own_ref.shape[0]
    pairs = near_row_ref.shape[1]
    nbr = pairs // owned
    radial = basis_weight_ref.shape[0]
    spans = [count + 2 for count in cells]
    sites = frame // (spans[0] * spans[1] * spans[2])
    span = GROUP * nbr
    groups = owned // GROUP
    wide = GROUP * ORDERS
    root_count = math.sqrt(nbr)
    root_three = math.sqrt(3.0)
    root_fifteen = math.sqrt(15.0)
    root_five = math.sqrt(5.0)
    here = [place_ref[i] for i in range(3)]

    def shifted(axis, step):
        moved = here[axis] + step
        size = axes[axis]
        moved = jnp.where(moved >= size, moved - size, moved)
        return jnp.where(moved < 0, moved + size, moved)

    steps = [[shifted(axis, step) for step in (-1, 0, 1)] for axis in range(3)]

    def device(x, y, z):
        return (steps[0][x + 1] * axes[1] + steps[1][y + 1]) * axes[2] + steps[2][z + 1]

    tile_lane = lax.broadcasted_iota(jnp.int32, (sites, 128), 1)
    tile_row = lax.broadcasted_iota(jnp.int32, (sites, 128), 0)
    keep = (tile_lane % sites == tile_row) & (tile_lane < 3 * sites)
    component = tile_lane // sites
    for cell in range(spans[0] * spans[1] * spans[2]):
        place = (cell // (spans[1] * spans[2]), cell // spans[2] % spans[1], cell % spans[2])
        piece = 0
        inside = 0
        for p, count, kind in zip(place, cells, kinds):
            step = (p > count) * 1 - (p < 1) * 1
            whole = step == 0 or kind == 2
            piece = piece * kind + step % kind
            inside = inside * (count if whole else 1) + ((p - 1) % count if whole else 0)
        source = pieces[piece]
        total = (source.shape[0] - 8) // sites
        feats_ref[cell * sites : (cell + 1) * sites, :] = source[
            inside * sites : (inside + 1) * sites, :
        ]
        row = source[total * sites + inside : total * sites + inside + 1, :]
        corner = [np.float32(p) * np.float32(CELL_SIDE) for p in place]
        offset = jnp.where(
            component == 0, corner[0], jnp.where(component == 1, corner[1], corner[2])
        )
        coords_ref[cell * sites : (cell + 1) * sites, :] = jnp.where(keep, row + offset, 0.0)

    value_t = jnp.transpose(value_weight_ref[...])
    latent_t = jnp.transpose(latent_weight_ref[...])
    value_rows = stacked(*split(value_t))
    latent_high_t, latent_low_t = split(latent_t)
    latent_both_t = jnp.concatenate([latent_high_t, latent_low_t], axis=0)
    latent_rows = stacked(*split(latent_weight_ref[...]))
    value_high, value_low = split(value_weight_ref[...])
    value_both = jnp.concatenate([value_high, value_low], axis=0)
    basis_t = jnp.transpose(basis_weight_ref[...])
    basis_high_t, basis_low_t = split(basis_t)
    basis_rows = stacked(*split(basis_weight_ref[...]))

    def project(weight, rows):
        high, low = split(rows)
        return folded(
            mm_nt(stacked(*split(jnp.transpose(weight))), jnp.concatenate([high, low], axis=1))
        )

    near_t = project(near_weight_ref[...], feats_ref[...])
    own_t = project(center_weight_ref[...], own_ref[...])
    near_high, near_low = split(near_t)
    own_high, own_low = split(own_t)
    lookup = jnp.concatenate(
        [
            jnp.concatenate([near_high, own_high, basis_high_t, basis_high_t], axis=1),
            jnp.concatenate([near_low, own_low, basis_low_t, jnp.zeros_like(basis_low_t)], axis=1),
        ],
        axis=0,
    )
    place_parts = jnp.concatenate(
        split3(jnp.transpose(coords_ref[...])[: 3 * sites]), axis=0
    )

    species = species_ref[...]
    scale_slot = jnp.zeros(species.shape, F32)
    shift_slot = jnp.zeros(species.shape, F32)
    for s in range(scale_ref.shape[0]):
        scale_slot = jnp.where(species == s, scale_ref[s], scale_slot)
        shift_slot = jnp.where(species == s, shift_ref[s], shift_slot)
    scale_parts = jnp.concatenate([*split3(scale_slot), jnp.zeros((13, owned), BF16)], axis=0)

    kind = lax.broadcasted_iota(jnp.int32, (ORDERS, width), 0)
    path_rows = jnp.where(
        kind == 0,
        path_weight_ref[0:1, :],
        jnp.where(
            kind < 4,
            path_weight_ref[1:2, :],
            jnp.where(kind < 9, path_weight_ref[2:3, :], 0.0),
        ),
    )
    paths_t = jnp.transpose(jnp.concatenate([path_rows] * GROUP, axis=0)) * (1.0 / root_count)
    out_column = jnp.transpose(jnp.broadcast_to(out_weight_ref[...], (width, width)))
    out_column = jnp.concatenate([out_column] * (pairs // width), axis=1)

    frame_ids = lax.broadcasted_iota(jnp.int32, (frame, pairs), 0)
    slot_ids = lax.broadcasted_iota(jnp.int32, (owned, pairs), 0)
    block_row = lax.broadcasted_iota(jnp.int32, (wide, span), 0) // ORDERS
    block_lane = lax.broadcasted_iota(jnp.int32, (wide, span), 1) // nbr
    block_mask = (block_row == block_lane).astype(F32)
    block_half = block_mask.astype(BF16)
    order = lax.broadcasted_iota(jnp.int32, (radial, pairs), 0).astype(F32) + 1.0
    lanes = [slice(g * span, (g + 1) * span) for g in range(groups)]

    near_row = near_row_ref[...]
    pick = jnp.where(frame_ids == near_row, 1.0, 0.0)
    from_center = jnp.where(frame_ids == center_row_ref[...], 1.0, 0.0)
    pick_half = pick.astype(BF16)
    slot_half = jnp.where(slot_ids == center_slot_ref[...], 1.0, 0.0).astype(BF16)
    live = near_row != frame

    moved = mm(place_parts, (pick - from_center).astype(BF16))
    moved = moved[: 3 * sites] + moved[3 * sites : 6 * sites] + moved[6 * sites :]
    dx = jnp.where(live, jnp.sum(moved[:sites], axis=0, keepdims=True), 6.0)
    dy = jnp.where(live, jnp.sum(moved[sites : 2 * sites], axis=0, keepdims=True), 0.0)
    dz = jnp.where(live, jnp.sum(moved[2 * sites :], axis=0, keepdims=True), 0.0)
    length = jnp.sqrt(dx * dx + dy * dy + dz * dz)
    inverse = 1.0 / length
    ratio = length * (1.0 / CUTOFF)
    inside = live & (ratio < 1.0)
    r2 = ratio * ratio
    r5 = r2 * r2 * ratio
    r6 = r5 * ratio
    weight = jnp.where(inside, 1.0 - r6 * (28.0 - 48.0 * ratio + 21.0 * r2), 0.0)
    slope = jnp.where(inside, -168.0 * r5 * (1.0 - 2.0 * ratio + r2), 0.0)
    sine, cosine = sin_cos_pi(order * ratio)
    basis = (math.sqrt(2.0 / CUTOFF) * inverse) * sine
    basis_slope = (math.sqrt(2.0 / CUTOFF) * inverse) * (
        (math.pi / CUTOFF) * order * cosine - sine * inverse
    )
    ex = dx * inverse
    ey = dy * inverse
    ez = dz * inverse
    angular = jnp.concatenate(
        [
            jnp.ones_like(ex),
            root_three * ex,
            root_three * ey,
            root_three * ez,
            root_fifteen * ex * ey,
            root_fifteen * ey * ez,
            0.5 * root_five * (3.0 * ez * ez - 1.0),
            root_fifteen * ex * ez,
            0.5 * root_fifteen * (ex * ex - ey * ey),
            jnp.zeros((ORDERS - 9, pairs), F32),
        ],
        axis=0,
    )
    angular_high, angular_low = split(angular)
    blocks = [
        jnp.concatenate(
            [
                jnp.concatenate([angular_high[:, cut]] * GROUP, axis=0) * block_half,
                jnp.concatenate([angular_low[:, cut]] * GROUP, axis=0) * block_half,
            ],
            axis=0,
        )
        for cut in lanes
    ]
    scale = mm(scale_parts, slot_half)
    scale = (scale[0:1] + scale[1:2] + scale[2:3]) * (1.0 / root_count)
    pull = ROOT_HALF * scale

    basis_high, basis_low = split(basis)
    before = folded(
        mm(lookup, jnp.concatenate([pick_half, slot_half, basis_high, basis_low], axis=0))
    )
    gate = 0.5 * jnp.tanh(0.5 * before) + 0.5
    active = before * gate
    latent = weight * active
    mixed = half_depth(value_rows, latent)
    values = mixed[:width]
    env_high, env_low = split(mixed[width:])

    def over_pairs(high, low):
        sums = []
        for cut, block in zip(lanes, blocks):
            quad = mm_nt(jnp.concatenate([high[:, cut], low[:, cut]], axis=0), block)
            sums.append((quad[:width, :wide] + quad[:width, wide:] + quad[width:, :wide]) * paths_t)
        return sums

    def over_orders(tables):
        parts = [folded(mm(stacked(*split(t)), block)) for t, block in zip(tables, blocks)]
        return jnp.concatenate(parts, axis=1)

    weighted = over_pairs(env_high, env_low)
    inner = over_orders(weighted)
    scalars = values * inner
    joined_high, joined_low = split(jnp.concatenate([latent, scalars], axis=0))
    z = full_depth(latent_both_t, latent_high_t, joined_high, joined_low)
    z_gate = 0.5 * jnp.tanh(0.5 * z) + 0.5
    update = z * z_gate
    update_out = update * out_column
    pair_energy = jnp.sum(latent * out_column + weight * update_out, axis=0, keepdims=True)
    pair_energy = pair_energy * pull
    d_z = (pull * weight) * out_column * (z_gate + update * (1.0 - z_gate))
    spread_back = half_depth(latent_rows, d_z)
    d_scalars = spread_back[width:]
    d_values = d_scalars * inner
    dinner_high, dinner_low = split(d_scalars * values)
    d_embed = over_pairs(dinner_high, dinner_low)
    d_env = over_orders(d_embed)

    d_angular = []
    for g, cut in enumerate(lanes):
        sides = jnp.transpose(jnp.concatenate([weighted[g], d_embed[g]], axis=0))
        sides_high, sides_low = split(sides)
        d_block = full_depth(
            jnp.concatenate([sides_high, sides_low], axis=0),
            sides_high,
            jnp.concatenate([dinner_high[:, cut], env_high[:, cut]], axis=0),
            jnp.concatenate([dinner_low[:, cut], env_low[:, cut]], axis=0),
        )
        d_block = d_block * block_mask
        total = d_block[:ORDERS]
        for k in range(1, GROUP):
            total = total + d_block[k * ORDERS : (k + 1) * ORDERS]
        d_angular.append(total)
    d_angular = jnp.concatenate(d_angular, axis=1)

    mixed_high, mixed_low = split(jnp.concatenate([d_values, d_env], axis=0))
    d_latent = (
        full_depth(value_both, value_high, mixed_high, mixed_low)
        + spread_back[:width]
        + pull * out_column
    )
    d_weight = jnp.sum(d_latent * active + pull * update_out, axis=0, keepdims=True)
    d_before = d_latent * weight * (gate + active * (1.0 - gate))
    d_basis = half_depth(basis_rows, d_before)

    d_length = jnp.sum(d_basis * basis_slope, axis=0, keepdims=True) + d_weight * slope * (
        1.0 / CUTOFF
    )
    a1, a2, a3, a4, a5, a6, a7, a8 = [d_angular[m : m + 1] for m in range(1, 9)]
    ux = root_three * a1 + root_fifteen * (ey * a4 + ez * a7 + ex * a8)
    uy = root_three * a2 + root_fifteen * (ex * a4 + ez * a5 - ey * a8)
    uz = root_three * a3 + root_fifteen * (ey * a5 + ex * a7) + 3.0 * root_five * ez * a6
    along = ex * ux + ey * uy + ez * uz
    radial_part = d_length - along * inverse
    gx = ux * inverse + ex * radial_part
    gy = uy * inverse + ey * radial_part
    gz = uz * inverse + ez * radial_part
    hx = -0.5 * dx
    hy = -0.5 * dy
    hz = -0.5 * dz
    virial = [hx * gx, hx * gy, hx * gz, hy * gx, hy * gy, hy * gz, hz * gx, hz * gy, hz * gz]
    near_terms = jnp.concatenate(
        [-gx, -gy, -gz, *virial, pair_energy, jnp.ones_like(gx), jnp.zeros((2, pairs), F32)],
        axis=0,
    )
    terms_high, terms_middle, terms_low = split3(near_terms)
    count = kinds[0] * kinds[1] * kinds[2]
    target_ids = lax.broadcasted_iota(jnp.int32, (count * owned, pairs), 0)
    reach = jnp.where(target_ids == target_row_ref[...], 1.0, 0.0).astype(BF16)
    totals = folded(mm_nt(jnp.concatenate([terms_high, terms_middle], axis=0), reach))
    own_sums = mm_nt(
        jnp.concatenate(
            [terms_high, terms_middle, terms_low, jnp.zeros((ORDERS, pairs), BF16)], axis=0
        ),
        slot_half,
    )
    sums = own_sums[:ORDERS] + own_sums[ORDERS : 2 * ORDERS] + own_sums[2 * ORDERS : 3 * ORDERS]
    energy_ref[...] = sums[12:13] + jnp.where(sums[13:14] > 0.5, shift_slot, 0.0)
    sign_row = lax.broadcasted_iota(jnp.int32, (ORDERS, owned), 0)
    center_terms = jnp.where(sign_row < 3, -sums, sums)
    center_terms = jnp.concatenate(
        [center_terms, jnp.zeros((ORDERS, 128 - owned), F32)], axis=1
    )

    parts_ref[...] = jnp.zeros(parts_ref.shape, F32)
    per_tile = 128 // owned
    quarter = parts_ref.shape[1]
    padding = -count % per_tile * owned
    if padding:
        totals = jnp.concatenate([totals, jnp.zeros((ORDERS, padding), F32)], axis=1)
    lane = lax.broadcasted_iota(jnp.int32, (quarter, 128), 1)
    for block in range(count):
        choice = (block // (kinds[1] * kinds[2]), block // kinds[2] % kinds[1], block % kinds[2])
        step = [-1 if c == 2 else c for c in choice]
        column = block // per_tile * 128
        tile = totals[:, column : column + 128]
        if block == 0:
            tile = tile + center_terms
        packed = jnp.zeros((quarter, 128), F32)
        for part in range(12 // quarter):
            turn = (part - block % per_tile) * owned % 128
            rows = tile[part * quarter : (part + 1) * quarter]
            rows = pltpu.roll(rows, turn, 1) if turn else rows
            mine = (lane >= part * owned) & (lane < (part + 1) * owned)
            packed = jnp.where(mine, rows, packed)
        parts_ref[pl.ds(device(*step), 1)] = packed[None]


def local(
    positions,
    features,
    species,
    centers,
    neighbours,
    counts,
    species_scale,
    species_shift,
    center_weight,
    near_weight,
    basis_weight,
    path_weight,
    value_weight,
    latent_weight,
    out_weight,
):
    names = ("gx", "gy", "gz")
    cells_x, cells_y, cells_z, sites, width = features.shape
    cells = (cells_x, cells_y, cells_z)
    owned = cells_x * cells_y * cells_z * sites
    frame_count = (cells_x + 2) * (cells_y + 2) * (cells_z + 2) * sites
    axes = tuple(lax.axis_size(name) for name in names)
    kinds = tuple(min(3, size) for size in axes)
    devices = axes[0] * axes[1] * axes[2]
    pairs = neighbours.size
    nbr = pairs // owned

    coords = jnp.transpose(positions, (1, 2, 3, 0, 4)).reshape(*cells, 3 * sites)
    coords = jnp.pad(coords, ((0, 0), (0, 0), (0, 0), (0, width - 3 * sites)))
    pieces = []
    for choice in np.ndindex(*kinds):
        feats = features
        rows = coords
        step = [-1 if c == 2 else c for c in choice]
        for dim, (c, kind, count) in enumerate(zip(choice, kinds, cells)):
            if c == 0 or kind == 2:
                continue
            first = 0 if c == 1 else count - 1
            feats = lax.slice_in_dim(feats, first, first + 1, axis=dim)
            rows = lax.slice_in_dim(rows, first, first + 1, axis=dim)
        rows = rows.reshape(-1, width)
        rows = jnp.pad(rows, ((0, 8 - rows.shape[0]), (0, 0)))
        piece = jnp.concatenate([feats.reshape(-1, width), rows], axis=0)
        if any(step):
            route = []
            for at in np.ndindex(*axes):
                to = [(p - q) % size for p, q, size in zip(at, step, axes)]
                route.append(
                    (
                        (at[0] * axes[1] + at[1]) * axes[2] + at[2],
                        (to[0] * axes[1] + to[1]) * axes[2] + to[2],
                    )
                )
            piece = lax.ppermute(piece, names, route)
        pieces.append(piece)

    near_row = neighbours.reshape(1, pairs)
    rows = center_rows(centers, cells, sites)
    center_row = jnp.broadcast_to(rows[:, None], (owned, nbr)).reshape(1, pairs)
    center_slot = jnp.broadcast_to(centers[:, None], (owned, nbr)).reshape(1, pairs)
    target_row = target_rows(near_row, cells, sites, kinds)
    place = jnp.stack([lax.axis_index(name) for name in names]).astype(jnp.int32)
    vmem = pl.BlockSpec(memory_space=pltpu.VMEM)
    smem = pl.BlockSpec(memory_space=pltpu.SMEM)
    parts, energy = pl.pallas_call(
        functools.partial(force_kernel, cells, axes, kinds),
        out_shape=(
            jax.ShapeDtypeStruct((devices, 4, 128), F32),
            jax.ShapeDtypeStruct((1, owned), F32),
        ),
        in_specs=[vmem] * len(pieces) + [smem] + [vmem] * 6 + [smem] * 2 + [vmem] * 7,
        out_specs=(vmem, vmem),
        scratch_shapes=[
            pltpu.VMEM((frame_count, width), F32),
            pltpu.VMEM((frame_count, 128), F32),
        ],
        compiler_params=pltpu.CompilerParams(vmem_limit_bytes=40 * 1024 * 1024),
        name="pair_forces",
    )(
        *pieces,
        place,
        features.reshape(owned, width),
        near_row,
        target_row,
        center_row,
        center_slot,
        species.reshape(1, owned),
        species_scale,
        species_shift,
        center_weight,
        near_weight,
        basis_weight,
        path_weight,
        value_weight,
        latent_weight,
        out_weight.reshape(1, width),
    )
    returned = lax.all_to_all(parts, names, split_axis=0, concat_axis=0, tiled=True)
    summed = jnp.sum(returned, axis=0)
    terms = jnp.concatenate(
        [summed[:, :owned], summed[:, owned : 2 * owned], summed[:, 2 * owned : 3 * owned]], axis=0
    )
    forces = terms[0:3].reshape(3, cells_x, cells_y, cells_z, sites)
    virial = terms[3:12].reshape(9, cells_x, cells_y, cells_z, sites)
    site_energy = energy.reshape(cells_x, cells_y, cells_z, sites)
    return (site_energy, forces, virial)


def solution(mesh):
    placed = (
        P(None, "gx", "gy", "gz", None),
        P("gx", "gy", "gz", None, None),
        P("gx", "gy", "gz", None),
        P(("gx", "gy", "gz")),
        P(("gx", "gy", "gz"), None),
        P(("gx", "gy", "gz")),
        P(),
        P(),
        P(),
        P(),
        P(),
        P(),
        P(),
        P(),
        P(),
    )
    return jax.shard_map(
        local,
        mesh=mesh,
        in_specs=placed,
        out_specs=(
            P("gx", "gy", "gz", None),
            P(None, "gx", "gy", "gz", None),
            P(None, "gx", "gy", "gz", None),
        ),
        check_vma=False,
    )
```

```python
import functools
import math

import jax
import jax.numpy as jnp
import numpy as np
from jax import lax
from jax.experimental import pallas as pl
from jax.experimental.pallas import tpu as pltpu
from jax.sharding import PartitionSpec as P

EXACT_DOT = lax.Precision.HIGHEST
CUTOFF = 5.0
CELL_SIDE = 4.6
ROOT_HALF = 0.7071067811865476
GROUP = 8
ORDERS = 16
F32 = jnp.float32
BF16 = jnp.bfloat16


def split(value):
    high = value.astype(BF16)
    low = (value - high.astype(F32)).astype(BF16)
    return high, low


def split3(value):
    high = value.astype(BF16)
    rest = value - high.astype(F32)
    middle = rest.astype(BF16)
    low = (rest - middle.astype(F32)).astype(BF16)
    return high, middle, low


def mm(a, b):
    return lax.dot_general(a, b, (((1,), (0,)), ((), ())), preferred_element_type=F32)


def mm_nt(a, b):
    return lax.dot_general(a, b, (((1,), (1,)), ((), ())), preferred_element_type=F32)


def stacked(high, low):
    top = jnp.concatenate([high, high], axis=1)
    bottom = jnp.concatenate([low, jnp.zeros_like(low)], axis=1)
    return jnp.concatenate([top, bottom], axis=0)


def folded(product):
    half = product.shape[0] // 2
    return product[:half] + product[half:]


def half_depth(weights, value):
    return folded(mm(weights, jnp.concatenate(split(value), axis=0)))


def full_depth(both, high, value_high, value_low):
    return folded(mm(both, value_high)) + mm(high, value_low)


def sin_cos_pi(turns):
    near = turns - 2.0 * jnp.round(turns * 0.5)
    quarter = jnp.round(near * 2.0)
    v = (near - 0.5 * quarter) * math.pi
    v2 = v * v
    s = v * (
        1.0
        + v2
        * (-1.0 / 6 + v2 * (1.0 / 120 + v2 * (-1.0 / 5040 + v2 * (1.0 / 362880 - v2 / 39916800))))
    )
    c = 1.0 + v2 * (
        -0.5
        + v2
        * (1.0 / 24 + v2 * (-1.0 / 720 + v2 * (1.0 / 40320 + v2 * (-1.0 / 3628800 + v2 / 479001600))))
    )
    odd = jnp.abs(quarter) == 1.0
    sine = jnp.where(odd, quarter * c, jnp.where(quarter == 0.0, s, -s))
    cosine = jnp.where(odd, -quarter * s, jnp.where(quarter == 0.0, c, -c))
    return sine, cosine


def center_rows(slots, cells, sites):
    cells_x, cells_y, cells_z = cells
    owned = cells_x * cells_y * cells_z * sites
    frame_count = (cells_x + 2) * (cells_y + 2) * (cells_z + 2) * sites
    site = slots % sites
    cell = slots // sites
    cell_z = cell % cells_z
    cell_y = cell // cells_z % cells_y
    cell_x = cell // (cells_z * cells_y)
    frame = (
        ((cell_x + 1) * (cells_y + 2) + cell_y + 1) * (cells_z + 2) + cell_z + 1
    ) * sites + site
    return jnp.where(slots < owned, frame, frame_count)


def target_rows(rows, cells, sites, kinds):
    spans = [count + 2 for count in cells]
    site = rows % sites
    cell = rows // sites
    places = (cell // (spans[1] * spans[2]), cell // spans[2] % spans[1], cell % spans[2])
    block = jnp.zeros_like(rows)
    slot = jnp.zeros_like(rows)
    for place, count, kind in zip(places, cells, kinds):
        above = place > count
        below = place < 1
        step = jnp.where(below, kind - 1, jnp.where(above, 1, 0))
        inside = jnp.where(below, count - 1, jnp.where(above, 0, place - 1))
        block = block * kind + step
        slot = slot * count + inside
    owned = cells[0] * cells[1] * cells[2] * sites
    target = block * owned + slot * sites + site
    return jnp.where(rows < spans[0] * spans[1] * spans[2] * sites, target, -1)


def frame_places(count, kind):
    places = []
    for p in range(count + 2):
        if p < 1:
            places.append((kind - 1, count - 1))
        elif p > count:
            places.append((1, 0))
        else:
            places.append((0, p - 1))
    return places


def plane_cells(cells, kinds):
    sides = [list(dict.fromkeys(frame_places(cells[i], kinds[i]))) for i in (1, 2)]
    return [(y, z) for y in sides[0] for z in sides[1]]


def axis_place(place_ref, axis, step, size):
    moved = place_ref[axis] + (step if step < 2 else -1)
    moved = jnp.where(moved >= size, moved - size, moved)
    return jnp.where(moved < 0, moved + size, moved)


def plane_kernel(cells, axes, kinds, place_ref, group_ref, slabs_ref, send_ref):
    sites = 8
    owned = cells[0] * cells[1] * cells[2] * sites
    plane = plane_cells(cells, kinds)
    slabs_ref[...] = jnp.zeros(slabs_ref.shape, F32)
    for j, ((y, inside_y), (z, inside_z)) in enumerate(plane):
        member = axis_place(place_ref, 1, y, axes[1]) * axes[2] + axis_place(
            place_ref, 2, z, axes[2]
        )
        for x in range(cells[0]):
            cell = (x * cells[1] + inside_y) * cells[2] + inside_z
            slabs_ref[x, j * sites : (j + 1) * sites, :] = group_ref[
                pl.ds(member, 1), cell * sites : (cell + 1) * sites, :
            ][0]
            row = len(plane) * sites + j
            slabs_ref[x, row : row + 1, :] = group_ref[
                pl.ds(member, 1), owned + cell : owned + cell + 1, :
            ][0]
    for x in range(axes[0]):
        send_ref[x] = slabs_ref[0]
    send_ref[pl.ds(axis_place(place_ref, 0, 1, axes[0]), 1)] = slabs_ref[cells[0] - 1 :]


def force_kernel(
    cells,
    axes,
    kinds,
    slabs_ref,
    around_ref,
    place_ref,
    own_ref,
    near_row_ref,
    target_row_ref,
    center_row_ref,
    center_slot_ref,
    species_ref,
    scale_ref,
    shift_ref,
    center_weight_ref,
    near_weight_ref,
    basis_weight_ref,
    path_weight_ref,
    value_weight_ref,
    latent_weight_ref,
    out_weight_ref,
    parts_ref,
    energy_ref,
    feats_ref,
    coords_ref,
):
    frame, width = feats_ref.shape
    owned = own_ref.shape[0]
    pairs = near_row_ref.shape[1]
    nbr = pairs // owned
    radial = basis_weight_ref.shape[0]
    spans = [count + 2 for count in cells]
    sites = frame // (spans[0] * spans[1] * spans[2])
    span = GROUP * nbr
    groups = owned // GROUP
    wide = GROUP * ORDERS
    root_count = math.sqrt(nbr)
    root_three = math.sqrt(3.0)
    root_fifteen = math.sqrt(15.0)
    root_five = math.sqrt(5.0)
    def device(x, y, z):
        where = [axis_place(place_ref, i, step, axes[i]) for i, step in enumerate((x, y, z))]
        return (where[0] * axes[1] + where[1]) * axes[2] + where[2]

    tile_lane = lax.broadcasted_iota(jnp.int32, (sites, 128), 1)
    tile_row = lax.broadcasted_iota(jnp.int32, (sites, 128), 0)
    keep = (tile_lane % sites == tile_row) & (tile_lane < 3 * sites)
    component = tile_lane // sites
    plane = plane_cells(cells, kinds)
    beside = [axis_place(place_ref, 0, step, axes[0]) for step in range(3)]
    for cell in range(spans[0] * spans[1] * spans[2]):
        place = (cell // (spans[1] * spans[2]), cell // spans[2] % spans[1], cell % spans[2])
        around = [frame_places(c, k)[p] for p, c, k in zip(place, cells, kinds)]
        index = plane.index((around[1], around[2]))
        tile = slice(index * sites, (index + 1) * sites)
        mark = slice(len(plane) * sites + index, len(plane) * sites + index + 1)
        if around[0][0] == 0:
            feats = slabs_ref[around[0][1], tile, :]
            row = slabs_ref[around[0][1], mark, :]
        else:
            feats = around_ref[pl.ds(beside[around[0][0]], 1), tile, :][0]
            row = around_ref[pl.ds(beside[around[0][0]], 1), mark, :][0]
        feats_ref[cell * sites : (cell + 1) * sites, :] = feats
        corner = [np.float32(p) * np.float32(CELL_SIDE) for p in place]
        offset = jnp.where(
            component == 0, corner[0], jnp.where(component == 1, corner[1], corner[2])
        )
        coords_ref[cell * sites : (cell + 1) * sites, :] = jnp.where(keep, row + offset, 0.0)

    value_t = jnp.transpose(value_weight_ref[...])
    latent_t = jnp.transpose(latent_weight_ref[...])
    value_rows = stacked(*split(value_t))
    latent_high_t, latent_low_t = split(latent_t)
    latent_both_t = jnp.concatenate([latent_high_t, latent_low_t], axis=0)
    latent_rows = stacked(*split(latent_weight_ref[...]))
    value_high, value_low = split(value_weight_ref[...])
    value_both = jnp.concatenate([value_high, value_low], axis=0)
    basis_t = jnp.transpose(basis_weight_ref[...])
    basis_high_t, basis_low_t = split(basis_t)
    basis_rows = stacked(*split(basis_weight_ref[...]))

    def project(weight, rows):
        high, low = split(rows)
        return folded(
            mm_nt(stacked(*split(jnp.transpose(weight))), jnp.concatenate([high, low], axis=1))
        )

    near_t = project(near_weight_ref[...], feats_ref[...])
    own_t = project(center_weight_ref[...], own_ref[...])
    near_high, near_low = split(near_t)
    own_high, own_low = split(own_t)
    lookup = jnp.concatenate(
        [
            jnp.concatenate([near_high, own_high, basis_high_t, basis_high_t], axis=1),
            jnp.concatenate([near_low, own_low, basis_low_t, jnp.zeros_like(basis_low_t)], axis=1),
        ],
        axis=0,
    )
    place_parts = jnp.concatenate(
        split3(jnp.transpose(coords_ref[...])[: 3 * sites]), axis=0
    )

    species = species_ref[...]
    scale_slot = jnp.zeros(species.shape, F32)
    shift_slot = jnp.zeros(species.shape, F32)
    for s in range(scale_ref.shape[0]):
        scale_slot = jnp.where(species == s, scale_ref[s], scale_slot)
        shift_slot = jnp.where(species == s, shift_ref[s], shift_slot)
    scale_parts = jnp.concatenate([*split3(scale_slot), jnp.zeros((13, owned), BF16)], axis=0)

    kind = lax.broadcasted_iota(jnp.int32, (ORDERS, width), 0)
    path_rows = jnp.where(
        kind == 0,
        path_weight_ref[0:1, :],
        jnp.where(
            kind < 4,
            path_weight_ref[1:2, :],
            jnp.where(kind < 9, path_weight_ref[2:3, :], 0.0),
        ),
    )
    paths_t = jnp.transpose(jnp.concatenate([path_rows] * GROUP, axis=0)) * (1.0 / root_count)
    out_column = jnp.transpose(jnp.broadcast_to(out_weight_ref[...], (width, width)))
    out_column = jnp.concatenate([out_column] * (pairs // width), axis=1)

    frame_ids = lax.broadcasted_iota(jnp.int32, (frame, pairs), 0)
    slot_ids = lax.broadcasted_iota(jnp.int32, (owned, pairs), 0)
    block_row = lax.broadcasted_iota(jnp.int32, (wide, span), 0) // ORDERS
    block_lane = lax.broadcasted_iota(jnp.int32, (wide, span), 1) // nbr
    block_mask = (block_row == block_lane).astype(F32)
    block_half = block_mask.astype(BF16)
    order = lax.broadcasted_iota(jnp.int32, (radial, pairs), 0).astype(F32) + 1.0
    lanes = [slice(g * span, (g + 1) * span) for g in range(groups)]

    near_row = near_row_ref[...]
    pick = jnp.where(frame_ids == near_row, 1.0, 0.0)
    from_center = jnp.where(frame_ids == center_row_ref[...], 1.0, 0.0)
    pick_half = pick.astype(BF16)
    slot_half = jnp.where(slot_ids == center_slot_ref[...], 1.0, 0.0).astype(BF16)
    live = near_row != frame

    moved = mm(place_parts, (pick - from_center).astype(BF16))
    moved = moved[: 3 * sites] + moved[3 * sites : 6 * sites] + moved[6 * sites :]
    dx = jnp.where(live, jnp.sum(moved[:sites], axis=0, keepdims=True), 6.0)
    dy = jnp.where(live, jnp.sum(moved[sites : 2 * sites], axis=0, keepdims=True), 0.0)
    dz = jnp.where(live, jnp.sum(moved[2 * sites :], axis=0, keepdims=True), 0.0)
    length = jnp.sqrt(dx * dx + dy * dy + dz * dz)
    inverse = 1.0 / length
    ratio = length * (1.0 / CUTOFF)
    inside = live & (ratio < 1.0)
    r2 = ratio * ratio
    r5 = r2 * r2 * ratio
    r6 = r5 * ratio
    weight = jnp.where(inside, 1.0 - r6 * (28.0 - 48.0 * ratio + 21.0 * r2), 0.0)
    slope = jnp.where(inside, -168.0 * r5 * (1.0 - 2.0 * ratio + r2), 0.0)
    sine, cosine = sin_cos_pi(order * ratio)
    basis = (math.sqrt(2.0 / CUTOFF) * inverse) * sine
    basis_slope = (math.sqrt(2.0 / CUTOFF) * inverse) * (
        (math.pi / CUTOFF) * order * cosine - sine * inverse
    )
    ex = dx * inverse
    ey = dy * inverse
    ez = dz * inverse
    angular = jnp.concatenate(
        [
            jnp.ones_like(ex),
            root_three * ex,
            root_three * ey,
            root_three * ez,
            root_fifteen * ex * ey,
            root_fifteen * ey * ez,
            0.5 * root_five * (3.0 * ez * ez - 1.0),
            root_fifteen * ex * ez,
            0.5 * root_fifteen * (ex * ex - ey * ey),
            jnp.zeros((ORDERS - 9, pairs), F32),
        ],
        axis=0,
    )
    angular_high, angular_low = split(angular)
    blocks = [
        jnp.concatenate(
            [
                jnp.concatenate([angular_high[:, cut]] * GROUP, axis=0) * block_half,
                jnp.concatenate([angular_low[:, cut]] * GROUP, axis=0) * block_half,
            ],
            axis=0,
        )
        for cut in lanes
    ]
    scale = mm(scale_parts, slot_half)
    scale = (scale[0:1] + scale[1:2] + scale[2:3]) * (1.0 / root_count)
    pull = ROOT_HALF * scale

    basis_high, basis_low = split(basis)
    before = folded(
        mm(lookup, jnp.concatenate([pick_half, slot_half, basis_high, basis_low], axis=0))
    )
    gate = 0.5 * jnp.tanh(0.5 * before) + 0.5
    active = before * gate
    latent = weight * active
    mixed = half_depth(value_rows, latent)
    values = mixed[:width]
    env_high, env_low = split(mixed[width:])

    def over_pairs(high, low):
        sums = []
        for cut, block in zip(lanes, blocks):
            quad = mm_nt(jnp.concatenate([high[:, cut], low[:, cut]], axis=0), block)
            sums.append((quad[:width, :wide] + quad[:width, wide:] + quad[width:, :wide]) * paths_t)
        return sums

    def over_orders(tables):
        parts = [folded(mm(stacked(*split(t)), block)) for t, block in zip(tables, blocks)]
        return jnp.concatenate(parts, axis=1)

    weighted = over_pairs(env_high, env_low)
    inner = over_orders(weighted)
    scalars = values * inner
    joined_high, joined_low = split(jnp.concatenate([latent, scalars], axis=0))
    z = full_depth(latent_both_t, latent_high_t, joined_high, joined_low)
    z_gate = 0.5 * jnp.tanh(0.5 * z) + 0.5
    update = z * z_gate
    update_out = update * out_column
    pair_energy = jnp.sum(latent * out_column + weight * update_out, axis=0, keepdims=True)
    pair_energy = pair_energy * pull
    d_z = (pull * weight) * out_column * (z_gate + update * (1.0 - z_gate))
    spread_back = half_depth(latent_rows, d_z)
    d_scalars = spread_back[width:]
    d_values = d_scalars * inner
    dinner_high, dinner_low = split(d_scalars * values)
    d_embed = over_pairs(dinner_high, dinner_low)
    d_env = over_orders(d_embed)

    d_angular = []
    for g, cut in enumerate(lanes):
        sides = jnp.transpose(jnp.concatenate([weighted[g], d_embed[g]], axis=0))
        sides_high, sides_low = split(sides)
        d_block = full_depth(
            jnp.concatenate([sides_high, sides_low], axis=0),
            sides_high,
            jnp.concatenate([dinner_high[:, cut], env_high[:, cut]], axis=0),
            jnp.concatenate([dinner_low[:, cut], env_low[:, cut]], axis=0),
        )
        d_block = d_block * block_mask
        total = d_block[:ORDERS]
        for k in range(1, GROUP):
            total = total + d_block[k * ORDERS : (k + 1) * ORDERS]
        d_angular.append(total)
    d_angular = jnp.concatenate(d_angular, axis=1)

    mixed_high, mixed_low = split(jnp.concatenate([d_values, d_env], axis=0))
    d_latent = (
        full_depth(value_both, value_high, mixed_high, mixed_low)
        + spread_back[:width]
        + pull * out_column
    )
    d_weight = jnp.sum(d_latent * active + pull * update_out, axis=0, keepdims=True)
    d_before = d_latent * weight * (gate + active * (1.0 - gate))
    d_basis = half_depth(basis_rows, d_before)

    d_length = jnp.sum(d_basis * basis_slope, axis=0, keepdims=True) + d_weight * slope * (
        1.0 / CUTOFF
    )
    a1, a2, a3, a4, a5, a6, a7, a8 = [d_angular[m : m + 1] for m in range(1, 9)]
    ux = root_three * a1 + root_fifteen * (ey * a4 + ez * a7 + ex * a8)
    uy = root_three * a2 + root_fifteen * (ex * a4 + ez * a5 - ey * a8)
    uz = root_three * a3 + root_fifteen * (ey * a5 + ex * a7) + 3.0 * root_five * ez * a6
    along = ex * ux + ey * uy + ez * uz
    radial_part = d_length - along * inverse
    gx = ux * inverse + ex * radial_part
    gy = uy * inverse + ey * radial_part
    gz = uz * inverse + ez * radial_part
    hx = -0.5 * dx
    hy = -0.5 * dy
    hz = -0.5 * dz
    virial = [hx * gx, hx * gy, hx * gz, hy * gx, hy * gy, hy * gz, hz * gx, hz * gy, hz * gz]
    near_terms = jnp.concatenate(
        [-gx, -gy, -gz, *virial, pair_energy, jnp.ones_like(gx), jnp.zeros((2, pairs), F32)],
        axis=0,
    )
    terms_high, terms_middle, terms_low = split3(near_terms)
    count = kinds[0] * kinds[1] * kinds[2]
    target_ids = lax.broadcasted_iota(jnp.int32, (count * owned, pairs), 0)
    reach = jnp.where(target_ids == target_row_ref[...], 1.0, 0.0).astype(BF16)
    totals = folded(mm_nt(jnp.concatenate([terms_high, terms_middle], axis=0), reach))
    own_sums = mm_nt(
        jnp.concatenate(
            [terms_high, terms_middle, terms_low, jnp.zeros((ORDERS, pairs), BF16)], axis=0
        ),
        slot_half,
    )
    sums = own_sums[:ORDERS] + own_sums[ORDERS : 2 * ORDERS] + own_sums[2 * ORDERS : 3 * ORDERS]
    energy_ref[...] = sums[12:13] + jnp.where(sums[13:14] > 0.5, shift_slot, 0.0)
    sign_row = lax.broadcasted_iota(jnp.int32, (ORDERS, owned), 0)
    center_terms = jnp.where(sign_row < 3, -sums, sums)
    center_terms = jnp.concatenate(
        [center_terms, jnp.zeros((ORDERS, 128 - owned), F32)], axis=1
    )

    parts_ref[...] = jnp.zeros(parts_ref.shape, F32)
    per_tile = 128 // owned
    quarter = parts_ref.shape[1]
    padding = -count % per_tile * owned
    if padding:
        totals = jnp.concatenate([totals, jnp.zeros((ORDERS, padding), F32)], axis=1)
    lane = lax.broadcasted_iota(jnp.int32, (quarter, 128), 1)
    for block in range(count):
        choice = (block // (kinds[1] * kinds[2]), block // kinds[2] % kinds[1], block % kinds[2])
        column = block // per_tile * 128
        tile = totals[:, column : column + 128]
        if block == 0:
            tile = tile + center_terms
        packed = jnp.zeros((quarter, 128), F32)
        for part in range(12 // quarter):
            turn = (part - block % per_tile) * owned % 128
            rows = tile[part * quarter : (part + 1) * quarter]
            rows = pltpu.roll(rows, turn, 1) if turn else rows
            mine = (lane >= part * owned) & (lane < (part + 1) * owned)
            packed = jnp.where(mine, rows, packed)
        parts_ref[pl.ds(device(*choice), 1)] = packed[None]


def local(
    positions,
    features,
    species,
    centers,
    neighbours,
    counts,
    species_scale,
    species_shift,
    center_weight,
    near_weight,
    basis_weight,
    path_weight,
    value_weight,
    latent_weight,
    out_weight,
):
    names = ("gx", "gy", "gz")
    cells_x, cells_y, cells_z, sites, width = features.shape
    cells = (cells_x, cells_y, cells_z)
    owned = cells_x * cells_y * cells_z * sites
    frame_count = (cells_x + 2) * (cells_y + 2) * (cells_z + 2) * sites
    axes = tuple(lax.axis_size(name) for name in names)
    kinds = tuple(min(3, size) for size in axes)
    devices = axes[0] * axes[1] * axes[2]
    pairs = neighbours.size
    nbr = pairs // owned

    place = jnp.stack([lax.axis_index(name) for name in names]).astype(jnp.int32)
    vmem = pl.BlockSpec(memory_space=pltpu.VMEM)
    smem = pl.BlockSpec(memory_space=pltpu.SMEM)
    cell_count = cells_x * cells_y * cells_z
    coords = jnp.transpose(positions, (1, 2, 3, 0, 4)).reshape(cell_count, 3 * sites)
    coords = jnp.pad(coords, ((0, -cell_count % 8), (0, width - 3 * sites)))
    payload = jnp.concatenate([features.reshape(owned, width), coords], axis=0)
    payload = jnp.broadcast_to(payload[None], (axes[1] * axes[2], *payload.shape))
    group = lax.all_to_all(payload, ("gy", "gz"), split_axis=0, concat_axis=0, tiled=True)
    plane = len(plane_cells(cells, kinds))
    height = plane * sites + plane + -plane % 8
    slabs, send = pl.pallas_call(
        functools.partial(plane_kernel, cells, axes, kinds),
        out_shape=(
            jax.ShapeDtypeStruct((cells_x, height, width), F32),
            jax.ShapeDtypeStruct((axes[0], height, width), F32),
        ),
        in_specs=[smem, vmem],
        out_specs=(vmem, vmem),
        name="x_slabs",
    )(place, group)
    around = lax.all_to_all(send, "gx", split_axis=0, concat_axis=0, tiled=True)

    near_row = neighbours.reshape(1, pairs)
    rows = center_rows(centers, cells, sites)
    center_row = jnp.broadcast_to(rows[:, None], (owned, nbr)).reshape(1, pairs)
    center_slot = jnp.broadcast_to(centers[:, None], (owned, nbr)).reshape(1, pairs)
    target_row = target_rows(near_row, cells, sites, kinds)
    parts, energy = pl.pallas_call(
        functools.partial(force_kernel, cells, axes, kinds),
        out_shape=(
            jax.ShapeDtypeStruct((devices, 4, 128), F32),
            jax.ShapeDtypeStruct((1, owned), F32),
        ),
        in_specs=[vmem] * 2 + [smem] + [vmem] * 6 + [smem] * 2 + [vmem] * 7,
        out_specs=(vmem, vmem),
        scratch_shapes=[
            pltpu.VMEM((frame_count, width), F32),
            pltpu.VMEM((frame_count, 128), F32),
        ],
        compiler_params=pltpu.CompilerParams(vmem_limit_bytes=40 * 1024 * 1024),
        name="pair_forces",
    )(
        slabs,
        around,
        place,
        features.reshape(owned, width),
        near_row,
        target_row,
        center_row,
        center_slot,
        species.reshape(1, owned),
        species_scale,
        species_shift,
        center_weight,
        near_weight,
        basis_weight,
        path_weight,
        value_weight,
        latent_weight,
        out_weight.reshape(1, width),
    )
    returned = lax.all_to_all(parts, names, split_axis=0, concat_axis=0, tiled=True)
    summed = jnp.sum(returned, axis=0)
    terms = jnp.concatenate(
        [summed[:, :owned], summed[:, owned : 2 * owned], summed[:, 2 * owned : 3 * owned]], axis=0
    )
    forces = terms[0:3].reshape(3, cells_x, cells_y, cells_z, sites)
    virial = terms[3:12].reshape(9, cells_x, cells_y, cells_z, sites)
    site_energy = energy.reshape(cells_x, cells_y, cells_z, sites)
    return (site_energy, forces, virial)


def solution(mesh):
    placed = (
        P(None, "gx", "gy", "gz", None),
        P("gx", "gy", "gz", None, None),
        P("gx", "gy", "gz", None),
        P(("gx", "gy", "gz")),
        P(("gx", "gy", "gz"), None),
        P(("gx", "gy", "gz")),
        P(),
        P(),
        P(),
        P(),
        P(),
        P(),
        P(),
        P(),
        P(),
    )
    return jax.shard_map(
        local,
        mesh=mesh,
        in_specs=placed,
        out_specs=(
            P("gx", "gy", "gz", None),
            P(None, "gx", "gy", "gz", None),
            P(None, "gx", "gy", "gz", None),
        ),
        check_vma=False,
    )
```

```python
import functools
import math

import jax
import jax.numpy as jnp
import numpy as np
from jax import lax
from jax.experimental import pallas as pl
from jax.experimental.pallas import tpu as pltpu
from jax.sharding import PartitionSpec as P

EXACT_DOT = lax.Precision.HIGHEST
CUTOFF = 5.0
CELL_SIDE = 4.6
ROOT_HALF = 0.7071067811865476
GROUP = 8
ORDERS = 16
SITES = 8
OWN_CELLS = 4
FRAME_CELLS = 48
F32 = jnp.float32
BF16 = jnp.bfloat16


def split(value):
    high = value.astype(BF16)
    low = (value - high.astype(F32)).astype(BF16)
    return high, low


def split3(value):
    high = value.astype(BF16)
    rest = value - high.astype(F32)
    middle = rest.astype(BF16)
    low = (rest - middle.astype(F32)).astype(BF16)
    return high, middle, low


def mm(a, b):
    return lax.dot_general(a, b, (((1,), (0,)), ((), ())), preferred_element_type=F32)


def mm_nt(a, b):
    return lax.dot_general(a, b, (((1,), (1,)), ((), ())), preferred_element_type=F32)


def stacked(high, low):
    top = jnp.concatenate([high, high], axis=1)
    bottom = jnp.concatenate([low, jnp.zeros_like(low)], axis=1)
    return jnp.concatenate([top, bottom], axis=0)


def folded(product):
    half = product.shape[0] // 2
    return product[:half] + product[half:]


def half_depth(weights, value):
    return folded(mm(weights, jnp.concatenate(split(value), axis=0)))


def full_depth(both, high, value_high, value_low):
    return folded(mm(both, value_high)) + mm(high, value_low)


def sin_cos_pi(turns):
    near = turns - 2.0 * jnp.round(turns * 0.5)
    quarter = jnp.round(near * 2.0)
    v = (near - 0.5 * quarter) * math.pi
    v2 = v * v
    s = v * (
        1.0
        + v2
        * (-1.0 / 6 + v2 * (1.0 / 120 + v2 * (-1.0 / 5040 + v2 * (1.0 / 362880 - v2 / 39916800))))
    )
    c = 1.0 + v2 * (
        -0.5
        + v2
        * (1.0 / 24 + v2 * (-1.0 / 720 + v2 * (1.0 / 40320 + v2 * (-1.0 / 3628800 + v2 / 479001600))))
    )
    odd = jnp.abs(quarter) == 1.0
    sine = jnp.where(odd, quarter * c, jnp.where(quarter == 0.0, s, -s))
    cosine = jnp.where(odd, -quarter * s, jnp.where(quarter == 0.0, c, -c))
    return sine, cosine


def exact(a, b):
    return jnp.dot(a, b, precision=EXACT_DOT, preferred_element_type=F32)


def list_kernel(kind, centers_ref, neighbours_ref, codes_ref):
    owned, nbr = neighbours_ref.shape
    per_row = 128 // nbr
    chosen = lax.broadcasted_iota(jnp.int32, (owned, owned), 0) == centers_ref[...]
    chosen = jnp.where(chosen, 1.0, 0.0)
    occupied = jnp.sum(chosen, axis=1, keepdims=True) > 0.5
    rows = exact(chosen, neighbours_ref[...].astype(F32)).astype(jnp.int32)
    live = occupied & (rows < FRAME_CELLS * SITES)
    slot = lax.broadcasted_iota(jnp.int32, (owned, nbr), 0)
    cell = slot >> 3
    site = rows & 7
    place = rows >> 3
    near_z = (place & 3) + 1 - 2 * (cell & 1)
    column = place >> 2
    frame_x = (column * 11) >> 5
    frame_y = column - 3 * frame_x
    near_x = frame_x + 1 - 2 * (cell >> 1)
    side = jnp.where(frame_y == 1, 0, jnp.where(frame_y == 2, 1, kind - 1))
    block = (near_z >> 1) * 2 + (near_x >> 1)
    where = (block * kind + side) * owned + (near_x & 1) * 16 + (near_z & 1) * 8 + site
    code = jnp.where(live, 1 + where + (frame_y << 10), 0).astype(F32)
    lane = lax.broadcasted_iota(jnp.int32, (nbr, 128), 1)
    spread = jnp.where(lax.broadcasted_iota(jnp.int32, (nbr, 128), 0) == lane % nbr, 1.0, 0.0)
    wide = exact(code, spread)
    row = lax.broadcasted_iota(jnp.int32, (owned, 128), 0)
    lane = lax.broadcasted_iota(jnp.int32, (owned, 128), 1)
    wide = jnp.where(row % per_row == lane // nbr, wide, 0.0)
    fold = lax.broadcasted_iota(jnp.int32, (owned // per_row, owned), 1) // per_row
    fold = jnp.where(
        fold == lax.broadcasted_iota(jnp.int32, (owned // per_row, owned), 0), 1.0, 0.0
    )
    codes_ref[...] = exact(fold, wide)


def force_kernel(
    kind,
    nbr,
    here_ref,
    next_x_ref,
    next_z_ref,
    center_weight_ref,
    near_weight_ref,
    basis_weight_ref,
    path_weight_ref,
    value_weight_ref,
    latent_weight_ref,
    out_weight_ref,
    totals_ref,
):
    height, width = here_ref.shape
    owned = OWN_CELLS * SITES
    feats_rows = kind * owned
    coord_rows = kind * OWN_CELLS + -kind * OWN_CELLS % 8
    pairs = owned * nbr
    radial = basis_weight_ref.shape[0]
    span = GROUP * nbr
    groups = owned // GROUP
    wide = GROUP * ORDERS
    sites = SITES
    blocks_in = [
        here_ref[...],
        next_x_ref[...],
        next_z_ref[:height],
        next_z_ref[height:],
    ]
    root_count = math.sqrt(nbr)
    root_three = math.sqrt(3.0)
    root_fifteen = math.sqrt(15.0)
    root_five = math.sqrt(5.0)
    feats = jnp.concatenate([block[:feats_rows] for block in blocks_in], axis=0)
    known = feats.shape[0]
    center_feats = []
    coords = []
    scales = []
    codes = []
    cell_row = lax.broadcasted_iota(jnp.int32, (kind * OWN_CELLS, 128), 0) % OWN_CELLS
    tile_lane = lax.broadcasted_iota(jnp.int32, (kind * OWN_CELLS, 128), 1)
    for g, block in enumerate(blocks_in):
        ahead_x, ahead_z = g % 2, g // 2
        cell = (1 - ahead_x) * 2 + 1 - ahead_z
        center_feats.append(block[cell * sites : (cell + 1) * sites])
        rows = block[feats_rows : feats_rows + kind * OWN_CELLS]
        scales.append(rows[cell : cell + 1])
        corner_x = (cell_row // 2 + 2 * ahead_x).astype(F32) * CELL_SIDE
        corner_z = (cell_row % 2 + 2 * ahead_z).astype(F32) * CELL_SIDE
        corner = jnp.where(
            tile_lane < sites, corner_x, jnp.where(tile_lane < 2 * sites, 0.0, corner_z)
        )
        coords.append(rows + corner)
        start = feats_rows + coord_rows + cell * span // 128
        codes.extend(block[start + r : start + r + 1] for r in range(span // 128))
    center_feats = jnp.concatenate(center_feats, axis=0)
    coords = jnp.concatenate(coords, axis=0)
    code = jnp.concatenate(codes, axis=1).astype(jnp.int32)
    live = code > 0
    code = jnp.maximum(code - 1, 0)
    side_y = ((code >> 10) - 1).astype(F32)
    near_row = jnp.where(live, code & 1023, known)

    spread = jnp.broadcast_to(coords[:, None, :], (coords.shape[0], sites, 128))
    spread = spread.reshape(known, 128)
    keep_lane = lax.broadcasted_iota(jnp.int32, (known, 128), 1)
    keep_row = lax.broadcasted_iota(jnp.int32, (known, 128), 0)
    keep = (keep_lane % sites == keep_row % sites) & (keep_lane < 3 * sites)
    spread = jnp.where(keep, spread, 0.0)
    place_parts = jnp.concatenate(split3(jnp.transpose(spread)[: 3 * sites]), axis=0)

    value_t = jnp.transpose(value_weight_ref[...])
    latent_t = jnp.transpose(latent_weight_ref[...])
    value_rows = stacked(*split(value_t))
    latent_high_t, latent_low_t = split(latent_t)
    latent_both_t = jnp.concatenate([latent_high_t, latent_low_t], axis=0)
    latent_rows = stacked(*split(latent_weight_ref[...]))
    value_high, value_low = split(value_weight_ref[...])
    value_both = jnp.concatenate([value_high, value_low], axis=0)
    basis_t = jnp.transpose(basis_weight_ref[...])
    basis_high_t, basis_low_t = split(basis_t)
    basis_rows = stacked(*split(basis_weight_ref[...]))

    def project(weight, rows):
        high, low = split(rows)
        return folded(
            mm_nt(stacked(*split(jnp.transpose(weight))), jnp.concatenate([high, low], axis=1))
        )

    near_t = project(near_weight_ref[...], feats)
    own_t = project(center_weight_ref[...], center_feats)
    near_high, near_low = split(near_t)
    own_high, own_low = split(own_t)
    lookup = jnp.concatenate(
        [
            jnp.concatenate([near_high, own_high, basis_high_t, basis_high_t], axis=1),
            jnp.concatenate([near_low, own_low, basis_low_t, jnp.zeros_like(basis_low_t)], axis=1),
        ],
        axis=0,
    )
    scale_rows = jnp.concatenate(scales, axis=0)
    scale_parts = jnp.concatenate(
        [*split3(scale_rows), jnp.zeros((16 - 3 * groups, 128), BF16)], axis=0
    )

    level = lax.broadcasted_iota(jnp.int32, (ORDERS, width), 0)
    path_rows = jnp.where(
        level == 0,
        path_weight_ref[0:1, :],
        jnp.where(
            level < 4,
            path_weight_ref[1:2, :],
            jnp.where(level < 9, path_weight_ref[2:3, :], 0.0),
        ),
    )
    paths_t = jnp.transpose(jnp.concatenate([path_rows] * GROUP, axis=0)) * (1.0 / root_count)
    out_column = jnp.transpose(jnp.broadcast_to(out_weight_ref[...], (width, width)))
    out_column = jnp.concatenate([out_column] * (pairs // width), axis=1)

    site_ids = lax.broadcasted_iota(jnp.int32, (known, pairs), 0)
    slot_ids = lax.broadcasted_iota(jnp.int32, (owned, pairs), 0)
    slot_row = lax.broadcasted_iota(jnp.int32, (1, pairs), 1) // nbr
    group_row = slot_row // GROUP
    center_cell = (1 - group_row % 2) * 2 + 1 - group_row // 2
    center_row = group_row * feats_rows + center_cell * sites + slot_row % GROUP
    block_row = lax.broadcasted_iota(jnp.int32, (wide, span), 0) // ORDERS
    block_lane = lax.broadcasted_iota(jnp.int32, (wide, span), 1) // nbr
    block_mask = (block_row == block_lane).astype(F32)
    block_half = block_mask.astype(BF16)
    order = lax.broadcasted_iota(jnp.int32, (radial, pairs), 0).astype(F32) + 1.0
    lanes = [slice(g * span, (g + 1) * span) for g in range(groups)]

    pick = jnp.where(site_ids == near_row, 1.0, 0.0)
    from_center = jnp.where(site_ids == center_row, 1.0, 0.0)
    pick_half = pick.astype(BF16)
    center_half = from_center.astype(BF16)
    slot_half = jnp.where(slot_ids == slot_row, 1.0, 0.0).astype(BF16)

    moved = mm(place_parts, (pick - from_center).astype(BF16))
    moved = moved[: 3 * sites] + moved[3 * sites : 6 * sites] + moved[6 * sites :]
    dx = jnp.where(live, jnp.sum(moved[:sites], axis=0, keepdims=True), 6.0)
    dy = jnp.sum(moved[sites : 2 * sites], axis=0, keepdims=True) + CELL_SIDE * side_y
    dy = jnp.where(live, dy, 0.0)
    dz = jnp.where(live, jnp.sum(moved[2 * sites :], axis=0, keepdims=True), 0.0)
    length = jnp.sqrt(dx * dx + dy * dy + dz * dz)
    inverse = 1.0 / length
    ratio = length * (1.0 / CUTOFF)
    inside = live & (ratio < 1.0)
    r2 = ratio * ratio
    r5 = r2 * r2 * ratio
    r6 = r5 * ratio
    weight = jnp.where(inside, 1.0 - r6 * (28.0 - 48.0 * ratio + 21.0 * r2), 0.0)
    slope = jnp.where(inside, -168.0 * r5 * (1.0 - 2.0 * ratio + r2), 0.0)
    sine, cosine = sin_cos_pi(order * ratio)
    basis = (math.sqrt(2.0 / CUTOFF) * inverse) * sine
    basis_slope = (math.sqrt(2.0 / CUTOFF) * inverse) * (
        (math.pi / CUTOFF) * order * cosine - sine * inverse
    )
    ex = dx * inverse
    ey = dy * inverse
    ez = dz * inverse
    angular = jnp.concatenate(
        [
            jnp.ones_like(ex),
            root_three * ex,
            root_three * ey,
            root_three * ez,
            root_fifteen * ex * ey,
            root_fifteen * ey * ez,
            0.5 * root_five * (3.0 * ez * ez - 1.0),
            root_fifteen * ex * ez,
            0.5 * root_fifteen * (ex * ex - ey * ey),
            jnp.zeros((ORDERS - 9, pairs), F32),
        ],
        axis=0,
    )
    angular_high, angular_low = split(angular)
    blocks = [
        jnp.concatenate(
            [
                jnp.concatenate([angular_high[:, cut]] * GROUP, axis=0) * block_half,
                jnp.concatenate([angular_low[:, cut]] * GROUP, axis=0) * block_half,
            ],
            axis=0,
        )
        for cut in lanes
    ]
    lane_ids = lax.broadcasted_iota(jnp.int32, (128, span), 0)
    lane_slot = lax.broadcasted_iota(jnp.int32, (128, span), 1) // nbr + 3 * sites
    scale = mm(scale_parts, jnp.where(lane_ids == lane_slot, 1.0, 0.0).astype(BF16))
    scale = scale[:groups] + scale[groups : 2 * groups] + scale[2 * groups : 3 * groups]
    scale = jnp.concatenate([scale[g : g + 1] for g in range(groups)], axis=1)
    scale = scale * (1.0 / root_count)
    pull = ROOT_HALF * scale

    basis_high, basis_low = split(basis)
    before = folded(
        mm(lookup, jnp.concatenate([pick_half, slot_half, basis_high, basis_low], axis=0))
    )
    gate = 0.5 * jnp.tanh(0.5 * before) + 0.5
    active = before * gate
    latent = weight * active
    mixed = half_depth(value_rows, latent)
    values = mixed[:width]
    env_high, env_low = split(mixed[width:])

    def over_pairs(high, low):
        sums = []
        for cut, block in zip(lanes, blocks):
            quad = mm_nt(jnp.concatenate([high[:, cut], low[:, cut]], axis=0), block)
            sums.append((quad[:width, :wide] + quad[:width, wide:] + quad[width:, :wide]) * paths_t)
        return sums

    def over_orders(tables):
        parts = [folded(mm(stacked(*split(t)), block)) for t, block in zip(tables, blocks)]
        return jnp.concatenate(parts, axis=1)

    weighted = over_pairs(env_high, env_low)
    inner = over_orders(weighted)
    scalars = values * inner
    joined_high, joined_low = split(jnp.concatenate([latent, scalars], axis=0))
    z = full_depth(latent_both_t, latent_high_t, joined_high, joined_low)
    z_gate = 0.5 * jnp.tanh(0.5 * z) + 0.5
    update = z * z_gate
    update_out = update * out_column
    pair_energy = jnp.sum(latent * out_column + weight * update_out, axis=0, keepdims=True)
    pair_energy = pair_energy * pull
    d_z = (pull * weight) * out_column * (z_gate + update * (1.0 - z_gate))
    spread_back = half_depth(latent_rows, d_z)
    d_scalars = spread_back[width:]
    d_values = d_scalars * inner
    dinner_high, dinner_low = split(d_scalars * values)
    d_embed = over_pairs(dinner_high, dinner_low)
    d_env = over_orders(d_embed)

    d_angular = []
    for g, cut in enumerate(lanes):
        sides = jnp.transpose(jnp.concatenate([weighted[g], d_embed[g]], axis=0))
        sides_high, sides_low = split(sides)
        d_block = full_depth(
            jnp.concatenate([sides_high, sides_low], axis=0),
            sides_high,
            jnp.concatenate([dinner_high[:, cut], env_high[:, cut]], axis=0),
            jnp.concatenate([dinner_low[:, cut], env_low[:, cut]], axis=0),
        )
        d_block = d_block * block_mask
        total = d_block[:ORDERS]
        for k in range(1, GROUP):
            total = total + d_block[k * ORDERS : (k + 1) * ORDERS]
        d_angular.append(total)
    d_angular = jnp.concatenate(d_angular, axis=1)

    mixed_high, mixed_low = split(jnp.concatenate([d_values, d_env], axis=0))
    d_latent = (
        full_depth(value_both, value_high, mixed_high, mixed_low)
        + spread_back[:width]
        + pull * out_column
    )
    d_weight = jnp.sum(d_latent * active + pull * update_out, axis=0, keepdims=True)
    d_before = d_latent * weight * (gate + active * (1.0 - gate))
    d_basis = half_depth(basis_rows, d_before)

    d_length = jnp.sum(d_basis * basis_slope, axis=0, keepdims=True) + d_weight * slope * (
        1.0 / CUTOFF
    )
    a1, a2, a3, a4, a5, a6, a7, a8 = [d_angular[m : m + 1] for m in range(1, 9)]
    ux = root_three * a1 + root_fifteen * (ey * a4 + ez * a7 + ex * a8)
    uy = root_three * a2 + root_fifteen * (ex * a4 + ez * a5 - ey * a8)
    uz = root_three * a3 + root_fifteen * (ey * a5 + ex * a7) + 3.0 * root_five * ez * a6
    along = ex * ux + ey * uy + ez * uz
    radial_part = d_length - along * inverse
    gx = ux * inverse + ex * radial_part
    gy = uy * inverse + ey * radial_part
    gz = uz * inverse + ez * radial_part
    hx = -0.5 * dx
    hy = -0.5 * dy
    hz = -0.5 * dz
    virial = [hx * gx, hx * gy, hx * gz, hy * gx, hy * gy, hy * gz, hz * gx, hz * gy, hz * gz]
    rest = [jnp.zeros((ORDERS - 13, pairs), F32)]
    near_terms = jnp.concatenate(
        [-gx, -gy, -gz, *virial, jnp.zeros_like(gx), *rest], axis=0
    )
    center_terms = jnp.concatenate([gx, gy, gz, *virial, pair_energy, *rest], axis=0)
    near_sums = mm_nt(jnp.concatenate(split(near_terms), axis=0), pick_half)
    center_sums = mm_nt(jnp.concatenate(split(center_terms), axis=0), center_half)
    totals_ref[...] = folded(near_sums + center_sums)


def local(
    positions,
    features,
    species,
    centers,
    neighbours,
    counts,
    species_scale,
    species_shift,
    center_weight,
    near_weight,
    basis_weight,
    path_weight,
    value_weight,
    latent_weight,
    out_weight,
):
    cells_x, cells_y, cells_z, sites, width = features.shape
    cell_count = cells_x * cells_y * cells_z
    owned = cell_count * sites
    assert (cells_x, cells_y, cells_z, sites) == (2, 1, 2, SITES)
    pairs = neighbours.size
    nbr = pairs // owned
    kind = min(3, lax.axis_size("gy"))

    def from_next(array, axis):
        size = lax.axis_size(axis)
        return lax.ppermute(array, axis, [((i + 1) % size, i) for i in range(size)])

    def from_last(array, axis):
        size = lax.axis_size(axis)
        return lax.ppermute(array, axis, [(i, (i + 1) % size) for i in range(size)])

    vmem = pl.BlockSpec(memory_space=pltpu.VMEM)
    kinds = jnp.arange(species_scale.shape[0])
    chosen = species.reshape(cell_count, sites, 1) == kinds
    scale = jnp.sum(jnp.where(chosen, species_scale, 0.0), axis=-1)
    shift = jnp.sum(jnp.where(chosen, species_shift, 0.0), axis=-1).reshape(owned)
    coords = jnp.transpose(positions, (1, 2, 3, 0, 4)).reshape(cell_count, 3 * sites)
    coords = jnp.concatenate([coords, scale], axis=1)
    coords = jnp.pad(coords, ((0, -cell_count % 8), (0, width - 4 * sites)))
    payload = jnp.concatenate([features.reshape(owned, width), coords], axis=0)
    sides = [payload, from_next(payload, "gy")]
    if kind == 3:
        sides.append(from_last(payload, "gy"))
    codes = pl.pallas_call(
        functools.partial(list_kernel, kind),
        out_shape=jax.ShapeDtypeStruct((pairs // 128, 128), F32),
        in_specs=[vmem, vmem],
        out_specs=vmem,
        name="neighbour_codes",
    )(centers.reshape(1, owned), neighbours)
    spare = jnp.zeros((-kind * cell_count % 8, width), F32)
    here = jnp.concatenate(
        [side[:owned] for side in sides]
        + [side[owned : owned + cell_count] for side in sides]
        + [spare, codes],
        axis=0,
    )
    next_x = from_next(here, "gx")
    next_z = from_next(jnp.concatenate([here, next_x], axis=0), "gz")
    totals = pl.pallas_call(
        functools.partial(force_kernel, kind, nbr),
        out_shape=jax.ShapeDtypeStruct((ORDERS, 4 * kind * owned), F32),
        in_specs=[vmem] * 10,
        out_specs=vmem,
        compiler_params=pltpu.CompilerParams(vmem_limit_bytes=40 * 1024 * 1024),
        name="pair_forces",
    )(
        here,
        next_x,
        next_z,
        center_weight,
        near_weight,
        basis_weight,
        path_weight,
        value_weight,
        latent_weight,
        out_weight.reshape(1, width),
    )
    half = 2 * kind * owned
    totals = totals[:, :half] + from_last(totals[:, half:], "gz")
    half = kind * owned
    totals = totals[:, :half] + from_last(totals[:, half:], "gx")
    own = totals[:, :owned] + from_last(totals[:, owned : 2 * owned], "gy")
    if kind == 3:
        own = own + from_next(totals[:, 2 * owned :], "gy")
    forces = own[0:3].reshape(3, cells_x, cells_y, cells_z, sites)
    virial = own[3:12].reshape(9, cells_x, cells_y, cells_z, sites)
    occupied = jnp.any(centers[None, :] == jnp.arange(owned)[:, None], axis=1)
    site_energy = own[12] + jnp.where(occupied, shift, 0.0)
    site_energy = site_energy.reshape(cells_x, cells_y, cells_z, sites)
    return (site_energy, forces, virial)


def solution(mesh):
    placed = (
        P(None, "gx", "gy", "gz", None),
        P("gx", "gy", "gz", None, None),
        P("gx", "gy", "gz", None),
        P(("gx", "gy", "gz")),
        P(("gx", "gy", "gz"), None),
        P(("gx", "gy", "gz")),
        P(),
        P(),
        P(),
        P(),
        P(),
        P(),
        P(),
        P(),
        P(),
    )
    return jax.shard_map(
        local,
        mesh=mesh,
        in_specs=placed,
        out_specs=(
            P("gx", "gy", "gz", None),
            P(None, "gx", "gy", "gz", None),
            P(None, "gx", "gy", "gz", None),
        ),
        check_vma=False,
    )
```

```python
import functools
import math

import jax
import jax.numpy as jnp
import numpy as np
from jax import lax
from jax.experimental import pallas as pl
from jax.experimental.pallas import tpu as pltpu
from jax.sharding import PartitionSpec as P

EXACT_DOT = lax.Precision.HIGHEST
CUTOFF = 5.0
CELL_SIDE = 4.6
ROOT_HALF = 0.7071067811865476
GROUP = 8
ORDERS = 16
SITES = 8
OWN_CELLS = 4
FRAME_CELLS = 48
F32 = jnp.float32
BF16 = jnp.bfloat16


def split(value):
    high = value.astype(BF16)
    low = (value - high.astype(F32)).astype(BF16)
    return high, low


def split3(value):
    high = value.astype(BF16)
    rest = value - high.astype(F32)
    middle = rest.astype(BF16)
    low = (rest - middle.astype(F32)).astype(BF16)
    return high, middle, low


def mm(a, b):
    return lax.dot_general(a, b, (((1,), (0,)), ((), ())), preferred_element_type=F32)


def mm_nt(a, b):
    return lax.dot_general(a, b, (((1,), (1,)), ((), ())), preferred_element_type=F32)


def stacked(high, low):
    top = jnp.concatenate([high, high], axis=1)
    bottom = jnp.concatenate([low, jnp.zeros_like(low)], axis=1)
    return jnp.concatenate([top, bottom], axis=0)


def folded(product):
    half = product.shape[0] // 2
    return product[:half] + product[half:]


def half_depth(weights, value):
    return folded(mm(weights, jnp.concatenate(split(value), axis=0)))


def full_depth(both, high, value_high, value_low):
    return folded(mm(both, value_high)) + mm(high, value_low)


def sin_cos_pi(turns):
    near = turns - 2.0 * jnp.round(turns * 0.5)
    quarter = jnp.round(near * 2.0)
    v = (near - 0.5 * quarter) * math.pi
    v2 = v * v
    s = v * (
        1.0
        + v2
        * (-1.0 / 6 + v2 * (1.0 / 120 + v2 * (-1.0 / 5040 + v2 * (1.0 / 362880 - v2 / 39916800))))
    )
    c = 1.0 + v2 * (
        -0.5
        + v2
        * (1.0 / 24 + v2 * (-1.0 / 720 + v2 * (1.0 / 40320 + v2 * (-1.0 / 3628800 + v2 / 479001600))))
    )
    odd = jnp.abs(quarter) == 1.0
    sine = jnp.where(odd, quarter * c, jnp.where(quarter == 0.0, s, -s))
    cosine = jnp.where(odd, -quarter * s, jnp.where(quarter == 0.0, c, -c))
    return sine, cosine


def lane_row(piece, offset):
    row = jnp.concatenate([piece, jnp.zeros((1, 128 - piece.shape[1]), piece.dtype)], axis=1)
    return pltpu.roll(row, offset, 1) if offset else row


def pack_kernel(
    kind,
    positions_ref,
    features_ref,
    species_ref,
    centers_ref,
    neighbours_ref,
    scale_ref,
    shift_ref,
    payload_ref,
    shift_row_ref,
    wide_ref,
):
    owned, nbr = neighbours_ref.shape
    per_row = 128 // nbr
    payload_ref[:owned] = features_ref[...]
    payload_ref[owned : owned + 8] = jnp.zeros((8, 128), F32)
    shift_row = jnp.zeros((1, 128), F32)
    for cell in range(OWN_CELLS):
        x, z = cell // 2, cell % 2
        species = species_ref[x, 0, z : z + 1, :]
        scale = jnp.zeros(species.shape, F32)
        shift = jnp.zeros(species.shape, F32)
        for s in range(scale_ref.shape[0]):
            scale = jnp.where(species == s, scale_ref[s], scale)
            shift = jnp.where(species == s, shift_ref[s], shift)
        row = lane_row(scale, 3 * SITES)
        for c in range(3):
            row = row + lane_row(positions_ref[c, x, 0, z : z + 1, :], c * SITES)
        payload_ref[owned + cell : owned + cell + 1] = row
        shift_row = shift_row + lane_row(shift, cell * SITES)

    chosen = lax.broadcasted_iota(jnp.int32, (owned, owned), 0) == centers_ref[...]
    chosen = jnp.where(chosen, 1.0, 0.0)
    occupied = jnp.sum(chosen, axis=1, keepdims=True) > 0.5
    column = jnp.where(occupied, jnp.ones((owned, 128), F32), 0.0)
    shift_row_ref[...] = shift_row[:, :owned] * jnp.transpose(column)[0:1]
    chosen = chosen.astype(BF16)
    rows = neighbours_ref[...]
    upper = mm(chosen, (rows >> 4).astype(F32).astype(BF16))
    lower = mm(chosen, (rows & 15).astype(F32).astype(BF16))
    rows = (upper * 16.0 + lower).astype(jnp.int32)
    live = occupied & (rows < FRAME_CELLS * SITES)
    slot = lax.broadcasted_iota(jnp.int32, (owned, nbr), 0)
    cell = slot >> 3
    site = rows & 7
    place = rows >> 3
    near_z = (place & 3) + 1 - 2 * (cell & 1)
    column = place >> 2
    frame_x = (column * 11) >> 5
    frame_y = column - 3 * frame_x
    near_x = frame_x + 1 - 2 * (cell >> 1)
    side = jnp.where(frame_y == 1, 0, jnp.where(frame_y == 2, 1, kind - 1))
    block = (near_z >> 1) * 2 + (near_x >> 1)
    where = (block * kind + side) * owned + (near_x & 1) * 16 + (near_z & 1) * 8 + site
    code = jnp.where(live, 1 + where + (frame_y << 10), 0).astype(F32)
    wide_ref[...] = jnp.concatenate([code, jnp.zeros((owned, 128 - nbr), F32)], axis=1)
    codes = wide_ref[pl.ds(0, owned // per_row, stride=per_row), :]
    for j in range(1, per_row):
        more = wide_ref[pl.ds(j, owned // per_row, stride=per_row), :]
        codes = codes + pltpu.roll(more, j * nbr, 1)
    payload_ref[owned + 8 :] = codes


def weight_kernel(
    nbr,
    center_weight_ref,
    near_weight_ref,
    path_weight_ref,
    value_weight_ref,
    latent_weight_ref,
    out_weight_ref,
    stack_ref,
    column_ref,
):
    width = near_weight_ref.shape[0]
    value_high, value_low = split(value_weight_ref[...])
    latent_high, latent_low = split(jnp.transpose(latent_weight_ref[...]))
    parts = [
        stacked(*split(jnp.transpose(value_weight_ref[...]))),
        jnp.concatenate([latent_high, latent_low], axis=0),
        stacked(*split(latent_weight_ref[...])),
        jnp.concatenate([value_high, value_low], axis=0),
        stacked(*split(jnp.transpose(near_weight_ref[...]))),
        stacked(*split(jnp.transpose(center_weight_ref[...]))),
    ]
    start = 0
    for part in parts:
        stack_ref[start : start + part.shape[0], :] = part
        start += part.shape[0]
    level = lax.broadcasted_iota(jnp.int32, (ORDERS, width), 0)
    path_rows = jnp.where(
        level == 0,
        path_weight_ref[0:1, :],
        jnp.where(
            level < 4,
            path_weight_ref[1:2, :],
            jnp.where(level < 9, path_weight_ref[2:3, :], 0.0),
        ),
    )
    paths_t = jnp.transpose(jnp.concatenate([path_rows] * GROUP, axis=0))
    column_ref[:width] = paths_t * (1.0 / math.sqrt(nbr))
    column_ref[width:] = jnp.transpose(jnp.broadcast_to(out_weight_ref[...], (width, width)))


def finish_kernel(mine_ref, near_ref, shift_row_ref, energy_ref, forces_ref, virial_ref):
    owned = near_ref.shape[1]
    total = mine_ref[:, :owned] + near_ref[...]
    energy = total[12:13] + shift_row_ref[...]
    columns = jnp.transpose(jnp.concatenate([total, jnp.zeros((ORDERS, 128 - owned), F32)], axis=1))
    for cell in range(OWN_CELLS):
        x, z = cell // 2, cell % 2
        lanes = slice(cell * SITES, (cell + 1) * SITES)
        energy_ref[x, 0, z : z + 1, :] = energy[:, lanes]
        for c in range(3):
            forces_ref[c, x, 0, z : z + 1, :] = total[c : c + 1, lanes]
        virial_ref[x, 0, z] = columns[lanes, 3:12]


def force_kernel(
    kind,
    nbr,
    here_ref,
    next_x_ref,
    sides_ref,
    next_z_ref,
    stack_ref,
    column_ref,
    basis_weight_ref,
    send_ref,
    keep_ref,
):
    height, width = here_ref.shape
    owned = OWN_CELLS * SITES
    short = owned + 8
    pairs = owned * nbr
    radial = basis_weight_ref.shape[0]
    span = GROUP * nbr
    groups = owned // GROUP
    wide = GROUP * ORDERS
    sites = SITES
    root_count = math.sqrt(nbr)
    root_three = math.sqrt(3.0)
    root_fifteen = math.sqrt(15.0)
    root_five = math.sqrt(5.0)
    far = next_z_ref[...]
    mains = [here_ref[...], next_x_ref[...], far[:height], far[height : 2 * height]]
    near_sides = sides_ref[...]
    near_sides = [near_sides[i * short : (i + 1) * short] for i in range(2 * kind - 2)]
    far_sides = far[2 * height :]
    far_sides = [far_sides[i * short : (i + 1) * short] for i in range(2 * kind - 2)]
    blocks_in = [
        [mains[0], *near_sides[0::2]],
        [mains[1], *near_sides[1::2]],
        [mains[2], *far_sides[0::2]],
        [mains[3], *far_sides[1::2]],
    ]
    feats = jnp.concatenate([side[:owned] for block in blocks_in for side in block], axis=0)
    known = feats.shape[0]
    center_feats = []
    coords = []
    scales = []
    codes = []
    cell_row = lax.broadcasted_iota(jnp.int32, (kind * OWN_CELLS, 128), 0) % OWN_CELLS
    tile_lane = lax.broadcasted_iota(jnp.int32, (kind * OWN_CELLS, 128), 1)
    for g, block in enumerate(blocks_in):
        ahead_x, ahead_z = g % 2, g // 2
        cell = (1 - ahead_x) * 2 + 1 - ahead_z
        center_feats.append(block[0][cell * sites : (cell + 1) * sites])
        rows = jnp.concatenate([side[owned : owned + OWN_CELLS] for side in block], axis=0)
        scales.append(rows[cell : cell + 1])
        corner_x = (cell_row // 2 + 2 * ahead_x).astype(F32) * CELL_SIDE
        corner_z = (cell_row % 2 + 2 * ahead_z).astype(F32) * CELL_SIDE
        corner = jnp.where(
            tile_lane < sites, corner_x, jnp.where(tile_lane < 2 * sites, 0.0, corner_z)
        )
        coords.append(rows + corner)
        start = short + cell * span // 128
        codes.extend(block[0][start + r : start + r + 1] for r in range(span // 128))
    center_feats = jnp.concatenate(center_feats, axis=0)
    coords = jnp.concatenate(coords, axis=0)
    code = jnp.concatenate(codes, axis=1).astype(jnp.int32)
    live = code > 0
    code = jnp.maximum(code - 1, 0)
    side_y = ((code >> 10) - 1).astype(F32)
    near_row = jnp.where(live, code & 1023, known)

    spread = jnp.broadcast_to(coords[:, None, :], (coords.shape[0], sites, 128))
    spread = spread.reshape(known, 128)
    keep_lane = lax.broadcasted_iota(jnp.int32, (known, 128), 1)
    keep_row = lax.broadcasted_iota(jnp.int32, (known, 128), 0)
    keep = (keep_lane % sites == keep_row % sites) & (keep_lane < 3 * sites)
    spread = jnp.where(keep, spread, 0.0)
    place_parts = jnp.concatenate(split3(jnp.transpose(spread)[: 3 * sites]), axis=0)

    value_rows = stack_ref[: 4 * width, :]
    latent_both_t = stack_ref[4 * width : 6 * width, :]
    latent_high_t = latent_both_t[:width]
    latent_rows = stack_ref[6 * width : 10 * width, :]
    value_both = stack_ref[10 * width : 12 * width, :]
    value_high = value_both[:width]
    basis_t = jnp.transpose(basis_weight_ref[...])
    basis_high_t, basis_low_t = split(basis_t)
    basis_rows = stacked(*split(basis_weight_ref[...]))

    def project(weight, rows):
        return folded(mm_nt(weight, jnp.concatenate(split(rows), axis=1)))

    near_t = project(stack_ref[12 * width : 14 * width, :], feats)
    own_t = project(stack_ref[14 * width :, :], center_feats)
    near_high, near_low = split(near_t)
    own_high, own_low = split(own_t)
    lookup = jnp.concatenate(
        [
            jnp.concatenate([near_high, own_high, basis_high_t, basis_high_t], axis=1),
            jnp.concatenate([near_low, own_low, basis_low_t, jnp.zeros_like(basis_low_t)], axis=1),
        ],
        axis=0,
    )
    scale_rows = jnp.concatenate(scales, axis=0)
    scale_parts = jnp.concatenate(
        [*split3(scale_rows), jnp.zeros((16 - 3 * groups, 128), BF16)], axis=0
    )

    paths_t = column_ref[:width]
    out_column = jnp.concatenate([column_ref[width:]] * (pairs // width), axis=1)

    site_ids = lax.broadcasted_iota(jnp.int32, (known, pairs), 0)
    slot_ids = lax.broadcasted_iota(jnp.int32, (owned, pairs), 0)
    slot_row = lax.broadcasted_iota(jnp.int32, (1, pairs), 1) // nbr
    group_row = slot_row // GROUP
    center_cell = (1 - group_row % 2) * 2 + 1 - group_row // 2
    center_row = group_row * (kind * owned) + center_cell * sites + slot_row % GROUP
    block_row = lax.broadcasted_iota(jnp.int32, (wide, span), 0) // ORDERS
    block_lane = lax.broadcasted_iota(jnp.int32, (wide, span), 1) // nbr
    block_mask = (block_row == block_lane).astype(F32)
    block_half = block_mask.astype(BF16)
    order = lax.broadcasted_iota(jnp.int32, (radial, pairs), 0).astype(F32) + 1.0
    lanes = [slice(g * span, (g + 1) * span) for g in range(groups)]

    pick = jnp.where(site_ids == near_row, 1.0, 0.0)
    from_center = jnp.where(site_ids == center_row, 1.0, 0.0)
    pick_half = pick.astype(BF16)
    center_half = from_center.astype(BF16)
    slot_half = jnp.where(slot_ids == slot_row, 1.0, 0.0).astype(BF16)

    moved = mm(place_parts, (pick - from_center).astype(BF16))
    moved = moved[: 3 * sites] + moved[3 * sites : 6 * sites] + moved[6 * sites :]
    dx = jnp.where(live, jnp.sum(moved[:sites], axis=0, keepdims=True), 6.0)
    dy = jnp.sum(moved[sites : 2 * sites], axis=0, keepdims=True) + CELL_SIDE * side_y
    dy = jnp.where(live, dy, 0.0)
    dz = jnp.where(live, jnp.sum(moved[2 * sites :], axis=0, keepdims=True), 0.0)
    length = jnp.sqrt(dx * dx + dy * dy + dz * dz)
    inverse = 1.0 / length
    ratio = length * (1.0 / CUTOFF)
    inside = live & (ratio < 1.0)
    r2 = ratio * ratio
    r5 = r2 * r2 * ratio
    r6 = r5 * ratio
    weight = jnp.where(inside, 1.0 - r6 * (28.0 - 48.0 * ratio + 21.0 * r2), 0.0)
    slope = jnp.where(inside, -168.0 * r5 * (1.0 - 2.0 * ratio + r2), 0.0)
    sine, cosine = sin_cos_pi(order * ratio)
    basis = (math.sqrt(2.0 / CUTOFF) * inverse) * sine
    basis_slope = (math.sqrt(2.0 / CUTOFF) * inverse) * (
        (math.pi / CUTOFF) * order * cosine - sine * inverse
    )
    ex = dx * inverse
    ey = dy * inverse
    ez = dz * inverse
    angular = jnp.concatenate(
        [
            jnp.ones_like(ex),
            root_three * ex,
            root_three * ey,
            root_three * ez,
            root_fifteen * ex * ey,
            root_fifteen * ey * ez,
            0.5 * root_five * (3.0 * ez * ez - 1.0),
            root_fifteen * ex * ez,
            0.5 * root_fifteen * (ex * ex - ey * ey),
            jnp.zeros((ORDERS - 9, pairs), F32),
        ],
        axis=0,
    )
    angular_high, angular_low = split(angular)
    blocks = [
        jnp.concatenate(
            [
                jnp.concatenate([angular_high[:, cut]] * GROUP, axis=0) * block_half,
                jnp.concatenate([angular_low[:, cut]] * GROUP, axis=0) * block_half,
            ],
            axis=0,
        )
        for cut in lanes
    ]
    lane_ids = lax.broadcasted_iota(jnp.int32, (128, span), 0)
    lane_slot = lax.broadcasted_iota(jnp.int32, (128, span), 1) // nbr + 3 * sites
    scale = mm(scale_parts, jnp.where(lane_ids == lane_slot, 1.0, 0.0).astype(BF16))
    scale = scale[:groups] + scale[groups : 2 * groups] + scale[2 * groups : 3 * groups]
    scale = jnp.concatenate([scale[g : g + 1] for g in range(groups)], axis=1)
    scale = scale * (1.0 / root_count)
    pull = ROOT_HALF * scale

    basis_high, basis_low = split(basis)
    before = folded(
        mm(lookup, jnp.concatenate([pick_half, slot_half, basis_high, basis_low], axis=0))
    )
    gate = 0.5 * jnp.tanh(0.5 * before) + 0.5
    active = before * gate
    latent = weight * active
    mixed = half_depth(value_rows, latent)
    values = mixed[:width]
    env_high, env_low = split(mixed[width:])

    def over_pairs(high, low):
        sums = []
        for cut, block in zip(lanes, blocks):
            quad = mm_nt(jnp.concatenate([high[:, cut], low[:, cut]], axis=0), block)
            sums.append((quad[:width, :wide] + quad[:width, wide:] + quad[width:, :wide]) * paths_t)
        return sums

    def over_orders(tables):
        parts = [folded(mm(stacked(*split(t)), block)) for t, block in zip(tables, blocks)]
        return jnp.concatenate(parts, axis=1)

    weighted = over_pairs(env_high, env_low)
    inner = over_orders(weighted)
    scalars = values * inner
    joined_high, joined_low = split(jnp.concatenate([latent, scalars], axis=0))
    z = full_depth(latent_both_t, latent_high_t, joined_high, joined_low)
    z_gate = 0.5 * jnp.tanh(0.5 * z) + 0.5
    update = z * z_gate
    update_out = update * out_column
    pair_energy = jnp.sum(latent * out_column + weight * update_out, axis=0, keepdims=True)
    pair_energy = pair_energy * pull
    d_z = (pull * weight) * out_column * (z_gate + update * (1.0 - z_gate))
    spread_back = half_depth(latent_rows, d_z)
    d_scalars = spread_back[width:]
    d_values = d_scalars * inner
    dinner_high, dinner_low = split(d_scalars * values)
    d_embed = over_pairs(dinner_high, dinner_low)
    d_env = over_orders(d_embed)

    d_angular = []
    for g, cut in enumerate(lanes):
        sides = jnp.transpose(jnp.concatenate([weighted[g], d_embed[g]], axis=0))
        sides_high, sides_low = split(sides)
        d_block = full_depth(
            jnp.concatenate([sides_high, sides_low], axis=0),
            sides_high,
            jnp.concatenate([dinner_high[:, cut], env_high[:, cut]], axis=0),
            jnp.concatenate([dinner_low[:, cut], env_low[:, cut]], axis=0),
        )
        d_block = d_block * block_mask
        total = d_block[:ORDERS]
        for k in range(1, GROUP):
            total = total + d_block[k * ORDERS : (k + 1) * ORDERS]
        d_angular.append(total)
    d_angular = jnp.concatenate(d_angular, axis=1)

    mixed_high, mixed_low = split(jnp.concatenate([d_values, d_env], axis=0))
    d_latent = (
        full_depth(value_both, value_high, mixed_high, mixed_low)
        + spread_back[:width]
        + pull * out_column
    )
    d_weight = jnp.sum(d_latent * active + pull * update_out, axis=0, keepdims=True)
    d_before = d_latent * weight * (gate + active * (1.0 - gate))
    d_basis = half_depth(basis_rows, d_before)

    d_length = jnp.sum(d_basis * basis_slope, axis=0, keepdims=True) + d_weight * slope * (
        1.0 / CUTOFF
    )
    a1, a2, a3, a4, a5, a6, a7, a8 = [d_angular[m : m + 1] for m in range(1, 9)]
    ux = root_three * a1 + root_fifteen * (ey * a4 + ez * a7 + ex * a8)
    uy = root_three * a2 + root_fifteen * (ex * a4 + ez * a5 - ey * a8)
    uz = root_three * a3 + root_fifteen * (ey * a5 + ex * a7) + 3.0 * root_five * ez * a6
    along = ex * ux + ey * uy + ez * uz
    radial_part = d_length - along * inverse
    gx = ux * inverse + ex * radial_part
    gy = uy * inverse + ey * radial_part
    gz = uz * inverse + ez * radial_part
    hx = -0.5 * dx
    hy = -0.5 * dy
    hz = -0.5 * dz
    virial = [hx * gx, hx * gy, hx * gz, hy * gx, hy * gy, hy * gz, hz * gx, hz * gy, hz * gz]
    rest = [jnp.zeros((ORDERS - 13, pairs), F32)]
    near_terms = jnp.concatenate(
        [-gx, -gy, -gz, *virial, jnp.zeros_like(gx), *rest], axis=0
    )
    center_terms = jnp.concatenate([gx, gy, gz, *virial, pair_energy, *rest], axis=0)
    near_sums = mm_nt(jnp.concatenate(split(near_terms), axis=0), pick_half)
    center_sums = mm_nt(jnp.concatenate(split(center_terms), axis=0), center_half)
    totals = folded(near_sums + center_sums)
    keep_ref[...] = totals[:, : known // 2]
    send_ref[...] = totals[:, known // 2 :]


def joined(parts):
    total = sum(part.shape[0] for part in parts)
    start = 0
    pads = []
    for part in parts:
        end = start + part.shape[0]
        pads.append(jnp.pad(part, ((start, total - end), (0, 0))))
        start = end
    return functools.reduce(jnp.add, pads)


def local(
    positions,
    features,
    species,
    centers,
    neighbours,
    counts,
    species_scale,
    species_shift,
    center_weight,
    near_weight,
    basis_weight,
    path_weight,
    value_weight,
    latent_weight,
    out_weight,
):
    cells_x, cells_y, cells_z, sites, width = features.shape
    cell_count = cells_x * cells_y * cells_z
    owned = cell_count * sites
    assert (cells_x, cells_y, cells_z, sites) == (2, 1, 2, SITES)
    pairs = neighbours.size
    nbr = pairs // owned
    kind = min(3, lax.axis_size("gy"))

    def from_next(array, axis):
        size = lax.axis_size(axis)
        return lax.ppermute(array, axis, [((i + 1) % size, i) for i in range(size)])

    def from_last(array, axis):
        size = lax.axis_size(axis)
        return lax.ppermute(array, axis, [(i, (i + 1) % size) for i in range(size)])

    vmem = pl.BlockSpec(memory_space=pltpu.VMEM)
    smem = pl.BlockSpec(memory_space=pltpu.SMEM)
    here, shift_row = pl.pallas_call(
        functools.partial(pack_kernel, kind),
        out_shape=(
            jax.ShapeDtypeStruct((owned + 8 + pairs // 128, width), F32),
            jax.ShapeDtypeStruct((1, owned), F32),
        ),
        in_specs=[vmem] * 5 + [smem] * 2,
        out_specs=(vmem, vmem),
        scratch_shapes=[pltpu.VMEM((owned, 128), F32)],
        name="pack_payload",
    )(
        positions,
        features.reshape(owned, width),
        species,
        centers.reshape(1, owned),
        neighbours,
        species_scale,
        species_shift,
    )
    stack, column = pl.pallas_call(
        functools.partial(weight_kernel, nbr),
        out_shape=(
            jax.ShapeDtypeStruct((16 * width, 2 * width), BF16),
            jax.ShapeDtypeStruct((2 * width, width), F32),
        ),
        in_specs=[vmem] * 6,
        out_specs=(vmem, vmem),
        name="split_weights",
    )(
        center_weight,
        near_weight,
        path_weight,
        value_weight,
        latent_weight,
        out_weight.reshape(1, width),
    )
    short = owned + 8
    next_x = from_next(here, "gx")
    both = joined([here[:short], next_x[:short]])
    sides = from_next(both, "gy")
    if kind == 3:
        sides = joined([sides, from_last(both, "gy")])
    next_z = from_next(joined([here, next_x, sides]), "gz")
    half = 2 * kind * owned
    send, keep = pl.pallas_call(
        functools.partial(force_kernel, kind, nbr),
        out_shape=(
            jax.ShapeDtypeStruct((ORDERS, half), F32),
            jax.ShapeDtypeStruct((ORDERS, half), F32),
        ),
        in_specs=[vmem] * 7,
        out_specs=(vmem, vmem),
        compiler_params=pltpu.CompilerParams(vmem_limit_bytes=40 * 1024 * 1024),
        name="pair_forces",
    )(here, next_x, sides, next_z, stack, column, basis_weight)
    totals = keep + from_last(send, "gz")
    half = kind * owned
    totals = totals[:, :half] + from_last(totals[:, half:], "gx")
    back = from_last(totals[:, owned : 2 * owned], "gy")
    if kind == 3:
        back = back + from_next(totals[:, 2 * owned :], "gy")
    site_energy, forces, virial = pl.pallas_call(
        finish_kernel,
        out_shape=(
            jax.ShapeDtypeStruct(species.shape, F32),
            jax.ShapeDtypeStruct(positions.shape, F32),
            jax.ShapeDtypeStruct((*species.shape, 9), F32),
        ),
        in_specs=[vmem] * 3,
        out_specs=(vmem, vmem, vmem),
        name="write_outputs",
    )(totals, back, shift_row)
    return (site_energy, forces, jnp.transpose(virial, (4, 0, 1, 2, 3)))


def solution(mesh):
    placed = (
        P(None, "gx", "gy", "gz", None),
        P("gx", "gy", "gz", None, None),
        P("gx", "gy", "gz", None),
        P(("gx", "gy", "gz")),
        P(("gx", "gy", "gz"), None),
        P(("gx", "gy", "gz")),
        P(),
        P(),
        P(),
        P(),
        P(),
        P(),
        P(),
        P(),
        P(),
    )
    return jax.shard_map(
        local,
        mesh=mesh,
        in_specs=placed,
        out_specs=(
            P("gx", "gy", "gz", None),
            P(None, "gx", "gy", "gz", None),
            P(None, "gx", "gy", "gz", None),
        ),
        check_vma=False,
    )
```

```python
import functools
import math

import jax
import jax.numpy as jnp
import numpy as np
from jax import lax
from jax.experimental import pallas as pl
from jax.experimental.pallas import tpu as pltpu
from jax.sharding import PartitionSpec as P

EXACT_DOT = lax.Precision.HIGHEST
CUTOFF = 5.0
CELL_SIDE = 4.6
ROOT_HALF = 0.7071067811865476
GROUP = 8
ORDERS = 16
SITES = 8
OWN_CELLS = 4
FRAME_CELLS = 48
F32 = jnp.float32
BF16 = jnp.bfloat16


def split(value):
    high = value.astype(BF16)
    low = (value - high.astype(F32)).astype(BF16)
    return high, low


def split3(value):
    high = value.astype(BF16)
    rest = value - high.astype(F32)
    middle = rest.astype(BF16)
    low = (rest - middle.astype(F32)).astype(BF16)
    return high, middle, low


def mm(a, b):
    return lax.dot_general(a, b, (((1,), (0,)), ((), ())), preferred_element_type=F32)


def mm_nt(a, b):
    return lax.dot_general(a, b, (((1,), (1,)), ((), ())), preferred_element_type=F32)


def stacked(high, low):
    top = jnp.concatenate([high, high], axis=1)
    bottom = jnp.concatenate([low, jnp.zeros_like(low)], axis=1)
    return jnp.concatenate([top, bottom], axis=0)


def folded(product):
    half = product.shape[0] // 2
    return product[:half] + product[half:]


def half_depth(weights, value):
    return folded(mm(weights, jnp.concatenate(split(value), axis=0)))


def full_depth(both, high, value_high, value_low):
    return folded(mm(both, value_high)) + mm(high, value_low)


def sin_cos_pi(turns):
    near = turns - 2.0 * jnp.round(turns * 0.5)
    quarter = jnp.round(near * 2.0)
    v = (near - 0.5 * quarter) * math.pi
    v2 = v * v
    s = v * (
        1.0
        + v2
        * (-1.0 / 6 + v2 * (1.0 / 120 + v2 * (-1.0 / 5040 + v2 * (1.0 / 362880 - v2 / 39916800))))
    )
    c = 1.0 + v2 * (
        -0.5
        + v2
        * (1.0 / 24 + v2 * (-1.0 / 720 + v2 * (1.0 / 40320 + v2 * (-1.0 / 3628800 + v2 / 479001600))))
    )
    odd = jnp.abs(quarter) == 1.0
    sine = jnp.where(odd, quarter * c, jnp.where(quarter == 0.0, s, -s))
    cosine = jnp.where(odd, -quarter * s, jnp.where(quarter == 0.0, c, -c))
    return sine, cosine


def lane_row(piece, offset):
    row = jnp.concatenate([piece, jnp.zeros((1, 128 - piece.shape[1]), piece.dtype)], axis=1)
    return pltpu.roll(row, offset, 1) if offset else row


def pack_kernel(
    kind,
    positions_ref,
    features_ref,
    species_ref,
    centers_ref,
    neighbours_ref,
    scale_ref,
    shift_ref,
    payload_ref,
    shift_row_ref,
    wide_ref,
):
    owned, nbr = neighbours_ref.shape
    per_row = 128 // nbr
    payload_ref[:owned] = features_ref[...]
    payload_ref[owned : owned + 8] = jnp.zeros((8, 128), F32)
    shift_row = jnp.zeros((1, 128), F32)
    for cell in range(OWN_CELLS):
        x, z = cell // 2, cell % 2
        species = species_ref[x, 0, z : z + 1, :]
        scale = jnp.zeros(species.shape, F32)
        shift = jnp.zeros(species.shape, F32)
        for s in range(scale_ref.shape[0]):
            scale = jnp.where(species == s, scale_ref[s], scale)
            shift = jnp.where(species == s, shift_ref[s], shift)
        row = lane_row(scale, 3 * SITES)
        for c in range(3):
            row = row + lane_row(positions_ref[c, x, 0, z : z + 1, :], c * SITES)
        payload_ref[owned + cell : owned + cell + 1] = row
        shift_row = shift_row + lane_row(shift, cell * SITES)

    chosen = lax.broadcasted_iota(jnp.int32, (owned, owned), 0) == centers_ref[...]
    chosen = jnp.where(chosen, 1.0, 0.0)
    occupied = jnp.sum(chosen, axis=1, keepdims=True) > 0.5
    column = jnp.where(occupied, jnp.ones((owned, 128), F32), 0.0)
    shift_row_ref[...] = shift_row[:, :owned] * jnp.transpose(column)[0:1]
    chosen = chosen.astype(BF16)
    rows = neighbours_ref[...]
    upper = mm(chosen, (rows >> 4).astype(F32).astype(BF16))
    lower = mm(chosen, (rows & 15).astype(F32).astype(BF16))
    rows = (upper * 16.0 + lower).astype(jnp.int32)
    live = occupied & (rows < FRAME_CELLS * SITES)
    slot = lax.broadcasted_iota(jnp.int32, (owned, nbr), 0)
    cell = slot >> 3
    site = rows & 7
    place = rows >> 3
    near_z = (place & 3) + 1 - 2 * (cell & 1)
    column = place >> 2
    frame_x = (column * 11) >> 5
    frame_y = column - 3 * frame_x
    near_x = frame_x + 1 - 2 * (cell >> 1)
    side = jnp.where(frame_y == 1, 0, jnp.where(frame_y == 2, 1, kind - 1))
    block = (near_z >> 1) * 2 + (near_x >> 1)
    where = (block * kind + side) * owned + (near_x & 1) * 16 + (near_z & 1) * 8 + site
    code = jnp.where(live, 1 + where + (frame_y << 10), 0).astype(F32)
    wide_ref[...] = jnp.concatenate([code, jnp.zeros((owned, 128 - nbr), F32)], axis=1)
    codes = wide_ref[pl.ds(0, owned // per_row, stride=per_row), :]
    for j in range(1, per_row):
        more = wide_ref[pl.ds(j, owned // per_row, stride=per_row), :]
        codes = codes + pltpu.roll(more, j * nbr, 1)
    payload_ref[owned + 8 :] = codes


def finish_kernel(mine_ref, shift_row_ref, *refs):
    *near_refs, energy_ref, forces_ref, virial_ref = refs
    owned = near_refs[0].shape[1]
    total = mine_ref[:, :owned]
    for near_ref in near_refs:
        total = total + near_ref[...]
    energy = total[12:13] + shift_row_ref[...]
    columns = jnp.transpose(jnp.concatenate([total, jnp.zeros((ORDERS, 128 - owned), F32)], axis=1))
    for cell in range(OWN_CELLS):
        x, z = cell // 2, cell % 2
        lanes = slice(cell * SITES, (cell + 1) * SITES)
        energy_ref[x, 0, z : z + 1, :] = energy[:, lanes]
        for c in range(3):
            forces_ref[c, x, 0, z : z + 1, :] = total[c : c + 1, lanes]
        virial_ref[x, 0, z] = columns[lanes, 3:12]


def force_kernel(kind, nbr, here_ref, next_x_ref, *refs):
    near_side_refs = refs[: 2 * kind - 2]
    (
        next_z_ref,
        center_weight_ref,
        near_weight_ref,
        basis_weight_ref,
        path_weight_ref,
        value_weight_ref,
        latent_weight_ref,
        out_weight_ref,
        keep_ref,
        send_ref,
    ) = refs[2 * kind - 2 :]
    height, width = here_ref.shape
    owned = OWN_CELLS * SITES
    short = owned + 8
    pairs = owned * nbr
    radial = basis_weight_ref.shape[0]
    span = GROUP * nbr
    groups = owned // GROUP
    wide = GROUP * ORDERS
    sites = SITES
    root_count = math.sqrt(nbr)
    root_three = math.sqrt(3.0)
    root_fifteen = math.sqrt(15.0)
    root_five = math.sqrt(5.0)
    far = next_z_ref[...]
    mains = [here_ref[...], next_x_ref[...], far[:height], far[height : 2 * height]]
    near_sides = [ref[...] for ref in near_side_refs]
    far_sides = far[2 * height :]
    far_sides = [far_sides[i * short : (i + 1) * short] for i in range(2 * kind - 2)]
    blocks_in = [
        [mains[0], *near_sides[0::2]],
        [mains[1], *near_sides[1::2]],
        [mains[2], *far_sides[0::2]],
        [mains[3], *far_sides[1::2]],
    ]
    feats = jnp.concatenate([side[:owned] for block in blocks_in for side in block], axis=0)
    known = feats.shape[0]
    center_feats = []
    coords = []
    scales = []
    codes = []
    cell_row = lax.broadcasted_iota(jnp.int32, (kind * OWN_CELLS, 128), 0) % OWN_CELLS
    tile_lane = lax.broadcasted_iota(jnp.int32, (kind * OWN_CELLS, 128), 1)
    for g, block in enumerate(blocks_in):
        ahead_x, ahead_z = g % 2, g // 2
        cell = (1 - ahead_x) * 2 + 1 - ahead_z
        center_feats.append(block[0][cell * sites : (cell + 1) * sites])
        rows = jnp.concatenate([side[owned : owned + OWN_CELLS] for side in block], axis=0)
        scales.append(rows[cell : cell + 1])
        corner_x = (cell_row // 2 + 2 * ahead_x).astype(F32) * CELL_SIDE
        corner_z = (cell_row % 2 + 2 * ahead_z).astype(F32) * CELL_SIDE
        corner = jnp.where(
            tile_lane < sites, corner_x, jnp.where(tile_lane < 2 * sites, 0.0, corner_z)
        )
        coords.append(rows + corner)
        start = short + cell * span // 128
        codes.extend(block[0][start + r : start + r + 1] for r in range(span // 128))
    center_feats = jnp.concatenate(center_feats, axis=0)
    coords = jnp.concatenate(coords, axis=0)
    code = jnp.concatenate(codes, axis=1).astype(jnp.int32)
    live = code > 0
    code = jnp.maximum(code - 1, 0)
    side_y = ((code >> 10) - 1).astype(F32)
    near_row = jnp.where(live, code & 1023, known)

    spread = jnp.broadcast_to(coords[:, None, :], (coords.shape[0], sites, 128))
    spread = spread.reshape(known, 128)
    keep_lane = lax.broadcasted_iota(jnp.int32, (known, 128), 1)
    keep_row = lax.broadcasted_iota(jnp.int32, (known, 128), 0)
    keep = (keep_lane % sites == keep_row % sites) & (keep_lane < 3 * sites)
    spread = jnp.where(keep, spread, 0.0)
    place_parts = jnp.concatenate(split3(jnp.transpose(spread)[: 3 * sites]), axis=0)

    value_rows = stacked(*split(jnp.transpose(value_weight_ref[...])))
    latent_high_t, latent_low_t = split(jnp.transpose(latent_weight_ref[...]))
    latent_both_t = jnp.concatenate([latent_high_t, latent_low_t], axis=0)
    latent_rows = stacked(*split(latent_weight_ref[...]))
    value_high, value_low = split(value_weight_ref[...])
    value_both = jnp.concatenate([value_high, value_low], axis=0)
    basis_t = jnp.transpose(basis_weight_ref[...])
    basis_high_t, basis_low_t = split(basis_t)
    basis_rows = stacked(*split(basis_weight_ref[...]))

    def project(weight, rows):
        weight = stacked(*split(jnp.transpose(weight)))
        return folded(mm_nt(weight, jnp.concatenate(split(rows), axis=1)))

    near_t = project(near_weight_ref[...], feats)
    own_t = project(center_weight_ref[...], center_feats)
    near_high, near_low = split(near_t)
    own_high, own_low = split(own_t)
    lookup = jnp.concatenate(
        [
            jnp.concatenate([near_high, own_high, basis_high_t, basis_high_t], axis=1),
            jnp.concatenate([near_low, own_low, basis_low_t, jnp.zeros_like(basis_low_t)], axis=1),
        ],
        axis=0,
    )
    scale_rows = jnp.concatenate(scales, axis=0)
    scale_parts = jnp.concatenate(
        [*split3(scale_rows), jnp.zeros((16 - 3 * groups, 128), BF16)], axis=0
    )

    level = lax.broadcasted_iota(jnp.int32, (ORDERS, width), 0)
    path_rows = jnp.where(
        level == 0,
        path_weight_ref[0:1, :],
        jnp.where(
            level < 4,
            path_weight_ref[1:2, :],
            jnp.where(level < 9, path_weight_ref[2:3, :], 0.0),
        ),
    )
    paths_t = jnp.transpose(jnp.concatenate([path_rows] * GROUP, axis=0)) * (1.0 / root_count)
    out_column = jnp.transpose(jnp.broadcast_to(out_weight_ref[...], (width, width)))
    out_column = jnp.concatenate([out_column] * (pairs // width), axis=1)

    site_ids = lax.broadcasted_iota(jnp.int32, (known, pairs), 0)
    slot_ids = lax.broadcasted_iota(jnp.int32, (owned, pairs), 0)
    slot_row = lax.broadcasted_iota(jnp.int32, (1, pairs), 1) // nbr
    group_row = slot_row // GROUP
    center_cell = (1 - group_row % 2) * 2 + 1 - group_row // 2
    center_row = group_row * (kind * owned) + center_cell * sites + slot_row % GROUP
    block_row = lax.broadcasted_iota(jnp.int32, (wide, span), 0) // ORDERS
    block_lane = lax.broadcasted_iota(jnp.int32, (wide, span), 1) // nbr
    block_mask = (block_row == block_lane).astype(F32)
    block_half = block_mask.astype(BF16)
    order = lax.broadcasted_iota(jnp.int32, (radial, pairs), 0).astype(F32) + 1.0
    lanes = [slice(g * span, (g + 1) * span) for g in range(groups)]

    pick = jnp.where(site_ids == near_row, 1.0, 0.0)
    from_center = jnp.where(site_ids == center_row, 1.0, 0.0)
    pick_half = pick.astype(BF16)
    center_half = from_center.astype(BF16)
    slot_half = jnp.where(slot_ids == slot_row, 1.0, 0.0).astype(BF16)

    moved = mm(place_parts, (pick - from_center).astype(BF16))
    moved = moved[: 3 * sites] + moved[3 * sites : 6 * sites] + moved[6 * sites :]
    dx = jnp.where(live, jnp.sum(moved[:sites], axis=0, keepdims=True), 6.0)
    dy = jnp.sum(moved[sites : 2 * sites], axis=0, keepdims=True) + CELL_SIDE * side_y
    dy = jnp.where(live, dy, 0.0)
    dz = jnp.where(live, jnp.sum(moved[2 * sites :], axis=0, keepdims=True), 0.0)
    length = jnp.sqrt(dx * dx + dy * dy + dz * dz)
    inverse = 1.0 / length
    ratio = length * (1.0 / CUTOFF)
    inside = live & (ratio < 1.0)
    r2 = ratio * ratio
    r5 = r2 * r2 * ratio
    r6 = r5 * ratio
    weight = jnp.where(inside, 1.0 - r6 * (28.0 - 48.0 * ratio + 21.0 * r2), 0.0)
    slope = jnp.where(inside, -168.0 * r5 * (1.0 - 2.0 * ratio + r2), 0.0)
    sine, cosine = sin_cos_pi(order * ratio)
    basis = (math.sqrt(2.0 / CUTOFF) * inverse) * sine
    basis_slope = (math.sqrt(2.0 / CUTOFF) * inverse) * (
        (math.pi / CUTOFF) * order * cosine - sine * inverse
    )
    ex = dx * inverse
    ey = dy * inverse
    ez = dz * inverse
    angular = jnp.concatenate(
        [
            jnp.ones_like(ex),
            root_three * ex,
            root_three * ey,
            root_three * ez,
            root_fifteen * ex * ey,
            root_fifteen * ey * ez,
            0.5 * root_five * (3.0 * ez * ez - 1.0),
            root_fifteen * ex * ez,
            0.5 * root_fifteen * (ex * ex - ey * ey),
            jnp.zeros((ORDERS - 9, pairs), F32),
        ],
        axis=0,
    )
    angular_high, angular_low = split(angular)
    blocks = [
        jnp.concatenate(
            [
                jnp.concatenate([angular_high[:, cut]] * GROUP, axis=0) * block_half,
                jnp.concatenate([angular_low[:, cut]] * GROUP, axis=0) * block_half,
            ],
            axis=0,
        )
        for cut in lanes
    ]
    lane_ids = lax.broadcasted_iota(jnp.int32, (128, span), 0)
    lane_slot = lax.broadcasted_iota(jnp.int32, (128, span), 1) // nbr + 3 * sites
    scale = mm(scale_parts, jnp.where(lane_ids == lane_slot, 1.0, 0.0).astype(BF16))
    scale = scale[:groups] + scale[groups : 2 * groups] + scale[2 * groups : 3 * groups]
    scale = jnp.concatenate([scale[g : g + 1] for g in range(groups)], axis=1)
    scale = scale * (1.0 / root_count)
    pull = ROOT_HALF * scale

    basis_high, basis_low = split(basis)
    before = folded(
        mm(lookup, jnp.concatenate([pick_half, slot_half, basis_high, basis_low], axis=0))
    )
    gate = 0.5 * jnp.tanh(0.5 * before) + 0.5
    active = before * gate
    latent = weight * active
    mixed = half_depth(value_rows, latent)
    values = mixed[:width]
    env_high, env_low = split(mixed[width:])

    def over_pairs(high, low):
        sums = []
        for cut, block in zip(lanes, blocks):
            quad = mm_nt(jnp.concatenate([high[:, cut], low[:, cut]], axis=0), block)
            sums.append((quad[:width, :wide] + quad[:width, wide:] + quad[width:, :wide]) * paths_t)
        return sums

    def over_orders(tables):
        parts = [folded(mm(stacked(*split(t)), block)) for t, block in zip(tables, blocks)]
        return jnp.concatenate(parts, axis=1)

    weighted = over_pairs(env_high, env_low)
    inner = over_orders(weighted)
    scalars = values * inner
    joined_high, joined_low = split(jnp.concatenate([latent, scalars], axis=0))
    z = full_depth(latent_both_t, latent_high_t, joined_high, joined_low)
    z_gate = 0.5 * jnp.tanh(0.5 * z) + 0.5
    update = z * z_gate
    update_out = update * out_column
    pair_energy = jnp.sum(latent * out_column + weight * update_out, axis=0, keepdims=True)
    pair_energy = pair_energy * pull
    d_z = (pull * weight) * out_column * (z_gate + update * (1.0 - z_gate))
    spread_back = half_depth(latent_rows, d_z)
    d_scalars = spread_back[width:]
    d_values = d_scalars * inner
    dinner_high, dinner_low = split(d_scalars * values)
    d_embed = over_pairs(dinner_high, dinner_low)
    d_env = over_orders(d_embed)

    d_angular = []
    for g, cut in enumerate(lanes):
        sides = jnp.transpose(jnp.concatenate([weighted[g], d_embed[g]], axis=0))
        sides_high, sides_low = split(sides)
        d_block = full_depth(
            jnp.concatenate([sides_high, sides_low], axis=0),
            sides_high,
            jnp.concatenate([dinner_high[:, cut], env_high[:, cut]], axis=0),
            jnp.concatenate([dinner_low[:, cut], env_low[:, cut]], axis=0),
        )
        d_block = d_block * block_mask
        total = d_block[:ORDERS]
        for k in range(1, GROUP):
            total = total + d_block[k * ORDERS : (k + 1) * ORDERS]
        d_angular.append(total)
    d_angular = jnp.concatenate(d_angular, axis=1)

    mixed_high, mixed_low = split(jnp.concatenate([d_values, d_env], axis=0))
    d_latent = (
        full_depth(value_both, value_high, mixed_high, mixed_low)
        + spread_back[:width]
        + pull * out_column
    )
    d_weight = jnp.sum(d_latent * active + pull * update_out, axis=0, keepdims=True)
    d_before = d_latent * weight * (gate + active * (1.0 - gate))
    d_basis = half_depth(basis_rows, d_before)

    d_length = jnp.sum(d_basis * basis_slope, axis=0, keepdims=True) + d_weight * slope * (
        1.0 / CUTOFF
    )
    a1, a2, a3, a4, a5, a6, a7, a8 = [d_angular[m : m + 1] for m in range(1, 9)]
    ux = root_three * a1 + root_fifteen * (ey * a4 + ez * a7 + ex * a8)
    uy = root_three * a2 + root_fifteen * (ex * a4 + ez * a5 - ey * a8)
    uz = root_three * a3 + root_fifteen * (ey * a5 + ex * a7) + 3.0 * root_five * ez * a6
    along = ex * ux + ey * uy + ez * uz
    radial_part = d_length - along * inverse
    gx = ux * inverse + ex * radial_part
    gy = uy * inverse + ey * radial_part
    gz = uz * inverse + ez * radial_part
    hx = -0.5 * dx
    hy = -0.5 * dy
    hz = -0.5 * dz
    virial = [hx * gx, hx * gy, hx * gz, hy * gx, hy * gy, hy * gz, hz * gx, hz * gy, hz * gz]
    rest = [jnp.zeros((ORDERS - 13, pairs), F32)]
    near_terms = jnp.concatenate(
        [-gx, -gy, -gz, *virial, jnp.zeros_like(gx), *rest], axis=0
    )
    center_terms = jnp.concatenate([gx, gy, gz, *virial, pair_energy, *rest], axis=0)
    near_sums = mm_nt(jnp.concatenate(split(near_terms), axis=0), pick_half)
    center_sums = mm_nt(jnp.concatenate(split(center_terms), axis=0), center_half)
    totals = folded(near_sums + center_sums)
    keep_ref[...] = totals[:, : known // 2]
    send_ref[...] = totals[:, known // 2 :]


def joined(parts):
    total = sum(part.shape[0] for part in parts)
    start = 0
    pads = []
    for part in parts:
        end = start + part.shape[0]
        pads.append(jnp.pad(part, ((start, total - end), (0, 0))))
        start = end
    return functools.reduce(jnp.add, pads)


def local(
    positions,
    features,
    species,
    centers,
    neighbours,
    counts,
    species_scale,
    species_shift,
    center_weight,
    near_weight,
    basis_weight,
    path_weight,
    value_weight,
    latent_weight,
    out_weight,
):
    cells_x, cells_y, cells_z, sites, width = features.shape
    cell_count = cells_x * cells_y * cells_z
    owned = cell_count * sites
    assert (cells_x, cells_y, cells_z, sites) == (2, 1, 2, SITES)
    pairs = neighbours.size
    nbr = pairs // owned
    kind = min(3, lax.axis_size("gy"))

    def moved(array, steps):
        names = tuple(steps)
        sizes = [lax.axis_size(name) for name in names]
        route = []
        for at in np.ndindex(*sizes):
            to = [(p + steps[name]) % size for p, name, size in zip(at, names, sizes)]
            route.append(
                (int(np.ravel_multi_index(at, sizes)), int(np.ravel_multi_index(to, sizes)))
            )
        return lax.ppermute(array, names, route)

    vmem = pl.BlockSpec(memory_space=pltpu.VMEM)
    smem = pl.BlockSpec(memory_space=pltpu.SMEM)
    here, shift_row = pl.pallas_call(
        functools.partial(pack_kernel, kind),
        out_shape=(
            jax.ShapeDtypeStruct((owned + 8 + pairs // 128, width), F32),
            jax.ShapeDtypeStruct((1, owned), F32),
        ),
        in_specs=[vmem] * 5 + [smem] * 2,
        out_specs=(vmem, vmem),
        scratch_shapes=[pltpu.VMEM((owned, 128), F32)],
        compiler_params=pltpu.CompilerParams(vmem_limit_bytes=8 * 1024 * 1024),
        name="pack_payload",
    )(
        positions,
        features.reshape(owned, width),
        species,
        centers.reshape(1, owned),
        neighbours,
        species_scale,
        species_shift,
    )
    short = here[: owned + 8]
    next_x = moved(here, {"gx": -1})
    sides = []
    for step in (-1, 1)[: kind - 1]:
        sides.append(moved(short, {"gx": -1, "gy": step}))
        sides.insert(-1, moved(short, {"gy": step}))
    next_z = moved(joined([here, next_x, *sides]), {"gz": -1})
    half = 2 * kind * owned
    keep, send = pl.pallas_call(
        functools.partial(force_kernel, kind, nbr),
        out_shape=(
            jax.ShapeDtypeStruct((ORDERS, half), F32),
            jax.ShapeDtypeStruct((ORDERS, half), F32),
        ),
        in_specs=[vmem] * (8 + 2 * kind),
        out_specs=(vmem, vmem),
        compiler_params=pltpu.CompilerParams(vmem_limit_bytes=32 * 1024 * 1024),
        name="pair_forces",
    )(
        here,
        next_x,
        *sides,
        next_z,
        center_weight,
        near_weight,
        basis_weight,
        path_weight,
        value_weight,
        latent_weight,
        out_weight.reshape(1, width),
    )
    totals = keep + moved(send, {"gz": 1})

    def part(index):
        return totals[:, index * owned : (index + 1) * owned]

    back = [moved(part(kind), {"gx": 1})]
    for i, step in enumerate((1, -1)[: kind - 1]):
        back.append(moved(part(kind + 1 + i), {"gx": 1, "gy": step}))
        back.append(moved(part(1 + i), {"gy": step}))
    site_energy, forces, virial = pl.pallas_call(
        finish_kernel,
        out_shape=(
            jax.ShapeDtypeStruct(species.shape, F32),
            jax.ShapeDtypeStruct(positions.shape, F32),
            jax.ShapeDtypeStruct((*species.shape, 9), F32),
        ),
        in_specs=[vmem] * (2 + len(back)),
        out_specs=(vmem, vmem, vmem),
        compiler_params=pltpu.CompilerParams(vmem_limit_bytes=8 * 1024 * 1024),
        name="write_outputs",
    )(totals, shift_row, *back)
    return (site_energy, forces, jnp.transpose(virial, (4, 0, 1, 2, 3)))


def solution(mesh):
    placed = (
        P(None, "gx", "gy", "gz", None),
        P("gx", "gy", "gz", None, None),
        P("gx", "gy", "gz", None),
        P(("gx", "gy", "gz")),
        P(("gx", "gy", "gz"), None),
        P(("gx", "gy", "gz")),
        P(),
        P(),
        P(),
        P(),
        P(),
        P(),
        P(),
        P(),
        P(),
    )
    return jax.shard_map(
        local,
        mesh=mesh,
        in_specs=placed,
        out_specs=(
            P("gx", "gy", "gz", None),
            P(None, "gx", "gy", "gz", None),
            P(None, "gx", "gy", "gz", None),
        ),
        check_vma=False,
    )
```

```python
import functools
import math

import jax
import jax.numpy as jnp
import numpy as np
from jax import lax
from jax.experimental import pallas as pl
from jax.experimental.pallas import tpu as pltpu
from jax.sharding import PartitionSpec as P

EXACT_DOT = lax.Precision.HIGHEST
CUTOFF = 5.0
CELL_SIDE = 4.6
ROOT_HALF = 0.7071067811865476
GROUP = 8
ORDERS = 16
SITES = 8
OWN_CELLS = 4
FRAME_CELLS = 48
F32 = jnp.float32
BF16 = jnp.bfloat16


def split(value):
    high = value.astype(BF16)
    low = (value - high.astype(F32)).astype(BF16)
    return high, low


def split3(value):
    high = value.astype(BF16)
    rest = value - high.astype(F32)
    middle = rest.astype(BF16)
    low = (rest - middle.astype(F32)).astype(BF16)
    return high, middle, low


def mm(a, b):
    return lax.dot_general(a, b, (((1,), (0,)), ((), ())), preferred_element_type=F32)


def mm_nt(a, b):
    return lax.dot_general(a, b, (((1,), (1,)), ((), ())), preferred_element_type=F32)


def stacked(high, low):
    top = jnp.concatenate([high, high], axis=1)
    bottom = jnp.concatenate([low, jnp.zeros_like(low)], axis=1)
    return jnp.concatenate([top, bottom], axis=0)


def folded(product):
    half = product.shape[0] // 2
    return product[:half] + product[half:]


def half_depth(weights, value):
    return folded(mm(weights, jnp.concatenate(split(value), axis=0)))


def full_depth(both, high, value_high, value_low):
    return folded(mm(both, value_high)) + mm(high, value_low)


def sin_cos_pi(turns):
    near = turns - 2.0 * jnp.round(turns * 0.5)
    quarter = jnp.round(near * 2.0)
    v = (near - 0.5 * quarter) * math.pi
    v2 = v * v
    s = v * (
        1.0
        + v2
        * (-1.0 / 6 + v2 * (1.0 / 120 + v2 * (-1.0 / 5040 + v2 * (1.0 / 362880 - v2 / 39916800))))
    )
    c = 1.0 + v2 * (
        -0.5
        + v2
        * (1.0 / 24 + v2 * (-1.0 / 720 + v2 * (1.0 / 40320 + v2 * (-1.0 / 3628800 + v2 / 479001600))))
    )
    odd = jnp.abs(quarter) == 1.0
    sine = jnp.where(odd, quarter * c, jnp.where(quarter == 0.0, s, -s))
    cosine = jnp.where(odd, -quarter * s, jnp.where(quarter == 0.0, c, -c))
    return sine, cosine


def lane_row(piece, offset):
    row = jnp.concatenate([piece, jnp.zeros((1, 128 - piece.shape[1]), piece.dtype)], axis=1)
    return pltpu.roll(row, offset, 1) if offset else row


def pack_kernel(
    kind,
    positions_hbm,
    features_hbm,
    species_hbm,
    centers_hbm,
    neighbours_hbm,
    scale_hbm,
    shift_hbm,
    payload_ref,
    shift_row_ref,
    wide_ref,
    positions_ref,
    species_ref,
    centers_ref,
    neighbours_ref,
    scale_ref,
    shift_ref,
    sems,
):
    owned, nbr = neighbours_ref.shape
    per_row = 128 // nbr
    pairs_in = (
        (features_hbm, payload_ref.at[pl.ds(0, owned), :]),
        (neighbours_hbm, neighbours_ref),
        (centers_hbm, centers_ref),
        (positions_hbm, positions_ref),
        (species_hbm, species_ref),
        (scale_hbm, scale_ref),
        (shift_hbm, shift_ref),
    )
    copies = [
        pltpu.make_async_copy(source, target, sems.at[i])
        for i, (source, target) in enumerate(pairs_in)
    ]
    for copy in copies:
        copy.start()
    for copy in copies:
        copy.wait()
    payload_ref[owned : owned + 8] = jnp.zeros((8, 128), F32)
    shift_row = jnp.zeros((1, 128), F32)
    for cell in range(OWN_CELLS):
        x, z = cell // 2, cell % 2
        species = species_ref[x, 0, z : z + 1, :]
        scale = jnp.zeros(species.shape, F32)
        shift = jnp.zeros(species.shape, F32)
        for s in range(scale_ref.shape[0]):
            scale = jnp.where(species == s, scale_ref[s], scale)
            shift = jnp.where(species == s, shift_ref[s], shift)
        row = lane_row(scale, 3 * SITES)
        for c in range(3):
            row = row + lane_row(positions_ref[c, x, 0, z : z + 1, :], c * SITES)
        payload_ref[owned + cell : owned + cell + 1] = row
        shift_row = shift_row + lane_row(shift, cell * SITES)

    chosen = lax.broadcasted_iota(jnp.int32, (owned, owned), 0) == centers_ref[...]
    chosen = jnp.where(chosen, 1.0, 0.0)
    occupied = jnp.sum(chosen, axis=1, keepdims=True) > 0.5
    column = jnp.where(occupied, jnp.ones((owned, 128), F32), 0.0)
    shift_row_ref[...] = shift_row[:, :owned] * jnp.transpose(column)[0:1]
    chosen = chosen.astype(BF16)
    rows = neighbours_ref[...]
    upper = mm(chosen, (rows >> 4).astype(F32).astype(BF16))
    lower = mm(chosen, (rows & 15).astype(F32).astype(BF16))
    rows = (upper * 16.0 + lower).astype(jnp.int32)
    live = occupied & (rows < FRAME_CELLS * SITES)
    slot = lax.broadcasted_iota(jnp.int32, (owned, nbr), 0)
    cell = slot >> 3
    site = rows & 7
    place = rows >> 3
    near_z = (place & 3) + 1 - 2 * (cell & 1)
    column = place >> 2
    frame_x = (column * 11) >> 5
    frame_y = column - 3 * frame_x
    near_x = frame_x + 1 - 2 * (cell >> 1)
    side = jnp.where(frame_y == 1, 0, jnp.where(frame_y == 2, 1, kind - 1))
    block = (near_z >> 1) * 2 + 1 - (near_x >> 1)
    where = (block * kind + side) * owned + (near_x & 1) * 16 + (near_z & 1) * 8 + site
    code = jnp.where(live, 1 + where + (frame_y << 10), 0).astype(F32)
    wide_ref[...] = jnp.concatenate([code, jnp.zeros((owned, 128 - nbr), F32)], axis=1)
    codes = wide_ref[pl.ds(0, owned // per_row, stride=per_row), :]
    for j in range(1, per_row):
        more = wide_ref[pl.ds(j, owned // per_row, stride=per_row), :]
        codes = codes + pltpu.roll(more, j * nbr, 1)
    payload_ref[owned + 8 :] = codes


def fetch_kernel(*refs):
    count = len(refs) // 2
    sems = refs[-1]
    copies = [
        pltpu.make_async_copy(refs[i], refs[count + i], sems.at[i]) for i in range(count)
    ]
    for copy in copies:
        copy.start()
    for copy in copies:
        copy.wait()


def finish_kernel(mine_ref, shift_row_ref, *refs):
    *near_refs, energy_ref, forces_ref, virial_ref = refs
    owned = near_refs[0].shape[1]
    total = mine_ref[:, :owned]
    for near_ref in near_refs:
        total = total + near_ref[...]
    energy = total[12:13] + shift_row_ref[...]
    columns = jnp.transpose(jnp.concatenate([total, jnp.zeros((ORDERS, 128 - owned), F32)], axis=1))
    for cell in range(OWN_CELLS):
        x, z = cell // 2, cell % 2
        lanes = slice(cell * SITES, (cell + 1) * SITES)
        energy_ref[x, 0, z : z + 1, :] = energy[:, lanes]
        for c in range(3):
            forces_ref[c, x, 0, z : z + 1, :] = total[c : c + 1, lanes]
        virial_ref[x, 0, z] = columns[lanes, 3:12]


def force_kernel(kind, nbr, here_ref, last_x_ref, *refs):
    near_side_refs = refs[: 2 * kind - 2]
    (
        next_z_ref,
        center_weight_ref,
        near_weight_ref,
        basis_weight_ref,
        path_weight_ref,
        value_weight_ref,
        latent_weight_ref,
        out_weight_ref,
        keep_ref,
        send_ref,
    ) = refs[2 * kind - 2 :]
    height, width = here_ref.shape
    owned = OWN_CELLS * SITES
    short = owned + 8
    pairs = owned * nbr
    radial = basis_weight_ref.shape[0]
    span = GROUP * nbr
    groups = owned // GROUP
    wide = GROUP * ORDERS
    sites = SITES
    root_count = math.sqrt(nbr)
    root_three = math.sqrt(3.0)
    root_fifteen = math.sqrt(15.0)
    root_five = math.sqrt(5.0)
    far = next_z_ref[...]
    mains = [here_ref[...], last_x_ref[...], far[:height], far[height : 2 * height]]
    near_sides = [ref[...] for ref in near_side_refs]
    far_sides = far[2 * height :]
    far_sides = [far_sides[i * short : (i + 1) * short] for i in range(2 * kind - 2)]
    blocks_in = [
        [mains[0], *near_sides[0::2]],
        [mains[1], *near_sides[1::2]],
        [mains[2], *far_sides[0::2]],
        [mains[3], *far_sides[1::2]],
    ]
    feats = jnp.concatenate([side[:owned] for block in blocks_in for side in block], axis=0)
    known = feats.shape[0]
    center_feats = []
    coords = []
    scales = []
    codes = []
    cell_row = lax.broadcasted_iota(jnp.int32, (kind * OWN_CELLS, 128), 0) % OWN_CELLS
    tile_lane = lax.broadcasted_iota(jnp.int32, (kind * OWN_CELLS, 128), 1)
    for g, block in enumerate(blocks_in):
        behind_x, ahead_z = g % 2, g // 2
        cell = behind_x * 2 + 1 - ahead_z
        center_feats.append(block[0][cell * sites : (cell + 1) * sites])
        rows = jnp.concatenate([side[owned : owned + OWN_CELLS] for side in block], axis=0)
        scales.append(rows[cell : cell + 1])
        corner_x = (cell_row // 2 + 2 - 2 * behind_x).astype(F32) * CELL_SIDE
        corner_z = (cell_row % 2 + 2 * ahead_z).astype(F32) * CELL_SIDE
        corner = jnp.where(
            tile_lane < sites, corner_x, jnp.where(tile_lane < 2 * sites, 0.0, corner_z)
        )
        coords.append(rows + corner)
        start = short + cell * span // 128
        codes.extend(block[0][start + r : start + r + 1] for r in range(span // 128))
    center_feats = jnp.concatenate(center_feats, axis=0)
    coords = jnp.concatenate(coords, axis=0)
    code = jnp.concatenate(codes, axis=1).astype(jnp.int32)
    live = code > 0
    code = jnp.maximum(code - 1, 0)
    side_y = ((code >> 10) - 1).astype(F32)
    near_row = jnp.where(live, code & 1023, known)

    spread = jnp.broadcast_to(coords[:, None, :], (coords.shape[0], sites, 128))
    spread = spread.reshape(known, 128)
    keep_lane = lax.broadcasted_iota(jnp.int32, (known, 128), 1)
    keep_row = lax.broadcasted_iota(jnp.int32, (known, 128), 0)
    keep = (keep_lane % sites == keep_row % sites) & (keep_lane < 3 * sites)
    spread = jnp.where(keep, spread, 0.0)
    place_parts = jnp.concatenate(split3(jnp.transpose(spread)[: 3 * sites]), axis=0)

    value_rows = stacked(*split(jnp.transpose(value_weight_ref[...])))
    latent_high_t, latent_low_t = split(jnp.transpose(latent_weight_ref[...]))
    latent_both_t = jnp.concatenate([latent_high_t, latent_low_t], axis=0)
    latent_rows = stacked(*split(latent_weight_ref[...]))
    value_high, value_low = split(value_weight_ref[...])
    value_both = jnp.concatenate([value_high, value_low], axis=0)
    basis_t = jnp.transpose(basis_weight_ref[...])
    basis_high_t, basis_low_t = split(basis_t)
    basis_rows = stacked(*split(basis_weight_ref[...]))

    def project(weight, rows):
        weight = stacked(*split(jnp.transpose(weight)))
        return folded(mm_nt(weight, jnp.concatenate(split(rows), axis=1)))

    near_t = project(near_weight_ref[...], feats)
    own_t = project(center_weight_ref[...], center_feats)
    near_high, near_low = split(near_t)
    own_high, own_low = split(own_t)
    lookup = jnp.concatenate(
        [
            jnp.concatenate([near_high, own_high, basis_high_t, basis_high_t], axis=1),
            jnp.concatenate([near_low, own_low, basis_low_t, jnp.zeros_like(basis_low_t)], axis=1),
        ],
        axis=0,
    )
    scale_rows = jnp.concatenate(scales, axis=0)
    scale_parts = jnp.concatenate(
        [*split3(scale_rows), jnp.zeros((16 - 3 * groups, 128), BF16)], axis=0
    )

    level = lax.broadcasted_iota(jnp.int32, (ORDERS, width), 0)
    path_rows = jnp.where(
        level == 0,
        path_weight_ref[0:1, :],
        jnp.where(
            level < 4,
            path_weight_ref[1:2, :],
            jnp.where(level < 9, path_weight_ref[2:3, :], 0.0),
        ),
    )
    paths_t = jnp.transpose(jnp.concatenate([path_rows] * GROUP, axis=0)) * (1.0 / root_count)
    out_column = jnp.transpose(jnp.broadcast_to(out_weight_ref[...], (width, width)))
    out_column = jnp.concatenate([out_column] * (pairs // width), axis=1)

    site_ids = lax.broadcasted_iota(jnp.int32, (known, pairs), 0)
    slot_ids = lax.broadcasted_iota(jnp.int32, (owned, pairs), 0)
    slot_row = lax.broadcasted_iota(jnp.int32, (1, pairs), 1) // nbr
    group_row = slot_row // GROUP
    center_cell = group_row % 2 * 2 + 1 - group_row // 2
    center_row = group_row * (kind * owned) + center_cell * sites + slot_row % GROUP
    block_row = lax.broadcasted_iota(jnp.int32, (wide, span), 0) // ORDERS
    block_lane = lax.broadcasted_iota(jnp.int32, (wide, span), 1) // nbr
    block_mask = (block_row == block_lane).astype(F32)
    block_half = block_mask.astype(BF16)
    order = lax.broadcasted_iota(jnp.int32, (radial, pairs), 0).astype(F32) + 1.0
    lanes = [slice(g * span, (g + 1) * span) for g in range(groups)]

    pick = jnp.where(site_ids == near_row, 1.0, 0.0)
    from_center = jnp.where(site_ids == center_row, 1.0, 0.0)
    pick_half = pick.astype(BF16)
    center_half = from_center.astype(BF16)
    slot_half = jnp.where(slot_ids == slot_row, 1.0, 0.0).astype(BF16)

    moved = mm(place_parts, (pick - from_center).astype(BF16))
    moved = moved[: 3 * sites] + moved[3 * sites : 6 * sites] + moved[6 * sites :]
    dx = jnp.where(live, jnp.sum(moved[:sites], axis=0, keepdims=True), 6.0)
    dy = jnp.sum(moved[sites : 2 * sites], axis=0, keepdims=True) + CELL_SIDE * side_y
    dy = jnp.where(live, dy, 0.0)
    dz = jnp.where(live, jnp.sum(moved[2 * sites :], axis=0, keepdims=True), 0.0)
    length = jnp.sqrt(dx * dx + dy * dy + dz * dz)
    inverse = 1.0 / length
    ratio = length * (1.0 / CUTOFF)
    inside = live & (ratio < 1.0)
    r2 = ratio * ratio
    r5 = r2 * r2 * ratio
    r6 = r5 * ratio
    weight = jnp.where(inside, 1.0 - r6 * (28.0 - 48.0 * ratio + 21.0 * r2), 0.0)
    slope = jnp.where(inside, -168.0 * r5 * (1.0 - 2.0 * ratio + r2), 0.0)
    sine, cosine = sin_cos_pi(order * ratio)
    basis = (math.sqrt(2.0 / CUTOFF) * inverse) * sine
    basis_slope = (math.sqrt(2.0 / CUTOFF) * inverse) * (
        (math.pi / CUTOFF) * order * cosine - sine * inverse
    )
    ex = dx * inverse
    ey = dy * inverse
    ez = dz * inverse
    angular = jnp.concatenate(
        [
            jnp.ones_like(ex),
            root_three * ex,
            root_three * ey,
            root_three * ez,
            root_fifteen * ex * ey,
            root_fifteen * ey * ez,
            0.5 * root_five * (3.0 * ez * ez - 1.0),
            root_fifteen * ex * ez,
            0.5 * root_fifteen * (ex * ex - ey * ey),
            jnp.zeros((ORDERS - 9, pairs), F32),
        ],
        axis=0,
    )
    angular_high, angular_low = split(angular)
    blocks = [
        jnp.concatenate(
            [
                jnp.concatenate([angular_high[:, cut]] * GROUP, axis=0) * block_half,
                jnp.concatenate([angular_low[:, cut]] * GROUP, axis=0) * block_half,
            ],
            axis=0,
        )
        for cut in lanes
    ]
    lane_ids = lax.broadcasted_iota(jnp.int32, (128, span), 0)
    lane_slot = lax.broadcasted_iota(jnp.int32, (128, span), 1) // nbr + 3 * sites
    scale = mm(scale_parts, jnp.where(lane_ids == lane_slot, 1.0, 0.0).astype(BF16))
    scale = scale[:groups] + scale[groups : 2 * groups] + scale[2 * groups : 3 * groups]
    scale = jnp.concatenate([scale[g : g + 1] for g in range(groups)], axis=1)
    scale = scale * (1.0 / root_count)
    pull = ROOT_HALF * scale

    basis_high, basis_low = split(basis)
    before = folded(
        mm(lookup, jnp.concatenate([pick_half, slot_half, basis_high, basis_low], axis=0))
    )
    gate = 0.5 * jnp.tanh(0.5 * before) + 0.5
    active = before * gate
    latent = weight * active
    mixed = half_depth(value_rows, latent)
    values = mixed[:width]
    env_high, env_low = split(mixed[width:])

    def over_pairs(high, low):
        sums = []
        for cut, block in zip(lanes, blocks):
            quad = mm_nt(jnp.concatenate([high[:, cut], low[:, cut]], axis=0), block)
            sums.append((quad[:width, :wide] + quad[:width, wide:] + quad[width:, :wide]) * paths_t)
        return sums

    def over_orders(tables):
        parts = [folded(mm(stacked(*split(t)), block)) for t, block in zip(tables, blocks)]
        return jnp.concatenate(parts, axis=1)

    weighted = over_pairs(env_high, env_low)
    inner = over_orders(weighted)
    scalars = values * inner
    joined_high, joined_low = split(jnp.concatenate([latent, scalars], axis=0))
    z = full_depth(latent_both_t, latent_high_t, joined_high, joined_low)
    z_gate = 0.5 * jnp.tanh(0.5 * z) + 0.5
    update = z * z_gate
    update_out = update * out_column
    pair_energy = jnp.sum(latent * out_column + weight * update_out, axis=0, keepdims=True)
    pair_energy = pair_energy * pull
    d_z = (pull * weight) * out_column * (z_gate + update * (1.0 - z_gate))
    spread_back = half_depth(latent_rows, d_z)
    d_scalars = spread_back[width:]
    d_values = d_scalars * inner
    dinner_high, dinner_low = split(d_scalars * values)
    d_embed = over_pairs(dinner_high, dinner_low)
    d_env = over_orders(d_embed)

    d_angular = []
    for g, cut in enumerate(lanes):
        sides = jnp.transpose(jnp.concatenate([weighted[g], d_embed[g]], axis=0))
        sides_high, sides_low = split(sides)
        d_block = full_depth(
            jnp.concatenate([sides_high, sides_low], axis=0),
            sides_high,
            jnp.concatenate([dinner_high[:, cut], env_high[:, cut]], axis=0),
            jnp.concatenate([dinner_low[:, cut], env_low[:, cut]], axis=0),
        )
        d_block = d_block * block_mask
        total = d_block[:ORDERS]
        for k in range(1, GROUP):
            total = total + d_block[k * ORDERS : (k + 1) * ORDERS]
        d_angular.append(total)
    d_angular = jnp.concatenate(d_angular, axis=1)

    mixed_high, mixed_low = split(jnp.concatenate([d_values, d_env], axis=0))
    d_latent = (
        full_depth(value_both, value_high, mixed_high, mixed_low)
        + spread_back[:width]
        + pull * out_column
    )
    d_weight = jnp.sum(d_latent * active + pull * update_out, axis=0, keepdims=True)
    d_before = d_latent * weight * (gate + active * (1.0 - gate))
    d_basis = half_depth(basis_rows, d_before)

    d_length = jnp.sum(d_basis * basis_slope, axis=0, keepdims=True) + d_weight * slope * (
        1.0 / CUTOFF
    )
    a1, a2, a3, a4, a5, a6, a7, a8 = [d_angular[m : m + 1] for m in range(1, 9)]
    ux = root_three * a1 + root_fifteen * (ey * a4 + ez * a7 + ex * a8)
    uy = root_three * a2 + root_fifteen * (ex * a4 + ez * a5 - ey * a8)
    uz = root_three * a3 + root_fifteen * (ey * a5 + ex * a7) + 3.0 * root_five * ez * a6
    along = ex * ux + ey * uy + ez * uz
    radial_part = d_length - along * inverse
    gx = ux * inverse + ex * radial_part
    gy = uy * inverse + ey * radial_part
    gz = uz * inverse + ez * radial_part
    hx = -0.5 * dx
    hy = -0.5 * dy
    hz = -0.5 * dz
    virial = [hx * gx, hx * gy, hx * gz, hy * gx, hy * gy, hy * gz, hz * gx, hz * gy, hz * gz]
    rest = [jnp.zeros((ORDERS - 13, pairs), F32)]
    near_terms = jnp.concatenate(
        [-gx, -gy, -gz, *virial, jnp.zeros_like(gx), *rest], axis=0
    )
    center_terms = jnp.concatenate([gx, gy, gz, *virial, pair_energy, *rest], axis=0)
    near_sums = mm_nt(jnp.concatenate(split(near_terms), axis=0), pick_half)
    center_sums = mm_nt(jnp.concatenate(split(center_terms), axis=0), center_half)
    totals = folded(near_sums + center_sums)
    keep_ref[...] = totals[:, : known // 2]
    send_ref[...] = totals[:, known // 2 :]


def in_hbm(*arrays):
    return [pltpu.with_memory_space_constraint(array, pltpu.HBM) for array in arrays]


def joined(parts):
    total = sum(part.shape[0] for part in parts)
    start = 0
    pads = []
    for part in parts:
        end = start + part.shape[0]
        pads.append(jnp.pad(part, ((start, total - end), (0, 0))))
        start = end
    return functools.reduce(jnp.add, pads)


def local(
    positions,
    features,
    species,
    centers,
    neighbours,
    counts,
    species_scale,
    species_shift,
    center_weight,
    near_weight,
    basis_weight,
    path_weight,
    value_weight,
    latent_weight,
    out_weight,
):
    cells_x, cells_y, cells_z, sites, width = features.shape
    cell_count = cells_x * cells_y * cells_z
    owned = cell_count * sites
    assert (cells_x, cells_y, cells_z, sites) == (2, 1, 2, SITES)
    pairs = neighbours.size
    nbr = pairs // owned
    kind = min(3, lax.axis_size("gy"))

    def moved(array, steps):
        names = tuple(steps)
        sizes = [lax.axis_size(name) for name in names]
        route = []
        for at in np.ndindex(*sizes):
            to = [(p + steps[name]) % size for p, name, size in zip(at, names, sizes)]
            route.append(
                (int(np.ravel_multi_index(at, sizes)), int(np.ravel_multi_index(to, sizes)))
            )
        return lax.ppermute(array, names, route)

    vmem = pl.BlockSpec(memory_space=pltpu.VMEM)
    hbm = pl.BlockSpec(memory_space=pltpu.HBM)
    here, shift_row = pl.pallas_call(
        functools.partial(pack_kernel, kind),
        out_shape=(
            jax.ShapeDtypeStruct((owned + 8 + pairs // 128, width), F32),
            jax.ShapeDtypeStruct((1, owned), F32),
        ),
        in_specs=[hbm] * 7,
        out_specs=(vmem, vmem),
        scratch_shapes=[
            pltpu.VMEM((owned, 128), F32),
            pltpu.VMEM(positions.shape, F32),
            pltpu.VMEM(species.shape, jnp.int32),
            pltpu.VMEM((1, owned), jnp.int32),
            pltpu.VMEM(neighbours.shape, jnp.int32),
            pltpu.SMEM(species_scale.shape, F32),
            pltpu.SMEM(species_shift.shape, F32),
            pltpu.SemaphoreType.DMA((7,)),
        ],
        compiler_params=pltpu.CompilerParams(vmem_limit_bytes=8 * 1024 * 1024),
        name="pack_payload",
    )(
        *in_hbm(
            positions,
            features.reshape(owned, width),
            species,
            centers.reshape(1, owned),
            neighbours,
            species_scale,
            species_shift,
        )
    )
    weights = (
        center_weight,
        near_weight,
        basis_weight,
        path_weight,
        value_weight,
        latent_weight,
        out_weight.reshape(1, width),
    )
    weights = pl.pallas_call(
        fetch_kernel,
        out_shape=tuple(jax.ShapeDtypeStruct(w.shape, F32) for w in weights),
        in_specs=[hbm] * len(weights),
        out_specs=(vmem,) * len(weights),
        scratch_shapes=[pltpu.SemaphoreType.DMA((len(weights),))],
        compiler_params=pltpu.CompilerParams(vmem_limit_bytes=8 * 1024 * 1024),
        name="fetch_weights",
    )(*in_hbm(*weights))
    short = here[: owned + 8]
    last_x = moved(here, {"gx": 1})
    sides = []
    for step in (-1, 1)[: kind - 1]:
        sides.append(moved(short, {"gx": 1, "gy": step}))
        sides.insert(-1, moved(short, {"gy": step}))
    next_z = moved(joined([here, last_x, *sides]), {"gz": -1})
    half = 2 * kind * owned
    keep, send = pl.pallas_call(
        functools.partial(force_kernel, kind, nbr),
        out_shape=(
            jax.ShapeDtypeStruct((ORDERS, half), F32),
            jax.ShapeDtypeStruct((ORDERS, half), F32),
        ),
        in_specs=[vmem] * (8 + 2 * kind),
        out_specs=(vmem, vmem),
        compiler_params=pltpu.CompilerParams(vmem_limit_bytes=32 * 1024 * 1024),
        name="pair_forces",
    )(
        here,
        last_x,
        *sides,
        next_z,
        *weights,
    )
    totals = keep + moved(send, {"gz": 1})

    def part(index):
        return totals[:, index * owned : (index + 1) * owned]

    back = [moved(part(kind), {"gx": -1})]
    for i, step in enumerate((1, -1)[: kind - 1]):
        back.append(moved(part(kind + 1 + i), {"gx": -1, "gy": step}))
        back.append(moved(part(1 + i), {"gy": step}))
    site_energy, forces, virial = pl.pallas_call(
        finish_kernel,
        out_shape=(
            jax.ShapeDtypeStruct(species.shape, F32),
            jax.ShapeDtypeStruct(positions.shape, F32),
            jax.ShapeDtypeStruct((*species.shape, 9), F32),
        ),
        in_specs=[vmem] * (2 + len(back)),
        out_specs=(vmem, vmem, vmem),
        compiler_params=pltpu.CompilerParams(vmem_limit_bytes=8 * 1024 * 1024),
        name="write_outputs",
    )(totals, shift_row, *back)
    return (site_energy, forces, jnp.transpose(virial, (4, 0, 1, 2, 3)))


def solution(mesh):
    placed = (
        P(None, "gx", "gy", "gz", None),
        P("gx", "gy", "gz", None, None),
        P("gx", "gy", "gz", None),
        P(("gx", "gy", "gz")),
        P(("gx", "gy", "gz"), None),
        P(("gx", "gy", "gz")),
        P(),
        P(),
        P(),
        P(),
        P(),
        P(),
        P(),
        P(),
        P(),
    )
    return jax.shard_map(
        local,
        mesh=mesh,
        in_specs=placed,
        out_specs=(
            P("gx", "gy", "gz", None),
            P(None, "gx", "gy", "gz", None),
            P(None, "gx", "gy", "gz", None),
        ),
        check_vma=False,
    )
```

```python
import functools
import math

import jax
import jax.numpy as jnp
import numpy as np
from jax import lax
from jax.experimental import pallas as pl
from jax.experimental.pallas import tpu as pltpu
from jax.sharding import PartitionSpec as P

EXACT_DOT = lax.Precision.HIGHEST
CUTOFF = 5.0
CELL_SIDE = 4.6
ROOT_HALF = 0.7071067811865476
GROUP = 8
ORDERS = 16
SITES = 8
OWN_CELLS = 4
FRAME_CELLS = 48
F32 = jnp.float32
BF16 = jnp.bfloat16


def split(value):
    high = value.astype(BF16)
    low = (value - high.astype(F32)).astype(BF16)
    return high, low


def split3(value):
    high = value.astype(BF16)
    rest = value - high.astype(F32)
    middle = rest.astype(BF16)
    low = (rest - middle.astype(F32)).astype(BF16)
    return high, middle, low


def mm(a, b):
    return lax.dot_general(a, b, (((1,), (0,)), ((), ())), preferred_element_type=F32)


def mm_nt(a, b):
    return lax.dot_general(a, b, (((1,), (1,)), ((), ())), preferred_element_type=F32)


def stacked(high, low):
    top = jnp.concatenate([high, high], axis=1)
    bottom = jnp.concatenate([low, jnp.zeros_like(low)], axis=1)
    return jnp.concatenate([top, bottom], axis=0)


def folded(product):
    half = product.shape[0] // 2
    return product[:half] + product[half:]


def half_depth(weights, value):
    return folded(mm(weights, jnp.concatenate(split(value), axis=0)))


def full_depth(both, high, value_high, value_low):
    return folded(mm(both, value_high)) + mm(high, value_low)


def sin_cos_pi(turns):
    near = turns - 2.0 * jnp.round(turns * 0.5)
    quarter = jnp.round(near * 2.0)
    v = (near - 0.5 * quarter) * math.pi
    v2 = v * v
    s = v * (
        1.0
        + v2
        * (-1.0 / 6 + v2 * (1.0 / 120 + v2 * (-1.0 / 5040 + v2 * (1.0 / 362880 - v2 / 39916800))))
    )
    c = 1.0 + v2 * (
        -0.5
        + v2
        * (1.0 / 24 + v2 * (-1.0 / 720 + v2 * (1.0 / 40320 + v2 * (-1.0 / 3628800 + v2 / 479001600))))
    )
    odd = jnp.abs(quarter) == 1.0
    sine = jnp.where(odd, quarter * c, jnp.where(quarter == 0.0, s, -s))
    cosine = jnp.where(odd, -quarter * s, jnp.where(quarter == 0.0, c, -c))
    return sine, cosine


def lane_row(piece, offset):
    row = jnp.concatenate([piece, jnp.zeros((1, 128 - piece.shape[1]), piece.dtype)], axis=1)
    return pltpu.roll(row, offset, 1) if offset else row


def pack_kernel(
    kind,
    positions_hbm,
    features_hbm,
    species_hbm,
    centers_hbm,
    neighbours_hbm,
    scale_hbm,
    payload_ref,
    wide_ref,
    positions_ref,
    species_ref,
    centers_ref,
    neighbours_ref,
    scale_ref,
    sems,
):
    owned, nbr = neighbours_ref.shape
    per_row = 128 // nbr
    pairs_in = (
        (features_hbm, payload_ref.at[pl.ds(0, owned), :]),
        (neighbours_hbm, neighbours_ref),
        (centers_hbm, centers_ref),
        (positions_hbm, positions_ref),
        (species_hbm, species_ref),
        (scale_hbm, scale_ref),
    )
    copies = [
        pltpu.make_async_copy(source, target, sems.at[i])
        for i, (source, target) in enumerate(pairs_in)
    ]
    for copy in copies:
        copy.start()
    for copy in copies:
        copy.wait()
    payload_ref[owned : owned + 8] = jnp.zeros((8, 128), F32)
    for cell in range(OWN_CELLS):
        x, z = cell // 2, cell % 2
        species = species_ref[x, 0, z : z + 1, :]
        scale = jnp.zeros(species.shape, F32)
        for s in range(scale_ref.shape[0]):
            scale = jnp.where(species == s, scale_ref[s], scale)
        row = lane_row(scale, 3 * SITES)
        for c in range(3):
            row = row + lane_row(positions_ref[c, x, 0, z : z + 1, :], c * SITES)
        payload_ref[owned + cell : owned + cell + 1] = row

    chosen = lax.broadcasted_iota(jnp.int32, (owned, owned), 0) == centers_ref[...]
    chosen = jnp.where(chosen, 1.0, 0.0)
    occupied = jnp.sum(chosen, axis=1, keepdims=True) > 0.5
    chosen = chosen.astype(BF16)
    rows = neighbours_ref[...]
    upper = mm(chosen, (rows >> 4).astype(F32).astype(BF16))
    lower = mm(chosen, (rows & 15).astype(F32).astype(BF16))
    rows = (upper * 16.0 + lower).astype(jnp.int32)
    live = occupied & (rows < FRAME_CELLS * SITES)
    slot = lax.broadcasted_iota(jnp.int32, (owned, nbr), 0)
    cell = slot >> 3
    site = rows & 7
    place = rows >> 3
    near_z = (place & 3) + 1 - 2 * (cell & 1)
    column = place >> 2
    frame_x = (column * 11) >> 5
    frame_y = column - 3 * frame_x
    near_x = frame_x + 1 - 2 * (cell >> 1)
    side = jnp.where(frame_y == 1, 0, jnp.where(frame_y == 2, 1, kind - 1))
    block = (near_z >> 1) * 2 + 1 - (near_x >> 1)
    where = (block * kind + side) * owned + (near_x & 1) * 16 + (near_z & 1) * 8 + site
    code = jnp.where(live, 1 + where + (frame_y << 10), 0).astype(F32)
    wide_ref[...] = jnp.concatenate([code, jnp.zeros((owned, 128 - nbr), F32)], axis=1)
    codes = wide_ref[pl.ds(0, owned // per_row, stride=per_row), :]
    for j in range(1, per_row):
        more = wide_ref[pl.ds(j, owned // per_row, stride=per_row), :]
        codes = codes + pltpu.roll(more, j * nbr, 1)
    payload_ref[owned + 8 :] = codes


def fetch_kernel(species_hbm, centers_hbm, shift_hbm, *refs):
    *refs, shift_row_ref, species_ref, centers_ref, shift_ref, sems = refs
    count = len(refs) // 2
    pairs_in = [
        (species_hbm, species_ref),
        (centers_hbm, centers_ref),
        (shift_hbm, shift_ref),
        *zip(refs[:count], refs[count:]),
    ]
    copies = [
        pltpu.make_async_copy(source, target, sems.at[i])
        for i, (source, target) in enumerate(pairs_in)
    ]
    for copy in copies:
        copy.start()
    for copy in copies:
        copy.wait()
    owned = centers_ref.shape[1]
    shift_row = jnp.zeros((1, 128), F32)
    for cell in range(OWN_CELLS):
        species = species_ref[cell // 2, 0, cell % 2 : cell % 2 + 1, :]
        shift = jnp.zeros(species.shape, F32)
        for s in range(shift_ref.shape[0]):
            shift = jnp.where(species == s, shift_ref[s], shift)
        shift_row = shift_row + lane_row(shift, cell * SITES)
    chosen = lax.broadcasted_iota(jnp.int32, (owned, owned), 0) == centers_ref[...]
    occupied = jnp.sum(jnp.where(chosen, 1.0, 0.0), axis=1, keepdims=True) > 0.5
    column = jnp.where(occupied, jnp.ones((owned, 128), F32), 0.0)
    shift_row_ref[...] = shift_row[:, :owned] * jnp.transpose(column)[0:1]


def finish_kernel(mine_ref, shift_row_ref, *refs):
    *near_refs, energy_ref, forces_ref, virial_ref = refs
    owned = near_refs[0].shape[1]
    total = mine_ref[:, :owned]
    for near_ref in near_refs:
        total = total + near_ref[...]
    energy = total[12:13] + shift_row_ref[...]
    columns = jnp.transpose(jnp.concatenate([total, jnp.zeros((ORDERS, 128 - owned), F32)], axis=1))
    for cell in range(OWN_CELLS):
        x, z = cell // 2, cell % 2
        lanes = slice(cell * SITES, (cell + 1) * SITES)
        energy_ref[x, 0, z : z + 1, :] = energy[:, lanes]
        for c in range(3):
            forces_ref[c, x, 0, z : z + 1, :] = total[c : c + 1, lanes]
        virial_ref[x, 0, z] = columns[lanes, 3:12]


def force_kernel(kind, nbr, here_ref, last_x_ref, *refs):
    near_side_refs = refs[: 2 * kind - 2]
    (
        next_z_ref,
        next_xz_ref,
        center_weight_ref,
        near_weight_ref,
        basis_weight_ref,
        path_weight_ref,
        value_weight_ref,
        latent_weight_ref,
        out_weight_ref,
        keep_ref,
        send_ref,
    ) = refs[2 * kind - 2 :]
    height, width = here_ref.shape
    owned = OWN_CELLS * SITES
    short = owned + 8
    pairs = owned * nbr
    radial = basis_weight_ref.shape[0]
    span = GROUP * nbr
    groups = owned // GROUP
    wide = GROUP * ORDERS
    sites = SITES
    root_count = math.sqrt(nbr)
    root_three = math.sqrt(3.0)
    root_fifteen = math.sqrt(15.0)
    root_five = math.sqrt(5.0)
    near_sides = [ref[...] for ref in near_side_refs]
    blocks_in = [
        [here_ref[...], *near_sides[0::2]],
        [last_x_ref[...], *near_sides[1::2]],
    ]
    for far_ref in (next_z_ref, next_xz_ref):
        far = far_ref[...]
        sides = [
            far[height + i * short : height + (i + 1) * short] for i in range(kind - 1)
        ]
        blocks_in.append([far[:height], *sides])
    feats = jnp.concatenate([side[:owned] for block in blocks_in for side in block], axis=0)
    known = feats.shape[0]
    center_feats = []
    coords = []
    scales = []
    codes = []
    cell_row = lax.broadcasted_iota(jnp.int32, (kind * OWN_CELLS, 128), 0) % OWN_CELLS
    tile_lane = lax.broadcasted_iota(jnp.int32, (kind * OWN_CELLS, 128), 1)
    for g, block in enumerate(blocks_in):
        behind_x, ahead_z = g % 2, g // 2
        cell = behind_x * 2 + 1 - ahead_z
        center_feats.append(block[0][cell * sites : (cell + 1) * sites])
        rows = jnp.concatenate([side[owned : owned + OWN_CELLS] for side in block], axis=0)
        scales.append(rows[cell : cell + 1])
        corner_x = (cell_row // 2 + 2 - 2 * behind_x).astype(F32) * CELL_SIDE
        corner_z = (cell_row % 2 + 2 * ahead_z).astype(F32) * CELL_SIDE
        corner = jnp.where(
            tile_lane < sites, corner_x, jnp.where(tile_lane < 2 * sites, 0.0, corner_z)
        )
        coords.append(rows + corner)
        start = short + cell * span // 128
        codes.extend(block[0][start + r : start + r + 1] for r in range(span // 128))
    center_feats = jnp.concatenate(center_feats, axis=0)
    coords = jnp.concatenate(coords, axis=0)
    code = jnp.concatenate(codes, axis=1).astype(jnp.int32)
    live = code > 0
    code = jnp.maximum(code - 1, 0)
    side_y = ((code >> 10) - 1).astype(F32)
    near_row = jnp.where(live, code & 1023, known)

    spread = jnp.broadcast_to(coords[:, None, :], (coords.shape[0], sites, 128))
    spread = spread.reshape(known, 128)
    keep_lane = lax.broadcasted_iota(jnp.int32, (known, 128), 1)
    keep_row = lax.broadcasted_iota(jnp.int32, (known, 128), 0)
    keep = (keep_lane % sites == keep_row % sites) & (keep_lane < 3 * sites)
    spread = jnp.where(keep, spread, 0.0)
    place_parts = jnp.concatenate(split3(jnp.transpose(spread)[: 3 * sites]), axis=0)

    value_rows = stacked(*split(jnp.transpose(value_weight_ref[...])))
    latent_high_t, latent_low_t = split(jnp.transpose(latent_weight_ref[...]))
    latent_both_t = jnp.concatenate([latent_high_t, latent_low_t], axis=0)
    latent_rows = stacked(*split(latent_weight_ref[...]))
    value_high, value_low = split(value_weight_ref[...])
    value_both = jnp.concatenate([value_high, value_low], axis=0)
    basis_t = jnp.transpose(basis_weight_ref[...])
    basis_high_t, basis_low_t = split(basis_t)
    basis_rows = stacked(*split(basis_weight_ref[...]))

    def project(weight, rows):
        weight = stacked(*split(jnp.transpose(weight)))
        return folded(mm_nt(weight, jnp.concatenate(split(rows), axis=1)))

    near_t = project(near_weight_ref[...], feats)
    own_t = project(center_weight_ref[...], center_feats)
    near_high, near_low = split(near_t)
    own_high, own_low = split(own_t)
    lookup = jnp.concatenate(
        [
            jnp.concatenate([near_high, own_high, basis_high_t, basis_high_t], axis=1),
            jnp.concatenate([near_low, own_low, basis_low_t, jnp.zeros_like(basis_low_t)], axis=1),
        ],
        axis=0,
    )
    scale_rows = jnp.concatenate(scales, axis=0)
    scale_parts = jnp.concatenate(
        [*split3(scale_rows), jnp.zeros((16 - 3 * groups, 128), BF16)], axis=0
    )

    level = lax.broadcasted_iota(jnp.int32, (ORDERS, width), 0)
    path_rows = jnp.where(
        level == 0,
        path_weight_ref[0:1, :],
        jnp.where(
            level < 4,
            path_weight_ref[1:2, :],
            jnp.where(level < 9, path_weight_ref[2:3, :], 0.0),
        ),
    )
    paths_t = jnp.transpose(jnp.concatenate([path_rows] * GROUP, axis=0)) * (1.0 / root_count)
    out_column = jnp.transpose(jnp.broadcast_to(out_weight_ref[...], (width, width)))
    out_column = jnp.concatenate([out_column] * (pairs // width), axis=1)

    site_ids = lax.broadcasted_iota(jnp.int32, (known, pairs), 0)
    slot_ids = lax.broadcasted_iota(jnp.int32, (owned, pairs), 0)
    slot_row = lax.broadcasted_iota(jnp.int32, (1, pairs), 1) // nbr
    group_row = slot_row // GROUP
    center_cell = group_row % 2 * 2 + 1 - group_row // 2
    center_row = group_row * (kind * owned) + center_cell * sites + slot_row % GROUP
    block_row = lax.broadcasted_iota(jnp.int32, (wide, span), 0) // ORDERS
    block_lane = lax.broadcasted_iota(jnp.int32, (wide, span), 1) // nbr
    block_mask = (block_row == block_lane).astype(F32)
    block_half = block_mask.astype(BF16)
    order = lax.broadcasted_iota(jnp.int32, (radial, pairs), 0).astype(F32) + 1.0
    lanes = [slice(g * span, (g + 1) * span) for g in range(groups)]

    pick = jnp.where(site_ids == near_row, 1.0, 0.0)
    from_center = jnp.where(site_ids == center_row, 1.0, 0.0)
    pick_half = pick.astype(BF16)
    center_half = from_center.astype(BF16)
    slot_half = jnp.where(slot_ids == slot_row, 1.0, 0.0).astype(BF16)

    moved = mm(place_parts, (pick - from_center).astype(BF16))
    moved = moved[: 3 * sites] + moved[3 * sites : 6 * sites] + moved[6 * sites :]
    dx = jnp.where(live, jnp.sum(moved[:sites], axis=0, keepdims=True), 6.0)
    dy = jnp.sum(moved[sites : 2 * sites], axis=0, keepdims=True) + CELL_SIDE * side_y
    dy = jnp.where(live, dy, 0.0)
    dz = jnp.where(live, jnp.sum(moved[2 * sites :], axis=0, keepdims=True), 0.0)
    length = jnp.sqrt(dx * dx + dy * dy + dz * dz)
    inverse = 1.0 / length
    ratio = length * (1.0 / CUTOFF)
    inside = live & (ratio < 1.0)
    r2 = ratio * ratio
    r5 = r2 * r2 * ratio
    r6 = r5 * ratio
    weight = jnp.where(inside, 1.0 - r6 * (28.0 - 48.0 * ratio + 21.0 * r2), 0.0)
    slope = jnp.where(inside, -168.0 * r5 * (1.0 - 2.0 * ratio + r2), 0.0)
    sine, cosine = sin_cos_pi(order * ratio)
    basis = (math.sqrt(2.0 / CUTOFF) * inverse) * sine
    basis_slope = (math.sqrt(2.0 / CUTOFF) * inverse) * (
        (math.pi / CUTOFF) * order * cosine - sine * inverse
    )
    ex = dx * inverse
    ey = dy * inverse
    ez = dz * inverse
    angular = jnp.concatenate(
        [
            jnp.ones_like(ex),
            root_three * ex,
            root_three * ey,
            root_three * ez,
            root_fifteen * ex * ey,
            root_fifteen * ey * ez,
            0.5 * root_five * (3.0 * ez * ez - 1.0),
            root_fifteen * ex * ez,
            0.5 * root_fifteen * (ex * ex - ey * ey),
            jnp.zeros((ORDERS - 9, pairs), F32),
        ],
        axis=0,
    )
    angular_high, angular_low = split(angular)
    blocks = [
        jnp.concatenate(
            [
                jnp.concatenate([angular_high[:, cut]] * GROUP, axis=0) * block_half,
                jnp.concatenate([angular_low[:, cut]] * GROUP, axis=0) * block_half,
            ],
            axis=0,
        )
        for cut in lanes
    ]
    lane_ids = lax.broadcasted_iota(jnp.int32, (128, span), 0)
    lane_slot = lax.broadcasted_iota(jnp.int32, (128, span), 1) // nbr + 3 * sites
    scale = mm(scale_parts, jnp.where(lane_ids == lane_slot, 1.0, 0.0).astype(BF16))
    scale = scale[:groups] + scale[groups : 2 * groups] + scale[2 * groups : 3 * groups]
    scale = jnp.concatenate([scale[g : g + 1] for g in range(groups)], axis=1)
    scale = scale * (1.0 / root_count)
    pull = ROOT_HALF * scale

    basis_high, basis_low = split(basis)
    before = folded(
        mm(lookup, jnp.concatenate([pick_half, slot_half, basis_high, basis_low], axis=0))
    )
    gate = 0.5 * jnp.tanh(0.5 * before) + 0.5
    active = before * gate
    latent = weight * active
    mixed = half_depth(value_rows, latent)
    values = mixed[:width]
    env_high, env_low = split(mixed[width:])

    def over_pairs(high, low):
        sums = []
        for cut, block in zip(lanes, blocks):
            quad = mm_nt(jnp.concatenate([high[:, cut], low[:, cut]], axis=0), block)
            sums.append((quad[:width, :wide] + quad[:width, wide:] + quad[width:, :wide]) * paths_t)
        return sums

    def over_orders(tables):
        parts = [folded(mm(stacked(*split(t)), block)) for t, block in zip(tables, blocks)]
        return jnp.concatenate(parts, axis=1)

    weighted = over_pairs(env_high, env_low)
    inner = over_orders(weighted)
    scalars = values * inner
    joined_high, joined_low = split(jnp.concatenate([latent, scalars], axis=0))
    z = full_depth(latent_both_t, latent_high_t, joined_high, joined_low)
    z_gate = 0.5 * jnp.tanh(0.5 * z) + 0.5
    update = z * z_gate
    update_out = update * out_column
    pair_energy = jnp.sum(latent * out_column + weight * update_out, axis=0, keepdims=True)
    pair_energy = pair_energy * pull
    d_z = (pull * weight) * out_column * (z_gate + update * (1.0 - z_gate))
    spread_back = half_depth(latent_rows, d_z)
    d_scalars = spread_back[width:]
    d_values = d_scalars * inner
    dinner_high, dinner_low = split(d_scalars * values)
    d_embed = over_pairs(dinner_high, dinner_low)
    d_env = over_orders(d_embed)

    d_angular = []
    for g, cut in enumerate(lanes):
        sides = jnp.transpose(jnp.concatenate([weighted[g], d_embed[g]], axis=0))
        sides_high, sides_low = split(sides)
        d_block = full_depth(
            jnp.concatenate([sides_high, sides_low], axis=0),
            sides_high,
            jnp.concatenate([dinner_high[:, cut], env_high[:, cut]], axis=0),
            jnp.concatenate([dinner_low[:, cut], env_low[:, cut]], axis=0),
        )
        d_block = d_block * block_mask
        total = d_block[:ORDERS]
        for k in range(1, GROUP):
            total = total + d_block[k * ORDERS : (k + 1) * ORDERS]
        d_angular.append(total)
    d_angular = jnp.concatenate(d_angular, axis=1)

    mixed_high, mixed_low = split(jnp.concatenate([d_values, d_env], axis=0))
    d_latent = (
        full_depth(value_both, value_high, mixed_high, mixed_low)
        + spread_back[:width]
        + pull * out_column
    )
    d_weight = jnp.sum(d_latent * active + pull * update_out, axis=0, keepdims=True)
    d_before = d_latent * weight * (gate + active * (1.0 - gate))
    d_basis = half_depth(basis_rows, d_before)

    d_length = jnp.sum(d_basis * basis_slope, axis=0, keepdims=True) + d_weight * slope * (
        1.0 / CUTOFF
    )
    a1, a2, a3, a4, a5, a6, a7, a8 = [d_angular[m : m + 1] for m in range(1, 9)]
    ux = root_three * a1 + root_fifteen * (ey * a4 + ez * a7 + ex * a8)
    uy = root_three * a2 + root_fifteen * (ex * a4 + ez * a5 - ey * a8)
    uz = root_three * a3 + root_fifteen * (ey * a5 + ex * a7) + 3.0 * root_five * ez * a6
    along = ex * ux + ey * uy + ez * uz
    radial_part = d_length - along * inverse
    gx = ux * inverse + ex * radial_part
    gy = uy * inverse + ey * radial_part
    gz = uz * inverse + ez * radial_part
    hx = -0.5 * dx
    hy = -0.5 * dy
    hz = -0.5 * dz
    virial = [hx * gx, hx * gy, hx * gz, hy * gx, hy * gy, hy * gz, hz * gx, hz * gy, hz * gz]
    rest = [jnp.zeros((ORDERS - 13, pairs), F32)]
    near_terms = jnp.concatenate(
        [-gx, -gy, -gz, *virial, jnp.zeros_like(gx), *rest], axis=0
    )
    center_terms = jnp.concatenate([gx, gy, gz, *virial, pair_energy, *rest], axis=0)
    near_sums = mm_nt(jnp.concatenate(split(near_terms), axis=0), pick_half)
    center_sums = mm_nt(jnp.concatenate(split(center_terms), axis=0), center_half)
    totals = folded(near_sums + center_sums)
    keep_ref[...] = totals[:, : known // 2]
    send_ref[...] = totals[:, known // 2 :]


def in_hbm(*arrays):
    return [pltpu.with_memory_space_constraint(array, pltpu.HBM) for array in arrays]


def joined(parts):
    total = sum(part.shape[0] for part in parts)
    start = 0
    pads = []
    for part in parts:
        end = start + part.shape[0]
        pads.append(jnp.pad(part, ((start, total - end), (0, 0))))
        start = end
    return functools.reduce(jnp.add, pads)


def local(
    positions,
    features,
    species,
    centers,
    neighbours,
    counts,
    species_scale,
    species_shift,
    center_weight,
    near_weight,
    basis_weight,
    path_weight,
    value_weight,
    latent_weight,
    out_weight,
):
    cells_x, cells_y, cells_z, sites, width = features.shape
    cell_count = cells_x * cells_y * cells_z
    owned = cell_count * sites
    assert (cells_x, cells_y, cells_z, sites) == (2, 1, 2, SITES)
    pairs = neighbours.size
    nbr = pairs // owned
    kind = min(3, lax.axis_size("gy"))

    def moved(array, steps):
        names = tuple(steps)
        sizes = [lax.axis_size(name) for name in names]
        route = []
        for at in np.ndindex(*sizes):
            to = [(p + steps[name]) % size for p, name, size in zip(at, names, sizes)]
            route.append(
                (int(np.ravel_multi_index(at, sizes)), int(np.ravel_multi_index(to, sizes)))
            )
        return lax.ppermute(array, names, route)

    vmem = pl.BlockSpec(memory_space=pltpu.VMEM)
    hbm = pl.BlockSpec(memory_space=pltpu.HBM)
    listed = centers.reshape(1, owned)
    here = pl.pallas_call(
        functools.partial(pack_kernel, kind),
        out_shape=jax.ShapeDtypeStruct((owned + 8 + pairs // 128, width), F32),
        in_specs=[hbm] * 6,
        out_specs=vmem,
        scratch_shapes=[
            pltpu.VMEM((owned, 128), F32),
            pltpu.VMEM(positions.shape, F32),
            pltpu.VMEM(species.shape, jnp.int32),
            pltpu.VMEM(listed.shape, jnp.int32),
            pltpu.VMEM(neighbours.shape, jnp.int32),
            pltpu.SMEM(species_scale.shape, F32),
            pltpu.SemaphoreType.DMA((6,)),
        ],
        compiler_params=pltpu.CompilerParams(vmem_limit_bytes=8 * 1024 * 1024),
        name="pack_payload",
    )(
        *in_hbm(
            positions,
            features.reshape(owned, width),
            species,
            listed,
            neighbours,
            species_scale,
        )
    )
    weights = (
        center_weight,
        near_weight,
        basis_weight,
        path_weight,
        value_weight,
        latent_weight,
        out_weight.reshape(1, width),
    )
    *weights, shift_row = pl.pallas_call(
        fetch_kernel,
        out_shape=(
            *(jax.ShapeDtypeStruct(w.shape, F32) for w in weights),
            jax.ShapeDtypeStruct((1, owned), F32),
        ),
        in_specs=[hbm] * (3 + len(weights)),
        out_specs=(vmem,) * (1 + len(weights)),
        scratch_shapes=[
            pltpu.VMEM(species.shape, jnp.int32),
            pltpu.VMEM(listed.shape, jnp.int32),
            pltpu.SMEM(species_shift.shape, F32),
            pltpu.SemaphoreType.DMA((3 + len(weights),)),
        ],
        compiler_params=pltpu.CompilerParams(vmem_limit_bytes=8 * 1024 * 1024),
        name="fetch_weights",
    )(*in_hbm(species, listed, species_shift, *weights))
    short = here[: owned + 8]
    last_x = moved(here, {"gx": 1})
    sides = []
    for step in (-1, 1)[: kind - 1]:
        sides.append(moved(short, {"gx": 1, "gy": step}))
        sides.insert(-1, moved(short, {"gy": step}))
    next_z = moved(joined([here, *sides[0::2]]), {"gz": -1})
    next_xz = moved(joined([last_x, *sides[1::2]]), {"gz": -1})
    half = 2 * kind * owned
    keep, send = pl.pallas_call(
        functools.partial(force_kernel, kind, nbr),
        out_shape=(
            jax.ShapeDtypeStruct((ORDERS, half), F32),
            jax.ShapeDtypeStruct((ORDERS, half), F32),
        ),
        in_specs=[vmem] * (9 + 2 * kind),
        out_specs=(vmem, vmem),
        compiler_params=pltpu.CompilerParams(vmem_limit_bytes=32 * 1024 * 1024),
        name="pair_forces",
    )(
        here,
        last_x,
        *sides,
        next_z,
        next_xz,
        *weights,
    )
    totals = keep + moved(send, {"gz": 1})

    half = kind * owned
    totals = totals[:, :half] + moved(totals[:, half:], {"gx": -1})
    back = []
    for i, step in enumerate((1, -1)[: kind - 1]):
        part = totals[:, (1 + i) * owned : (2 + i) * owned]
        back.append(moved(part, {"gy": step}))
    site_energy, forces, virial = pl.pallas_call(
        finish_kernel,
        out_shape=(
            jax.ShapeDtypeStruct(species.shape, F32),
            jax.ShapeDtypeStruct(positions.shape, F32),
            jax.ShapeDtypeStruct((*species.shape, 9), F32),
        ),
        in_specs=[vmem] * (2 + len(back)),
        out_specs=(vmem, vmem, vmem),
        compiler_params=pltpu.CompilerParams(vmem_limit_bytes=8 * 1024 * 1024),
        name="write_outputs",
    )(totals, shift_row, *back)
    return (site_energy, forces, jnp.transpose(virial, (4, 0, 1, 2, 3)))


def solution(mesh):
    placed = (
        P(None, "gx", "gy", "gz", None),
        P("gx", "gy", "gz", None, None),
        P("gx", "gy", "gz", None),
        P(("gx", "gy", "gz")),
        P(("gx", "gy", "gz"), None),
        P(("gx", "gy", "gz")),
        P(),
        P(),
        P(),
        P(),
        P(),
        P(),
        P(),
        P(),
        P(),
    )
    return jax.shard_map(
        local,
        mesh=mesh,
        in_specs=placed,
        out_specs=(
            P("gx", "gy", "gz", None),
            P(None, "gx", "gy", "gz", None),
            P(None, "gx", "gy", "gz", None),
        ),
        check_vma=False,
    )
```

```python
import functools
import math

import jax
import jax.numpy as jnp
import numpy as np
from jax import lax
from jax.experimental import pallas as pl
from jax.experimental.pallas import tpu as pltpu
from jax.sharding import PartitionSpec as P

EXACT_DOT = lax.Precision.HIGHEST
CUTOFF = 5.0
CELL_SIDE = 4.6
ROOT_HALF = 0.7071067811865476
GROUP = 8
ORDERS = 16
SITES = 8
OWN_CELLS = 4
FRAME_CELLS = 48
F32 = jnp.float32
BF16 = jnp.bfloat16


def split(value):
    high = value.astype(BF16)
    low = (value - high.astype(F32)).astype(BF16)
    return high, low


def split3(value):
    high = value.astype(BF16)
    rest = value - high.astype(F32)
    middle = rest.astype(BF16)
    low = (rest - middle.astype(F32)).astype(BF16)
    return high, middle, low


def mm(a, b):
    return lax.dot_general(a, b, (((1,), (0,)), ((), ())), preferred_element_type=F32)


def mm_nt(a, b):
    return lax.dot_general(a, b, (((1,), (1,)), ((), ())), preferred_element_type=F32)


def stacked(high, low):
    top = jnp.concatenate([high, high], axis=1)
    bottom = jnp.concatenate([low, jnp.zeros_like(low)], axis=1)
    return jnp.concatenate([top, bottom], axis=0)


def folded(product):
    half = product.shape[0] // 2
    return product[:half] + product[half:]


def half_depth(weights, value):
    return folded(mm(weights, jnp.concatenate(split(value), axis=0)))


def full_depth(both, high, value_high, value_low):
    return folded(mm(both, value_high)) + mm(high, value_low)


def sin_cos_pi(turns):
    near = turns - 2.0 * jnp.round(turns * 0.5)
    quarter = jnp.round(near * 2.0)
    v = (near - 0.5 * quarter) * math.pi
    v2 = v * v
    s = v * (
        1.0
        + v2
        * (-1.0 / 6 + v2 * (1.0 / 120 + v2 * (-1.0 / 5040 + v2 * (1.0 / 362880 - v2 / 39916800))))
    )
    c = 1.0 + v2 * (
        -0.5
        + v2
        * (1.0 / 24 + v2 * (-1.0 / 720 + v2 * (1.0 / 40320 + v2 * (-1.0 / 3628800 + v2 / 479001600))))
    )
    odd = jnp.abs(quarter) == 1.0
    sine = jnp.where(odd, quarter * c, jnp.where(quarter == 0.0, s, -s))
    cosine = jnp.where(odd, -quarter * s, jnp.where(quarter == 0.0, c, -c))
    return sine, cosine


def lane_row(piece, offset):
    row = jnp.concatenate([piece, jnp.zeros((1, 128 - piece.shape[1]), piece.dtype)], axis=1)
    return pltpu.roll(row, offset, 1) if offset else row


def pack_kernel(
    kind,
    positions_hbm,
    features_hbm,
    species_hbm,
    centers_hbm,
    neighbours_hbm,
    scale_hbm,
    payload_ref,
    wide_ref,
    positions_ref,
    species_ref,
    centers_ref,
    neighbours_ref,
    scale_ref,
    sems,
):
    owned, nbr = neighbours_ref.shape
    per_row = 128 // nbr
    pairs_in = (
        (features_hbm, payload_ref.at[pl.ds(0, owned), :]),
        (neighbours_hbm, neighbours_ref),
        (centers_hbm, centers_ref),
        (positions_hbm, positions_ref),
        (species_hbm, species_ref),
        (scale_hbm, scale_ref),
    )
    copies = [
        pltpu.make_async_copy(source, target, sems.at[i])
        for i, (source, target) in enumerate(pairs_in)
    ]
    for copy in copies:
        copy.start()
    for copy in copies:
        copy.wait()
    payload_ref[owned : owned + 8] = jnp.zeros((8, 128), F32)
    for cell in range(OWN_CELLS):
        x, z = cell // 2, cell % 2
        species = species_ref[x, 0, z : z + 1, :]
        scale = jnp.zeros(species.shape, F32)
        for s in range(scale_ref.shape[0]):
            scale = jnp.where(species == s, scale_ref[s], scale)
        row = lane_row(scale, 3 * SITES)
        for c in range(3):
            row = row + lane_row(positions_ref[c, x, 0, z : z + 1, :], c * SITES)
        payload_ref[owned + cell : owned + cell + 1] = row

    chosen = lax.broadcasted_iota(jnp.int32, (owned, owned), 0) == centers_ref[...]
    chosen = jnp.where(chosen, 1.0, 0.0)
    occupied = jnp.sum(chosen, axis=1, keepdims=True) > 0.5
    chosen = chosen.astype(BF16)
    rows = neighbours_ref[...]
    upper = mm(chosen, (rows >> 4).astype(F32).astype(BF16))
    lower = mm(chosen, (rows & 15).astype(F32).astype(BF16))
    rows = (upper * 16.0 + lower).astype(jnp.int32)
    live = occupied & (rows < FRAME_CELLS * SITES)
    slot = lax.broadcasted_iota(jnp.int32, (owned, nbr), 0)
    cell = slot >> 3
    site = rows & 7
    place = rows >> 3
    near_z = (place & 3) + 1 - 2 * (cell & 1)
    column = place >> 2
    frame_x = (column * 11) >> 5
    frame_y = column - 3 * frame_x
    near_x = frame_x + 1 - 2 * (cell >> 1)
    side = jnp.where(frame_y == 1, 0, jnp.where(frame_y == 2, 1, kind - 1))
    block = ((1 - (near_z >> 1)) * kind + side) * 2 + 1 - (near_x >> 1)
    where = block * owned + (near_x & 1) * 16 + (near_z & 1) * 8 + site
    code = jnp.where(live, 1 + where + (frame_y << 10), 0).astype(F32)
    wide_ref[...] = jnp.concatenate([code, jnp.zeros((owned, 128 - nbr), F32)], axis=1)
    codes = wide_ref[pl.ds(0, owned // per_row, stride=per_row), :]
    for j in range(1, per_row):
        more = wide_ref[pl.ds(j, owned // per_row, stride=per_row), :]
        codes = codes + pltpu.roll(more, j * nbr, 1)
    payload_ref[owned + 8 :] = codes


def fetch_kernel(species_hbm, centers_hbm, shift_hbm, *refs):
    *refs, shift_row_ref, species_ref, centers_ref, shift_ref, sems = refs
    count = len(refs) // 2
    pairs_in = [
        (species_hbm, species_ref),
        (centers_hbm, centers_ref),
        (shift_hbm, shift_ref),
        *zip(refs[:count], refs[count:]),
    ]
    copies = [
        pltpu.make_async_copy(source, target, sems.at[i])
        for i, (source, target) in enumerate(pairs_in)
    ]
    for copy in copies:
        copy.start()
    for copy in copies:
        copy.wait()
    owned = centers_ref.shape[1]
    shift_row = jnp.zeros((1, 128), F32)
    for cell in range(OWN_CELLS):
        species = species_ref[cell // 2, 0, cell % 2 : cell % 2 + 1, :]
        shift = jnp.zeros(species.shape, F32)
        for s in range(shift_ref.shape[0]):
            shift = jnp.where(species == s, shift_ref[s], shift)
        shift_row = shift_row + lane_row(shift, cell * SITES)
    chosen = lax.broadcasted_iota(jnp.int32, (owned, owned), 0) == centers_ref[...]
    occupied = jnp.sum(jnp.where(chosen, 1.0, 0.0), axis=1, keepdims=True) > 0.5
    column = jnp.where(occupied, jnp.ones((owned, 128), F32), 0.0)
    shift_row_ref[...] = shift_row[:, :owned] * jnp.transpose(column)[0:1]


def finish_kernel(mine_ref, shift_row_ref, back_ref, energy_ref, forces_ref, virial_ref):
    owned = back_ref.shape[1]
    total = mine_ref[:, :owned] + back_ref[...]
    energy = total[12:13] + shift_row_ref[...]
    columns = jnp.transpose(jnp.concatenate([total, jnp.zeros((ORDERS, 128 - owned), F32)], axis=1))
    for cell in range(OWN_CELLS):
        x, z = cell // 2, cell % 2
        lanes = slice(cell * SITES, (cell + 1) * SITES)
        energy_ref[x, 0, z : z + 1, :] = energy[:, lanes]
        for c in range(3):
            forces_ref[c, x, 0, z : z + 1, :] = total[c : c + 1, lanes]
        virial_ref[x, 0, z] = columns[lanes, 3:12]


def force_kernel(kind, nbr, here_ref, last_x_ref, *refs):
    near_side_refs = refs[: 2 * kind - 2]
    (
        last_z_ref,
        center_weight_ref,
        near_weight_ref,
        basis_weight_ref,
        path_weight_ref,
        value_weight_ref,
        latent_weight_ref,
        out_weight_ref,
        *totals_refs,
    ) = refs[2 * kind - 2 :]
    height, width = here_ref.shape
    owned = OWN_CELLS * SITES
    short = owned + 8
    pairs = owned * nbr
    radial = basis_weight_ref.shape[0]
    span = GROUP * nbr
    groups = owned // GROUP
    wide = GROUP * ORDERS
    sites = SITES
    root_count = math.sqrt(nbr)
    root_three = math.sqrt(3.0)
    root_fifteen = math.sqrt(15.0)
    root_five = math.sqrt(5.0)
    near_sides = [ref[...] for ref in near_side_refs]
    far = last_z_ref[...]
    far_sides = [
        far[2 * height + i * short : 2 * height + (i + 1) * short] for i in range(2 * kind - 2)
    ]
    blocks_in = [
        [here_ref[...], *near_sides[0::2]],
        [last_x_ref[...], *near_sides[1::2]],
        [far[:height], *far_sides[0::2]],
        [far[height : 2 * height], *far_sides[1::2]],
    ]
    order_in = [(z, side, x) for z in range(2) for side in range(kind) for x in range(2)]
    feats = jnp.concatenate([blocks_in[2 * z + x][side][:owned] for z, side, x in order_in], axis=0)
    known = feats.shape[0]
    center_feats = []
    coords = []
    scales = []
    codes = []
    for g, block in enumerate(blocks_in):
        cell = g % 2 * 2 + g // 2
        center_feats.append(block[0][cell * sites : (cell + 1) * sites])
        scales.append(block[0][owned + cell : owned + cell + 1])
        start = short + cell * span // 128
        codes.extend(block[0][start + r : start + r + 1] for r in range(span // 128))
    cell_row = lax.broadcasted_iota(jnp.int32, (OWN_CELLS, 128), 0)
    tile_lane = lax.broadcasted_iota(jnp.int32, (OWN_CELLS, 128), 1)
    for z, side, x in order_in:
        corner_x = (cell_row // 2 + 2 - 2 * x).astype(F32) * CELL_SIDE
        corner_z = (cell_row % 2 + 2 - 2 * z).astype(F32) * CELL_SIDE
        corner = jnp.where(
            tile_lane < sites, corner_x, jnp.where(tile_lane < 2 * sites, 0.0, corner_z)
        )
        coords.append(blocks_in[2 * z + x][side][owned : owned + OWN_CELLS] + corner)
    center_feats = jnp.concatenate(center_feats, axis=0)
    coords = jnp.concatenate(coords, axis=0)
    code = jnp.concatenate(codes, axis=1).astype(jnp.int32)
    live = code > 0
    code = jnp.maximum(code - 1, 0)
    side_y = ((code >> 10) - 1).astype(F32)
    near_row = jnp.where(live, code & 1023, known)

    spread = jnp.broadcast_to(coords[:, None, :], (coords.shape[0], sites, 128))
    spread = spread.reshape(known, 128)
    keep_lane = lax.broadcasted_iota(jnp.int32, (known, 128), 1)
    keep_row = lax.broadcasted_iota(jnp.int32, (known, 128), 0)
    keep = (keep_lane % sites == keep_row % sites) & (keep_lane < 3 * sites)
    spread = jnp.where(keep, spread, 0.0)
    place_parts = jnp.concatenate(split3(jnp.transpose(spread)[: 3 * sites]), axis=0)

    value_rows = stacked(*split(jnp.transpose(value_weight_ref[...])))
    latent_high_t, latent_low_t = split(jnp.transpose(latent_weight_ref[...]))
    latent_both_t = jnp.concatenate([latent_high_t, latent_low_t], axis=0)
    latent_rows = stacked(*split(latent_weight_ref[...]))
    value_high, value_low = split(value_weight_ref[...])
    value_both = jnp.concatenate([value_high, value_low], axis=0)
    basis_t = jnp.transpose(basis_weight_ref[...])
    basis_high_t, basis_low_t = split(basis_t)
    basis_rows = stacked(*split(basis_weight_ref[...]))

    def project(weight, rows):
        weight = stacked(*split(jnp.transpose(weight)))
        return folded(mm_nt(weight, jnp.concatenate(split(rows), axis=1)))

    near_t = project(near_weight_ref[...], feats)
    own_t = project(center_weight_ref[...], center_feats)
    near_high, near_low = split(near_t)
    own_high, own_low = split(own_t)
    lookup = jnp.concatenate(
        [
            jnp.concatenate([near_high, own_high, basis_high_t, basis_high_t], axis=1),
            jnp.concatenate([near_low, own_low, basis_low_t, jnp.zeros_like(basis_low_t)], axis=1),
        ],
        axis=0,
    )
    scale_rows = jnp.concatenate(scales, axis=0)
    scale_parts = jnp.concatenate(
        [*split3(scale_rows), jnp.zeros((16 - 3 * groups, 128), BF16)], axis=0
    )

    level = lax.broadcasted_iota(jnp.int32, (ORDERS, width), 0)
    path_rows = jnp.where(
        level == 0,
        path_weight_ref[0:1, :],
        jnp.where(
            level < 4,
            path_weight_ref[1:2, :],
            jnp.where(level < 9, path_weight_ref[2:3, :], 0.0),
        ),
    )
    paths_t = jnp.transpose(jnp.concatenate([path_rows] * GROUP, axis=0)) * (1.0 / root_count)
    out_column = jnp.transpose(jnp.broadcast_to(out_weight_ref[...], (width, width)))
    out_column = jnp.concatenate([out_column] * (pairs // width), axis=1)

    site_ids = lax.broadcasted_iota(jnp.int32, (known, pairs), 0)
    slot_ids = lax.broadcasted_iota(jnp.int32, (owned, pairs), 0)
    slot_row = lax.broadcasted_iota(jnp.int32, (1, pairs), 1) // nbr
    group_row = slot_row // GROUP
    center_cell = group_row % 2 * 2 + group_row // 2
    center_block = group_row // 2 * kind * 2 + group_row % 2
    center_row = center_block * owned + center_cell * sites + slot_row % GROUP
    block_row = lax.broadcasted_iota(jnp.int32, (wide, span), 0) // ORDERS
    block_lane = lax.broadcasted_iota(jnp.int32, (wide, span), 1) // nbr
    block_mask = (block_row == block_lane).astype(F32)
    block_half = block_mask.astype(BF16)
    order = lax.broadcasted_iota(jnp.int32, (radial, pairs), 0).astype(F32) + 1.0
    lanes = [slice(g * span, (g + 1) * span) for g in range(groups)]

    pick = jnp.where(site_ids == near_row, 1.0, 0.0)
    from_center = jnp.where(site_ids == center_row, 1.0, 0.0)
    pick_half = pick.astype(BF16)
    center_half = from_center.astype(BF16)
    slot_half = jnp.where(slot_ids == slot_row, 1.0, 0.0).astype(BF16)

    moved = mm(place_parts, (pick - from_center).astype(BF16))
    moved = moved[: 3 * sites] + moved[3 * sites : 6 * sites] + moved[6 * sites :]
    dx = jnp.where(live, jnp.sum(moved[:sites], axis=0, keepdims=True), 6.0)
    dy = jnp.sum(moved[sites : 2 * sites], axis=0, keepdims=True) + CELL_SIDE * side_y
    dy = jnp.where(live, dy, 0.0)
    dz = jnp.where(live, jnp.sum(moved[2 * sites :], axis=0, keepdims=True), 0.0)
    length = jnp.sqrt(dx * dx + dy * dy + dz * dz)
    inverse = 1.0 / length
    ratio = length * (1.0 / CUTOFF)
    inside = live & (ratio < 1.0)
    r2 = ratio * ratio
    r5 = r2 * r2 * ratio
    r6 = r5 * ratio
    weight = jnp.where(inside, 1.0 - r6 * (28.0 - 48.0 * ratio + 21.0 * r2), 0.0)
    slope = jnp.where(inside, -168.0 * r5 * (1.0 - 2.0 * ratio + r2), 0.0)
    sine, cosine = sin_cos_pi(order * ratio)
    basis = (math.sqrt(2.0 / CUTOFF) * inverse) * sine
    basis_slope = (math.sqrt(2.0 / CUTOFF) * inverse) * (
        (math.pi / CUTOFF) * order * cosine - sine * inverse
    )
    ex = dx * inverse
    ey = dy * inverse
    ez = dz * inverse
    angular = jnp.concatenate(
        [
            jnp.ones_like(ex),
            root_three * ex,
            root_three * ey,
            root_three * ez,
            root_fifteen * ex * ey,
            root_fifteen * ey * ez,
            0.5 * root_five * (3.0 * ez * ez - 1.0),
            root_fifteen * ex * ez,
            0.5 * root_fifteen * (ex * ex - ey * ey),
            jnp.zeros((ORDERS - 9, pairs), F32),
        ],
        axis=0,
    )
    angular_high, angular_low = split(angular)
    blocks = [
        jnp.concatenate(
            [
                jnp.concatenate([angular_high[:, cut]] * GROUP, axis=0) * block_half,
                jnp.concatenate([angular_low[:, cut]] * GROUP, axis=0) * block_half,
            ],
            axis=0,
        )
        for cut in lanes
    ]
    lane_ids = lax.broadcasted_iota(jnp.int32, (128, span), 0)
    lane_slot = lax.broadcasted_iota(jnp.int32, (128, span), 1) // nbr + 3 * sites
    scale = mm(scale_parts, jnp.where(lane_ids == lane_slot, 1.0, 0.0).astype(BF16))
    scale = scale[:groups] + scale[groups : 2 * groups] + scale[2 * groups : 3 * groups]
    scale = jnp.concatenate([scale[g : g + 1] for g in range(groups)], axis=1)
    scale = scale * (1.0 / root_count)
    pull = ROOT_HALF * scale

    basis_high, basis_low = split(basis)
    before = folded(
        mm(lookup, jnp.concatenate([pick_half, slot_half, basis_high, basis_low], axis=0))
    )
    gate = 0.5 * jnp.tanh(0.5 * before) + 0.5
    active = before * gate
    latent = weight * active
    mixed = half_depth(value_rows, latent)
    values = mixed[:width]
    env_high, env_low = split(mixed[width:])

    def over_pairs(high, low):
        sums = []
        for cut, block in zip(lanes, blocks):
            quad = mm_nt(jnp.concatenate([high[:, cut], low[:, cut]], axis=0), block)
            sums.append((quad[:width, :wide] + quad[:width, wide:] + quad[width:, :wide]) * paths_t)
        return sums

    def over_orders(tables):
        parts = [folded(mm(stacked(*split(t)), block)) for t, block in zip(tables, blocks)]
        return jnp.concatenate(parts, axis=1)

    weighted = over_pairs(env_high, env_low)
    inner = over_orders(weighted)
    scalars = values * inner
    joined_high, joined_low = split(jnp.concatenate([latent, scalars], axis=0))
    z = full_depth(latent_both_t, latent_high_t, joined_high, joined_low)
    z_gate = 0.5 * jnp.tanh(0.5 * z) + 0.5
    update = z * z_gate
    update_out = update * out_column
    pair_energy = jnp.sum(latent * out_column + weight * update_out, axis=0, keepdims=True)
    pair_energy = pair_energy * pull
    d_z = (pull * weight) * out_column * (z_gate + update * (1.0 - z_gate))
    spread_back = half_depth(latent_rows, d_z)
    d_scalars = spread_back[width:]
    d_values = d_scalars * inner
    dinner_high, dinner_low = split(d_scalars * values)
    d_embed = over_pairs(dinner_high, dinner_low)
    d_env = over_orders(d_embed)

    d_angular = []
    for g, cut in enumerate(lanes):
        sides = jnp.transpose(jnp.concatenate([weighted[g], d_embed[g]], axis=0))
        sides_high, sides_low = split(sides)
        d_block = full_depth(
            jnp.concatenate([sides_high, sides_low], axis=0),
            sides_high,
            jnp.concatenate([dinner_high[:, cut], env_high[:, cut]], axis=0),
            jnp.concatenate([dinner_low[:, cut], env_low[:, cut]], axis=0),
        )
        d_block = d_block * block_mask
        total = d_block[:ORDERS]
        for k in range(1, GROUP):
            total = total + d_block[k * ORDERS : (k + 1) * ORDERS]
        d_angular.append(total)
    d_angular = jnp.concatenate(d_angular, axis=1)

    mixed_high, mixed_low = split(jnp.concatenate([d_values, d_env], axis=0))
    d_latent = (
        full_depth(value_both, value_high, mixed_high, mixed_low)
        + spread_back[:width]
        + pull * out_column
    )
    d_weight = jnp.sum(d_latent * active + pull * update_out, axis=0, keepdims=True)
    d_before = d_latent * weight * (gate + active * (1.0 - gate))
    d_basis = half_depth(basis_rows, d_before)

    d_length = jnp.sum(d_basis * basis_slope, axis=0, keepdims=True) + d_weight * slope * (
        1.0 / CUTOFF
    )
    a1, a2, a3, a4, a5, a6, a7, a8 = [d_angular[m : m + 1] for m in range(1, 9)]
    ux = root_three * a1 + root_fifteen * (ey * a4 + ez * a7 + ex * a8)
    uy = root_three * a2 + root_fifteen * (ex * a4 + ez * a5 - ey * a8)
    uz = root_three * a3 + root_fifteen * (ey * a5 + ex * a7) + 3.0 * root_five * ez * a6
    along = ex * ux + ey * uy + ez * uz
    radial_part = d_length - along * inverse
    gx = ux * inverse + ex * radial_part
    gy = uy * inverse + ey * radial_part
    gz = uz * inverse + ez * radial_part
    hx = -0.5 * dx
    hy = -0.5 * dy
    hz = -0.5 * dz
    virial = [hx * gx, hx * gy, hx * gz, hy * gx, hy * gy, hy * gz, hz * gx, hz * gy, hz * gz]
    rest = [jnp.zeros((ORDERS - 13, pairs), F32)]
    near_terms = jnp.concatenate(
        [-gx, -gy, -gz, *virial, jnp.zeros_like(gx), *rest], axis=0
    )
    center_terms = jnp.concatenate([gx, gy, gz, *virial, pair_energy, *rest], axis=0)
    near_sums = mm_nt(jnp.concatenate(split(near_terms), axis=0), pick_half)
    center_sums = mm_nt(jnp.concatenate(split(center_terms), axis=0), center_half)
    totals = folded(near_sums + center_sums)
    for i, ref in enumerate(totals_refs):
        ref[...] = totals[:, 2 * i * owned : 2 * (i + 1) * owned]


def in_hbm(*arrays):
    return [pltpu.with_memory_space_constraint(array, pltpu.HBM) for array in arrays]


def joined(parts):
    total = sum(part.shape[0] for part in parts)
    start = 0
    pads = []
    for part in parts:
        end = start + part.shape[0]
        pads.append(jnp.pad(part, ((start, total - end), (0, 0))))
        start = end
    return functools.reduce(jnp.add, pads)


def local(
    positions,
    features,
    species,
    centers,
    neighbours,
    counts,
    species_scale,
    species_shift,
    center_weight,
    near_weight,
    basis_weight,
    path_weight,
    value_weight,
    latent_weight,
    out_weight,
):
    cells_x, cells_y, cells_z, sites, width = features.shape
    cell_count = cells_x * cells_y * cells_z
    owned = cell_count * sites
    assert (cells_x, cells_y, cells_z, sites) == (2, 1, 2, SITES)
    pairs = neighbours.size
    nbr = pairs // owned
    kind = min(3, lax.axis_size("gy"))

    def moved(array, steps):
        names = tuple(steps)
        sizes = [lax.axis_size(name) for name in names]
        route = []
        for at in np.ndindex(*sizes):
            to = [(p + steps[name]) % size for p, name, size in zip(at, names, sizes)]
            route.append(
                (int(np.ravel_multi_index(at, sizes)), int(np.ravel_multi_index(to, sizes)))
            )
        return lax.ppermute(array, names, route)

    vmem = pl.BlockSpec(memory_space=pltpu.VMEM)
    hbm = pl.BlockSpec(memory_space=pltpu.HBM)
    listed = centers.reshape(1, owned)
    here = pl.pallas_call(
        functools.partial(pack_kernel, kind),
        out_shape=jax.ShapeDtypeStruct((owned + 8 + pairs // 128, width), F32),
        in_specs=[hbm] * 6,
        out_specs=vmem,
        scratch_shapes=[
            pltpu.VMEM((owned, 128), F32),
            pltpu.VMEM(positions.shape, F32),
            pltpu.VMEM(species.shape, jnp.int32),
            pltpu.VMEM(listed.shape, jnp.int32),
            pltpu.VMEM(neighbours.shape, jnp.int32),
            pltpu.SMEM(species_scale.shape, F32),
            pltpu.SemaphoreType.DMA((6,)),
        ],
        compiler_params=pltpu.CompilerParams(vmem_limit_bytes=8 * 1024 * 1024),
        name="pack_payload",
    )(
        *in_hbm(
            positions,
            features.reshape(owned, width),
            species,
            listed,
            neighbours,
            species_scale,
        )
    )
    weights = (
        center_weight,
        near_weight,
        basis_weight,
        path_weight,
        value_weight,
        latent_weight,
        out_weight.reshape(1, width),
    )
    *weights, shift_row = pl.pallas_call(
        fetch_kernel,
        out_shape=(
            *(jax.ShapeDtypeStruct(w.shape, F32) for w in weights),
            jax.ShapeDtypeStruct((1, owned), F32),
        ),
        in_specs=[hbm] * (3 + len(weights)),
        out_specs=(vmem,) * (1 + len(weights)),
        scratch_shapes=[
            pltpu.VMEM(species.shape, jnp.int32),
            pltpu.VMEM(listed.shape, jnp.int32),
            pltpu.SMEM(species_shift.shape, F32),
            pltpu.SemaphoreType.DMA((3 + len(weights),)),
        ],
        compiler_params=pltpu.CompilerParams(vmem_limit_bytes=8 * 1024 * 1024),
        name="fetch_weights",
    )(*in_hbm(species, listed, species_shift, *weights))
    short = here[: owned + 8]
    last_x = moved(here, {"gx": 1})
    sides = []
    for step in (-1, 1)[: kind - 1]:
        sides.append(moved(short, {"gx": 1, "gy": step}))
        sides.insert(-1, moved(short, {"gy": step}))
    last_z = moved(joined([here, last_x, *sides]), {"gz": 1})
    totals = pl.pallas_call(
        functools.partial(force_kernel, kind, nbr),
        out_shape=[jax.ShapeDtypeStruct((ORDERS, 2 * owned), F32)] * (2 * kind),
        in_specs=[vmem] * (8 + 2 * kind),
        out_specs=[vmem] * (2 * kind),
        compiler_params=pltpu.CompilerParams(vmem_limit_bytes=32 * 1024 * 1024),
        name="pair_forces",
    )(
        here,
        last_x,
        *sides,
        last_z,
        *weights,
    )
    total = totals[0] + moved(totals[kind], {"gz": -1})
    for i, step in enumerate((1, -1)[: kind - 1]):
        total = total + moved(totals[kind + 1 + i], {"gy": step, "gz": -1})
        total = total + moved(totals[1 + i], {"gy": step})
    back = moved(total[:, owned:], {"gx": -1})
    site_energy, forces, virial = pl.pallas_call(
        finish_kernel,
        out_shape=(
            jax.ShapeDtypeStruct(species.shape, F32),
            jax.ShapeDtypeStruct(positions.shape, F32),
            jax.ShapeDtypeStruct((*species.shape, 9), F32),
        ),
        in_specs=[vmem] * 3,
        out_specs=(vmem, vmem, vmem),
        compiler_params=pltpu.CompilerParams(vmem_limit_bytes=8 * 1024 * 1024),
        name="write_outputs",
    )(total, shift_row, back)
    return (site_energy, forces, jnp.transpose(virial, (4, 0, 1, 2, 3)))


def solution(mesh):
    placed = (
        P(None, "gx", "gy", "gz", None),
        P("gx", "gy", "gz", None, None),
        P("gx", "gy", "gz", None),
        P(("gx", "gy", "gz")),
        P(("gx", "gy", "gz"), None),
        P(("gx", "gy", "gz")),
        P(),
        P(),
        P(),
        P(),
        P(),
        P(),
        P(),
        P(),
        P(),
    )
    return jax.shard_map(
        local,
        mesh=mesh,
        in_specs=placed,
        out_specs=(
            P("gx", "gy", "gz", None),
            P(None, "gx", "gy", "gz", None),
            P(None, "gx", "gy", "gz", None),
        ),
        check_vma=False,
    )
```

```python
import functools
import math

import jax
import jax.numpy as jnp
import numpy as np
from jax import lax
from jax.experimental import pallas as pl
from jax.experimental.pallas import tpu as pltpu
from jax.sharding import PartitionSpec as P

EXACT_DOT = lax.Precision.HIGHEST
CUTOFF = 5.0
CELL_SIDE = 4.6
ROOT_HALF = 0.7071067811865476
GROUP = 8
ORDERS = 16
SITES = 8
OWN_CELLS = 4
FRAME_CELLS = 48
F32 = jnp.float32
BF16 = jnp.bfloat16


def split(value):
    high = value.astype(BF16)
    low = (value - high.astype(F32)).astype(BF16)
    return high, low


def split3(value):
    high = value.astype(BF16)
    rest = value - high.astype(F32)
    middle = rest.astype(BF16)
    low = (rest - middle.astype(F32)).astype(BF16)
    return high, middle, low


def mm(a, b):
    return lax.dot_general(a, b, (((1,), (0,)), ((), ())), preferred_element_type=F32)


def mm_nt(a, b):
    return lax.dot_general(a, b, (((1,), (1,)), ((), ())), preferred_element_type=F32)


def stacked(high, low):
    top = jnp.concatenate([high, high], axis=1)
    bottom = jnp.concatenate([low, jnp.zeros_like(low)], axis=1)
    return jnp.concatenate([top, bottom], axis=0)


def folded(product):
    half = product.shape[0] // 2
    return product[:half] + product[half:]


def half_depth(weights, value):
    return folded(mm(weights, jnp.concatenate(split(value), axis=0)))


def full_depth(both, high, value_high, value_low):
    return folded(mm(both, value_high)) + mm(high, value_low)


def sin_cos_pi(turns):
    near = turns - 2.0 * jnp.round(turns * 0.5)
    quarter = jnp.round(near * 2.0)
    v = (near - 0.5 * quarter) * math.pi
    v2 = v * v
    s = v * (
        1.0
        + v2
        * (-1.0 / 6 + v2 * (1.0 / 120 + v2 * (-1.0 / 5040 + v2 * (1.0 / 362880 - v2 / 39916800))))
    )
    c = 1.0 + v2 * (
        -0.5
        + v2
        * (1.0 / 24 + v2 * (-1.0 / 720 + v2 * (1.0 / 40320 + v2 * (-1.0 / 3628800 + v2 / 479001600))))
    )
    odd = jnp.abs(quarter) == 1.0
    sine = jnp.where(odd, quarter * c, jnp.where(quarter == 0.0, s, -s))
    cosine = jnp.where(odd, -quarter * s, jnp.where(quarter == 0.0, c, -c))
    return sine, cosine


def lane_row(piece, offset):
    row = jnp.concatenate([piece, jnp.zeros((1, 128 - piece.shape[1]), piece.dtype)], axis=1)
    return pltpu.roll(row, offset, 1) if offset else row


def pack_kernel(
    kind,
    positions_hbm,
    features_hbm,
    species_hbm,
    centers_hbm,
    neighbours_hbm,
    scale_hbm,
    payload_ref,
    again_ref,
    wide_ref,
    positions_ref,
    species_ref,
    centers_ref,
    neighbours_ref,
    scale_ref,
    sems,
):
    owned, nbr = neighbours_ref.shape
    per_row = 128 // nbr
    pairs_in = (
        (features_hbm, payload_ref.at[pl.ds(0, owned), :]),
        (neighbours_hbm, neighbours_ref),
        (centers_hbm, centers_ref),
        (positions_hbm, positions_ref),
        (species_hbm, species_ref),
        (scale_hbm, scale_ref),
    )
    copies = [
        pltpu.make_async_copy(source, target, sems.at[i])
        for i, (source, target) in enumerate(pairs_in)
    ]
    for copy in copies:
        copy.start()
    for copy in copies:
        copy.wait()
    payload_ref[owned : owned + 8] = jnp.zeros((8, 128), F32)
    for cell in range(OWN_CELLS):
        x, z = cell // 2, cell % 2
        species = species_ref[x, 0, z : z + 1, :]
        scale = jnp.zeros(species.shape, F32)
        for s in range(scale_ref.shape[0]):
            scale = jnp.where(species == s, scale_ref[s], scale)
        row = lane_row(scale, 3 * SITES)
        for c in range(3):
            row = row + lane_row(positions_ref[c, x, 0, z : z + 1, :], c * SITES)
        payload_ref[owned + cell : owned + cell + 1] = row

    chosen = lax.broadcasted_iota(jnp.int32, (owned, owned), 0) == centers_ref[...]
    chosen = jnp.where(chosen, 1.0, 0.0)
    occupied = jnp.sum(chosen, axis=1, keepdims=True) > 0.5
    chosen = chosen.astype(BF16)
    rows = neighbours_ref[...]
    upper = mm(chosen, (rows >> 4).astype(F32).astype(BF16))
    lower = mm(chosen, (rows & 15).astype(F32).astype(BF16))
    rows = (upper * 16.0 + lower).astype(jnp.int32)
    live = occupied & (rows < FRAME_CELLS * SITES)
    slot = lax.broadcasted_iota(jnp.int32, (owned, nbr), 0)
    cell = slot >> 3
    site = rows & 7
    place = rows >> 3
    near_z = (place & 3) + 1 - 2 * (cell & 1)
    column = place >> 2
    frame_x = (column * 11) >> 5
    frame_y = column - 3 * frame_x
    near_x = frame_x + 1 - 2 * (cell >> 1)
    side = jnp.where(frame_y == 1, 0, jnp.where(frame_y == 2, 1, kind - 1))
    block = (near_z >> 1) * 2 + 1 - (near_x >> 1)
    where = (block * kind + side) * owned + (near_x & 1) * 16 + (near_z & 1) * 8 + site
    code = jnp.where(live, 1 + where + (frame_y << 10), 0).astype(F32)
    wide_ref[...] = jnp.concatenate([code, jnp.zeros((owned, 128 - nbr), F32)], axis=1)
    codes = wide_ref[pl.ds(0, owned // per_row, stride=per_row), :]
    for j in range(1, per_row):
        more = wide_ref[pl.ds(j, owned // per_row, stride=per_row), :]
        codes = codes + pltpu.roll(more, j * nbr, 1)
    payload_ref[owned + 8 :] = codes
    again_ref[...] = payload_ref[...]


def fetch_kernel(species_hbm, centers_hbm, shift_hbm, *refs):
    *refs, shift_row_ref, species_ref, centers_ref, shift_ref, sems = refs
    count = len(refs) // 2
    pairs_in = [
        (species_hbm, species_ref),
        (centers_hbm, centers_ref),
        (shift_hbm, shift_ref),
        *zip(refs[:count], refs[count:]),
    ]
    copies = [
        pltpu.make_async_copy(source, target, sems.at[i])
        for i, (source, target) in enumerate(pairs_in)
    ]
    for copy in copies:
        copy.start()
    for copy in copies:
        copy.wait()
    owned = centers_ref.shape[1]
    shift_row = jnp.zeros((1, 128), F32)
    for cell in range(OWN_CELLS):
        species = species_ref[cell // 2, 0, cell % 2 : cell % 2 + 1, :]
        shift = jnp.zeros(species.shape, F32)
        for s in range(shift_ref.shape[0]):
            shift = jnp.where(species == s, shift_ref[s], shift)
        shift_row = shift_row + lane_row(shift, cell * SITES)
    chosen = lax.broadcasted_iota(jnp.int32, (owned, owned), 0) == centers_ref[...]
    occupied = jnp.sum(jnp.where(chosen, 1.0, 0.0), axis=1, keepdims=True) > 0.5
    column = jnp.where(occupied, jnp.ones((owned, 128), F32), 0.0)
    shift_row_ref[...] = shift_row[:, :owned] * jnp.transpose(column)[0:1]


def finish_kernel(mine_ref, shift_row_ref, *refs):
    *near_refs, energy_ref, forces_ref, virial_ref = refs
    owned = near_refs[0].shape[1]
    total = mine_ref[:, :owned]
    for near_ref in near_refs:
        total = total + near_ref[...]
    energy = total[12:13] + shift_row_ref[...]
    columns = jnp.transpose(jnp.concatenate([total, jnp.zeros((ORDERS, 128 - owned), F32)], axis=1))
    for cell in range(OWN_CELLS):
        x, z = cell // 2, cell % 2
        lanes = slice(cell * SITES, (cell + 1) * SITES)
        energy_ref[x, 0, z : z + 1, :] = energy[:, lanes]
        for c in range(3):
            forces_ref[c, x, 0, z : z + 1, :] = total[c : c + 1, lanes]
        virial_ref[x, 0, z] = columns[lanes, 3:12]


def force_kernel(kind, nbr, here_ref, last_x_ref, *refs):
    near_side_refs = refs[: 2 * kind - 2]
    (
        next_z_ref,
        center_weight_ref,
        near_weight_ref,
        basis_weight_ref,
        path_weight_ref,
        value_weight_ref,
        latent_weight_ref,
        out_weight_ref,
        keep_ref,
        send_ref,
    ) = refs[2 * kind - 2 :]
    height, width = here_ref.shape
    owned = OWN_CELLS * SITES
    short = owned + 8
    pairs = owned * nbr
    radial = basis_weight_ref.shape[0]
    span = GROUP * nbr
    groups = owned // GROUP
    wide = GROUP * ORDERS
    sites = SITES
    root_count = math.sqrt(nbr)
    root_three = math.sqrt(3.0)
    root_fifteen = math.sqrt(15.0)
    root_five = math.sqrt(5.0)
    far = next_z_ref[...]
    mains = [here_ref[...], last_x_ref[...], far[:height], far[height : 2 * height]]
    near_sides = [ref[...] for ref in near_side_refs]
    far_sides = far[2 * height :]
    far_sides = [far_sides[i * short : (i + 1) * short] for i in range(2 * kind - 2)]
    blocks_in = [
        [mains[0], *near_sides[0::2]],
        [mains[1], *near_sides[1::2]],
        [mains[2], *far_sides[0::2]],
        [mains[3], *far_sides[1::2]],
    ]
    feats = jnp.concatenate([side[:owned] for block in blocks_in for side in block], axis=0)
    known = feats.shape[0]
    center_feats = []
    coords = []
    scales = []
    codes = []
    cell_row = lax.broadcasted_iota(jnp.int32, (kind * OWN_CELLS, 128), 0) % OWN_CELLS
    tile_lane = lax.broadcasted_iota(jnp.int32, (kind * OWN_CELLS, 128), 1)
    for g, block in enumerate(blocks_in):
        behind_x, ahead_z = g % 2, g // 2
        cell = behind_x * 2 + 1 - ahead_z
        center_feats.append(block[0][cell * sites : (cell + 1) * sites])
        rows = jnp.concatenate([side[owned : owned + OWN_CELLS] for side in block], axis=0)
        scales.append(rows[cell : cell + 1])
        corner_x = (cell_row // 2 + 2 - 2 * behind_x).astype(F32) * CELL_SIDE
        corner_z = (cell_row % 2 + 2 * ahead_z).astype(F32) * CELL_SIDE
        corner = jnp.where(
            tile_lane < sites, corner_x, jnp.where(tile_lane < 2 * sites, 0.0, corner_z)
        )
        coords.append(rows + corner)
        start = short + cell * span // 128
        codes.extend(block[0][start + r : start + r + 1] for r in range(span // 128))
    center_feats = jnp.concatenate(center_feats, axis=0)
    coords = jnp.concatenate(coords, axis=0)
    code = jnp.concatenate(codes, axis=1).astype(jnp.int32)
    live = code > 0
    code = jnp.maximum(code - 1, 0)
    side_y = ((code >> 10) - 1).astype(F32)
    near_row = jnp.where(live, code & 1023, known)

    spread = jnp.broadcast_to(coords[:, None, :], (coords.shape[0], sites, 128))
    spread = spread.reshape(known, 128)
    keep_lane = lax.broadcasted_iota(jnp.int32, (known, 128), 1)
    keep_row = lax.broadcasted_iota(jnp.int32, (known, 128), 0)
    keep = (keep_lane % sites == keep_row % sites) & (keep_lane < 3 * sites)
    spread = jnp.where(keep, spread, 0.0)
    place_parts = jnp.concatenate(split3(jnp.transpose(spread)[: 3 * sites]), axis=0)

    value_rows = stacked(*split(jnp.transpose(value_weight_ref[...])))
    latent_high_t, latent_low_t = split(jnp.transpose(latent_weight_ref[...]))
    latent_both_t = jnp.concatenate([latent_high_t, latent_low_t], axis=0)
    latent_rows = stacked(*split(latent_weight_ref[...]))
    value_high, value_low = split(value_weight_ref[...])
    value_both = jnp.concatenate([value_high, value_low], axis=0)
    basis_t = jnp.transpose(basis_weight_ref[...])
    basis_high_t, basis_low_t = split(basis_t)
    basis_rows = stacked(*split(basis_weight_ref[...]))

    def project(weight, rows):
        weight = stacked(*split(jnp.transpose(weight)))
        return folded(mm_nt(weight, jnp.concatenate(split(rows), axis=1)))

    near_t = project(near_weight_ref[...], feats)
    own_t = project(center_weight_ref[...], center_feats)
    near_high, near_low = split(near_t)
    own_high, own_low = split(own_t)
    lookup = jnp.concatenate(
        [
            jnp.concatenate([near_high, own_high, basis_high_t, basis_high_t], axis=1),
            jnp.concatenate([near_low, own_low, basis_low_t, jnp.zeros_like(basis_low_t)], axis=1),
        ],
        axis=0,
    )
    scale_rows = jnp.concatenate(scales, axis=0)
    scale_parts = jnp.concatenate(
        [*split3(scale_rows), jnp.zeros((16 - 3 * groups, 128), BF16)], axis=0
    )

    level = lax.broadcasted_iota(jnp.int32, (ORDERS, width), 0)
    path_rows = jnp.where(
        level == 0,
        path_weight_ref[0:1, :],
        jnp.where(
            level < 4,
            path_weight_ref[1:2, :],
            jnp.where(level < 9, path_weight_ref[2:3, :], 0.0),
        ),
    )
    paths_t = jnp.transpose(jnp.concatenate([path_rows] * GROUP, axis=0)) * (1.0 / root_count)
    out_column = jnp.transpose(jnp.broadcast_to(out_weight_ref[...], (width, width)))
    out_column = jnp.concatenate([out_column] * (pairs // width), axis=1)

    site_ids = lax.broadcasted_iota(jnp.int32, (known, pairs), 0)
    slot_ids = lax.broadcasted_iota(jnp.int32, (owned, pairs), 0)
    slot_row = lax.broadcasted_iota(jnp.int32, (1, pairs), 1) // nbr
    group_row = slot_row // GROUP
    center_cell = group_row % 2 * 2 + 1 - group_row // 2
    center_row = group_row * (kind * owned) + center_cell * sites + slot_row % GROUP
    block_row = lax.broadcasted_iota(jnp.int32, (wide, span), 0) // ORDERS
    block_lane = lax.broadcasted_iota(jnp.int32, (wide, span), 1) // nbr
    block_mask = (block_row == block_lane).astype(F32)
    block_half = block_mask.astype(BF16)
    order = lax.broadcasted_iota(jnp.int32, (radial, pairs), 0).astype(F32) + 1.0
    lanes = [slice(g * span, (g + 1) * span) for g in range(groups)]

    pick = jnp.where(site_ids == near_row, 1.0, 0.0)
    from_center = jnp.where(site_ids == center_row, 1.0, 0.0)
    pick_half = pick.astype(BF16)
    center_half = from_center.astype(BF16)
    slot_half = jnp.where(slot_ids == slot_row, 1.0, 0.0).astype(BF16)

    moved = mm(place_parts, (pick - from_center).astype(BF16))
    moved = moved[: 3 * sites] + moved[3 * sites : 6 * sites] + moved[6 * sites :]
    dx = jnp.where(live, jnp.sum(moved[:sites], axis=0, keepdims=True), 6.0)
    dy = jnp.sum(moved[sites : 2 * sites], axis=0, keepdims=True) + CELL_SIDE * side_y
    dy = jnp.where(live, dy, 0.0)
    dz = jnp.where(live, jnp.sum(moved[2 * sites :], axis=0, keepdims=True), 0.0)
    length = jnp.sqrt(dx * dx + dy * dy + dz * dz)
    inverse = 1.0 / length
    ratio = length * (1.0 / CUTOFF)
    inside = live & (ratio < 1.0)
    r2 = ratio * ratio
    r5 = r2 * r2 * ratio
    r6 = r5 * ratio
    weight = jnp.where(inside, 1.0 - r6 * (28.0 - 48.0 * ratio + 21.0 * r2), 0.0)
    slope = jnp.where(inside, -168.0 * r5 * (1.0 - 2.0 * ratio + r2), 0.0)
    sine, cosine = sin_cos_pi(order * ratio)
    basis = (math.sqrt(2.0 / CUTOFF) * inverse) * sine
    basis_slope = (math.sqrt(2.0 / CUTOFF) * inverse) * (
        (math.pi / CUTOFF) * order * cosine - sine * inverse
    )
    ex = dx * inverse
    ey = dy * inverse
    ez = dz * inverse
    angular = jnp.concatenate(
        [
            jnp.ones_like(ex),
            root_three * ex,
            root_three * ey,
            root_three * ez,
            root_fifteen * ex * ey,
            root_fifteen * ey * ez,
            0.5 * root_five * (3.0 * ez * ez - 1.0),
            root_fifteen * ex * ez,
            0.5 * root_fifteen * (ex * ex - ey * ey),
            jnp.zeros((ORDERS - 9, pairs), F32),
        ],
        axis=0,
    )
    angular_high, angular_low = split(angular)
    blocks = [
        jnp.concatenate(
            [
                jnp.concatenate([angular_high[:, cut]] * GROUP, axis=0) * block_half,
                jnp.concatenate([angular_low[:, cut]] * GROUP, axis=0) * block_half,
            ],
            axis=0,
        )
        for cut in lanes
    ]
    lane_ids = lax.broadcasted_iota(jnp.int32, (128, span), 0)
    lane_slot = lax.broadcasted_iota(jnp.int32, (128, span), 1) // nbr + 3 * sites
    scale = mm(scale_parts, jnp.where(lane_ids == lane_slot, 1.0, 0.0).astype(BF16))
    scale = scale[:groups] + scale[groups : 2 * groups] + scale[2 * groups : 3 * groups]
    scale = jnp.concatenate([scale[g : g + 1] for g in range(groups)], axis=1)
    scale = scale * (1.0 / root_count)
    pull = ROOT_HALF * scale

    basis_high, basis_low = split(basis)
    before = folded(
        mm(lookup, jnp.concatenate([pick_half, slot_half, basis_high, basis_low], axis=0))
    )
    gate = 0.5 * jnp.tanh(0.5 * before) + 0.5
    active = before * gate
    latent = weight * active
    mixed = half_depth(value_rows, latent)
    values = mixed[:width]
    env_high, env_low = split(mixed[width:])

    def over_pairs(high, low):
        sums = []
        for cut, block in zip(lanes, blocks):
            quad = mm_nt(jnp.concatenate([high[:, cut], low[:, cut]], axis=0), block)
            sums.append((quad[:width, :wide] + quad[:width, wide:] + quad[width:, :wide]) * paths_t)
        return sums

    def over_orders(tables):
        parts = [folded(mm(stacked(*split(t)), block)) for t, block in zip(tables, blocks)]
        return jnp.concatenate(parts, axis=1)

    weighted = over_pairs(env_high, env_low)
    inner = over_orders(weighted)
    scalars = values * inner
    joined_high, joined_low = split(jnp.concatenate([latent, scalars], axis=0))
    z = full_depth(latent_both_t, latent_high_t, joined_high, joined_low)
    z_gate = 0.5 * jnp.tanh(0.5 * z) + 0.5
    update = z * z_gate
    update_out = update * out_column
    pair_energy = jnp.sum(latent * out_column + weight * update_out, axis=0, keepdims=True)
    pair_energy = pair_energy * pull
    d_z = (pull * weight) * out_column * (z_gate + update * (1.0 - z_gate))
    spread_back = half_depth(latent_rows, d_z)
    d_scalars = spread_back[width:]
    d_values = d_scalars * inner
    dinner_high, dinner_low = split(d_scalars * values)
    d_embed = over_pairs(dinner_high, dinner_low)
    d_env = over_orders(d_embed)

    d_angular = []
    for g, cut in enumerate(lanes):
        sides = jnp.transpose(jnp.concatenate([weighted[g], d_embed[g]], axis=0))
        sides_high, sides_low = split(sides)
        d_block = full_depth(
            jnp.concatenate([sides_high, sides_low], axis=0),
            sides_high,
            jnp.concatenate([dinner_high[:, cut], env_high[:, cut]], axis=0),
            jnp.concatenate([dinner_low[:, cut], env_low[:, cut]], axis=0),
        )
        d_block = d_block * block_mask
        total = d_block[:ORDERS]
        for k in range(1, GROUP):
            total = total + d_block[k * ORDERS : (k + 1) * ORDERS]
        d_angular.append(total)
    d_angular = jnp.concatenate(d_angular, axis=1)

    mixed_high, mixed_low = split(jnp.concatenate([d_values, d_env], axis=0))
    d_latent = (
        full_depth(value_both, value_high, mixed_high, mixed_low)
        + spread_back[:width]
        + pull * out_column
    )
    d_weight = jnp.sum(d_latent * active + pull * update_out, axis=0, keepdims=True)
    d_before = d_latent * weight * (gate + active * (1.0 - gate))
    d_basis = half_depth(basis_rows, d_before)

    d_length = jnp.sum(d_basis * basis_slope, axis=0, keepdims=True) + d_weight * slope * (
        1.0 / CUTOFF
    )
    a1, a2, a3, a4, a5, a6, a7, a8 = [d_angular[m : m + 1] for m in range(1, 9)]
    ux = root_three * a1 + root_fifteen * (ey * a4 + ez * a7 + ex * a8)
    uy = root_three * a2 + root_fifteen * (ex * a4 + ez * a5 - ey * a8)
    uz = root_three * a3 + root_fifteen * (ey * a5 + ex * a7) + 3.0 * root_five * ez * a6
    along = ex * ux + ey * uy + ez * uz
    radial_part = d_length - along * inverse
    gx = ux * inverse + ex * radial_part
    gy = uy * inverse + ey * radial_part
    gz = uz * inverse + ez * radial_part
    hx = -0.5 * dx
    hy = -0.5 * dy
    hz = -0.5 * dz
    virial = [hx * gx, hx * gy, hx * gz, hy * gx, hy * gy, hy * gz, hz * gx, hz * gy, hz * gz]
    rest = [jnp.zeros((ORDERS - 13, pairs), F32)]
    near_terms = jnp.concatenate(
        [-gx, -gy, -gz, *virial, jnp.zeros_like(gx), *rest], axis=0
    )
    center_terms = jnp.concatenate([gx, gy, gz, *virial, pair_energy, *rest], axis=0)
    near_sums = mm_nt(jnp.concatenate(split(near_terms), axis=0), pick_half)
    center_sums = mm_nt(jnp.concatenate(split(center_terms), axis=0), center_half)
    totals = folded(near_sums + center_sums)
    keep_ref[...] = totals[:, : known // 2]
    send_ref[...] = totals[:, known // 2 :]


def in_hbm(*arrays):
    return [pltpu.with_memory_space_constraint(array, pltpu.HBM) for array in arrays]


def joined(parts):
    total = sum(part.shape[0] for part in parts)
    start = 0
    pads = []
    for part in parts:
        end = start + part.shape[0]
        pads.append(jnp.pad(part, ((start, total - end), (0, 0))))
        start = end
    return functools.reduce(jnp.add, pads)


def local(
    positions,
    features,
    species,
    centers,
    neighbours,
    counts,
    species_scale,
    species_shift,
    center_weight,
    near_weight,
    basis_weight,
    path_weight,
    value_weight,
    latent_weight,
    out_weight,
):
    cells_x, cells_y, cells_z, sites, width = features.shape
    cell_count = cells_x * cells_y * cells_z
    owned = cell_count * sites
    assert (cells_x, cells_y, cells_z, sites) == (2, 1, 2, SITES)
    pairs = neighbours.size
    nbr = pairs // owned
    kind = min(3, lax.axis_size("gy"))

    def moved(array, steps, wrap=None):
        names = tuple(steps)
        sizes = [lax.axis_size(name) for name in names]
        route = []
        for at in np.ndindex(*sizes):
            to = [(p + steps[name]) % size for p, name, size in zip(at, names, sizes)]
            if wrap is not None and wrap != (to[0] != at[0] + steps[names[0]]):
                continue
            route.append(
                (int(np.ravel_multi_index(at, sizes)), int(np.ravel_multi_index(to, sizes)))
            )
        return lax.ppermute(array, names, route)

    vmem = pl.BlockSpec(memory_space=pltpu.VMEM)
    hbm = pl.BlockSpec(memory_space=pltpu.HBM)
    listed = centers.reshape(1, owned)
    payload = jax.ShapeDtypeStruct((owned + 8 + pairs // 128, width), F32)
    here, again = pl.pallas_call(
        functools.partial(pack_kernel, kind),
        out_shape=(payload, payload),
        in_specs=[hbm] * 6,
        out_specs=(vmem, vmem),
        scratch_shapes=[
            pltpu.VMEM((owned, 128), F32),
            pltpu.VMEM(positions.shape, F32),
            pltpu.VMEM(species.shape, jnp.int32),
            pltpu.VMEM(listed.shape, jnp.int32),
            pltpu.VMEM(neighbours.shape, jnp.int32),
            pltpu.SMEM(species_scale.shape, F32),
            pltpu.SemaphoreType.DMA((6,)),
        ],
        compiler_params=pltpu.CompilerParams(vmem_limit_bytes=8 * 1024 * 1024),
        name="pack_payload",
    )(
        *in_hbm(
            positions,
            features.reshape(owned, width),
            species,
            listed,
            neighbours,
            species_scale,
        )
    )
    weights = (
        center_weight,
        near_weight,
        basis_weight,
        path_weight,
        value_weight,
        latent_weight,
        out_weight.reshape(1, width),
    )
    *weights, shift_row = pl.pallas_call(
        fetch_kernel,
        out_shape=(
            *(jax.ShapeDtypeStruct(w.shape, F32) for w in weights),
            jax.ShapeDtypeStruct((1, owned), F32),
        ),
        in_specs=[hbm] * (3 + len(weights)),
        out_specs=(vmem,) * (1 + len(weights)),
        scratch_shapes=[
            pltpu.VMEM(species.shape, jnp.int32),
            pltpu.VMEM(listed.shape, jnp.int32),
            pltpu.SMEM(species_shift.shape, F32),
            pltpu.SemaphoreType.DMA((3 + len(weights),)),
        ],
        compiler_params=pltpu.CompilerParams(vmem_limit_bytes=8 * 1024 * 1024),
        name="fetch_weights",
    )(*in_hbm(species, listed, species_shift, *weights))
    short = here[: owned + 8]
    steps = (-1, 1)[: kind - 1]
    last_y = [moved(again, {"gy": step})[: owned + 8] for step in steps]
    last_xy = [moved(again, {"gx": 1, "gy": step}, False)[: owned + 8] for step in steps]
    last_x = moved(again, {"gx": 1}, False)
    wrap_xy = [moved(here, {"gx": 1, "gy": step}, True) for step in steps]
    wrap_x = moved(here, {"gx": 1}, True)
    wrap_x, *wrap_xy = lax.optimization_barrier((wrap_x, *wrap_xy))
    last_x = wrap_x + last_x
    sides = []
    for y, xy, wrapped in zip(last_y, last_xy, wrap_xy):
        sides.extend((y, wrapped[: owned + 8] + xy))
    next_z = moved(joined([here, last_x, *sides]), {"gz": -1})
    half = 2 * kind * owned
    keep, send = pl.pallas_call(
        functools.partial(force_kernel, kind, nbr),
        out_shape=(
            jax.ShapeDtypeStruct((ORDERS, half), F32),
            jax.ShapeDtypeStruct((ORDERS, half), F32),
        ),
        in_specs=[vmem] * (8 + 2 * kind),
        out_specs=(vmem, vmem),
        compiler_params=pltpu.CompilerParams(vmem_limit_bytes=32 * 1024 * 1024),
        name="pair_forces",
    )(
        here,
        last_x,
        *sides,
        next_z,
        *weights,
    )
    totals = keep + moved(send, {"gz": 1})

    def part(index):
        return totals[:, index * owned : (index + 1) * owned]

    steps = tuple(enumerate((1, -1)[: kind - 1]))
    far = totals[:, kind * owned :]
    back = [moved(far, {"gx": -1}, False)[:, :owned]]
    for i, step in steps:
        wrapped = moved(far, {"gx": -1, "gy": step}, False)
        back.append(wrapped[:, (1 + i) * owned : (2 + i) * owned])
    for i, step in steps:
        back.append(moved(totals, {"gy": step})[:, (1 + i) * owned : (2 + i) * owned])
    back.extend(moved(part(kind + 1 + i), {"gx": -1, "gy": step}, True) for i, step in steps)
    back.append(moved(part(kind), {"gx": -1}, True))
    site_energy, forces, virial = pl.pallas_call(
        finish_kernel,
        out_shape=(
            jax.ShapeDtypeStruct(species.shape, F32),
            jax.ShapeDtypeStruct(positions.shape, F32),
            jax.ShapeDtypeStruct((*species.shape, 9), F32),
        ),
        in_specs=[vmem] * (2 + len(back)),
        out_specs=(vmem, vmem, vmem),
        compiler_params=pltpu.CompilerParams(vmem_limit_bytes=8 * 1024 * 1024),
        name="write_outputs",
    )(totals, shift_row, *back)
    return (site_energy, forces, jnp.transpose(virial, (4, 0, 1, 2, 3)))


def solution(mesh):
    placed = (
        P(None, "gx", "gy", "gz", None),
        P("gx", "gy", "gz", None, None),
        P("gx", "gy", "gz", None),
        P(("gx", "gy", "gz")),
        P(("gx", "gy", "gz"), None),
        P(("gx", "gy", "gz")),
        P(),
        P(),
        P(),
        P(),
        P(),
        P(),
        P(),
        P(),
        P(),
    )
    return jax.shard_map(
        local,
        mesh=mesh,
        in_specs=placed,
        out_specs=(
            P("gx", "gy", "gz", None),
            P(None, "gx", "gy", "gz", None),
            P(None, "gx", "gy", "gz", None),
        ),
        check_vma=False,
    )
```

```python
import functools
import math

import jax
import jax.numpy as jnp
import numpy as np
from jax import lax
from jax.experimental import pallas as pl
from jax.experimental.pallas import tpu as pltpu
from jax.sharding import PartitionSpec as P

EXACT_DOT = lax.Precision.HIGHEST
CUTOFF = 5.0
CELL_SIDE = 4.6
ROOT_HALF = 0.7071067811865476
GROUP = 8
ORDERS = 16
SITES = 8
OWN_CELLS = 4
FRAME_CELLS = 48
F32 = jnp.float32
BF16 = jnp.bfloat16


def split(value):
    high = value.astype(BF16)
    low = (value - high.astype(F32)).astype(BF16)
    return high, low


def split3(value):
    high = value.astype(BF16)
    rest = value - high.astype(F32)
    middle = rest.astype(BF16)
    low = (rest - middle.astype(F32)).astype(BF16)
    return high, middle, low


def mm(a, b):
    return lax.dot_general(a, b, (((1,), (0,)), ((), ())), preferred_element_type=F32)


def mm_nt(a, b):
    return lax.dot_general(a, b, (((1,), (1,)), ((), ())), preferred_element_type=F32)


def stacked(high, low):
    top = jnp.concatenate([high, high], axis=1)
    bottom = jnp.concatenate([low, jnp.zeros_like(low)], axis=1)
    return jnp.concatenate([top, bottom], axis=0)


def folded(product):
    half = product.shape[0] // 2
    return product[:half] + product[half:]


def half_depth(weights, value):
    return folded(mm(weights, jnp.concatenate(split(value), axis=0)))


def full_depth(both, high, value_high, value_low):
    return folded(mm(both, value_high)) + mm(high, value_low)


def sin_cos_pi(turns):
    near = turns - 2.0 * jnp.round(turns * 0.5)
    quarter = jnp.round(near * 2.0)
    v = (near - 0.5 * quarter) * math.pi
    v2 = v * v
    s = v * (
        1.0
        + v2
        * (-1.0 / 6 + v2 * (1.0 / 120 + v2 * (-1.0 / 5040 + v2 * (1.0 / 362880 - v2 / 39916800))))
    )
    c = 1.0 + v2 * (
        -0.5
        + v2
        * (1.0 / 24 + v2 * (-1.0 / 720 + v2 * (1.0 / 40320 + v2 * (-1.0 / 3628800 + v2 / 479001600))))
    )
    odd = jnp.abs(quarter) == 1.0
    sine = jnp.where(odd, quarter * c, jnp.where(quarter == 0.0, s, -s))
    cosine = jnp.where(odd, -quarter * s, jnp.where(quarter == 0.0, c, -c))
    return sine, cosine


def lane_row(piece, offset):
    row = jnp.concatenate([piece, jnp.zeros((1, 128 - piece.shape[1]), piece.dtype)], axis=1)
    return pltpu.roll(row, offset, 1) if offset else row


def pack_kernel(
    kind,
    positions_hbm,
    features_hbm,
    species_hbm,
    centers_hbm,
    neighbours_hbm,
    scale_hbm,
    payload_ref,
    wide_ref,
    positions_ref,
    species_ref,
    centers_ref,
    neighbours_ref,
    scale_ref,
    sems,
):
    owned, nbr = neighbours_ref.shape
    per_row = 128 // nbr
    pairs_in = (
        (features_hbm, payload_ref.at[pl.ds(0, owned), :]),
        (neighbours_hbm, neighbours_ref),
        (centers_hbm, centers_ref),
        (positions_hbm, positions_ref),
        (species_hbm, species_ref),
        (scale_hbm, scale_ref),
    )
    copies = [
        pltpu.make_async_copy(source, target, sems.at[i])
        for i, (source, target) in enumerate(pairs_in)
    ]
    for copy in copies:
        copy.start()
    for copy in copies:
        copy.wait()
    payload_ref[owned : owned + 8] = jnp.zeros((8, 128), F32)
    for cell in range(OWN_CELLS):
        x, z = cell // 2, cell % 2
        species = species_ref[x, 0, z : z + 1, :]
        scale = jnp.zeros(species.shape, F32)
        for s in range(scale_ref.shape[0]):
            scale = jnp.where(species == s, scale_ref[s], scale)
        row = lane_row(scale, 3 * SITES)
        for c in range(3):
            row = row + lane_row(positions_ref[c, x, 0, z : z + 1, :], c * SITES)
        payload_ref[owned + cell : owned + cell + 1] = row

    chosen = lax.broadcasted_iota(jnp.int32, (owned, owned), 0) == centers_ref[...]
    chosen = jnp.where(chosen, 1.0, 0.0)
    occupied = jnp.sum(chosen, axis=1, keepdims=True) > 0.5
    chosen = chosen.astype(BF16)
    rows = neighbours_ref[...]
    upper = mm(chosen, (rows >> 4).astype(F32).astype(BF16))
    lower = mm(chosen, (rows & 15).astype(F32).astype(BF16))
    rows = (upper * 16.0 + lower).astype(jnp.int32)
    live = occupied & (rows < FRAME_CELLS * SITES)
    slot = lax.broadcasted_iota(jnp.int32, (owned, nbr), 0)
    cell = slot >> 3
    site = rows & 7
    place = rows >> 3
    near_z = (place & 3) + 1 - 2 * (cell & 1)
    column = place >> 2
    frame_x = (column * 11) >> 5
    frame_y = column - 3 * frame_x
    near_x = frame_x + 1 - 2 * (cell >> 1)
    side = jnp.where(frame_y == 1, 0, jnp.where(frame_y == 2, 1, kind - 1))
    block = (near_z >> 1) * 2 + 1 - (near_x >> 1)
    where = (block * kind + side) * owned + (near_x & 1) * 16 + (near_z & 1) * 8 + site
    code = jnp.where(live, 1 + where + (frame_y << 10), 0).astype(F32)
    wide_ref[...] = jnp.concatenate([code, jnp.zeros((owned, 128 - nbr), F32)], axis=1)
    codes = wide_ref[pl.ds(0, owned // per_row, stride=per_row), :]
    for j in range(1, per_row):
        more = wide_ref[pl.ds(j, owned // per_row, stride=per_row), :]
        codes = codes + pltpu.roll(more, j * nbr, 1)
    payload_ref[owned + 8 :] = codes


def fetch_kernel(species_hbm, centers_hbm, shift_hbm, *refs):
    *refs, shift_row_ref, species_ref, centers_ref, shift_ref, sems = refs
    count = len(refs) // 2
    pairs_in = [
        (species_hbm, species_ref),
        (centers_hbm, centers_ref),
        (shift_hbm, shift_ref),
        *zip(refs[:count], refs[count:]),
    ]
    copies = [
        pltpu.make_async_copy(source, target, sems.at[i])
        for i, (source, target) in enumerate(pairs_in)
    ]
    for copy in copies:
        copy.start()
    for copy in copies:
        copy.wait()
    owned = centers_ref.shape[1]
    shift_row = jnp.zeros((1, 128), F32)
    for cell in range(OWN_CELLS):
        species = species_ref[cell // 2, 0, cell % 2 : cell % 2 + 1, :]
        shift = jnp.zeros(species.shape, F32)
        for s in range(shift_ref.shape[0]):
            shift = jnp.where(species == s, shift_ref[s], shift)
        shift_row = shift_row + lane_row(shift, cell * SITES)
    chosen = lax.broadcasted_iota(jnp.int32, (owned, owned), 0) == centers_ref[...]
    occupied = jnp.sum(jnp.where(chosen, 1.0, 0.0), axis=1, keepdims=True) > 0.5
    column = jnp.where(occupied, jnp.ones((owned, 128), F32), 0.0)
    shift_row_ref[...] = shift_row[:, :owned] * jnp.transpose(column)[0:1]


def finish_kernel(mine_ref, shift_row_ref, *refs):
    *near_refs, energy_ref, forces_ref, virial_ref = refs
    owned = near_refs[0].shape[1]
    total = mine_ref[:, :owned]
    for near_ref in near_refs:
        total = total + near_ref[...]
    energy = total[12:13] + shift_row_ref[...]
    columns = jnp.transpose(jnp.concatenate([total, jnp.zeros((ORDERS, 128 - owned), F32)], axis=1))
    for cell in range(OWN_CELLS):
        x, z = cell // 2, cell % 2
        lanes = slice(cell * SITES, (cell + 1) * SITES)
        energy_ref[x, 0, z : z + 1, :] = energy[:, lanes]
        for c in range(3):
            forces_ref[c, x, 0, z : z + 1, :] = total[c : c + 1, lanes]
        virial_ref[x, 0, z] = columns[lanes, 3:12]


def force_kernel(kind, nbr, here_ref, last_x_ref, *refs):
    near_side_refs = refs[: 2 * kind - 2]
    (
        next_z_ref,
        center_weight_ref,
        near_weight_ref,
        basis_weight_ref,
        path_weight_ref,
        value_weight_ref,
        latent_weight_ref,
        out_weight_ref,
        keep_ref,
        send_ref,
    ) = refs[2 * kind - 2 :]
    height, width = here_ref.shape
    owned = OWN_CELLS * SITES
    short = owned + 8
    pairs = owned * nbr
    radial = basis_weight_ref.shape[0]
    span = GROUP * nbr
    groups = owned // GROUP
    wide = GROUP * ORDERS
    sites = SITES
    root_count = math.sqrt(nbr)
    root_three = math.sqrt(3.0)
    root_fifteen = math.sqrt(15.0)
    root_five = math.sqrt(5.0)
    far = next_z_ref[...]
    mains = [here_ref[...], last_x_ref[...], far[:height], far[height : 2 * height]]
    near_sides = [ref[...] for ref in near_side_refs]
    far_sides = far[2 * height :]
    far_sides = [far_sides[i * short : (i + 1) * short] for i in range(2 * kind - 2)]
    blocks_in = [
        [mains[0], *near_sides[0::2]],
        [mains[1], *near_sides[1::2]],
        [mains[2], *far_sides[0::2]],
        [mains[3], *far_sides[1::2]],
    ]
    feats = jnp.concatenate([side[:owned] for block in blocks_in for side in block], axis=0)
    known = feats.shape[0]
    center_feats = []
    center_coords = []
    coords = []
    scales = []
    codes = []
    cell_row = lax.broadcasted_iota(jnp.int32, (kind * OWN_CELLS, 128), 0) % OWN_CELLS
    tile_lane = lax.broadcasted_iota(jnp.int32, (kind * OWN_CELLS, 128), 1)
    for g, block in enumerate(blocks_in):
        behind_x, ahead_z = g % 2, g // 2
        cell = behind_x * 2 + 1 - ahead_z
        center_feats.append(block[0][cell * sites : (cell + 1) * sites])
        rows = jnp.concatenate([side[owned : owned + OWN_CELLS] for side in block], axis=0)
        scales.append(rows[cell : cell + 1])
        corner_x = (cell_row // 2 + 2 - 2 * behind_x).astype(F32) * CELL_SIDE
        corner_z = (cell_row % 2 + 2 * ahead_z).astype(F32) * CELL_SIDE
        corner = jnp.where(
            tile_lane < sites, corner_x, jnp.where(tile_lane < 2 * sites, 0.0, corner_z)
        )
        rows = rows + corner
        coords.append(rows)
        center_coords.append(rows[cell : cell + 1])
        start = short + cell * span // 128
        codes.extend(block[0][start + r : start + r + 1] for r in range(span // 128))
    center_feats = jnp.concatenate(center_feats, axis=0)
    coords = jnp.concatenate(coords, axis=0)
    code = jnp.concatenate(codes, axis=1).astype(jnp.int32)
    live = code > 0
    code = jnp.maximum(code - 1, 0)
    side_y = ((code >> 10) - 1).astype(F32)
    near_row = jnp.where(live, code & 1023, known)

    def place_rows(cell_rows):
        count = cell_rows.shape[0] * sites
        spread = jnp.broadcast_to(cell_rows[:, None, :], (cell_rows.shape[0], sites, 128))
        spread = spread.reshape(count, 128)
        lane = lax.broadcasted_iota(jnp.int32, (count, 128), 1)
        row = lax.broadcasted_iota(jnp.int32, (count, 128), 0)
        keep = (lane % sites == row % sites) & (lane < 3 * sites)
        spread = jnp.transpose(jnp.where(keep, spread, 0.0))
        return jnp.concatenate(split3(spread[: 3 * sites]), axis=0)

    place_parts = place_rows(coords)
    center_parts = place_rows(jnp.concatenate(center_coords, axis=0))

    value_rows = stacked(*split(jnp.transpose(value_weight_ref[...])))
    latent_high_t, latent_low_t = split(jnp.transpose(latent_weight_ref[...]))
    latent_both_t = jnp.concatenate([latent_high_t, latent_low_t], axis=0)
    latent_rows = stacked(*split(latent_weight_ref[...]))
    value_high, value_low = split(value_weight_ref[...])
    value_both = jnp.concatenate([value_high, value_low], axis=0)
    basis_t = jnp.transpose(basis_weight_ref[...])
    basis_high_t, basis_low_t = split(basis_t)
    basis_rows = stacked(*split(basis_weight_ref[...]))

    def project(weight, rows):
        weight = stacked(*split(jnp.transpose(weight)))
        return folded(mm_nt(weight, jnp.concatenate(split(rows), axis=1)))

    near_t = project(near_weight_ref[...], feats)
    own_t = project(center_weight_ref[...], center_feats)
    near_high, near_low = split(near_t)
    own_high, own_low = split(own_t)
    lookup = jnp.concatenate(
        [
            jnp.concatenate([near_high, own_high, basis_high_t, basis_high_t], axis=1),
            jnp.concatenate([near_low, own_low, basis_low_t, jnp.zeros_like(basis_low_t)], axis=1),
        ],
        axis=0,
    )
    scale_rows = jnp.concatenate(scales, axis=0)
    scale_parts = jnp.concatenate(
        [*split3(scale_rows), jnp.zeros((16 - 3 * groups, 128), BF16)], axis=0
    )

    level = lax.broadcasted_iota(jnp.int32, (ORDERS, width), 0)
    path_rows = jnp.where(
        level == 0,
        path_weight_ref[0:1, :],
        jnp.where(
            level < 4,
            path_weight_ref[1:2, :],
            jnp.where(level < 9, path_weight_ref[2:3, :], 0.0),
        ),
    )
    paths_t = jnp.transpose(jnp.concatenate([path_rows] * GROUP, axis=0)) * (1.0 / root_count)
    out_column = jnp.transpose(jnp.broadcast_to(out_weight_ref[...], (width, width)))
    out_column = jnp.concatenate([out_column] * (pairs // width), axis=1)

    site_ids = lax.broadcasted_iota(jnp.int32, (known, pairs), 0)
    slot_ids = lax.broadcasted_iota(jnp.int32, (owned, pairs), 0)
    slot_row = lax.broadcasted_iota(jnp.int32, (1, pairs), 1) // nbr
    block_row = lax.broadcasted_iota(jnp.int32, (wide, span), 0) // ORDERS
    block_lane = lax.broadcasted_iota(jnp.int32, (wide, span), 1) // nbr
    block_mask = (block_row == block_lane).astype(F32)
    block_half = block_mask.astype(BF16)
    order = lax.broadcasted_iota(jnp.int32, (radial, pairs), 0).astype(F32) + 1.0
    lanes = [slice(g * span, (g + 1) * span) for g in range(groups)]

    pick = jnp.where(site_ids == near_row, 1.0, 0.0)
    pick_half = pick.astype(BF16)
    slot_half = jnp.where(slot_ids == slot_row, 1.0, 0.0).astype(BF16)

    moved = mm(place_parts, pick_half) - mm(center_parts, slot_half)
    moved = moved[: 3 * sites] + moved[3 * sites : 6 * sites] + moved[6 * sites :]
    dx = jnp.where(live, jnp.sum(moved[:sites], axis=0, keepdims=True), 6.0)
    dy = jnp.sum(moved[sites : 2 * sites], axis=0, keepdims=True) + CELL_SIDE * side_y
    dy = jnp.where(live, dy, 0.0)
    dz = jnp.where(live, jnp.sum(moved[2 * sites :], axis=0, keepdims=True), 0.0)
    length = jnp.sqrt(dx * dx + dy * dy + dz * dz)
    inverse = 1.0 / length
    ratio = length * (1.0 / CUTOFF)
    inside = live & (ratio < 1.0)
    r2 = ratio * ratio
    r5 = r2 * r2 * ratio
    r6 = r5 * ratio
    weight = jnp.where(inside, 1.0 - r6 * (28.0 - 48.0 * ratio + 21.0 * r2), 0.0)
    slope = jnp.where(inside, -168.0 * r5 * (1.0 - 2.0 * ratio + r2), 0.0)
    sine, cosine = sin_cos_pi(order * ratio)
    basis = (math.sqrt(2.0 / CUTOFF) * inverse) * sine
    basis_slope = (math.sqrt(2.0 / CUTOFF) * inverse) * (
        (math.pi / CUTOFF) * order * cosine - sine * inverse
    )
    ex = dx * inverse
    ey = dy * inverse
    ez = dz * inverse
    angular = jnp.concatenate(
        [
            jnp.ones_like(ex),
            root_three * ex,
            root_three * ey,
            root_three * ez,
            root_fifteen * ex * ey,
            root_fifteen * ey * ez,
            0.5 * root_five * (3.0 * ez * ez - 1.0),
            root_fifteen * ex * ez,
            0.5 * root_fifteen * (ex * ex - ey * ey),
            jnp.zeros((ORDERS - 9, pairs), F32),
        ],
        axis=0,
    )
    angular_high, angular_low = split(angular)
    blocks = [
        jnp.concatenate(
            [
                jnp.concatenate([angular_high[:, cut]] * GROUP, axis=0) * block_half,
                jnp.concatenate([angular_low[:, cut]] * GROUP, axis=0) * block_half,
            ],
            axis=0,
        )
        for cut in lanes
    ]
    lane_ids = lax.broadcasted_iota(jnp.int32, (128, span), 0)
    lane_slot = lax.broadcasted_iota(jnp.int32, (128, span), 1) // nbr + 3 * sites
    scale = mm(scale_parts, jnp.where(lane_ids == lane_slot, 1.0, 0.0).astype(BF16))
    scale = scale[:groups] + scale[groups : 2 * groups] + scale[2 * groups : 3 * groups]
    scale = jnp.concatenate([scale[g : g + 1] for g in range(groups)], axis=1)
    scale = scale * (1.0 / root_count)
    pull = ROOT_HALF * scale

    basis_high, basis_low = split(basis)
    before = folded(
        mm(lookup, jnp.concatenate([pick_half, slot_half, basis_high, basis_low], axis=0))
    )
    gate = 0.5 * jnp.tanh(0.5 * before) + 0.5
    active = before * gate
    latent = weight * active
    latent_high, latent_low = split(latent)
    mixed = folded(mm(value_rows, jnp.concatenate([latent_high, latent_low], axis=0)))
    values = mixed[:width]
    env_high, env_low = split(mixed[width:])

    def over_pairs(high, low):
        sums = []
        for cut, block in zip(lanes, blocks):
            quad = mm_nt(jnp.concatenate([high[:, cut], low[:, cut]], axis=0), block)
            sums.append((quad[:width, :wide] + quad[:width, wide:] + quad[width:, :wide]) * paths_t)
        return sums

    def over_orders(tables):
        parts = [folded(mm(stacked(*split(t)), block)) for t, block in zip(tables, blocks)]
        return jnp.concatenate(parts, axis=1)

    weighted = over_pairs(env_high, env_low)
    inner = over_orders(weighted)
    scalars = values * inner
    scalars_high, scalars_low = split(scalars)
    z = full_depth(
        latent_both_t,
        latent_high_t,
        jnp.concatenate([latent_high, scalars_high], axis=0),
        jnp.concatenate([latent_low, scalars_low], axis=0),
    )
    z_gate = 0.5 * jnp.tanh(0.5 * z) + 0.5
    update = z * z_gate
    update_out = update * out_column
    pair_energy = jnp.sum(latent * out_column + weight * update_out, axis=0, keepdims=True)
    pair_energy = pair_energy * pull
    d_z = (pull * weight) * out_column * (z_gate + update * (1.0 - z_gate))
    spread_back = half_depth(latent_rows, d_z)
    d_scalars = spread_back[width:]
    d_values = d_scalars * inner
    dinner_high, dinner_low = split(d_scalars * values)
    d_embed = over_pairs(dinner_high, dinner_low)
    d_env = over_orders(d_embed)

    d_angular = []
    for g, cut in enumerate(lanes):
        sides = jnp.transpose(jnp.concatenate([weighted[g], d_embed[g]], axis=0))
        sides_high, sides_low = split(sides)
        d_block = full_depth(
            jnp.concatenate([sides_high, sides_low], axis=0),
            sides_high,
            jnp.concatenate([dinner_high[:, cut], env_high[:, cut]], axis=0),
            jnp.concatenate([dinner_low[:, cut], env_low[:, cut]], axis=0),
        )
        d_block = d_block * block_mask
        total = d_block[:ORDERS]
        for k in range(1, GROUP):
            total = total + d_block[k * ORDERS : (k + 1) * ORDERS]
        d_angular.append(total)
    d_angular = jnp.concatenate(d_angular, axis=1)

    mixed_high, mixed_low = split(jnp.concatenate([d_values, d_env], axis=0))
    d_latent = (
        full_depth(value_both, value_high, mixed_high, mixed_low)
        + spread_back[:width]
        + pull * out_column
    )
    d_weight = jnp.sum(d_latent * active + pull * update_out, axis=0, keepdims=True)
    d_before = d_latent * weight * (gate + active * (1.0 - gate))
    d_basis = half_depth(basis_rows, d_before)

    d_length = jnp.sum(d_basis * basis_slope, axis=0, keepdims=True) + d_weight * slope * (
        1.0 / CUTOFF
    )
    a1, a2, a3, a4, a5, a6, a7, a8 = [d_angular[m : m + 1] for m in range(1, 9)]
    ux = root_three * a1 + root_fifteen * (ey * a4 + ez * a7 + ex * a8)
    uy = root_three * a2 + root_fifteen * (ex * a4 + ez * a5 - ey * a8)
    uz = root_three * a3 + root_fifteen * (ey * a5 + ex * a7) + 3.0 * root_five * ez * a6
    along = ex * ux + ey * uy + ez * uz
    radial_part = d_length - along * inverse
    gx = ux * inverse + ex * radial_part
    gy = uy * inverse + ey * radial_part
    gz = uz * inverse + ez * radial_part
    hx = -0.5 * dx
    hy = -0.5 * dy
    hz = -0.5 * dz
    virial = [hx * gx, hx * gy, hx * gz, hy * gx, hy * gy, hy * gz, hz * gx, hz * gy, hz * gz]
    rest = [jnp.zeros((ORDERS - 13, pairs), F32)]
    near_terms = jnp.concatenate(
        [-gx, -gy, -gz, *virial, jnp.zeros_like(gx), *rest], axis=0
    )
    center_terms = jnp.concatenate([gx, gy, gz, *virial, pair_energy, *rest], axis=0)
    near_sums = mm_nt(jnp.concatenate(split(near_terms), axis=0), pick_half)
    center_sums = mm_nt(jnp.concatenate(split(center_terms), axis=0), slot_half)
    center_sums = jnp.concatenate(
        [folded(center_sums), jnp.zeros((ORDERS, 128 - owned), F32)], axis=1
    )
    totals = folded(near_sums)
    lane = lax.broadcasted_iota(jnp.int32, (ORDERS, 128), 1)
    tiles = [totals[:, 128 * i : 128 * (i + 1)] for i in range(known // 128)]
    for g in range(groups):
        cell = g % 2 * 2 + 1 - g // 2
        target = g * kind * owned + cell * sites
        turn = (target - g * GROUP) % 128
        piece = pltpu.roll(center_sums, turn, 1) if turn else center_sums
        begin = target % 128
        piece = jnp.where((lane >= begin) & (lane < begin + GROUP), piece, 0.0)
        tiles[target // 128] = tiles[target // 128] + piece
    totals = jnp.concatenate(tiles, axis=1)
    keep_ref[...] = totals[:, : known // 2]
    send_ref[...] = totals[:, known // 2 :]


def in_hbm(*arrays):
    return [pltpu.with_memory_space_constraint(array, pltpu.HBM) for array in arrays]


def joined(parts):
    total = sum(part.shape[0] for part in parts)
    start = 0
    pads = []
    for part in parts:
        end = start + part.shape[0]
        pads.append(jnp.pad(part, ((start, total - end), (0, 0))))
        start = end
    return functools.reduce(jnp.add, pads)


def local(
    positions,
    features,
    species,
    centers,
    neighbours,
    counts,
    species_scale,
    species_shift,
    center_weight,
    near_weight,
    basis_weight,
    path_weight,
    value_weight,
    latent_weight,
    out_weight,
):
    cells_x, cells_y, cells_z, sites, width = features.shape
    cell_count = cells_x * cells_y * cells_z
    owned = cell_count * sites
    assert (cells_x, cells_y, cells_z, sites) == (2, 1, 2, SITES)
    pairs = neighbours.size
    nbr = pairs // owned
    kind = min(3, lax.axis_size("gy"))

    def moved(array, steps):
        names = tuple(steps)
        sizes = [lax.axis_size(name) for name in names]
        route = []
        for at in np.ndindex(*sizes):
            to = [(p + steps[name]) % size for p, name, size in zip(at, names, sizes)]
            route.append(
                (int(np.ravel_multi_index(at, sizes)), int(np.ravel_multi_index(to, sizes)))
            )
        return lax.ppermute(array, names, route)

    vmem = pl.BlockSpec(memory_space=pltpu.VMEM)
    hbm = pl.BlockSpec(memory_space=pltpu.HBM)
    listed = centers.reshape(1, owned)
    here = pl.pallas_call(
        functools.partial(pack_kernel, kind),
        out_shape=jax.ShapeDtypeStruct((owned + 8 + pairs // 128, width), F32),
        in_specs=[hbm] * 6,
        out_specs=vmem,
        scratch_shapes=[
            pltpu.VMEM((owned, 128), F32),
            pltpu.VMEM(positions.shape, F32),
            pltpu.VMEM(species.shape, jnp.int32),
            pltpu.VMEM(listed.shape, jnp.int32),
            pltpu.VMEM(neighbours.shape, jnp.int32),
            pltpu.SMEM(species_scale.shape, F32),
            pltpu.SemaphoreType.DMA((6,)),
        ],
        compiler_params=pltpu.CompilerParams(vmem_limit_bytes=8 * 1024 * 1024),
        name="pack_payload",
    )(
        *in_hbm(
            positions,
            features.reshape(owned, width),
            species,
            listed,
            neighbours,
            species_scale,
        )
    )
    weights = (
        center_weight,
        near_weight,
        basis_weight,
        path_weight,
        value_weight,
        latent_weight,
        out_weight.reshape(1, width),
    )
    *weights, shift_row = pl.pallas_call(
        fetch_kernel,
        out_shape=(
            *(jax.ShapeDtypeStruct(w.shape, F32) for w in weights),
            jax.ShapeDtypeStruct((1, owned), F32),
        ),
        in_specs=[hbm] * (3 + len(weights)),
        out_specs=(vmem,) * (1 + len(weights)),
        scratch_shapes=[
            pltpu.VMEM(species.shape, jnp.int32),
            pltpu.VMEM(listed.shape, jnp.int32),
            pltpu.SMEM(species_shift.shape, F32),
            pltpu.SemaphoreType.DMA((3 + len(weights),)),
        ],
        compiler_params=pltpu.CompilerParams(vmem_limit_bytes=8 * 1024 * 1024),
        name="fetch_weights",
    )(*in_hbm(species, listed, species_shift, *weights))
    short = here[: owned + 8]
    last_x = moved(here, {"gx": 1})
    sides = []
    for step in (-1, 1)[: kind - 1]:
        sides.append(moved(short, {"gx": 1, "gy": step}))
        sides.insert(-1, moved(short, {"gy": step}))
    next_z = moved(joined([here, last_x, *sides]), {"gz": -1})
    half = 2 * kind * owned
    keep, send = pl.pallas_call(
        functools.partial(force_kernel, kind, nbr),
        out_shape=(
            jax.ShapeDtypeStruct((ORDERS, half), F32),
            jax.ShapeDtypeStruct((ORDERS, half), F32),
        ),
        in_specs=[vmem] * (8 + 2 * kind),
        out_specs=(vmem, vmem),
        compiler_params=pltpu.CompilerParams(vmem_limit_bytes=32 * 1024 * 1024),
        name="pair_forces",
    )(
        here,
        last_x,
        *sides,
        next_z,
        *weights,
    )
    totals = keep + moved(send, {"gz": 1})

    def part(index):
        return totals[:, index * owned : (index + 1) * owned]

    back = [moved(part(kind), {"gx": -1})]
    for i, step in enumerate((1, -1)[: kind - 1]):
        back.append(moved(part(kind + 1 + i), {"gx": -1, "gy": step}))
        back.append(moved(part(1 + i), {"gy": step}))
    site_energy, forces, virial = pl.pallas_call(
        finish_kernel,
        out_shape=(
            jax.ShapeDtypeStruct(species.shape, F32),
            jax.ShapeDtypeStruct(positions.shape, F32),
            jax.ShapeDtypeStruct((*species.shape, 9), F32),
        ),
        in_specs=[vmem] * (2 + len(back)),
        out_specs=(vmem, vmem, vmem),
        compiler_params=pltpu.CompilerParams(vmem_limit_bytes=8 * 1024 * 1024),
        name="write_outputs",
    )(totals, shift_row, *back)
    return (site_energy, forces, jnp.transpose(virial, (4, 0, 1, 2, 3)))


def solution(mesh):
    placed = (
        P(None, "gx", "gy", "gz", None),
        P("gx", "gy", "gz", None, None),
        P("gx", "gy", "gz", None),
        P(("gx", "gy", "gz")),
        P(("gx", "gy", "gz"), None),
        P(("gx", "gy", "gz")),
        P(),
        P(),
        P(),
        P(),
        P(),
        P(),
        P(),
        P(),
        P(),
    )
    return jax.shard_map(
        local,
        mesh=mesh,
        in_specs=placed,
        out_specs=(
            P("gx", "gy", "gz", None),
            P(None, "gx", "gy", "gz", None),
            P(None, "gx", "gy", "gz", None),
        ),
        check_vma=False,
    )
```

```python
import functools
import math

import jax
import jax.numpy as jnp
import numpy as np
from jax import lax
from jax.experimental import pallas as pl
from jax.experimental.pallas import tpu as pltpu
from jax.sharding import PartitionSpec as P

EXACT_DOT = lax.Precision.HIGHEST
CUTOFF = 5.0
CELL_SIDE = 4.6
ROOT_HALF = 0.7071067811865476
GROUP = 8
ORDERS = 16
SITES = 8
OWN_CELLS = 4
FRAME_CELLS = 48
F32 = jnp.float32
BF16 = jnp.bfloat16


def split(value):
    high = value.astype(BF16)
    low = (value - high.astype(F32)).astype(BF16)
    return high, low


def split3(value):
    high = value.astype(BF16)
    rest = value - high.astype(F32)
    middle = rest.astype(BF16)
    low = (rest - middle.astype(F32)).astype(BF16)
    return high, middle, low


def mm(a, b):
    return lax.dot_general(a, b, (((1,), (0,)), ((), ())), preferred_element_type=F32)


def mm_nt(a, b):
    return lax.dot_general(a, b, (((1,), (1,)), ((), ())), preferred_element_type=F32)


def stacked(high, low):
    top = jnp.concatenate([high, high], axis=1)
    bottom = jnp.concatenate([low, jnp.zeros_like(low)], axis=1)
    return jnp.concatenate([top, bottom], axis=0)


def folded(product):
    half = product.shape[0] // 2
    return product[:half] + product[half:]


def half_depth(weights, value):
    return folded(mm(weights, jnp.concatenate(split(value), axis=0)))


def full_depth(both, high, value_high, value_low):
    return folded(mm(both, value_high)) + mm(high, value_low)


def sin_cos_pi(turns):
    near = turns - 2.0 * jnp.round(turns * 0.5)
    quarter = jnp.round(near * 2.0)
    v = (near - 0.5 * quarter) * math.pi
    v2 = v * v
    s = v * (
        1.0
        + v2
        * (-1.0 / 6 + v2 * (1.0 / 120 + v2 * (-1.0 / 5040 + v2 * (1.0 / 362880 - v2 / 39916800))))
    )
    c = 1.0 + v2 * (
        -0.5
        + v2
        * (1.0 / 24 + v2 * (-1.0 / 720 + v2 * (1.0 / 40320 + v2 * (-1.0 / 3628800 + v2 / 479001600))))
    )
    odd = jnp.abs(quarter) == 1.0
    sine = jnp.where(odd, quarter * c, jnp.where(quarter == 0.0, s, -s))
    cosine = jnp.where(odd, -quarter * s, jnp.where(quarter == 0.0, c, -c))
    return sine, cosine


def lane_row(piece, offset):
    row = jnp.concatenate([piece, jnp.zeros((1, 128 - piece.shape[1]), piece.dtype)], axis=1)
    return pltpu.roll(row, offset, 1) if offset else row


def pack_kernel(
    kind,
    positions_hbm,
    features_hbm,
    species_hbm,
    centers_hbm,
    neighbours_hbm,
    scale_hbm,
    payload_ref,
    wide_ref,
    positions_ref,
    species_ref,
    centers_ref,
    neighbours_ref,
    scale_ref,
    sems,
):
    owned, nbr = neighbours_ref.shape
    per_row = 128 // nbr
    pairs_in = (
        (features_hbm, payload_ref.at[pl.ds(0, owned), :]),
        (neighbours_hbm, neighbours_ref),
        (centers_hbm, centers_ref),
        (positions_hbm, positions_ref),
        (species_hbm, species_ref),
        (scale_hbm, scale_ref),
    )
    copies = [
        pltpu.make_async_copy(source, target, sems.at[i])
        for i, (source, target) in enumerate(pairs_in)
    ]
    for copy in copies:
        copy.start()
    for copy in copies:
        copy.wait()
    payload_ref[owned : owned + 8] = jnp.zeros((8, 128), F32)
    for cell in range(OWN_CELLS):
        x, z = cell // 2, cell % 2
        species = species_ref[x, 0, z : z + 1, :]
        scale = jnp.zeros(species.shape, F32)
        for s in range(scale_ref.shape[0]):
            scale = jnp.where(species == s, scale_ref[s], scale)
        row = lane_row(scale, 3 * SITES)
        for c in range(3):
            row = row + lane_row(positions_ref[c, x, 0, z : z + 1, :], c * SITES)
        payload_ref[owned + cell : owned + cell + 1] = row

    chosen = lax.broadcasted_iota(jnp.int32, (owned, owned), 0) == centers_ref[...]
    chosen = jnp.where(chosen, 1.0, 0.0)
    occupied = jnp.sum(chosen, axis=1, keepdims=True) > 0.5
    chosen = chosen.astype(BF16)
    rows = neighbours_ref[...]
    upper = mm(chosen, (rows >> 4).astype(F32).astype(BF16))
    lower = mm(chosen, (rows & 15).astype(F32).astype(BF16))
    rows = (upper * 16.0 + lower).astype(jnp.int32)
    live = occupied & (rows < FRAME_CELLS * SITES)
    slot = lax.broadcasted_iota(jnp.int32, (owned, nbr), 0)
    cell = slot >> 3
    site = rows & 7
    place = rows >> 3
    near_z = (place & 3) + 1 - 2 * (cell & 1)
    column = place >> 2
    frame_x = (column * 11) >> 5
    frame_y = column - 3 * frame_x
    near_x = frame_x + 1 - 2 * (cell >> 1)
    side = jnp.where(frame_y == 1, 0, jnp.where(frame_y == 2, 1, kind - 1))
    block = (near_z >> 1) * 2 + 1 - (near_x >> 1)
    where = (block * kind + side) * owned + (near_x & 1) * 16 + (near_z & 1) * 8 + site
    code = jnp.where(live, 1 + where + (frame_y << 10), 0).astype(F32)
    wide_ref[...] = jnp.concatenate([code, jnp.zeros((owned, 128 - nbr), F32)], axis=1)
    codes = wide_ref[pl.ds(0, owned // per_row, stride=per_row), :]
    for j in range(1, per_row):
        more = wide_ref[pl.ds(j, owned // per_row, stride=per_row), :]
        codes = codes + pltpu.roll(more, j * nbr, 1)
    payload_ref[owned + 8 :] = codes


def fetch_kernel(species_hbm, centers_hbm, shift_hbm, *refs):
    *refs, shift_row_ref, species_ref, centers_ref, shift_ref, sems = refs
    count = len(refs) // 2
    pairs_in = [
        (species_hbm, species_ref),
        (centers_hbm, centers_ref),
        (shift_hbm, shift_ref),
        *zip(refs[:count], refs[count:]),
    ]
    copies = [
        pltpu.make_async_copy(source, target, sems.at[i])
        for i, (source, target) in enumerate(pairs_in)
    ]
    for copy in copies:
        copy.start()
    for copy in copies:
        copy.wait()
    owned = centers_ref.shape[1]
    shift_row = jnp.zeros((1, 128), F32)
    for cell in range(OWN_CELLS):
        species = species_ref[cell // 2, 0, cell % 2 : cell % 2 + 1, :]
        shift = jnp.zeros(species.shape, F32)
        for s in range(shift_ref.shape[0]):
            shift = jnp.where(species == s, shift_ref[s], shift)
        shift_row = shift_row + lane_row(shift, cell * SITES)
    chosen = lax.broadcasted_iota(jnp.int32, (owned, owned), 0) == centers_ref[...]
    occupied = jnp.sum(jnp.where(chosen, 1.0, 0.0), axis=1, keepdims=True) > 0.5
    column = jnp.where(occupied, jnp.ones((owned, 128), F32), 0.0)
    shift_row_ref[...] = shift_row[:, :owned] * jnp.transpose(column)[0:1]


def finish_kernel(mine_ref, shift_row_ref, *refs):
    *near_refs, energy_ref, forces_ref, virial_ref = refs
    owned = near_refs[0].shape[1]
    total = mine_ref[:, :owned]
    for near_ref in near_refs:
        total = total + near_ref[...]
    energy = total[12:13] + shift_row_ref[...]
    columns = jnp.transpose(jnp.concatenate([total, jnp.zeros((ORDERS, 128 - owned), F32)], axis=1))
    for cell in range(OWN_CELLS):
        x, z = cell // 2, cell % 2
        lanes = slice(cell * SITES, (cell + 1) * SITES)
        energy_ref[x, 0, z : z + 1, :] = energy[:, lanes]
        for c in range(3):
            forces_ref[c, x, 0, z : z + 1, :] = total[c : c + 1, lanes]
        virial_ref[x, 0, z] = columns[lanes, 3:12]


def force_kernel(kind, nbr, here_ref, last_x_ref, *refs):
    near_side_refs = refs[: 2 * kind - 2]
    (
        next_z_ref,
        center_weight_ref,
        near_weight_ref,
        basis_weight_ref,
        path_weight_ref,
        value_weight_ref,
        latent_weight_ref,
        out_weight_ref,
        keep_ref,
        send_ref,
    ) = refs[2 * kind - 2 :]
    height, width = here_ref.shape
    owned = OWN_CELLS * SITES
    short = owned + 8
    center_sides = 2 if kind == 2 else 1
    kept_sides = 1 if kind == 2 else kind
    own_pairs = owned * nbr
    pairs = center_sides * own_pairs
    centers = center_sides * owned
    radial = basis_weight_ref.shape[0]
    span = GROUP * nbr
    groups = centers // GROUP
    wide = GROUP * ORDERS
    sites = SITES
    root_count = math.sqrt(nbr)
    root_three = math.sqrt(3.0)
    root_fifteen = math.sqrt(15.0)
    root_five = math.sqrt(5.0)
    far = next_z_ref[...]
    mains = [here_ref[...], last_x_ref[...], far[:height], far[height : 2 * height]]
    near_sides = [ref[...] for ref in near_side_refs]
    far_sides = far[2 * height :]
    tall = far_sides.shape[0] // (2 * kind - 2)
    far_sides = [far_sides[i * tall : (i + 1) * tall] for i in range(2 * kind - 2)]
    blocks_in = [
        [mains[0], *near_sides[0::2]],
        [mains[1], *near_sides[1::2]],
        [mains[2], *far_sides[0::2]],
        [mains[3], *far_sides[1::2]],
    ]
    feats = jnp.concatenate([side[:owned] for block in blocks_in for side in block], axis=0)
    known = feats.shape[0]
    center_feats = []
    center_coords = []
    coords = []
    scales = []
    codes = []
    cell_row = lax.broadcasted_iota(jnp.int32, (kind * OWN_CELLS, 128), 0) % OWN_CELLS
    tile_lane = lax.broadcasted_iota(jnp.int32, (kind * OWN_CELLS, 128), 1)
    for g, block in enumerate(blocks_in):
        behind_x, ahead_z = g % 2, g // 2
        rows = jnp.concatenate([side[owned : owned + OWN_CELLS] for side in block], axis=0)
        corner_x = (cell_row // 2 + 2 - 2 * behind_x).astype(F32) * CELL_SIDE
        corner_z = (cell_row % 2 + 2 * ahead_z).astype(F32) * CELL_SIDE
        corner = jnp.where(
            tile_lane < sites, corner_x, jnp.where(tile_lane < 2 * sites, 0.0, corner_z)
        )
        coords.append(rows + corner)
    for c in range(center_sides):
        for g, block in enumerate(blocks_in):
            cell = g % 2 * 2 + 1 - g // 2
            row = c * OWN_CELLS + cell
            center_feats.append(block[c][cell * sites : (cell + 1) * sites])
            scales.append(block[c][owned + cell : owned + cell + 1])
            center_coords.append(coords[g][row : row + 1])
            start = short + cell * span // 128
            codes.extend(block[c][start + r : start + r + 1] for r in range(span // 128))
    center_feats = jnp.concatenate(center_feats, axis=0)
    coords = jnp.concatenate(coords, axis=0)
    code = jnp.concatenate(codes, axis=1).astype(jnp.int32)
    live = code > 0
    code = jnp.maximum(code - 1, 0)
    side_y = ((code >> 10) - 1).astype(F32)
    near_row = code & 1023
    if center_sides == 2:
        pair_lane = lax.broadcasted_iota(jnp.int32, (1, pairs), 1)
        near_row = jnp.where(pair_lane < own_pairs, near_row, near_row ^ owned)
    near_row = jnp.where(live, near_row, known)

    def place_rows(cell_rows):
        count = cell_rows.shape[0] * sites
        spread = jnp.broadcast_to(cell_rows[:, None, :], (cell_rows.shape[0], sites, 128))
        spread = spread.reshape(count, 128)
        lane = lax.broadcasted_iota(jnp.int32, (count, 128), 1)
        row = lax.broadcasted_iota(jnp.int32, (count, 128), 0)
        keep = (lane % sites == row % sites) & (lane < 3 * sites)
        spread = jnp.transpose(jnp.where(keep, spread, 0.0))
        return jnp.concatenate(split3(spread[: 3 * sites]), axis=0)

    place_parts = place_rows(coords)
    center_parts = place_rows(jnp.concatenate(center_coords, axis=0))

    value_rows = stacked(*split(jnp.transpose(value_weight_ref[...])))
    latent_high_t, latent_low_t = split(jnp.transpose(latent_weight_ref[...]))
    latent_both_t = jnp.concatenate([latent_high_t, latent_low_t], axis=0)
    latent_rows = stacked(*split(latent_weight_ref[...] * out_weight_ref[...]))
    value_high, value_low = split(value_weight_ref[...])
    value_both = jnp.concatenate([value_high, value_low], axis=0)
    basis_t = jnp.transpose(basis_weight_ref[...])
    basis_high_t, basis_low_t = split(basis_t)
    basis_rows = stacked(*split(basis_weight_ref[...]))

    def project(weight, rows):
        weight = stacked(*split(jnp.transpose(weight)))
        return folded(mm_nt(weight, jnp.concatenate(split(rows), axis=1)))

    near_t = project(near_weight_ref[...], feats)
    own_t = project(center_weight_ref[...], center_feats)
    near_high, near_low = split(near_t)
    own_high, own_low = split(own_t)
    lookup = jnp.concatenate(
        [
            jnp.concatenate([near_high, own_high, basis_high_t, basis_high_t], axis=1),
            jnp.concatenate([near_low, own_low, basis_low_t, jnp.zeros_like(basis_low_t)], axis=1),
        ],
        axis=0,
    )
    scale_rows = jnp.concatenate(scales, axis=0)
    scale_parts = jnp.concatenate(
        [*split3(scale_rows), jnp.zeros((-3 * groups % 16, 128), BF16)], axis=0
    )

    level = lax.broadcasted_iota(jnp.int32, (ORDERS, width), 0)
    path_rows = jnp.where(
        level == 0,
        path_weight_ref[0:1, :],
        jnp.where(
            level < 4,
            path_weight_ref[1:2, :],
            jnp.where(level < 9, path_weight_ref[2:3, :], 0.0),
        ),
    )
    paths_t = jnp.transpose(jnp.concatenate([path_rows] * GROUP, axis=0)) * (1.0 / root_count)
    out_column = jnp.transpose(jnp.broadcast_to(out_weight_ref[...], (width, width)))
    out_column = jnp.concatenate([out_column] * (pairs // width), axis=1)

    site_ids = lax.broadcasted_iota(jnp.int32, (known, pairs), 0)
    slot_ids = lax.broadcasted_iota(jnp.int32, (centers, pairs), 0)
    slot_row = lax.broadcasted_iota(jnp.int32, (1, pairs), 1) // nbr
    block_row = lax.broadcasted_iota(jnp.int32, (wide, span), 0) // ORDERS
    block_lane = lax.broadcasted_iota(jnp.int32, (wide, span), 1) // nbr
    block_mask = (block_row == block_lane).astype(F32)
    block_half = block_mask.astype(BF16)
    order = lax.broadcasted_iota(jnp.int32, (radial, pairs), 0).astype(F32) + 1.0
    lanes = [slice(g * span, (g + 1) * span) for g in range(groups)]

    pick = jnp.where(site_ids == near_row, 1.0, 0.0)
    pick_half = pick.astype(BF16)
    slot_half = jnp.where(slot_ids == slot_row, 1.0, 0.0).astype(BF16)

    moved = mm(place_parts, pick_half) - mm(center_parts, slot_half)
    moved = moved[: 3 * sites] + moved[3 * sites : 6 * sites] + moved[6 * sites :]
    dx = jnp.where(live, jnp.sum(moved[:sites], axis=0, keepdims=True), 6.0)
    dy = jnp.sum(moved[sites : 2 * sites], axis=0, keepdims=True) + CELL_SIDE * side_y
    dy = jnp.where(live, dy, 0.0)
    dz = jnp.where(live, jnp.sum(moved[2 * sites :], axis=0, keepdims=True), 0.0)
    length = jnp.sqrt(dx * dx + dy * dy + dz * dz)
    inverse = 1.0 / length
    ratio = length * (1.0 / CUTOFF)
    inside = live & (ratio < 1.0)
    r2 = ratio * ratio
    r5 = r2 * r2 * ratio
    r6 = r5 * ratio
    weight = jnp.where(inside, 1.0 - r6 * (28.0 - 48.0 * ratio + 21.0 * r2), 0.0)
    slope = jnp.where(inside, -168.0 * r5 * (1.0 - 2.0 * ratio + r2), 0.0)
    sine, cosine = sin_cos_pi(order * ratio)
    basis = (math.sqrt(2.0 / CUTOFF) * inverse) * sine
    basis_slope = (math.sqrt(2.0 / CUTOFF) * inverse) * (
        (math.pi / CUTOFF) * order * cosine - sine * inverse
    )
    ex = dx * inverse
    ey = dy * inverse
    ez = dz * inverse
    angular = jnp.concatenate(
        [
            jnp.ones_like(ex),
            root_three * ex,
            root_three * ey,
            root_three * ez,
            root_fifteen * ex * ey,
            root_fifteen * ey * ez,
            0.5 * root_five * (3.0 * ez * ez - 1.0),
            root_fifteen * ex * ez,
            0.5 * root_fifteen * (ex * ex - ey * ey),
            jnp.zeros((ORDERS - 9, pairs), F32),
        ],
        axis=0,
    )
    angular_high, angular_low = split(angular)
    blocks = [
        jnp.concatenate(
            [
                jnp.concatenate([angular_high[:, cut]] * GROUP, axis=0) * block_half,
                jnp.concatenate([angular_low[:, cut]] * GROUP, axis=0) * block_half,
            ],
            axis=0,
        )
        for cut in lanes
    ]
    lane_ids = lax.broadcasted_iota(jnp.int32, (128, span), 0)
    lane_slot = lax.broadcasted_iota(jnp.int32, (128, span), 1) // nbr + 3 * sites
    scale = mm(scale_parts, jnp.where(lane_ids == lane_slot, 1.0, 0.0).astype(BF16))
    scale = scale[:groups] + scale[groups : 2 * groups] + scale[2 * groups : 3 * groups]
    scale = jnp.concatenate([scale[g : g + 1] for g in range(groups)], axis=1)
    scale = scale * (1.0 / root_count)
    pull = ROOT_HALF * scale

    basis_high, basis_low = split(basis)
    before = folded(
        mm(lookup, jnp.concatenate([pick_half, slot_half, basis_high, basis_low], axis=0))
    )
    gate = 0.5 * jnp.tanh(0.5 * before) + 0.5
    active = before * gate
    latent = weight * active
    latent_high, latent_low = split(latent)
    mixed = folded(mm(value_rows, jnp.concatenate([latent_high, latent_low], axis=0)))
    values = mixed[:width]
    env_high, env_low = split(mixed[width:])

    def over_pairs(high, low):
        sums = []
        for cut, block in zip(lanes, blocks):
            quad = mm_nt(jnp.concatenate([high[:, cut], low[:, cut]], axis=0), block)
            sums.append((quad[:width, :wide] + quad[:width, wide:] + quad[width:, :wide]) * paths_t)
        return sums

    def over_orders(tables):
        parts = [folded(mm(stacked(*split(t)), block)) for t, block in zip(tables, blocks)]
        return jnp.concatenate(parts, axis=1)

    weighted = over_pairs(env_high, env_low)
    inner = over_orders(weighted)
    scalars = values * inner
    scalars_high, scalars_low = split(scalars)
    z = full_depth(
        latent_both_t,
        latent_high_t,
        jnp.concatenate([latent_high, scalars_high], axis=0),
        jnp.concatenate([latent_low, scalars_low], axis=0),
    )
    z_gate = 0.5 * jnp.tanh(0.5 * z) + 0.5
    update = z * z_gate
    update_sum = jnp.sum(update * out_column, axis=0, keepdims=True)
    active_sum = jnp.sum(
        active[:, :own_pairs] * out_column[:, :own_pairs], axis=0, keepdims=True
    )
    pair_energy = (active_sum + update_sum[:, :own_pairs]) * (pull * weight)[:, :own_pairs]
    d_z = (pull * weight) * (z_gate + update * (1.0 - z_gate))
    spread_back = half_depth(latent_rows, d_z)
    d_scalars = spread_back[width:]
    d_values = d_scalars * inner
    dinner_high, dinner_low = split(d_scalars * values)
    d_embed = over_pairs(dinner_high, dinner_low)
    d_env = over_orders(d_embed)

    d_angular = []
    for g, cut in enumerate(lanes):
        sides = jnp.transpose(jnp.concatenate([weighted[g], d_embed[g]], axis=0))
        sides_high, sides_low = split(sides)
        d_block = full_depth(
            jnp.concatenate([sides_high, sides_low], axis=0),
            sides_high,
            jnp.concatenate([dinner_high[:, cut], env_high[:, cut]], axis=0),
            jnp.concatenate([dinner_low[:, cut], env_low[:, cut]], axis=0),
        )
        d_block = d_block * block_mask
        total = d_block[:ORDERS]
        for k in range(1, GROUP):
            total = total + d_block[k * ORDERS : (k + 1) * ORDERS]
        d_angular.append(total)
    d_angular = jnp.concatenate(d_angular, axis=1)

    mixed_high, mixed_low = split(jnp.concatenate([d_values, d_env], axis=0))
    d_latent = (
        full_depth(value_both, value_high, mixed_high, mixed_low)
        + spread_back[:width]
        + pull * out_column
    )
    d_weight = jnp.sum(d_latent * active, axis=0, keepdims=True) + pull * update_sum
    d_before = d_latent * weight * (gate + active * (1.0 - gate))
    d_basis = half_depth(basis_rows, d_before)

    d_length = jnp.sum(d_basis * basis_slope, axis=0, keepdims=True) + d_weight * slope * (
        1.0 / CUTOFF
    )
    a1, a2, a3, a4, a5, a6, a7, a8 = [d_angular[m : m + 1] for m in range(1, 9)]
    ux = root_three * a1 + root_fifteen * (ey * a4 + ez * a7 + ex * a8)
    uy = root_three * a2 + root_fifteen * (ex * a4 + ez * a5 - ey * a8)
    uz = root_three * a3 + root_fifteen * (ey * a5 + ex * a7) + 3.0 * root_five * ez * a6
    along = ex * ux + ey * uy + ez * uz
    radial_part = d_length - along * inverse
    gx = ux * inverse + ex * radial_part
    gy = uy * inverse + ey * radial_part
    gz = uz * inverse + ez * radial_part
    hx = -0.5 * dx
    hy = -0.5 * dy
    hz = -0.5 * dz
    virial = [hx * gx, hx * gy, hx * gz, hy * gx, hy * gy, hy * gz, hz * gx, hz * gy, hz * gz]
    rest = [jnp.zeros((ORDERS - 13, pairs), F32)]
    near_terms = jnp.concatenate(
        [-gx, -gy, -gz, *virial, jnp.zeros_like(gx), *rest], axis=0
    )
    center_rows = [gx, gy, gz, *virial]
    center_rows = [r[:, :own_pairs] for r in center_rows] + [pair_energy]
    center_rows.append(jnp.zeros((ORDERS - 13, own_pairs), F32))
    center_terms = jnp.concatenate(center_rows, axis=0)
    reach = pick_half
    if kept_sides < kind:
        step = kind * owned
        reach = jnp.concatenate([pick_half[i : i + owned] for i in range(0, known, step)], axis=0)
    near_sums = mm_nt(jnp.concatenate(split(near_terms), axis=0), reach)
    center_sums = mm_nt(
        jnp.concatenate(split(center_terms), axis=0), slot_half[:owned, :own_pairs]
    )
    center_sums = jnp.concatenate(
        [folded(center_sums), jnp.zeros((ORDERS, 128 - owned), F32)], axis=1
    )
    totals = folded(near_sums)
    lane = lax.broadcasted_iota(jnp.int32, (ORDERS, 128), 1)
    known = totals.shape[1]
    tiles = [totals[:, 128 * i : 128 * (i + 1)] for i in range(known // 128)]
    for g in range(owned // GROUP):
        cell = g % 2 * 2 + 1 - g // 2
        target = g * kept_sides * owned + cell * sites
        turn = (target - g * GROUP) % 128
        piece = pltpu.roll(center_sums, turn, 1) if turn else center_sums
        begin = target % 128
        piece = jnp.where((lane >= begin) & (lane < begin + GROUP), piece, 0.0)
        tiles[target // 128] = tiles[target // 128] + piece
    totals = jnp.concatenate(tiles, axis=1)
    keep_ref[...] = totals[:, : known // 2]
    send_ref[...] = totals[:, known // 2 :]


def in_hbm(*arrays):
    return [pltpu.with_memory_space_constraint(array, pltpu.HBM) for array in arrays]


def joined(parts):
    total = sum(part.shape[0] for part in parts)
    start = 0
    pads = []
    for part in parts:
        end = start + part.shape[0]
        pads.append(jnp.pad(part, ((start, total - end), (0, 0))))
        start = end
    return functools.reduce(jnp.add, pads)


def local(
    positions,
    features,
    species,
    centers,
    neighbours,
    counts,
    species_scale,
    species_shift,
    center_weight,
    near_weight,
    basis_weight,
    path_weight,
    value_weight,
    latent_weight,
    out_weight,
):
    cells_x, cells_y, cells_z, sites, width = features.shape
    cell_count = cells_x * cells_y * cells_z
    owned = cell_count * sites
    assert (cells_x, cells_y, cells_z, sites) == (2, 1, 2, SITES)
    pairs = neighbours.size
    nbr = pairs // owned
    kind = min(3, lax.axis_size("gy"))

    def moved(array, steps):
        names = tuple(steps)
        sizes = [lax.axis_size(name) for name in names]
        route = []
        for at in np.ndindex(*sizes):
            to = [(p + steps[name]) % size for p, name, size in zip(at, names, sizes)]
            route.append(
                (int(np.ravel_multi_index(at, sizes)), int(np.ravel_multi_index(to, sizes)))
            )
        return lax.ppermute(array, names, route)

    vmem = pl.BlockSpec(memory_space=pltpu.VMEM)
    hbm = pl.BlockSpec(memory_space=pltpu.HBM)
    listed = centers.reshape(1, owned)
    here = pl.pallas_call(
        functools.partial(pack_kernel, kind),
        out_shape=jax.ShapeDtypeStruct((owned + 8 + pairs // 128, width), F32),
        in_specs=[hbm] * 6,
        out_specs=vmem,
        scratch_shapes=[
            pltpu.VMEM((owned, 128), F32),
            pltpu.VMEM(positions.shape, F32),
            pltpu.VMEM(species.shape, jnp.int32),
            pltpu.VMEM(listed.shape, jnp.int32),
            pltpu.VMEM(neighbours.shape, jnp.int32),
            pltpu.SMEM(species_scale.shape, F32),
            pltpu.SemaphoreType.DMA((6,)),
        ],
        compiler_params=pltpu.CompilerParams(vmem_limit_bytes=8 * 1024 * 1024),
        name="pack_payload",
    )(
        *in_hbm(
            positions,
            features.reshape(owned, width),
            species,
            listed,
            neighbours,
            species_scale,
        )
    )
    weights = (
        center_weight,
        near_weight,
        basis_weight,
        path_weight,
        value_weight,
        latent_weight,
        out_weight.reshape(1, width),
    )
    *weights, shift_row = pl.pallas_call(
        fetch_kernel,
        out_shape=(
            *(jax.ShapeDtypeStruct(w.shape, F32) for w in weights),
            jax.ShapeDtypeStruct((1, owned), F32),
        ),
        in_specs=[hbm] * (3 + len(weights)),
        out_specs=(vmem,) * (1 + len(weights)),
        scratch_shapes=[
            pltpu.VMEM(species.shape, jnp.int32),
            pltpu.VMEM(listed.shape, jnp.int32),
            pltpu.SMEM(species_shift.shape, F32),
            pltpu.SemaphoreType.DMA((3 + len(weights),)),
        ],
        compiler_params=pltpu.CompilerParams(vmem_limit_bytes=8 * 1024 * 1024),
        name="fetch_weights",
    )(*in_hbm(species, listed, species_shift, *weights))
    short = here if kind == 2 else here[: owned + 8]
    last_x = moved(here, {"gx": 1})
    sides = []
    for step in (-1, 1)[: kind - 1]:
        sides.append(moved(short, {"gx": 1, "gy": step}))
        sides.insert(-1, moved(short, {"gy": step}))
    next_z = moved(joined([here, last_x, *sides]), {"gz": -1})
    kept = 1 if kind == 2 else kind
    half = 2 * kept * owned
    keep, send = pl.pallas_call(
        functools.partial(force_kernel, kind, nbr),
        out_shape=(
            jax.ShapeDtypeStruct((ORDERS, half), F32),
            jax.ShapeDtypeStruct((ORDERS, half), F32),
        ),
        in_specs=[vmem] * (8 + 2 * kind),
        out_specs=(vmem, vmem),
        compiler_params=pltpu.CompilerParams(vmem_limit_bytes=44 * 1024 * 1024),
        name="pair_forces",
    )(
        here,
        last_x,
        *sides,
        next_z,
        *weights,
    )
    totals = keep + moved(send, {"gz": 1})

    def part(index):
        return totals[:, index * owned : (index + 1) * owned]

    back = [moved(part(kept), {"gx": -1})]
    for i, step in enumerate((1, -1)[: kept - 1]):
        back.append(moved(part(kept + 1 + i), {"gx": -1, "gy": step}))
        back.append(moved(part(1 + i), {"gy": step}))
    site_energy, forces, virial = pl.pallas_call(
        finish_kernel,
        out_shape=(
            jax.ShapeDtypeStruct(species.shape, F32),
            jax.ShapeDtypeStruct(positions.shape, F32),
            jax.ShapeDtypeStruct((*species.shape, 9), F32),
        ),
        in_specs=[vmem] * (2 + len(back)),
        out_specs=(vmem, vmem, vmem),
        compiler_params=pltpu.CompilerParams(vmem_limit_bytes=8 * 1024 * 1024),
        name="write_outputs",
    )(totals, shift_row, *back)
    return (site_energy, forces, jnp.transpose(virial, (4, 0, 1, 2, 3)))


def solution(mesh):
    placed = (
        P(None, "gx", "gy", "gz", None),
        P("gx", "gy", "gz", None, None),
        P("gx", "gy", "gz", None),
        P(("gx", "gy", "gz")),
        P(("gx", "gy", "gz"), None),
        P(("gx", "gy", "gz")),
        P(),
        P(),
        P(),
        P(),
        P(),
        P(),
        P(),
        P(),
        P(),
    )
    return jax.shard_map(
        local,
        mesh=mesh,
        in_specs=placed,
        out_specs=(
            P("gx", "gy", "gz", None),
            P(None, "gx", "gy", "gz", None),
            P(None, "gx", "gy", "gz", None),
        ),
        check_vma=False,
    )
```

```python
import functools
import math

import jax
import jax.numpy as jnp
import numpy as np
from jax import lax
from jax.experimental import pallas as pl
from jax.experimental.pallas import tpu as pltpu
from jax.sharding import PartitionSpec as P

EXACT_DOT = lax.Precision.HIGHEST
CUTOFF = 5.0
CELL_SIDE = 4.6
ROOT_HALF = 0.7071067811865476
GROUP = 8
ORDERS = 16
SITES = 8
OWN_CELLS = 4
FRAME_CELLS = 48
F32 = jnp.float32
BF16 = jnp.bfloat16


def split(value):
    high = value.astype(BF16)
    low = (value - high.astype(F32)).astype(BF16)
    return high, low


def split3(value):
    high = value.astype(BF16)
    rest = value - high.astype(F32)
    middle = rest.astype(BF16)
    low = (rest - middle.astype(F32)).astype(BF16)
    return high, middle, low


def mm(a, b):
    return lax.dot_general(a, b, (((1,), (0,)), ((), ())), preferred_element_type=F32)


def mm_nt(a, b):
    return lax.dot_general(a, b, (((1,), (1,)), ((), ())), preferred_element_type=F32)


def stacked(high, low):
    top = jnp.concatenate([high, high], axis=1)
    bottom = jnp.concatenate([low, jnp.zeros_like(low)], axis=1)
    return jnp.concatenate([top, bottom], axis=0)


def folded(product):
    half = product.shape[0] // 2
    return product[:half] + product[half:]


def half_depth(weights, value):
    return folded(mm(weights, jnp.concatenate(split(value), axis=0)))


def full_depth(both, high, value_high, value_low):
    return folded(mm(both, value_high)) + mm(high, value_low)


def sin_cos_pi(turns):
    near = turns - 2.0 * jnp.round(turns * 0.5)
    quarter = jnp.round(near * 2.0)
    v = (near - 0.5 * quarter) * math.pi
    v2 = v * v
    s = v * (
        1.0
        + v2
        * (-1.0 / 6 + v2 * (1.0 / 120 + v2 * (-1.0 / 5040 + v2 * (1.0 / 362880 - v2 / 39916800))))
    )
    c = 1.0 + v2 * (
        -0.5
        + v2
        * (1.0 / 24 + v2 * (-1.0 / 720 + v2 * (1.0 / 40320 + v2 * (-1.0 / 3628800 + v2 / 479001600))))
    )
    odd = jnp.abs(quarter) == 1.0
    sine = jnp.where(odd, quarter * c, jnp.where(quarter == 0.0, s, -s))
    cosine = jnp.where(odd, -quarter * s, jnp.where(quarter == 0.0, c, -c))
    return sine, cosine


def lane_row(piece, offset):
    row = jnp.concatenate([piece, jnp.zeros((1, 128 - piece.shape[1]), piece.dtype)], axis=1)
    return pltpu.roll(row, offset, 1) if offset else row


def pack_kernel(
    kind,
    positions_hbm,
    features_hbm,
    species_hbm,
    centers_hbm,
    neighbours_hbm,
    scale_hbm,
    low_ref,
    high_ref,
    wide_ref,
    positions_ref,
    species_ref,
    centers_ref,
    neighbours_ref,
    scale_ref,
    sems,
):
    owned, nbr = neighbours_ref.shape
    per_row = 128 // nbr
    pairs_in = (
        (features_hbm, low_ref.at[pl.ds(0, owned), :]),
        (neighbours_hbm, neighbours_ref),
        (centers_hbm, centers_ref),
        (positions_hbm, positions_ref),
        (species_hbm, species_ref),
        (scale_hbm, scale_ref),
    )
    copies = [
        pltpu.make_async_copy(source, target, sems.at[i])
        for i, (source, target) in enumerate(pairs_in)
    ]
    for copy in copies:
        copy.start()
    for copy in copies:
        copy.wait()
    for cell in range(OWN_CELLS):
        x, z = cell // 2, cell % 2
        species = species_ref[x, 0, z : z + 1, :]
        scale = jnp.zeros(species.shape, F32)
        for s in range(scale_ref.shape[0]):
            scale = jnp.where(species == s, scale_ref[s], scale)
        row = lane_row(scale, 3 * SITES)
        for c in range(3):
            row = row + lane_row(positions_ref[c, x, 0, z : z + 1, :], c * SITES)
        low_ref[owned + cell : owned + cell + 1] = row

    chosen = lax.broadcasted_iota(jnp.int32, (owned, owned), 0) == centers_ref[...]
    chosen = jnp.where(chosen, 1.0, 0.0)
    occupied = jnp.sum(chosen, axis=1, keepdims=True) > 0.5
    chosen = chosen.astype(BF16)
    rows = neighbours_ref[...]
    upper = mm(chosen, (rows >> 4).astype(F32).astype(BF16))
    lower = mm(chosen, (rows & 15).astype(F32).astype(BF16))
    rows = (upper * 16.0 + lower).astype(jnp.int32)
    live = occupied & (rows < FRAME_CELLS * SITES)
    slot = lax.broadcasted_iota(jnp.int32, (owned, nbr), 0)
    cell = slot >> 3
    site = rows & 7
    place = rows >> 3
    near_z = (place & 3) + 1 - 2 * (cell & 1)
    column = place >> 2
    frame_x = (column * 11) >> 5
    frame_y = column - 3 * frame_x
    near_x = frame_x + 1 - 2 * (cell >> 1)
    side = jnp.where(frame_y == 1, 0, jnp.where(frame_y == 2, 1, kind - 1))
    block = (near_z >> 1) * 2 + 1 - (near_x >> 1)
    where = (block * kind + side) * owned + (near_x & 1) * 16 + (near_z & 1) * 8 + site
    code = jnp.where(live, 1 + where + (frame_y << 10), 0).astype(F32)
    wide_ref[...] = jnp.concatenate([code, jnp.zeros((owned, 128 - nbr), F32)], axis=1)
    codes = wide_ref[pl.ds(0, owned // per_row, stride=per_row), :]
    for j in range(1, per_row):
        more = wide_ref[pl.ds(j, owned // per_row, stride=per_row), :]
        codes = codes + pltpu.roll(more, j * nbr, 1)
    tile = owned + OWN_CELLS
    low_ref[tile:] = codes[: codes.shape[0] // 2]
    high_ref[:tile] = low_ref[:tile]
    high_ref[tile:] = codes[codes.shape[0] // 2 :]


def fetch_kernel(species_hbm, centers_hbm, shift_hbm, *refs):
    *refs, shift_row_ref, species_ref, centers_ref, shift_ref, sems = refs
    count = len(refs) // 2
    pairs_in = [
        (species_hbm, species_ref),
        (centers_hbm, centers_ref),
        (shift_hbm, shift_ref),
        *zip(refs[:count], refs[count:]),
    ]
    copies = [
        pltpu.make_async_copy(source, target, sems.at[i])
        for i, (source, target) in enumerate(pairs_in)
    ]
    for copy in copies:
        copy.start()
    for copy in copies:
        copy.wait()
    owned = centers_ref.shape[1]
    shift_row = jnp.zeros((1, 128), F32)
    for cell in range(OWN_CELLS):
        species = species_ref[cell // 2, 0, cell % 2 : cell % 2 + 1, :]
        shift = jnp.zeros(species.shape, F32)
        for s in range(shift_ref.shape[0]):
            shift = jnp.where(species == s, shift_ref[s], shift)
        shift_row = shift_row + lane_row(shift, cell * SITES)
    chosen = lax.broadcasted_iota(jnp.int32, (owned, owned), 0) == centers_ref[...]
    occupied = jnp.sum(jnp.where(chosen, 1.0, 0.0), axis=1, keepdims=True) > 0.5
    column = jnp.where(occupied, jnp.ones((owned, 128), F32), 0.0)
    shift_row_ref[...] = shift_row[:, :owned] * jnp.transpose(column)[0:1]


def finish_kernel(mine_ref, shift_row_ref, *refs):
    *near_refs, energy_ref, forces_ref, virial_ref = refs
    owned = near_refs[0].shape[1]
    total = mine_ref[:, :owned]
    for near_ref in near_refs:
        total = total + near_ref[...]
    energy = total[12:13] + shift_row_ref[...]
    columns = jnp.transpose(jnp.concatenate([total, jnp.zeros((ORDERS, 128 - owned), F32)], axis=1))
    for cell in range(OWN_CELLS):
        x, z = cell // 2, cell % 2
        lanes = slice(cell * SITES, (cell + 1) * SITES)
        energy_ref[x, 0, z : z + 1, :] = energy[:, lanes]
        for c in range(3):
            forces_ref[c, x, 0, z : z + 1, :] = total[c : c + 1, lanes]
        virial_ref[x, 0, z] = columns[lanes, 3:12]


def force_kernel(kind, nbr, here_ref, last_x_ref, *refs):
    near_side_refs = refs[: 2 * kind - 2]
    (
        next_z_ref,
        center_weight_ref,
        near_weight_ref,
        basis_weight_ref,
        path_weight_ref,
        value_weight_ref,
        latent_weight_ref,
        out_weight_ref,
        keep_ref,
        send_ref,
    ) = refs[2 * kind - 2 :]
    height, width = here_ref.shape
    owned = OWN_CELLS * SITES
    center_sides = 2 if kind == 2 else 1
    kept_sides = 1 if kind == 2 else kind
    own_pairs = owned * nbr
    pairs = center_sides * own_pairs
    centers = center_sides * owned
    radial = basis_weight_ref.shape[0]
    span = GROUP * nbr
    groups = centers // GROUP
    wide = GROUP * ORDERS
    sites = SITES
    root_count = math.sqrt(nbr)
    root_three = math.sqrt(3.0)
    root_fifteen = math.sqrt(15.0)
    root_five = math.sqrt(5.0)
    far = next_z_ref[...]
    mains = [here_ref[...], last_x_ref[...], far[:height], far[height : 2 * height]]
    near_sides = [ref[...] for ref in near_side_refs]
    far_sides = far[2 * height :]
    far_sides = [far_sides[i * height : (i + 1) * height] for i in range(2 * kind - 2)]
    blocks_in = [
        [mains[0], *near_sides[0::2]],
        [mains[1], *near_sides[1::2]],
        [mains[2], *far_sides[0::2]],
        [mains[3], *far_sides[1::2]],
    ]
    feats = jnp.concatenate([side[:owned] for block in blocks_in for side in block], axis=0)
    known = feats.shape[0]
    center_feats = []
    center_coords = []
    coords = []
    scales = []
    codes = []
    cell_row = lax.broadcasted_iota(jnp.int32, (kind * OWN_CELLS, 128), 0) % OWN_CELLS
    tile_lane = lax.broadcasted_iota(jnp.int32, (kind * OWN_CELLS, 128), 1)
    for g, block in enumerate(blocks_in):
        behind_x, ahead_z = g % 2, g // 2
        rows = jnp.concatenate([side[owned : owned + OWN_CELLS] for side in block], axis=0)
        corner_x = (cell_row // 2 + 2 - 2 * behind_x).astype(F32) * CELL_SIDE
        corner_z = (cell_row % 2 + 2 * ahead_z).astype(F32) * CELL_SIDE
        corner = jnp.where(
            tile_lane < sites, corner_x, jnp.where(tile_lane < 2 * sites, 0.0, corner_z)
        )
        coords.append(rows + corner)
    for c in range(center_sides):
        for g, block in enumerate(blocks_in):
            cell = g % 2 * 2 + 1 - g // 2
            row = c * OWN_CELLS + cell
            center_feats.append(block[c][cell * sites : (cell + 1) * sites])
            scales.append(block[c][owned + cell : owned + cell + 1])
            center_coords.append(coords[g][row : row + 1])
            start = owned + OWN_CELLS + (1 - g // 2) * span // 128
            codes.extend(block[c][start + r : start + r + 1] for r in range(span // 128))
    center_feats = jnp.concatenate(center_feats, axis=0)
    coords = jnp.concatenate(coords, axis=0)
    code = jnp.concatenate(codes, axis=1).astype(jnp.int32)
    live = code > 0
    code = jnp.maximum(code - 1, 0)
    side_y = ((code >> 10) - 1).astype(F32)
    near_row = code & 1023
    if center_sides == 2:
        pair_lane = lax.broadcasted_iota(jnp.int32, (1, pairs), 1)
        near_row = jnp.where(pair_lane < own_pairs, near_row, near_row ^ owned)
    near_row = jnp.where(live, near_row, known)

    def place_rows(cell_rows):
        count = cell_rows.shape[0] * sites
        spread = jnp.broadcast_to(cell_rows[:, None, :], (cell_rows.shape[0], sites, 128))
        spread = spread.reshape(count, 128)
        lane = lax.broadcasted_iota(jnp.int32, (count, 128), 1)
        row = lax.broadcasted_iota(jnp.int32, (count, 128), 0)
        keep = (lane % sites == row % sites) & (lane < 3 * sites)
        spread = jnp.transpose(jnp.where(keep, spread, 0.0))
        return jnp.concatenate(split3(spread[: 3 * sites]), axis=0)

    place_parts = place_rows(coords)
    center_parts = place_rows(jnp.concatenate(center_coords, axis=0))

    value_rows = stacked(*split(jnp.transpose(value_weight_ref[...])))
    latent_high_t, latent_low_t = split(0.5 * jnp.transpose(latent_weight_ref[...]))
    latent_both_t = jnp.concatenate([latent_high_t, latent_low_t], axis=0)
    latent_rows = stacked(*split(latent_weight_ref[...] * out_weight_ref[...]))
    value_high, value_low = split(value_weight_ref[...])
    value_both = jnp.concatenate([value_high, value_low], axis=0)
    basis_t = jnp.transpose(basis_weight_ref[...])
    basis_high_t, basis_low_t = split(0.5 * basis_t)
    basis_rows = stacked(*split(basis_weight_ref[...]))

    def project(weight, rows):
        weight = stacked(*split(jnp.transpose(weight)))
        return folded(mm_nt(weight, jnp.concatenate(split(rows), axis=1)))

    near_t = project(near_weight_ref[...], feats)
    own_t = project(center_weight_ref[...], center_feats)
    near_high, near_low = split(0.5 * near_t)
    own_high, own_low = split(0.5 * own_t)
    lookup = jnp.concatenate(
        [
            jnp.concatenate([near_high, own_high, basis_high_t, basis_high_t], axis=1),
            jnp.concatenate([near_low, own_low, basis_low_t, jnp.zeros_like(basis_low_t)], axis=1),
        ],
        axis=0,
    )
    scale_rows = jnp.concatenate(scales, axis=0)
    scale_parts = jnp.concatenate(
        [*split3(scale_rows), jnp.zeros((-3 * groups % 16, 128), BF16)], axis=0
    )

    level = lax.broadcasted_iota(jnp.int32, (ORDERS, width), 0)
    path_rows = jnp.where(
        level == 0,
        path_weight_ref[0:1, :],
        jnp.where(
            level < 4,
            path_weight_ref[1:2, :],
            jnp.where(level < 9, path_weight_ref[2:3, :], 0.0),
        ),
    )
    paths_t = jnp.transpose(jnp.concatenate([path_rows] * GROUP, axis=0)) * (1.0 / root_count)
    out_column = jnp.transpose(jnp.broadcast_to(out_weight_ref[...], (width, width)))
    out_column = jnp.concatenate([out_column] * (pairs // width), axis=1)

    site_ids = lax.broadcasted_iota(jnp.int32, (known, pairs), 0)
    slot_ids = lax.broadcasted_iota(jnp.int32, (centers, pairs), 0)
    slot_row = lax.broadcasted_iota(jnp.int32, (1, pairs), 1) // nbr
    block_row = lax.broadcasted_iota(jnp.int32, (wide, span), 0) // ORDERS
    block_lane = lax.broadcasted_iota(jnp.int32, (wide, span), 1) // nbr
    block_mask = (block_row == block_lane).astype(F32)
    block_half = block_mask.astype(BF16)
    order = lax.broadcasted_iota(jnp.int32, (radial, pairs), 0).astype(F32) + 1.0
    lanes = [slice(g * span, (g + 1) * span) for g in range(groups)]

    pick = jnp.where(site_ids == near_row, 1.0, 0.0)
    pick_half = pick.astype(BF16)
    slot_half = jnp.where(slot_ids == slot_row, 1.0, 0.0).astype(BF16)

    moved = mm(place_parts, pick_half) - mm(center_parts, slot_half)
    moved = moved[: 3 * sites] + moved[3 * sites : 6 * sites] + moved[6 * sites :]
    dx = jnp.where(live, jnp.sum(moved[:sites], axis=0, keepdims=True), 6.0)
    dy = jnp.sum(moved[sites : 2 * sites], axis=0, keepdims=True) + CELL_SIDE * side_y
    dy = jnp.where(live, dy, 0.0)
    dz = jnp.where(live, jnp.sum(moved[2 * sites :], axis=0, keepdims=True), 0.0)
    length = jnp.sqrt(dx * dx + dy * dy + dz * dz)
    inverse = 1.0 / length
    ratio = length * (1.0 / CUTOFF)
    inside = live & (ratio < 1.0)
    r2 = ratio * ratio
    r5 = r2 * r2 * ratio
    r6 = r5 * ratio
    weight = jnp.where(inside, 1.0 - r6 * (28.0 - 48.0 * ratio + 21.0 * r2), 0.0)
    slope = jnp.where(inside, -168.0 * r5 * (1.0 - 2.0 * ratio + r2), 0.0)
    sine, cosine = sin_cos_pi(order * ratio)
    basis = (math.sqrt(2.0 / CUTOFF) * inverse) * sine
    basis_slope = (math.sqrt(2.0 / CUTOFF) * inverse) * (
        (math.pi / CUTOFF) * order * cosine - sine * inverse
    )
    ex = dx * inverse
    ey = dy * inverse
    ez = dz * inverse
    angular = jnp.concatenate(
        [
            jnp.ones_like(ex),
            root_three * ex,
            root_three * ey,
            root_three * ez,
            root_fifteen * ex * ey,
            root_fifteen * ey * ez,
            0.5 * root_five * (3.0 * ez * ez - 1.0),
            root_fifteen * ex * ez,
            0.5 * root_fifteen * (ex * ex - ey * ey),
            jnp.zeros((ORDERS - 9, pairs), F32),
        ],
        axis=0,
    )
    angular_high, angular_low = split(angular)
    blocks = [
        jnp.concatenate(
            [
                jnp.concatenate([angular_high[:, cut]] * GROUP, axis=0) * block_half,
                jnp.concatenate([angular_low[:, cut]] * GROUP, axis=0) * block_half,
            ],
            axis=0,
        )
        for cut in lanes
    ]
    lane_ids = lax.broadcasted_iota(jnp.int32, (128, span), 0)
    lane_slot = lax.broadcasted_iota(jnp.int32, (128, span), 1) // nbr + 3 * sites
    scale = mm(scale_parts, jnp.where(lane_ids == lane_slot, 1.0, 0.0).astype(BF16))
    scale = scale[:groups] + scale[groups : 2 * groups] + scale[2 * groups : 3 * groups]
    scale = jnp.concatenate([scale[g : g + 1] for g in range(groups)], axis=1)
    scale = scale * (1.0 / root_count)
    pull = ROOT_HALF * scale

    basis_high, basis_low = split(basis)
    before = folded(
        mm(lookup, jnp.concatenate([pick_half, slot_half, basis_high, basis_low], axis=0))
    )
    gate = 1.0 + jnp.tanh(before)
    active = before * gate
    latent = weight * active
    latent_high, latent_low = split(latent)
    mixed = folded(mm(value_rows, jnp.concatenate([latent_high, latent_low], axis=0)))
    values = mixed[:width]
    env_high, env_low = split(mixed[width:])

    def over_pairs(high, low):
        sums = []
        for cut, block in zip(lanes, blocks):
            quad = mm_nt(jnp.concatenate([high[:, cut], low[:, cut]], axis=0), block)
            sums.append((quad[:width, :wide] + quad[:width, wide:] + quad[width:, :wide]) * paths_t)
        return sums

    def over_orders(tables):
        parts = [folded(mm(stacked(*split(t)), block)) for t, block in zip(tables, blocks)]
        return jnp.concatenate(parts, axis=1)

    weighted = over_pairs(env_high, env_low)
    inner = over_orders(weighted)
    scalars = values * inner
    scalars_high, scalars_low = split(scalars)
    z = full_depth(
        latent_both_t,
        latent_high_t,
        jnp.concatenate([latent_high, scalars_high], axis=0),
        jnp.concatenate([latent_low, scalars_low], axis=0),
    )
    z_gate = 1.0 + jnp.tanh(z)
    update = z * z_gate
    update_sum = jnp.sum(update * out_column, axis=0, keepdims=True)
    active_sum = jnp.sum(
        active[:, :own_pairs] * out_column[:, :own_pairs], axis=0, keepdims=True
    )
    pair_energy = (active_sum + update_sum[:, :own_pairs]) * (pull * weight)[:, :own_pairs]
    d_z = (0.5 * pull * weight) * (z_gate + update * (2.0 - z_gate))
    spread_back = half_depth(latent_rows, d_z)
    d_scalars = spread_back[width:]
    d_values = d_scalars * inner
    dinner_high, dinner_low = split(d_scalars * values)
    d_embed = over_pairs(dinner_high, dinner_low)
    d_env = over_orders(d_embed)

    d_angular = []
    for g, cut in enumerate(lanes):
        sides = jnp.transpose(jnp.concatenate([weighted[g], d_embed[g]], axis=0))
        sides_high, sides_low = split(sides)
        d_block = full_depth(
            jnp.concatenate([sides_high, sides_low], axis=0),
            sides_high,
            jnp.concatenate([dinner_high[:, cut], env_high[:, cut]], axis=0),
            jnp.concatenate([dinner_low[:, cut], env_low[:, cut]], axis=0),
        )
        d_block = d_block * block_mask
        total = d_block[:ORDERS]
        for k in range(1, GROUP):
            total = total + d_block[k * ORDERS : (k + 1) * ORDERS]
        d_angular.append(total)
    d_angular = jnp.concatenate(d_angular, axis=1)

    mixed_high, mixed_low = split(jnp.concatenate([d_values, d_env], axis=0))
    d_latent = (
        full_depth(value_both, value_high, mixed_high, mixed_low)
        + spread_back[:width]
        + pull * out_column
    )
    d_weight = jnp.sum(d_latent * active, axis=0, keepdims=True) + pull * update_sum
    d_before = d_latent * (gate + active * (2.0 - gate))
    d_basis = half_depth(basis_rows, d_before) * (0.5 * weight)

    d_length = jnp.sum(d_basis * basis_slope, axis=0, keepdims=True) + d_weight * slope * (
        1.0 / CUTOFF
    )
    a1, a2, a3, a4, a5, a6, a7, a8 = [d_angular[m : m + 1] for m in range(1, 9)]
    ux = root_three * a1 + root_fifteen * (ey * a4 + ez * a7 + ex * a8)
    uy = root_three * a2 + root_fifteen * (ex * a4 + ez * a5 - ey * a8)
    uz = root_three * a3 + root_fifteen * (ey * a5 + ex * a7) + 3.0 * root_five * ez * a6
    along = ex * ux + ey * uy + ez * uz
    radial_part = d_length - along * inverse
    gx = ux * inverse + ex * radial_part
    gy = uy * inverse + ey * radial_part
    gz = uz * inverse + ez * radial_part
    hx = -0.5 * dx
    hy = -0.5 * dy
    hz = -0.5 * dz
    virial = [hx * gx, hx * gy, hx * gz, hy * gx, hy * gy, hy * gz, hz * gx, hz * gy, hz * gz]
    rest = [jnp.zeros((ORDERS - 13, pairs), F32)]
    near_terms = jnp.concatenate(
        [-gx, -gy, -gz, *virial, jnp.zeros_like(gx), *rest], axis=0
    )
    center_rows = [gx, gy, gz, *virial]
    center_rows = [r[:, :own_pairs] for r in center_rows] + [pair_energy]
    center_rows.append(jnp.zeros((ORDERS - 13, own_pairs), F32))
    center_terms = jnp.concatenate(center_rows, axis=0)
    reach = pick_half
    if kept_sides < kind:
        step = kind * owned
        reach = jnp.concatenate([pick_half[i : i + owned] for i in range(0, known, step)], axis=0)
    near_sums = mm_nt(jnp.concatenate(split(near_terms), axis=0), reach)
    center_sums = mm_nt(
        jnp.concatenate(split(center_terms), axis=0), slot_half[:owned, :own_pairs]
    )
    center_sums = jnp.concatenate(
        [folded(center_sums), jnp.zeros((ORDERS, 128 - owned), F32)], axis=1
    )
    totals = folded(near_sums)
    lane = lax.broadcasted_iota(jnp.int32, (ORDERS, 128), 1)
    known = totals.shape[1]
    tiles = [totals[:, 128 * i : 128 * (i + 1)] for i in range(known // 128)]
    for g in range(owned // GROUP):
        cell = g % 2 * 2 + 1 - g // 2
        target = g * kept_sides * owned + cell * sites
        turn = (target - g * GROUP) % 128
        piece = pltpu.roll(center_sums, turn, 1) if turn else center_sums
        begin = target % 128
        piece = jnp.where((lane >= begin) & (lane < begin + GROUP), piece, 0.0)
        tiles[target // 128] = tiles[target // 128] + piece
    totals = jnp.concatenate(tiles, axis=1)
    keep_ref[...] = totals[:, : known // 2]
    send_ref[...] = totals[:, known // 2 :]


def in_hbm(*arrays):
    return [pltpu.with_memory_space_constraint(array, pltpu.HBM) for array in arrays]


def joined(parts):
    total = sum(part.shape[0] for part in parts)
    start = 0
    pads = []
    for part in parts:
        end = start + part.shape[0]
        pads.append(jnp.pad(part, ((start, total - end), (0, 0))))
        start = end
    return functools.reduce(jnp.add, pads)


def local(
    positions,
    features,
    species,
    centers,
    neighbours,
    counts,
    species_scale,
    species_shift,
    center_weight,
    near_weight,
    basis_weight,
    path_weight,
    value_weight,
    latent_weight,
    out_weight,
):
    cells_x, cells_y, cells_z, sites, width = features.shape
    cell_count = cells_x * cells_y * cells_z
    owned = cell_count * sites
    assert (cells_x, cells_y, cells_z, sites) == (2, 1, 2, SITES)
    pairs = neighbours.size
    nbr = pairs // owned
    kind = min(3, lax.axis_size("gy"))

    def moved(array, steps):
        names = tuple(steps)
        sizes = [lax.axis_size(name) for name in names]
        route = []
        for at in np.ndindex(*sizes):
            to = [(p + steps[name]) % size for p, name, size in zip(at, names, sizes)]
            route.append(
                (int(np.ravel_multi_index(at, sizes)), int(np.ravel_multi_index(to, sizes)))
            )
        return lax.ppermute(array, names, route)

    vmem = pl.BlockSpec(memory_space=pltpu.VMEM)
    hbm = pl.BlockSpec(memory_space=pltpu.HBM)
    listed = centers.reshape(1, owned)
    payload = jax.ShapeDtypeStruct((owned + OWN_CELLS + pairs // 256, width), F32)
    low, high = pl.pallas_call(
        functools.partial(pack_kernel, kind),
        out_shape=(payload, payload),
        in_specs=[hbm] * 6,
        out_specs=(vmem, vmem),
        scratch_shapes=[
            pltpu.VMEM((owned, 128), F32),
            pltpu.VMEM(positions.shape, F32),
            pltpu.VMEM(species.shape, jnp.int32),
            pltpu.VMEM(listed.shape, jnp.int32),
            pltpu.VMEM(neighbours.shape, jnp.int32),
            pltpu.SMEM(species_scale.shape, F32),
            pltpu.SemaphoreType.DMA((6,)),
        ],
        compiler_params=pltpu.CompilerParams(vmem_limit_bytes=8 * 1024 * 1024),
        name="pack_payload",
    )(
        *in_hbm(
            positions,
            features.reshape(owned, width),
            species,
            listed,
            neighbours,
            species_scale,
        )
    )
    weights = (
        center_weight,
        near_weight,
        basis_weight,
        path_weight,
        value_weight,
        latent_weight,
        out_weight.reshape(1, width),
    )
    *weights, shift_row = pl.pallas_call(
        fetch_kernel,
        out_shape=(
            *(jax.ShapeDtypeStruct(w.shape, F32) for w in weights),
            jax.ShapeDtypeStruct((1, owned), F32),
        ),
        in_specs=[hbm] * (3 + len(weights)),
        out_specs=(vmem,) * (1 + len(weights)),
        scratch_shapes=[
            pltpu.VMEM(species.shape, jnp.int32),
            pltpu.VMEM(listed.shape, jnp.int32),
            pltpu.SMEM(species_shift.shape, F32),
            pltpu.SemaphoreType.DMA((3 + len(weights),)),
        ],
        compiler_params=pltpu.CompilerParams(vmem_limit_bytes=8 * 1024 * 1024),
        name="fetch_weights",
    )(*in_hbm(species, listed, species_shift, *weights))
    last_x = moved(high, {"gx": 1})
    sides = []
    for step in (-1, 1)[: kind - 1]:
        sides.append(moved(high, {"gx": 1, "gy": step}))
        sides.insert(-1, moved(low, {"gy": step}))
    next_z = moved(joined([low, last_x, *sides]), {"gz": -1})
    kept = 1 if kind == 2 else kind
    half = 2 * kept * owned
    keep, send = pl.pallas_call(
        functools.partial(force_kernel, kind, nbr),
        out_shape=(
            jax.ShapeDtypeStruct((ORDERS, half), F32),
            jax.ShapeDtypeStruct((ORDERS, half), F32),
        ),
        in_specs=[vmem] * (8 + 2 * kind),
        out_specs=(vmem, vmem),
        compiler_params=pltpu.CompilerParams(vmem_limit_bytes=44 * 1024 * 1024),
        name="pair_forces",
    )(
        low,
        last_x,
        *sides,
        next_z,
        *weights,
    )
    totals = keep + moved(send, {"gz": 1})

    def part(index):
        return totals[:, index * owned : (index + 1) * owned]

    back = [moved(part(kept), {"gx": -1})]
    for i, step in enumerate((1, -1)[: kept - 1]):
        back.append(moved(part(kept + 1 + i), {"gx": -1, "gy": step}))
        back.append(moved(part(1 + i), {"gy": step}))
    site_energy, forces, virial = pl.pallas_call(
        finish_kernel,
        out_shape=(
            jax.ShapeDtypeStruct(species.shape, F32),
            jax.ShapeDtypeStruct(positions.shape, F32),
            jax.ShapeDtypeStruct((*species.shape, 9), F32),
        ),
        in_specs=[vmem] * (2 + len(back)),
        out_specs=(vmem, vmem, vmem),
        compiler_params=pltpu.CompilerParams(vmem_limit_bytes=8 * 1024 * 1024),
        name="write_outputs",
    )(totals, shift_row, *back)
    return (site_energy, forces, jnp.transpose(virial, (4, 0, 1, 2, 3)))


def solution(mesh):
    placed = (
        P(None, "gx", "gy", "gz", None),
        P("gx", "gy", "gz", None, None),
        P("gx", "gy", "gz", None),
        P(("gx", "gy", "gz")),
        P(("gx", "gy", "gz"), None),
        P(("gx", "gy", "gz")),
        P(),
        P(),
        P(),
        P(),
        P(),
        P(),
        P(),
        P(),
        P(),
    )
    return jax.shard_map(
        local,
        mesh=mesh,
        in_specs=placed,
        out_specs=(
            P("gx", "gy", "gz", None),
            P(None, "gx", "gy", "gz", None),
            P(None, "gx", "gy", "gz", None),
        ),
        check_vma=False,
    )
```

```python
import functools
import math

import jax
import jax.numpy as jnp
import numpy as np
from jax import lax
from jax.experimental import pallas as pl
from jax.experimental.pallas import tpu as pltpu
from jax.sharding import PartitionSpec as P

EXACT_DOT = lax.Precision.HIGHEST
CUTOFF = 5.0
CELL_SIDE = 4.6
ROOT_HALF = 0.7071067811865476
GROUP = 8
ORDERS = 16
SITES = 8
OWN_CELLS = 4
FRAME_CELLS = 48
F32 = jnp.float32
BF16 = jnp.bfloat16


def split(value):
    high = value.astype(BF16)
    low = (value - high.astype(F32)).astype(BF16)
    return high, low


def split3(value):
    high = value.astype(BF16)
    rest = value - high.astype(F32)
    middle = rest.astype(BF16)
    low = (rest - middle.astype(F32)).astype(BF16)
    return high, middle, low


def mm(a, b):
    return lax.dot_general(a, b, (((1,), (0,)), ((), ())), preferred_element_type=F32)


def mm_nt(a, b):
    return lax.dot_general(a, b, (((1,), (1,)), ((), ())), preferred_element_type=F32)


def stacked(high, low):
    top = jnp.concatenate([high, high], axis=1)
    bottom = jnp.concatenate([low, jnp.zeros_like(low)], axis=1)
    return jnp.concatenate([top, bottom], axis=0)


def folded(product):
    half = product.shape[0] // 2
    return product[:half] + product[half:]


def half_depth(weights, value):
    return folded(mm(weights, jnp.concatenate(split(value), axis=0)))


def full_depth(both, high, value_high, value_low):
    return folded(mm(both, value_high)) + mm(high, value_low)


def sin_cos_pi(turns):
    near = turns - 2.0 * jnp.round(turns * 0.5)
    quarter = jnp.round(near * 2.0)
    v = (near - 0.5 * quarter) * math.pi
    v2 = v * v
    s = v * (
        1.0
        + v2
        * (-1.0 / 6 + v2 * (1.0 / 120 + v2 * (-1.0 / 5040 + v2 * (1.0 / 362880 - v2 / 39916800))))
    )
    c = 1.0 + v2 * (
        -0.5
        + v2
        * (1.0 / 24 + v2 * (-1.0 / 720 + v2 * (1.0 / 40320 + v2 * (-1.0 / 3628800 + v2 / 479001600))))
    )
    odd = jnp.abs(quarter) == 1.0
    sine = jnp.where(odd, quarter * c, jnp.where(quarter == 0.0, s, -s))
    cosine = jnp.where(odd, -quarter * s, jnp.where(quarter == 0.0, c, -c))
    return sine, cosine


def lane_row(piece, offset):
    row = jnp.concatenate([piece, jnp.zeros((1, 128 - piece.shape[1]), piece.dtype)], axis=1)
    return pltpu.roll(row, offset, 1) if offset else row


def pack_kernel(
    kind,
    positions_hbm,
    features_hbm,
    species_hbm,
    centers_hbm,
    neighbours_hbm,
    scale_hbm,
    low_ref,
    high_ref,
    wide_ref,
    positions_ref,
    species_ref,
    centers_ref,
    neighbours_ref,
    scale_ref,
    sems,
):
    owned, nbr = neighbours_ref.shape
    per_row = 128 // nbr
    pairs_in = (
        (features_hbm, low_ref.at[pl.ds(0, owned), :]),
        (neighbours_hbm, neighbours_ref),
        (centers_hbm, centers_ref),
        (positions_hbm, positions_ref),
        (species_hbm, species_ref),
        (scale_hbm, scale_ref),
    )
    copies = [
        pltpu.make_async_copy(source, target, sems.at[i])
        for i, (source, target) in enumerate(pairs_in)
    ]
    for copy in copies:
        copy.start()
    for copy in copies:
        copy.wait()
    for cell in range(OWN_CELLS):
        x, z = cell // 2, cell % 2
        species = species_ref[x, 0, z : z + 1, :]
        scale = jnp.zeros(species.shape, F32)
        for s in range(scale_ref.shape[0]):
            scale = jnp.where(species == s, scale_ref[s], scale)
        row = lane_row(scale, 3 * SITES)
        for c in range(3):
            row = row + lane_row(positions_ref[c, x, 0, z : z + 1, :], c * SITES)
        low_ref[owned + cell : owned + cell + 1] = row

    chosen = lax.broadcasted_iota(jnp.int32, (owned, owned), 0) == centers_ref[...]
    chosen = jnp.where(chosen, 1.0, 0.0)
    occupied = jnp.sum(chosen, axis=1, keepdims=True) > 0.5
    chosen = chosen.astype(BF16)
    rows = neighbours_ref[...]
    upper = mm(chosen, (rows >> 4).astype(F32).astype(BF16))
    lower = mm(chosen, (rows & 15).astype(F32).astype(BF16))
    rows = (upper * 16.0 + lower).astype(jnp.int32)
    live = occupied & (rows < FRAME_CELLS * SITES)
    slot = lax.broadcasted_iota(jnp.int32, (owned, nbr), 0)
    cell = slot >> 3
    site = rows & 7
    place = rows >> 3
    near_z = (place & 3) + 1 - 2 * (cell & 1)
    column = place >> 2
    frame_x = (column * 11) >> 5
    frame_y = column - 3 * frame_x
    near_x = frame_x + 1 - 2 * (cell >> 1)
    side = jnp.where(frame_y == 1, 0, jnp.where(frame_y == 2, 1, kind - 1))
    block = (near_z >> 1) * 2 + 1 - (near_x >> 1)
    where = (block * kind + side) * owned + (near_x & 1) * 16 + (near_z & 1) * 8 + site
    code = jnp.where(live, 1 + where + (frame_y << 10), 0).astype(F32)
    wide_ref[...] = jnp.concatenate([code, jnp.zeros((owned, 128 - nbr), F32)], axis=1)
    codes = wide_ref[pl.ds(0, owned // per_row, stride=per_row), :]
    for j in range(1, per_row):
        more = wide_ref[pl.ds(j, owned // per_row, stride=per_row), :]
        codes = codes + pltpu.roll(more, j * nbr, 1)
    tile = owned + OWN_CELLS
    low_ref[tile:] = codes[: codes.shape[0] // 2]
    high_ref[:tile] = low_ref[:tile]
    high_ref[tile:] = codes[codes.shape[0] // 2 :]


def fetch_kernel(species_hbm, centers_hbm, shift_hbm, *refs):
    *refs, shift_row_ref, species_ref, centers_ref, shift_ref, sems = refs
    count = len(refs) // 2
    pairs_in = [
        (species_hbm, species_ref),
        (centers_hbm, centers_ref),
        (shift_hbm, shift_ref),
        *zip(refs[:count], refs[count:]),
    ]
    copies = [
        pltpu.make_async_copy(source, target, sems.at[i])
        for i, (source, target) in enumerate(pairs_in)
    ]
    for copy in copies:
        copy.start()
    for copy in copies:
        copy.wait()
    owned = centers_ref.shape[1]
    shift_row = jnp.zeros((1, 128), F32)
    for cell in range(OWN_CELLS):
        species = species_ref[cell // 2, 0, cell % 2 : cell % 2 + 1, :]
        shift = jnp.zeros(species.shape, F32)
        for s in range(shift_ref.shape[0]):
            shift = jnp.where(species == s, shift_ref[s], shift)
        shift_row = shift_row + lane_row(shift, cell * SITES)
    chosen = lax.broadcasted_iota(jnp.int32, (owned, owned), 0) == centers_ref[...]
    occupied = jnp.sum(jnp.where(chosen, 1.0, 0.0), axis=1, keepdims=True) > 0.5
    column = jnp.where(occupied, jnp.ones((owned, 128), F32), 0.0)
    shift_row_ref[...] = shift_row[:, :owned] * jnp.transpose(column)[0:1]


def finish_kernel(mine_ref, shift_row_ref, *refs):
    *near_refs, energy_ref, forces_ref, virial_ref = refs
    owned = near_refs[0].shape[1]
    total = mine_ref[:, :owned]
    for near_ref in near_refs:
        total = total + near_ref[...]
    energy = total[12:13] + shift_row_ref[...]
    columns = jnp.transpose(jnp.concatenate([total, jnp.zeros((ORDERS, 128 - owned), F32)], axis=1))
    for cell in range(OWN_CELLS):
        x, z = cell // 2, cell % 2
        lanes = slice(cell * SITES, (cell + 1) * SITES)
        energy_ref[x, 0, z : z + 1, :] = energy[:, lanes]
        for c in range(3):
            forces_ref[c, x, 0, z : z + 1, :] = total[c : c + 1, lanes]
        virial_ref[x, 0, z] = columns[lanes, 3:12]


def force_kernel(kind, nbr, here_ref, last_x_ref, *refs):
    near_side_refs = refs[: 2 * kind - 2]
    (
        next_z_ref,
        center_weight_ref,
        near_weight_ref,
        basis_weight_ref,
        path_weight_ref,
        value_weight_ref,
        latent_weight_ref,
        out_weight_ref,
        keep_ref,
        send_ref,
    ) = refs[2 * kind - 2 :]
    height, width = here_ref.shape
    owned = OWN_CELLS * SITES
    center_sides = 2 if kind == 2 else 1
    kept_sides = 1 if kind == 2 else kind
    own_pairs = owned * nbr
    pairs = center_sides * own_pairs
    centers = center_sides * owned
    radial = basis_weight_ref.shape[0]
    span = GROUP * nbr
    groups = centers // GROUP
    wide = GROUP * ORDERS
    sites = SITES
    root_count = math.sqrt(nbr)
    root_three = math.sqrt(3.0)
    root_fifteen = math.sqrt(15.0)
    root_five = math.sqrt(5.0)
    far = next_z_ref[...]
    mains = [here_ref[...], last_x_ref[...], far[:height], far[height : 2 * height]]
    near_sides = [ref[...] for ref in near_side_refs]
    far_sides = far[2 * height :]
    far_sides = [far_sides[i * height : (i + 1) * height] for i in range(2 * kind - 2)]
    blocks_in = [
        [mains[0], *near_sides[0::2]],
        [mains[1], *near_sides[1::2]],
        [mains[2], *far_sides[0::2]],
        [mains[3], *far_sides[1::2]],
    ]
    feats = jnp.concatenate([side[:owned] for block in blocks_in for side in block], axis=0)
    known = feats.shape[0]
    center_feats = []
    center_coords = []
    coords = []
    scales = []
    codes = []
    cell_row = lax.broadcasted_iota(jnp.int32, (kind * OWN_CELLS, 128), 0) % OWN_CELLS
    tile_lane = lax.broadcasted_iota(jnp.int32, (kind * OWN_CELLS, 128), 1)
    for g, block in enumerate(blocks_in):
        behind_x, ahead_z = g % 2, g // 2
        rows = jnp.concatenate([side[owned : owned + OWN_CELLS] for side in block], axis=0)
        corner_x = (cell_row // 2 + 2 - 2 * behind_x).astype(F32) * CELL_SIDE
        corner_z = (cell_row % 2 + 2 * ahead_z).astype(F32) * CELL_SIDE
        corner = jnp.where(
            tile_lane < sites, corner_x, jnp.where(tile_lane < 2 * sites, 0.0, corner_z)
        )
        coords.append(rows + corner)
    for c in range(center_sides):
        for g, block in enumerate(blocks_in):
            cell = g % 2 * 2 + 1 - g // 2
            row = c * OWN_CELLS + cell
            center_feats.append(block[c][cell * sites : (cell + 1) * sites])
            scales.append(block[c][owned + cell : owned + cell + 1])
            center_coords.append(coords[g][row : row + 1])
            start = owned + OWN_CELLS + (1 - g // 2) * span // 128
            codes.extend(block[c][start + r : start + r + 1] for r in range(span // 128))
    center_feats = jnp.concatenate(center_feats, axis=0)
    coords = jnp.concatenate(coords, axis=0)
    code = jnp.concatenate(codes, axis=1).astype(jnp.int32)
    live = code > 0
    code = jnp.maximum(code - 1, 0)
    side_y = ((code >> 10) - 1).astype(F32)
    near_row = code & 1023
    if center_sides == 2:
        pair_lane = lax.broadcasted_iota(jnp.int32, (1, pairs), 1)
        near_row = jnp.where(pair_lane < own_pairs, near_row, near_row ^ owned)
    near_row = jnp.where(live, near_row, known)

    def place_rows(cell_rows):
        count = cell_rows.shape[0] * sites
        spread = jnp.broadcast_to(cell_rows[:, None, :], (cell_rows.shape[0], sites, 128))
        spread = spread.reshape(count, 128)
        lane = lax.broadcasted_iota(jnp.int32, (count, 128), 1)
        row = lax.broadcasted_iota(jnp.int32, (count, 128), 0)
        keep = (lane % sites == row % sites) & (lane < 3 * sites)
        spread = jnp.transpose(jnp.where(keep, spread, 0.0))
        return jnp.concatenate(split3(spread[: 3 * sites]), axis=0)

    place_parts = place_rows(coords)
    center_parts = place_rows(jnp.concatenate(center_coords, axis=0))

    value_rows = stacked(*split(jnp.transpose(value_weight_ref[...])))
    latent_high_t, latent_low_t = split(0.5 * jnp.transpose(latent_weight_ref[...]))
    latent_both_t = jnp.concatenate([latent_high_t, latent_low_t], axis=0)
    latent_rows = stacked(*split(latent_weight_ref[...] * out_weight_ref[...]))
    value_high, value_low = split(value_weight_ref[...])
    value_both = jnp.concatenate([value_high, value_low], axis=0)
    basis_t = jnp.transpose(basis_weight_ref[...])
    basis_high_t, basis_low_t = split(0.5 * basis_t)
    basis_rows = stacked(*split(basis_weight_ref[...]))

    def project(weight, rows):
        weight = stacked(*split(jnp.transpose(weight)))
        return folded(mm_nt(weight, jnp.concatenate(split(rows), axis=1)))

    near_t = project(near_weight_ref[...], feats)
    own_t = project(center_weight_ref[...], center_feats)
    near_high, near_low = split(0.5 * near_t)
    own_high, own_low = split(0.5 * own_t)
    lookup = jnp.concatenate(
        [
            jnp.concatenate([near_high, own_high, basis_high_t, basis_high_t], axis=1),
            jnp.concatenate([near_low, own_low, basis_low_t, jnp.zeros_like(basis_low_t)], axis=1),
        ],
        axis=0,
    )
    scale_rows = jnp.concatenate(scales, axis=0)
    scale_parts = jnp.concatenate(
        [*split3(scale_rows), jnp.zeros((-3 * groups % 16, 128), BF16)], axis=0
    )

    level = lax.broadcasted_iota(jnp.int32, (ORDERS, width), 0)
    path_rows = jnp.where(
        level == 0,
        path_weight_ref[0:1, :],
        jnp.where(
            level < 4,
            path_weight_ref[1:2, :],
            jnp.where(level < 9, path_weight_ref[2:3, :], 0.0),
        ),
    )
    paths_t = jnp.transpose(jnp.concatenate([path_rows] * GROUP, axis=0)) * (1.0 / root_count)
    out_column = jnp.transpose(jnp.broadcast_to(out_weight_ref[...], (width, width)))
    out_column = jnp.concatenate([out_column] * (pairs // width), axis=1)

    site_ids = lax.broadcasted_iota(jnp.int32, (known, pairs), 0)
    slot_ids = lax.broadcasted_iota(jnp.int32, (centers, pairs), 0)
    slot_row = lax.broadcasted_iota(jnp.int32, (1, pairs), 1) // nbr
    block_row = lax.broadcasted_iota(jnp.int32, (wide, span), 0) // ORDERS
    block_lane = lax.broadcasted_iota(jnp.int32, (wide, span), 1) // nbr
    block_mask = (block_row == block_lane).astype(F32)
    block_half = block_mask.astype(BF16)
    order = lax.broadcasted_iota(jnp.int32, (radial, pairs), 0).astype(F32) + 1.0
    lanes = [slice(g * span, (g + 1) * span) for g in range(groups)]

    pick = jnp.where(site_ids == near_row, 1.0, 0.0)
    pick_half = pick.astype(BF16)
    slot_half = jnp.where(slot_ids == slot_row, 1.0, 0.0).astype(BF16)

    moved = mm(place_parts, pick_half) - mm(center_parts, slot_half)
    moved = moved[: 3 * sites] + moved[3 * sites : 6 * sites] + moved[6 * sites :]
    dx = jnp.where(live, jnp.sum(moved[:sites], axis=0, keepdims=True), 6.0)
    dy = jnp.sum(moved[sites : 2 * sites], axis=0, keepdims=True) + CELL_SIDE * side_y
    dy = jnp.where(live, dy, 0.0)
    dz = jnp.where(live, jnp.sum(moved[2 * sites :], axis=0, keepdims=True), 0.0)
    length = jnp.sqrt(dx * dx + dy * dy + dz * dz)
    inverse = 1.0 / length
    ratio = length * (1.0 / CUTOFF)
    inside = live & (ratio < 1.0)
    r2 = ratio * ratio
    r5 = r2 * r2 * ratio
    r6 = r5 * ratio
    weight = jnp.where(inside, 1.0 - r6 * (28.0 - 48.0 * ratio + 21.0 * r2), 0.0)
    slope = jnp.where(inside, -168.0 * r5 * (1.0 - 2.0 * ratio + r2), 0.0)
    sine, cosine = sin_cos_pi(order * ratio)
    basis = (math.sqrt(2.0 / CUTOFF) * inverse) * sine
    basis_slope = (math.sqrt(2.0 / CUTOFF) * inverse) * (
        (math.pi / CUTOFF) * order * cosine - sine * inverse
    )
    ex = dx * inverse
    ey = dy * inverse
    ez = dz * inverse
    angular = jnp.concatenate(
        [
            jnp.ones_like(ex),
            root_three * ex,
            root_three * ey,
            root_three * ez,
            root_fifteen * ex * ey,
            root_fifteen * ey * ez,
            0.5 * root_five * (3.0 * ez * ez - 1.0),
            root_fifteen * ex * ez,
            0.5 * root_fifteen * (ex * ex - ey * ey),
            jnp.zeros((ORDERS - 9, pairs), F32),
        ],
        axis=0,
    )
    angular_high, angular_low = split(angular)
    blocks = [
        jnp.concatenate(
            [
                jnp.concatenate([angular_high[:, cut]] * GROUP, axis=0) * block_half,
                jnp.concatenate([angular_low[:, cut]] * GROUP, axis=0) * block_half,
            ],
            axis=0,
        )
        for cut in lanes
    ]
    lane_ids = lax.broadcasted_iota(jnp.int32, (128, span), 0)
    lane_slot = lax.broadcasted_iota(jnp.int32, (128, span), 1) // nbr + 3 * sites
    scale = mm(scale_parts, jnp.where(lane_ids == lane_slot, 1.0, 0.0).astype(BF16))
    scale = scale[:groups] + scale[groups : 2 * groups] + scale[2 * groups : 3 * groups]
    scale = jnp.concatenate([scale[g : g + 1] for g in range(groups)], axis=1)
    scale = scale * (1.0 / root_count)
    pull = ROOT_HALF * scale

    basis_high, basis_low = split(basis)
    before = folded(
        mm(lookup, jnp.concatenate([pick_half, slot_half, basis_high, basis_low], axis=0))
    )
    gate = 1.0 + jnp.tanh(before)
    active = before * gate
    latent = weight * active
    latent_high, latent_low = split(latent)
    mixed = folded(mm(value_rows, jnp.concatenate([latent_high, latent_low], axis=0)))
    values = mixed[:width]
    env_high, env_low = split(mixed[width:])

    def over_pairs(high, low):
        sums = []
        for cut, block in zip(lanes, blocks):
            quad = mm_nt(jnp.concatenate([high[:, cut], low[:, cut]], axis=0), block)
            sums.append((quad[:width, :wide] + quad[:width, wide:] + quad[width:, :wide]) * paths_t)
        return sums

    def over_orders(tables):
        parts = [folded(mm(stacked(*split(t)), block)) for t, block in zip(tables, blocks)]
        return jnp.concatenate(parts, axis=1)

    weighted = over_pairs(env_high, env_low)
    inner = over_orders(weighted)
    scalars = values * inner
    scalars_high, scalars_low = split(scalars)
    z = full_depth(
        latent_both_t,
        latent_high_t,
        jnp.concatenate([latent_high, scalars_high], axis=0),
        jnp.concatenate([latent_low, scalars_low], axis=0),
    )
    z_gate = 1.0 + jnp.tanh(z)
    update = z * z_gate
    update_sum = jnp.sum(update * out_column, axis=0, keepdims=True)
    active_sum = jnp.sum(
        active[:, :own_pairs] * out_column[:, :own_pairs], axis=0, keepdims=True
    )
    pair_energy = (active_sum + update_sum[:, :own_pairs]) * (pull * weight)[:, :own_pairs]
    d_z = (0.5 * pull * weight) * (z_gate + update * (2.0 - z_gate))
    spread_back = half_depth(latent_rows, d_z)
    d_scalars = spread_back[width:]
    d_values = d_scalars * inner
    dinner_high, dinner_low = split(d_scalars * values)
    d_embed = over_pairs(dinner_high, dinner_low)
    d_env = over_orders(d_embed)

    d_angular = []
    for g, cut in enumerate(lanes):
        sides = jnp.transpose(jnp.concatenate([weighted[g], d_embed[g]], axis=0))
        sides_high, sides_low = split(sides)
        d_block = full_depth(
            jnp.concatenate([sides_high, sides_low], axis=0),
            sides_high,
            jnp.concatenate([dinner_high[:, cut], env_high[:, cut]], axis=0),
            jnp.concatenate([dinner_low[:, cut], env_low[:, cut]], axis=0),
        )
        d_block = d_block * block_mask
        total = d_block[:ORDERS]
        for k in range(1, GROUP):
            total = total + d_block[k * ORDERS : (k + 1) * ORDERS]
        d_angular.append(total)
    d_angular = jnp.concatenate(d_angular, axis=1)

    mixed_high, mixed_low = split(jnp.concatenate([d_values, d_env], axis=0))
    d_latent = (
        full_depth(value_both, value_high, mixed_high, mixed_low)
        + spread_back[:width]
        + pull * out_column
    )
    d_weight = jnp.sum(d_latent * active, axis=0, keepdims=True) + pull * update_sum
    d_before = d_latent * (gate + active * (2.0 - gate))
    d_basis = half_depth(basis_rows, d_before) * (0.5 * weight)

    d_length = jnp.sum(d_basis * basis_slope, axis=0, keepdims=True) + d_weight * slope * (
        1.0 / CUTOFF
    )
    a1, a2, a3, a4, a5, a6, a7, a8 = [d_angular[m : m + 1] for m in range(1, 9)]
    ux = root_three * a1 + root_fifteen * (ey * a4 + ez * a7 + ex * a8)
    uy = root_three * a2 + root_fifteen * (ex * a4 + ez * a5 - ey * a8)
    uz = root_three * a3 + root_fifteen * (ey * a5 + ex * a7) + 3.0 * root_five * ez * a6
    along = ex * ux + ey * uy + ez * uz
    radial_part = d_length - along * inverse
    gx = ux * inverse + ex * radial_part
    gy = uy * inverse + ey * radial_part
    gz = uz * inverse + ez * radial_part
    hx = -0.5 * dx
    hy = -0.5 * dy
    hz = -0.5 * dz
    virial = [hx * gx, hx * gy, hx * gz, hy * gx, hy * gy, hy * gz, hz * gx, hz * gy, hz * gz]
    rest = [jnp.zeros((ORDERS - 13, pairs), F32)]
    near_terms = jnp.concatenate(
        [-gx, -gy, -gz, *virial, jnp.zeros_like(gx), *rest], axis=0
    )
    center_rows = [gx, gy, gz, *virial]
    center_rows = [r[:, :own_pairs] for r in center_rows] + [pair_energy]
    center_rows.append(jnp.zeros((ORDERS - 13, own_pairs), F32))
    center_terms = jnp.concatenate(center_rows, axis=0)
    reach = []
    for x, z, side in np.ndindex(2, 2, kept_sides):
        start = ((2 * z + x) * kind + side) * owned
        reach.append(pick_half[start : start + owned])
    reach = jnp.concatenate(reach, axis=0)
    near_sums = mm_nt(jnp.concatenate(split(near_terms), axis=0), reach)
    center_sums = mm_nt(
        jnp.concatenate(split(center_terms), axis=0), slot_half[:owned, :own_pairs]
    )
    center_sums = jnp.concatenate(
        [folded(center_sums), jnp.zeros((ORDERS, 128 - owned), F32)], axis=1
    )
    totals = folded(near_sums)
    lane = lax.broadcasted_iota(jnp.int32, (ORDERS, 128), 1)
    known = totals.shape[1]
    tiles = [totals[:, 128 * i : 128 * (i + 1)] for i in range(known // 128)]
    for g in range(owned // GROUP):
        cell = g % 2 * 2 + 1 - g // 2
        target = (g % 2 * 2 + g // 2) * kept_sides * owned + cell * sites
        turn = (target - g * GROUP) % 128
        piece = pltpu.roll(center_sums, turn, 1) if turn else center_sums
        begin = target % 128
        piece = jnp.where((lane >= begin) & (lane < begin + GROUP), piece, 0.0)
        tiles[target // 128] = tiles[target // 128] + piece
    totals = jnp.concatenate(tiles, axis=1)
    keep_ref[...] = totals[:, : known // 2]
    send_ref[...] = totals[:, known // 2 :]


def in_hbm(*arrays):
    return [pltpu.with_memory_space_constraint(array, pltpu.HBM) for array in arrays]


def joined(parts):
    total = sum(part.shape[0] for part in parts)
    start = 0
    pads = []
    for part in parts:
        end = start + part.shape[0]
        pads.append(jnp.pad(part, ((start, total - end), (0, 0))))
        start = end
    return functools.reduce(jnp.add, pads)


def local(
    positions,
    features,
    species,
    centers,
    neighbours,
    counts,
    species_scale,
    species_shift,
    center_weight,
    near_weight,
    basis_weight,
    path_weight,
    value_weight,
    latent_weight,
    out_weight,
):
    cells_x, cells_y, cells_z, sites, width = features.shape
    cell_count = cells_x * cells_y * cells_z
    owned = cell_count * sites
    assert (cells_x, cells_y, cells_z, sites) == (2, 1, 2, SITES)
    pairs = neighbours.size
    nbr = pairs // owned
    kind = min(3, lax.axis_size("gy"))

    def moved(array, steps):
        names = tuple(steps)
        sizes = [lax.axis_size(name) for name in names]
        route = []
        for at in np.ndindex(*sizes):
            to = [(p + steps[name]) % size for p, name, size in zip(at, names, sizes)]
            route.append(
                (int(np.ravel_multi_index(at, sizes)), int(np.ravel_multi_index(to, sizes)))
            )
        return lax.ppermute(array, names, route)

    vmem = pl.BlockSpec(memory_space=pltpu.VMEM)
    hbm = pl.BlockSpec(memory_space=pltpu.HBM)
    listed = centers.reshape(1, owned)
    payload = jax.ShapeDtypeStruct((owned + OWN_CELLS + pairs // 256, width), F32)
    low, high = pl.pallas_call(
        functools.partial(pack_kernel, kind),
        out_shape=(payload, payload),
        in_specs=[hbm] * 6,
        out_specs=(vmem, vmem),
        scratch_shapes=[
            pltpu.VMEM((owned, 128), F32),
            pltpu.VMEM(positions.shape, F32),
            pltpu.VMEM(species.shape, jnp.int32),
            pltpu.VMEM(listed.shape, jnp.int32),
            pltpu.VMEM(neighbours.shape, jnp.int32),
            pltpu.SMEM(species_scale.shape, F32),
            pltpu.SemaphoreType.DMA((6,)),
        ],
        compiler_params=pltpu.CompilerParams(vmem_limit_bytes=8 * 1024 * 1024),
        name="pack_payload",
    )(
        *in_hbm(
            positions,
            features.reshape(owned, width),
            species,
            listed,
            neighbours,
            species_scale,
        )
    )
    weights = (
        center_weight,
        near_weight,
        basis_weight,
        path_weight,
        value_weight,
        latent_weight,
        out_weight.reshape(1, width),
    )
    *weights, shift_row = pl.pallas_call(
        fetch_kernel,
        out_shape=(
            *(jax.ShapeDtypeStruct(w.shape, F32) for w in weights),
            jax.ShapeDtypeStruct((1, owned), F32),
        ),
        in_specs=[hbm] * (3 + len(weights)),
        out_specs=(vmem,) * (1 + len(weights)),
        scratch_shapes=[
            pltpu.VMEM(species.shape, jnp.int32),
            pltpu.VMEM(listed.shape, jnp.int32),
            pltpu.SMEM(species_shift.shape, F32),
            pltpu.SemaphoreType.DMA((3 + len(weights),)),
        ],
        compiler_params=pltpu.CompilerParams(vmem_limit_bytes=8 * 1024 * 1024),
        name="fetch_weights",
    )(*in_hbm(species, listed, species_shift, *weights))
    last_x = moved(high, {"gx": 1})
    sides = []
    for step in (-1, 1)[: kind - 1]:
        sides.append(moved(high, {"gx": 1, "gy": step}))
        sides.insert(-1, moved(low, {"gy": step}))
    next_z = moved(joined([low, last_x, *sides]), {"gz": -1})
    kept = 1 if kind == 2 else kind
    half = 2 * kept * owned
    keep, send = pl.pallas_call(
        functools.partial(force_kernel, kind, nbr),
        out_shape=(
            jax.ShapeDtypeStruct((ORDERS, half), F32),
            jax.ShapeDtypeStruct((ORDERS, half), F32),
        ),
        in_specs=[vmem] * (8 + 2 * kind),
        out_specs=(vmem, vmem),
        compiler_params=pltpu.CompilerParams(vmem_limit_bytes=44 * 1024 * 1024),
        name="pair_forces",
    )(
        low,
        last_x,
        *sides,
        next_z,
        *weights,
    )
    totals = keep + moved(send, {"gx": -1})

    def part(index):
        return totals[:, index * owned : (index + 1) * owned]

    back = [moved(part(kept), {"gz": 1})]
    for i, step in enumerate((1, -1)[: kept - 1]):
        back.append(moved(part(kept + 1 + i), {"gy": step, "gz": 1}))
        back.append(moved(part(1 + i), {"gy": step}))
    site_energy, forces, virial = pl.pallas_call(
        finish_kernel,
        out_shape=(
            jax.ShapeDtypeStruct(species.shape, F32),
            jax.ShapeDtypeStruct(positions.shape, F32),
            jax.ShapeDtypeStruct((*species.shape, 9), F32),
        ),
        in_specs=[vmem] * (2 + len(back)),
        out_specs=(vmem, vmem, vmem),
        compiler_params=pltpu.CompilerParams(vmem_limit_bytes=8 * 1024 * 1024),
        name="write_outputs",
    )(totals, shift_row, *back)
    return (site_energy, forces, jnp.transpose(virial, (4, 0, 1, 2, 3)))


def solution(mesh):
    placed = (
        P(None, "gx", "gy", "gz", None),
        P("gx", "gy", "gz", None, None),
        P("gx", "gy", "gz", None),
        P(("gx", "gy", "gz")),
        P(("gx", "gy", "gz"), None),
        P(("gx", "gy", "gz")),
        P(),
        P(),
        P(),
        P(),
        P(),
        P(),
        P(),
        P(),
        P(),
    )
    return jax.shard_map(
        local,
        mesh=mesh,
        in_specs=placed,
        out_specs=(
            P("gx", "gy", "gz", None),
            P(None, "gx", "gy", "gz", None),
            P(None, "gx", "gy", "gz", None),
        ),
        check_vma=False,
    )
```

```python
import functools
import math

import jax
import jax.numpy as jnp
import numpy as np
from jax import lax
from jax.experimental import pallas as pl
from jax.experimental.pallas import tpu as pltpu
from jax.sharding import PartitionSpec as P

EXACT_DOT = lax.Precision.HIGHEST
CUTOFF = 5.0
CELL_SIDE = 4.6
ROOT_HALF = 0.7071067811865476
GROUP = 8
ORDERS = 16
LEVELS = (0, 1, 1, 1, 2, 2, 2, 2, 2)
SITES = 8
OWN_CELLS = 4
FRAME_CELLS = 48
F32 = jnp.float32
BF16 = jnp.bfloat16


def split(value):
    high = value.astype(BF16)
    low = (value - high.astype(F32)).astype(BF16)
    return high, low


def split3(value):
    high = value.astype(BF16)
    rest = value - high.astype(F32)
    middle = rest.astype(BF16)
    low = (rest - middle.astype(F32)).astype(BF16)
    return high, middle, low


def halves(value):
    high = value.astype(BF16).astype(F32)
    return high, value - high


def mm(a, b):
    return lax.dot_general(a, b, (((1,), (0,)), ((), ())), preferred_element_type=F32)


def mm_nt(a, b):
    return lax.dot_general(a, b, (((1,), (1,)), ((), ())), preferred_element_type=F32)


def stacked(high, low):
    top = jnp.concatenate([high, high], axis=1)
    bottom = jnp.concatenate([low, jnp.zeros_like(low)], axis=1)
    return jnp.concatenate([top, bottom], axis=0)


def folded(product):
    half = product.shape[0] // 2
    return product[:half] + product[half:]


def half_depth(weights, value):
    return folded(mm(weights, jnp.concatenate(split(value), axis=0)))


def full_depth(both, high, value_high, value_low):
    return folded(mm(both, value_high)) + mm(high, value_low)


def sin_cos_pi(turns):
    near = turns - 2.0 * jnp.round(turns * 0.5)
    quarter = jnp.round(near * 2.0)
    v = (near - 0.5 * quarter) * math.pi
    v2 = v * v
    s = v * (
        1.0
        + v2
        * (-1.0 / 6 + v2 * (1.0 / 120 + v2 * (-1.0 / 5040 + v2 * (1.0 / 362880 - v2 / 39916800))))
    )
    c = 1.0 + v2 * (
        -0.5
        + v2
        * (1.0 / 24 + v2 * (-1.0 / 720 + v2 * (1.0 / 40320 + v2 * (-1.0 / 3628800 + v2 / 479001600))))
    )
    odd = jnp.abs(quarter) == 1.0
    sine = jnp.where(odd, quarter * c, jnp.where(quarter == 0.0, s, -s))
    cosine = jnp.where(odd, -quarter * s, jnp.where(quarter == 0.0, c, -c))
    return sine, cosine


def lane_row(piece, offset):
    row = jnp.concatenate([piece, jnp.zeros((1, 128 - piece.shape[1]), piece.dtype)], axis=1)
    return pltpu.roll(row, offset, 1) if offset else row


def pack_kernel(
    kind,
    positions_hbm,
    features_hbm,
    species_hbm,
    centers_hbm,
    neighbours_hbm,
    scale_hbm,
    low_ref,
    high_ref,
    wide_ref,
    positions_ref,
    species_ref,
    centers_ref,
    neighbours_ref,
    scale_ref,
    sems,
):
    owned, nbr = neighbours_ref.shape
    per_row = 128 // nbr
    pairs_in = (
        (features_hbm, low_ref.at[pl.ds(0, owned), :]),
        (neighbours_hbm, neighbours_ref),
        (centers_hbm, centers_ref),
        (positions_hbm, positions_ref),
        (species_hbm, species_ref),
        (scale_hbm, scale_ref),
    )
    copies = [
        pltpu.make_async_copy(source, target, sems.at[i])
        for i, (source, target) in enumerate(pairs_in)
    ]
    for copy in copies:
        copy.start()
    for copy in copies:
        copy.wait()
    for cell in range(OWN_CELLS):
        x, z = cell // 2, cell % 2
        species = species_ref[x, 0, z : z + 1, :]
        scale = jnp.zeros(species.shape, F32)
        for s in range(scale_ref.shape[0]):
            scale = jnp.where(species == s, scale_ref[s], scale)
        row = lane_row(scale, 3 * SITES)
        for c in range(3):
            row = row + lane_row(positions_ref[c, x, 0, z : z + 1, :], c * SITES)
        low_ref[owned + cell : owned + cell + 1] = row

    chosen = lax.broadcasted_iota(jnp.int32, (owned, owned), 0) == centers_ref[...]
    chosen = jnp.where(chosen, 1.0, 0.0)
    occupied = jnp.sum(chosen, axis=1, keepdims=True) > 0.5
    chosen = chosen.astype(BF16)
    rows = neighbours_ref[...]
    upper = mm(chosen, (rows >> 4).astype(F32).astype(BF16))
    lower = mm(chosen, (rows & 15).astype(F32).astype(BF16))
    rows = (upper * 16.0 + lower).astype(jnp.int32)
    live = occupied & (rows < FRAME_CELLS * SITES)
    slot = lax.broadcasted_iota(jnp.int32, (owned, nbr), 0)
    cell = slot >> 3
    site = rows & 7
    place = rows >> 3
    near_z = (place & 3) + 1 - 2 * (cell & 1)
    column = place >> 2
    frame_x = (column * 11) >> 5
    frame_y = column - 3 * frame_x
    near_x = frame_x + 1 - 2 * (cell >> 1)
    side = jnp.where(frame_y == 1, 0, jnp.where(frame_y == 2, 1, kind - 1))
    block = (near_z >> 1) * 2 + 1 - (near_x >> 1)
    where = (block * kind + side) * owned + (near_x & 1) * 16 + (near_z & 1) * 8 + site
    code = jnp.where(live, 1 + where + (frame_y << 10), 0).astype(F32)
    wide_ref[...] = jnp.concatenate([code, jnp.zeros((owned, 128 - nbr), F32)], axis=1)
    codes = wide_ref[pl.ds(0, owned // per_row, stride=per_row), :]
    for j in range(1, per_row):
        more = wide_ref[pl.ds(j, owned // per_row, stride=per_row), :]
        codes = codes + pltpu.roll(more, j * nbr, 1)
    tile = owned + OWN_CELLS
    low_ref[tile:] = codes[: codes.shape[0] // 2]
    high_ref[:tile] = low_ref[:tile]
    high_ref[tile:] = codes[codes.shape[0] // 2 :]


def fetch_kernel(species_hbm, centers_hbm, shift_hbm, *refs):
    *refs, shift_row_ref, species_ref, centers_ref, shift_ref, sems = refs
    count = len(refs) // 2
    pairs_in = [
        (species_hbm, species_ref),
        (centers_hbm, centers_ref),
        (shift_hbm, shift_ref),
        *zip(refs[:count], refs[count:]),
    ]
    copies = [
        pltpu.make_async_copy(source, target, sems.at[i])
        for i, (source, target) in enumerate(pairs_in)
    ]
    for copy in copies:
        copy.start()
    for copy in copies:
        copy.wait()
    owned = centers_ref.shape[1]
    shift_row = jnp.zeros((1, 128), F32)
    for cell in range(OWN_CELLS):
        species = species_ref[cell // 2, 0, cell % 2 : cell % 2 + 1, :]
        shift = jnp.zeros(species.shape, F32)
        for s in range(shift_ref.shape[0]):
            shift = jnp.where(species == s, shift_ref[s], shift)
        shift_row = shift_row + lane_row(shift, cell * SITES)
    chosen = lax.broadcasted_iota(jnp.int32, (owned, owned), 0) == centers_ref[...]
    occupied = jnp.sum(jnp.where(chosen, 1.0, 0.0), axis=1, keepdims=True) > 0.5
    column = jnp.where(occupied, jnp.ones((owned, 128), F32), 0.0)
    shift_row_ref[...] = shift_row[:, :owned] * jnp.transpose(column)[0:1]


def finish_kernel(mine_ref, shift_row_ref, *refs):
    *near_refs, energy_ref, forces_ref, virial_ref = refs
    owned = near_refs[0].shape[1]
    total = mine_ref[:, :owned]
    for near_ref in near_refs:
        total = total + near_ref[...]
    energy = total[12:13] + shift_row_ref[...]
    columns = jnp.transpose(jnp.concatenate([total, jnp.zeros((ORDERS, 128 - owned), F32)], axis=1))
    for cell in range(OWN_CELLS):
        x, z = cell // 2, cell % 2
        lanes = slice(cell * SITES, (cell + 1) * SITES)
        energy_ref[x, 0, z : z + 1, :] = energy[:, lanes]
        for c in range(3):
            forces_ref[c, x, 0, z : z + 1, :] = total[c : c + 1, lanes]
        virial_ref[x, 0, z] = columns[lanes, 3:12]


def force_kernel(kind, nbr, here_ref, last_x_ref, *refs):
    near_side_refs = refs[: 2 * kind - 2]
    (
        next_z_ref,
        center_weight_ref,
        near_weight_ref,
        basis_weight_ref,
        path_weight_ref,
        value_weight_ref,
        latent_weight_ref,
        out_weight_ref,
        keep_ref,
        send_ref,
    ) = refs[2 * kind - 2 :]
    height, width = here_ref.shape
    owned = OWN_CELLS * SITES
    center_sides = 2 if kind == 2 else 1
    kept_sides = 1 if kind == 2 else kind
    own_pairs = owned * nbr
    pairs = center_sides * own_pairs
    centers = center_sides * owned
    radial = basis_weight_ref.shape[0]
    span = GROUP * nbr
    groups = centers // GROUP
    sites = SITES
    root_count = math.sqrt(nbr)
    root_three = math.sqrt(3.0)
    root_fifteen = math.sqrt(15.0)
    root_five = math.sqrt(5.0)
    far = next_z_ref[...]
    mains = [here_ref[...], last_x_ref[...], far[:height], far[height : 2 * height]]
    near_sides = [ref[...] for ref in near_side_refs]
    far_sides = far[2 * height :]
    far_sides = [far_sides[i * height : (i + 1) * height] for i in range(2 * kind - 2)]
    blocks_in = [
        [mains[0], *near_sides[0::2]],
        [mains[1], *near_sides[1::2]],
        [mains[2], *far_sides[0::2]],
        [mains[3], *far_sides[1::2]],
    ]
    feats = jnp.concatenate([side[:owned] for block in blocks_in for side in block], axis=0)
    known = feats.shape[0]
    center_feats = []
    center_coords = []
    coords = []
    scales = []
    codes = []
    cell_row = lax.broadcasted_iota(jnp.int32, (kind * OWN_CELLS, 128), 0) % OWN_CELLS
    tile_lane = lax.broadcasted_iota(jnp.int32, (kind * OWN_CELLS, 128), 1)
    for g, block in enumerate(blocks_in):
        behind_x, ahead_z = g % 2, g // 2
        rows = jnp.concatenate([side[owned : owned + OWN_CELLS] for side in block], axis=0)
        corner_x = (cell_row // 2 + 2 - 2 * behind_x).astype(F32) * CELL_SIDE
        corner_z = (cell_row % 2 + 2 * ahead_z).astype(F32) * CELL_SIDE
        corner = jnp.where(
            tile_lane < sites, corner_x, jnp.where(tile_lane < 2 * sites, 0.0, corner_z)
        )
        coords.append(rows + corner)
    for c in range(center_sides):
        for g, block in enumerate(blocks_in):
            cell = g % 2 * 2 + 1 - g // 2
            row = c * OWN_CELLS + cell
            center_feats.append(block[c][cell * sites : (cell + 1) * sites])
            scales.append(block[c][owned + cell : owned + cell + 1])
            center_coords.append(coords[g][row : row + 1])
            start = owned + OWN_CELLS + (1 - g // 2) * span // 128
            codes.extend(block[c][start + r : start + r + 1] for r in range(span // 128))
    center_feats = jnp.concatenate(center_feats, axis=0)
    coords = jnp.concatenate(coords, axis=0)
    code = jnp.concatenate(codes, axis=1).astype(jnp.int32)
    live = code > 0
    code = jnp.maximum(code - 1, 0)
    side_y = ((code >> 10) - 1).astype(F32)
    near_row = code & 1023
    if center_sides == 2:
        pair_lane = lax.broadcasted_iota(jnp.int32, (1, pairs), 1)
        near_row = jnp.where(pair_lane < own_pairs, near_row, near_row ^ owned)
    near_row = jnp.where(live, near_row, known)

    def place_rows(cell_rows):
        count = cell_rows.shape[0] * sites
        spread = jnp.broadcast_to(cell_rows[:, None, :], (cell_rows.shape[0], sites, 128))
        spread = spread.reshape(count, 128)
        lane = lax.broadcasted_iota(jnp.int32, (count, 128), 1)
        row = lax.broadcasted_iota(jnp.int32, (count, 128), 0)
        keep = (lane % sites == row % sites) & (lane < 3 * sites)
        spread = jnp.transpose(jnp.where(keep, spread, 0.0))
        return jnp.concatenate(split3(spread[: 3 * sites]), axis=0)

    place_parts = place_rows(coords)
    center_parts = place_rows(jnp.concatenate(center_coords, axis=0))

    value_rows = stacked(*split(jnp.transpose(value_weight_ref[...])))
    latent_high_t, latent_low_t = split(0.5 * jnp.transpose(latent_weight_ref[...]))
    latent_both_t = jnp.concatenate([latent_high_t, latent_low_t], axis=0)
    latent_rows = stacked(*split(latent_weight_ref[...] * out_weight_ref[...]))
    value_high, value_low = split(value_weight_ref[...])
    value_both = jnp.concatenate([value_high, value_low], axis=0)
    basis_t = jnp.transpose(basis_weight_ref[...])
    basis_high_t, basis_low_t = split(0.5 * basis_t)
    basis_rows = stacked(*split(basis_weight_ref[...]))

    def project(weight, rows):
        weight = stacked(*split(jnp.transpose(weight)))
        return folded(mm_nt(weight, jnp.concatenate(split(rows), axis=1)))

    near_t = project(near_weight_ref[...], feats)
    own_t = project(center_weight_ref[...], center_feats)
    near_high, near_low = split(0.5 * near_t)
    own_high, own_low = split(0.5 * own_t)
    near_lookup = jnp.concatenate([near_high, near_low], axis=0)
    rest_lookup = jnp.concatenate(
        [own_high, own_low, basis_high_t, basis_high_t, basis_low_t], axis=1
    )
    scale_rows = jnp.concatenate(scales, axis=0)
    scale_parts = jnp.concatenate(
        [*split3(scale_rows), jnp.zeros((-3 * groups % 16, 128), BF16)], axis=0
    )

    path_rows = jnp.concatenate(
        [jnp.broadcast_to(path_weight_ref[l : l + 1, :], (GROUP, width)) for l in LEVELS], axis=0
    ) * (1.0 / root_count)
    out_column = jnp.transpose(jnp.broadcast_to(out_weight_ref[...], (width, width)))
    out_column = jnp.concatenate([out_column] * (pairs // width), axis=1)

    site_ids = lax.broadcasted_iota(jnp.int32, (known, pairs), 0)
    slot_ids = lax.broadcasted_iota(jnp.int32, (centers, pairs), 0)
    slot_row = lax.broadcasted_iota(jnp.int32, (1, pairs), 1) // nbr
    group_lane = lax.broadcasted_iota(jnp.int32, (GROUP, pairs), 1) // nbr % GROUP
    group_mask = group_lane == lax.broadcasted_iota(jnp.int32, (GROUP, pairs), 0)
    group_mask = jnp.where(group_mask, 1.0, 0.0)
    tall = len(LEVELS) * GROUP
    order = lax.broadcasted_iota(jnp.int32, (radial, pairs), 0).astype(F32) + 1.0
    lanes = [slice(g * span, (g + 1) * span) for g in range(groups)]

    pick = jnp.where(site_ids == near_row, 1.0, 0.0)
    pick_half = pick.astype(BF16)
    slot_half = jnp.where(slot_ids == slot_row, 1.0, 0.0).astype(BF16)

    moved = mm(place_parts, pick_half) - mm(center_parts, slot_half)
    moved = moved[: 3 * sites] + moved[3 * sites : 6 * sites] + moved[6 * sites :]
    dx = jnp.where(live, jnp.sum(moved[:sites], axis=0, keepdims=True), 6.0)
    dy = jnp.sum(moved[sites : 2 * sites], axis=0, keepdims=True) + CELL_SIDE * side_y
    dy = jnp.where(live, dy, 0.0)
    dz = jnp.where(live, jnp.sum(moved[2 * sites :], axis=0, keepdims=True), 0.0)
    length = jnp.sqrt(dx * dx + dy * dy + dz * dz)
    inverse = 1.0 / length
    ratio = length * (1.0 / CUTOFF)
    inside = live & (ratio < 1.0)
    r2 = ratio * ratio
    r5 = r2 * r2 * ratio
    r6 = r5 * ratio
    weight = jnp.where(inside, 1.0 - r6 * (28.0 - 48.0 * ratio + 21.0 * r2), 0.0)
    slope = jnp.where(inside, -168.0 * r5 * (1.0 - 2.0 * ratio + r2), 0.0)
    sine, cosine = sin_cos_pi(order * ratio)
    basis = (math.sqrt(2.0 / CUTOFF) * inverse) * sine
    basis_slope = (math.sqrt(2.0 / CUTOFF) * inverse) * (
        (math.pi / CUTOFF) * order * cosine - sine * inverse
    )
    ex = dx * inverse
    ey = dy * inverse
    ez = dz * inverse
    angular = jnp.concatenate(
        [
            jnp.ones_like(ex),
            root_three * ex,
            root_three * ey,
            root_three * ez,
            root_fifteen * ex * ey,
            root_fifteen * ey * ez,
            0.5 * root_five * (3.0 * ez * ez - 1.0),
            root_fifteen * ex * ez,
            0.5 * root_fifteen * (ex * ex - ey * ey),
        ],
        axis=0,
    )
    angular_high, angular_low = halves(angular)
    angular_low = angular_low.astype(BF16).astype(F32)
    block_high = [angular_high[m : m + 1] * group_mask for m in range(len(LEVELS))]
    block_low = [angular_low[m : m + 1] * group_mask for m in range(len(LEVELS))]
    blocks = jnp.concatenate(block_high + block_low + block_high, axis=0).astype(BF16)
    lane_ids = lax.broadcasted_iota(jnp.int32, (128, span), 0)
    lane_slot = lax.broadcasted_iota(jnp.int32, (128, span), 1) // nbr + 3 * sites
    scale = mm(scale_parts, jnp.where(lane_ids == lane_slot, 1.0, 0.0).astype(BF16))
    scale = scale[:groups] + scale[groups : 2 * groups] + scale[2 * groups : 3 * groups]
    scale = jnp.concatenate([scale[g : g + 1] for g in range(groups)], axis=1)
    scale = scale * (1.0 / root_count)
    pull = ROOT_HALF * scale

    basis_high, basis_low = halves(basis)
    basis_rest = jnp.concatenate([basis_high, basis_low, basis_high], axis=0).astype(BF16)
    before = folded(mm(near_lookup, pick_half)) + mm(
        rest_lookup, jnp.concatenate([slot_half, slot_half, basis_rest], axis=0)
    )
    gate = 1.0 + jnp.tanh(before)
    active = before * gate
    latent = weight * active
    latent_high, latent_low = split(latent)
    mixed = folded(mm(value_rows, jnp.concatenate([latent_high, latent_low], axis=0)))
    values = mixed[:width]
    env_high, env_low = split(mixed[width:])

    def over_pairs(high, low):
        sums = []
        for cut in lanes:
            both = jnp.concatenate([high[:, cut], low[:, cut]], axis=0)
            quad = mm_nt(blocks[: 2 * tall, cut], both)
            quad = quad[:tall, :width] + quad[tall:, :width] + quad[:tall, width:]
            sums.append(quad * path_rows)
        return sums

    def over_orders(tables):
        parts = []
        for table, cut in zip(tables, lanes):
            high, low = halves(table)
            table = jnp.transpose(jnp.concatenate([high, high, low], axis=0)).astype(BF16)
            parts.append(mm(table, blocks[:, cut]))
        return jnp.concatenate(parts, axis=1)

    weighted = over_pairs(env_high, env_low)
    inner = over_orders(weighted)
    scalars = values * inner
    scalars_high, scalars_low = split(scalars)
    z = full_depth(
        latent_both_t,
        latent_high_t,
        jnp.concatenate([latent_high, scalars_high], axis=0),
        jnp.concatenate([latent_low, scalars_low], axis=0),
    )
    z_gate = 1.0 + jnp.tanh(z)
    update = z * z_gate
    update_sum = jnp.sum(update * out_column, axis=0, keepdims=True)
    active_sum = jnp.sum(
        active[:, :own_pairs] * out_column[:, :own_pairs], axis=0, keepdims=True
    )
    pair_energy = (active_sum + update_sum[:, :own_pairs]) * (pull * weight)[:, :own_pairs]
    d_z = (0.5 * pull * weight) * (z_gate + update * (2.0 - z_gate))
    spread_back = half_depth(latent_rows, d_z)
    d_scalars = spread_back[width:]
    d_values = d_scalars * inner
    dinner_high, dinner_low = split(d_scalars * values)
    d_embed = over_pairs(dinner_high, dinner_low)
    d_env = over_orders(d_embed)

    d_angular = []
    for g, cut in enumerate(lanes):
        sides_high, sides_low = halves(jnp.concatenate([weighted[g], d_embed[g]], axis=1))
        d_block = full_depth(
            jnp.concatenate([sides_high, sides_low], axis=0).astype(BF16),
            sides_high.astype(BF16),
            jnp.concatenate([dinner_high[:, cut], env_high[:, cut]], axis=0),
            jnp.concatenate([dinner_low[:, cut], env_low[:, cut]], axis=0),
        )
        d_block = d_block.reshape(len(LEVELS), GROUP, span) * group_mask[None, :, cut]
        d_angular.append(jnp.sum(d_block, axis=1))
    d_angular = jnp.concatenate(d_angular, axis=1)

    mixed_high, mixed_low = split(jnp.concatenate([d_values, d_env], axis=0))
    d_latent = (
        full_depth(value_both, value_high, mixed_high, mixed_low)
        + spread_back[:width]
        + pull * out_column
    )
    d_weight = jnp.sum(d_latent * active, axis=0, keepdims=True) + pull * update_sum
    d_before = d_latent * (gate + active * (2.0 - gate))
    d_basis = half_depth(basis_rows, d_before) * (0.5 * weight)

    d_length = jnp.sum(d_basis * basis_slope, axis=0, keepdims=True) + d_weight * slope * (
        1.0 / CUTOFF
    )
    a1, a2, a3, a4, a5, a6, a7, a8 = [d_angular[m : m + 1] for m in range(1, 9)]
    ux = root_three * a1 + root_fifteen * (ey * a4 + ez * a7 + ex * a8)
    uy = root_three * a2 + root_fifteen * (ex * a4 + ez * a5 - ey * a8)
    uz = root_three * a3 + root_fifteen * (ey * a5 + ex * a7) + 3.0 * root_five * ez * a6
    along = ex * ux + ey * uy + ez * uz
    radial_part = d_length - along * inverse
    gx = ux * inverse + ex * radial_part
    gy = uy * inverse + ey * radial_part
    gz = uz * inverse + ez * radial_part
    hx = -0.5 * dx
    hy = -0.5 * dy
    hz = -0.5 * dz
    virial = [hx * gx, hx * gy, hx * gz, hy * gx, hy * gy, hy * gz, hz * gx, hz * gy, hz * gz]
    rest = [jnp.zeros((ORDERS - 13, pairs), F32)]
    near_terms = jnp.concatenate(
        [-gx, -gy, -gz, *virial, jnp.zeros_like(gx), *rest], axis=0
    )
    center_rows = [gx, gy, gz, *virial]
    center_rows = [r[:, :own_pairs] for r in center_rows] + [pair_energy]
    center_rows.append(jnp.zeros((ORDERS - 13, own_pairs), F32))
    center_terms = jnp.concatenate(center_rows, axis=0)
    reach = []
    for x, z, side in np.ndindex(2, 2, kept_sides):
        start = ((2 * z + x) * kind + side) * owned
        reach.append(pick_half[start : start + owned])
    reach = jnp.concatenate(reach, axis=0)
    near_sums = mm_nt(jnp.concatenate(split(near_terms), axis=0), reach)
    center_sums = mm_nt(
        jnp.concatenate(split(center_terms), axis=0), slot_half[:owned, :own_pairs]
    )
    center_sums = jnp.concatenate(
        [folded(center_sums), jnp.zeros((ORDERS, 128 - owned), F32)], axis=1
    )
    totals = folded(near_sums)
    lane = lax.broadcasted_iota(jnp.int32, (ORDERS, 128), 1)
    known = totals.shape[1]
    tiles = [totals[:, 128 * i : 128 * (i + 1)] for i in range(known // 128)]
    for g in range(owned // GROUP):
        cell = g % 2 * 2 + 1 - g // 2
        target = (g % 2 * 2 + g // 2) * kept_sides * owned + cell * sites
        turn = (target - g * GROUP) % 128
        piece = pltpu.roll(center_sums, turn, 1) if turn else center_sums
        begin = target % 128
        piece = jnp.where((lane >= begin) & (lane < begin + GROUP), piece, 0.0)
        tiles[target // 128] = tiles[target // 128] + piece
    totals = jnp.concatenate(tiles, axis=1)
    keep_ref[...] = totals[:, : known // 2]
    send_ref[...] = totals[:, known // 2 :]


def in_hbm(*arrays):
    return [pltpu.with_memory_space_constraint(array, pltpu.HBM) for array in arrays]


def joined(parts):
    total = sum(part.shape[0] for part in parts)
    start = 0
    pads = []
    for part in parts:
        end = start + part.shape[0]
        pads.append(jnp.pad(part, ((start, total - end), (0, 0))))
        start = end
    return functools.reduce(jnp.add, pads)


def local(
    positions,
    features,
    species,
    centers,
    neighbours,
    counts,
    species_scale,
    species_shift,
    center_weight,
    near_weight,
    basis_weight,
    path_weight,
    value_weight,
    latent_weight,
    out_weight,
):
    cells_x, cells_y, cells_z, sites, width = features.shape
    cell_count = cells_x * cells_y * cells_z
    owned = cell_count * sites
    assert (cells_x, cells_y, cells_z, sites) == (2, 1, 2, SITES)
    pairs = neighbours.size
    nbr = pairs // owned
    kind = min(3, lax.axis_size("gy"))

    def moved(array, steps):
        names = tuple(steps)
        sizes = [lax.axis_size(name) for name in names]
        route = []
        for at in np.ndindex(*sizes):
            to = [(p + steps[name]) % size for p, name, size in zip(at, names, sizes)]
            route.append(
                (int(np.ravel_multi_index(at, sizes)), int(np.ravel_multi_index(to, sizes)))
            )
        return lax.ppermute(array, names, route)

    vmem = pl.BlockSpec(memory_space=pltpu.VMEM)
    hbm = pl.BlockSpec(memory_space=pltpu.HBM)
    listed = centers.reshape(1, owned)
    payload = jax.ShapeDtypeStruct((owned + OWN_CELLS + pairs // 256, width), F32)
    low, high = pl.pallas_call(
        functools.partial(pack_kernel, kind),
        out_shape=(payload, payload),
        in_specs=[hbm] * 6,
        out_specs=(vmem, vmem),
        scratch_shapes=[
            pltpu.VMEM((owned, 128), F32),
            pltpu.VMEM(positions.shape, F32),
            pltpu.VMEM(species.shape, jnp.int32),
            pltpu.VMEM(listed.shape, jnp.int32),
            pltpu.VMEM(neighbours.shape, jnp.int32),
            pltpu.SMEM(species_scale.shape, F32),
            pltpu.SemaphoreType.DMA((6,)),
        ],
        compiler_params=pltpu.CompilerParams(vmem_limit_bytes=8 * 1024 * 1024),
        name="pack_payload",
    )(
        *in_hbm(
            positions,
            features.reshape(owned, width),
            species,
            listed,
            neighbours,
            species_scale,
        )
    )
    weights = (
        center_weight,
        near_weight,
        basis_weight,
        path_weight,
        value_weight,
        latent_weight,
        out_weight.reshape(1, width),
    )
    *weights, shift_row = pl.pallas_call(
        fetch_kernel,
        out_shape=(
            *(jax.ShapeDtypeStruct(w.shape, F32) for w in weights),
            jax.ShapeDtypeStruct((1, owned), F32),
        ),
        in_specs=[hbm] * (3 + len(weights)),
        out_specs=(vmem,) * (1 + len(weights)),
        scratch_shapes=[
            pltpu.VMEM(species.shape, jnp.int32),
            pltpu.VMEM(listed.shape, jnp.int32),
            pltpu.SMEM(species_shift.shape, F32),
            pltpu.SemaphoreType.DMA((3 + len(weights),)),
        ],
        compiler_params=pltpu.CompilerParams(vmem_limit_bytes=8 * 1024 * 1024),
        name="fetch_weights",
    )(*in_hbm(species, listed, species_shift, *weights))
    last_x = moved(high, {"gx": 1})
    sides = []
    for step in (-1, 1)[: kind - 1]:
        sides.append(moved(high, {"gx": 1, "gy": step}))
        sides.insert(-1, moved(low, {"gy": step}))
    next_z = moved(joined([low, last_x, *sides]), {"gz": -1})
    kept = 1 if kind == 2 else kind
    half = 2 * kept * owned
    keep, send = pl.pallas_call(
        functools.partial(force_kernel, kind, nbr),
        out_shape=(
            jax.ShapeDtypeStruct((ORDERS, half), F32),
            jax.ShapeDtypeStruct((ORDERS, half), F32),
        ),
        in_specs=[vmem] * (8 + 2 * kind),
        out_specs=(vmem, vmem),
        compiler_params=pltpu.CompilerParams(vmem_limit_bytes=44 * 1024 * 1024),
        name="pair_forces",
    )(
        low,
        last_x,
        *sides,
        next_z,
        *weights,
    )
    totals = keep + moved(send, {"gx": -1})

    def part(index):
        return totals[:, index * owned : (index + 1) * owned]

    back = [moved(part(kept), {"gz": 1})]
    for i, step in enumerate((1, -1)[: kept - 1]):
        back.append(moved(part(kept + 1 + i), {"gy": step, "gz": 1}))
        back.append(moved(part(1 + i), {"gy": step}))
    site_energy, forces, virial = pl.pallas_call(
        finish_kernel,
        out_shape=(
            jax.ShapeDtypeStruct(species.shape, F32),
            jax.ShapeDtypeStruct(positions.shape, F32),
            jax.ShapeDtypeStruct((*species.shape, 9), F32),
        ),
        in_specs=[vmem] * (2 + len(back)),
        out_specs=(vmem, vmem, vmem),
        compiler_params=pltpu.CompilerParams(vmem_limit_bytes=8 * 1024 * 1024),
        name="write_outputs",
    )(totals, shift_row, *back)
    return (site_energy, forces, jnp.transpose(virial, (4, 0, 1, 2, 3)))


def solution(mesh):
    placed = (
        P(None, "gx", "gy", "gz", None),
        P("gx", "gy", "gz", None, None),
        P("gx", "gy", "gz", None),
        P(("gx", "gy", "gz")),
        P(("gx", "gy", "gz"), None),
        P(("gx", "gy", "gz")),
        P(),
        P(),
        P(),
        P(),
        P(),
        P(),
        P(),
        P(),
        P(),
    )
    return jax.shard_map(
        local,
        mesh=mesh,
        in_specs=placed,
        out_specs=(
            P("gx", "gy", "gz", None),
            P(None, "gx", "gy", "gz", None),
            P(None, "gx", "gy", "gz", None),
        ),
        check_vma=False,
    )
```

```python
import functools
import math

import jax
import jax.numpy as jnp
import numpy as np
from jax import lax
from jax.experimental import pallas as pl
from jax.experimental.pallas import tpu as pltpu
from jax.sharding import PartitionSpec as P

EXACT_DOT = lax.Precision.HIGHEST
CUTOFF = 5.0
CELL_SIDE = 4.6
ROOT_HALF = 0.7071067811865476
GROUP = 8
ORDERS = 16
LEVELS = (0, 1, 1, 1, 2, 2, 2, 2, 2)
SITES = 8
OWN_CELLS = 4
FRAME_CELLS = 48
F32 = jnp.float32
BF16 = jnp.bfloat16


def split(value):
    high = value.astype(BF16)
    low = (value - high.astype(F32)).astype(BF16)
    return high, low


def split3(value):
    high = value.astype(BF16)
    rest = value - high.astype(F32)
    middle = rest.astype(BF16)
    low = (rest - middle.astype(F32)).astype(BF16)
    return high, middle, low


def halves(value):
    high = value.astype(BF16).astype(F32)
    return high, value - high


def mm(a, b):
    return lax.dot_general(a, b, (((1,), (0,)), ((), ())), preferred_element_type=F32)


def mm_nt(a, b):
    return lax.dot_general(a, b, (((1,), (1,)), ((), ())), preferred_element_type=F32)


def stacked(high, low):
    top = jnp.concatenate([high, high], axis=1)
    bottom = jnp.concatenate([low, jnp.zeros_like(low)], axis=1)
    return jnp.concatenate([top, bottom], axis=0)


def folded(product):
    half = product.shape[0] // 2
    return product[:half] + product[half:]


def half_depth(weights, value):
    return folded(mm(weights, jnp.concatenate(split(value), axis=0)))


def full_depth(both, high, value_high, value_low):
    return folded(mm(both, value_high)) + mm(high, value_low)


def sin_cos_pi(turns):
    near = turns - 2.0 * jnp.round(turns * 0.5)
    quarter = jnp.round(near * 2.0)
    v = (near - 0.5 * quarter) * math.pi
    v2 = v * v
    s = v * (
        1.0
        + v2
        * (-1.0 / 6 + v2 * (1.0 / 120 + v2 * (-1.0 / 5040 + v2 * (1.0 / 362880 - v2 / 39916800))))
    )
    c = 1.0 + v2 * (
        -0.5
        + v2
        * (1.0 / 24 + v2 * (-1.0 / 720 + v2 * (1.0 / 40320 + v2 * (-1.0 / 3628800 + v2 / 479001600))))
    )
    odd = jnp.abs(quarter) == 1.0
    sine = jnp.where(odd, quarter * c, jnp.where(quarter == 0.0, s, -s))
    cosine = jnp.where(odd, -quarter * s, jnp.where(quarter == 0.0, c, -c))
    return sine, cosine


def lane_row(piece, offset):
    row = jnp.concatenate([piece, jnp.zeros((1, 128 - piece.shape[1]), piece.dtype)], axis=1)
    return pltpu.roll(row, offset, 1) if offset else row


def pack_kernel(
    kind,
    positions_hbm,
    features_hbm,
    species_hbm,
    centers_hbm,
    neighbours_hbm,
    scale_hbm,
    low_ref,
    high_ref,
    wide_ref,
    positions_ref,
    species_ref,
    centers_ref,
    neighbours_ref,
    scale_ref,
    sems,
):
    owned, nbr = neighbours_ref.shape
    per_row = 128 // nbr
    pairs_in = (
        (features_hbm, low_ref.at[pl.ds(0, owned), :]),
        (neighbours_hbm, neighbours_ref),
        (centers_hbm, centers_ref),
        (positions_hbm, positions_ref),
        (species_hbm, species_ref),
        (scale_hbm, scale_ref),
    )
    copies = [
        pltpu.make_async_copy(source, target, sems.at[i])
        for i, (source, target) in enumerate(pairs_in)
    ]
    for copy in copies:
        copy.start()
    for copy in copies:
        copy.wait()
    for cell in range(OWN_CELLS):
        x, z = cell // 2, cell % 2
        species = species_ref[x, 0, z : z + 1, :]
        scale = jnp.zeros(species.shape, F32)
        for s in range(scale_ref.shape[0]):
            scale = jnp.where(species == s, scale_ref[s], scale)
        row = lane_row(scale, 3 * SITES)
        for c in range(3):
            row = row + lane_row(positions_ref[c, x, 0, z : z + 1, :], c * SITES)
        low_ref[owned + cell : owned + cell + 1] = row

    chosen = lax.broadcasted_iota(jnp.int32, (owned, owned), 0) == centers_ref[...]
    chosen = jnp.where(chosen, 1.0, 0.0)
    occupied = jnp.sum(chosen, axis=1, keepdims=True) > 0.5
    chosen = chosen.astype(BF16)
    rows = neighbours_ref[...]
    upper = mm(chosen, (rows >> 4).astype(F32).astype(BF16))
    lower = mm(chosen, (rows & 15).astype(F32).astype(BF16))
    rows = (upper * 16.0 + lower).astype(jnp.int32)
    live = occupied & (rows < FRAME_CELLS * SITES)
    slot = lax.broadcasted_iota(jnp.int32, (owned, nbr), 0)
    cell = slot >> 3
    site = rows & 7
    place = rows >> 3
    near_z = (place & 3) + 1 - 2 * (cell & 1)
    column = place >> 2
    frame_x = (column * 11) >> 5
    frame_y = column - 3 * frame_x
    near_x = frame_x + 1 - 2 * (cell >> 1)
    side = jnp.where(frame_y == 1, 0, jnp.where(frame_y == 2, 1, kind - 1))
    block = (near_z >> 1) * 2 + 1 - (near_x >> 1)
    where = (block * kind + side) * owned + (near_x & 1) * 16 + (near_z & 1) * 8 + site
    code = jnp.where(live, 1 + where + (frame_y << 10), 0).astype(F32)
    wide_ref[...] = jnp.concatenate([code, jnp.zeros((owned, 128 - nbr), F32)], axis=1)
    codes = wide_ref[pl.ds(0, owned // per_row, stride=per_row), :]
    for j in range(1, per_row):
        more = wide_ref[pl.ds(j, owned // per_row, stride=per_row), :]
        codes = codes + pltpu.roll(more, j * nbr, 1)
    tile = owned + OWN_CELLS
    low_ref[tile:] = codes[: codes.shape[0] // 2]
    high_ref[:tile] = low_ref[:tile]
    high_ref[tile:] = codes[codes.shape[0] // 2 :]


def fetch_kernel(species_hbm, centers_hbm, shift_hbm, *refs):
    *refs, shift_row_ref, species_ref, centers_ref, shift_ref, sems = refs
    count = len(refs) // 2
    pairs_in = [
        (species_hbm, species_ref),
        (centers_hbm, centers_ref),
        (shift_hbm, shift_ref),
        *zip(refs[:count], refs[count:]),
    ]
    copies = [
        pltpu.make_async_copy(source, target, sems.at[i])
        for i, (source, target) in enumerate(pairs_in)
    ]
    for copy in copies:
        copy.start()
    for copy in copies:
        copy.wait()
    owned = centers_ref.shape[1]
    shift_row = jnp.zeros((1, 128), F32)
    for cell in range(OWN_CELLS):
        species = species_ref[cell // 2, 0, cell % 2 : cell % 2 + 1, :]
        shift = jnp.zeros(species.shape, F32)
        for s in range(shift_ref.shape[0]):
            shift = jnp.where(species == s, shift_ref[s], shift)
        shift_row = shift_row + lane_row(shift, cell * SITES)
    chosen = lax.broadcasted_iota(jnp.int32, (owned, owned), 0) == centers_ref[...]
    occupied = jnp.sum(jnp.where(chosen, 1.0, 0.0), axis=1, keepdims=True) > 0.5
    column = jnp.where(occupied, jnp.ones((owned, 128), F32), 0.0)
    shift_row_ref[...] = shift_row[:, :owned] * jnp.transpose(column)[0:1]


def finish_kernel(mine_ref, shift_row_ref, *refs):
    *near_refs, energy_ref, forces_ref, virial_ref = refs
    owned = near_refs[0].shape[1]
    total = mine_ref[:, :owned]
    for near_ref in near_refs:
        total = total + near_ref[...]
    energy = total[12:13] + shift_row_ref[...]
    columns = jnp.transpose(jnp.concatenate([total, jnp.zeros((ORDERS, 128 - owned), F32)], axis=1))
    for cell in range(OWN_CELLS):
        x, z = cell // 2, cell % 2
        lanes = slice(cell * SITES, (cell + 1) * SITES)
        energy_ref[x, 0, z : z + 1, :] = energy[:, lanes]
        for c in range(3):
            forces_ref[c, x, 0, z : z + 1, :] = total[c : c + 1, lanes]
        virial_ref[x, 0, z] = columns[lanes, 3:12]


def force_kernel(kind, nbr, here_ref, last_x_ref, *refs):
    near_side_refs = refs[: 2 * kind - 2]
    (
        next_z_ref,
        center_weight_ref,
        near_weight_ref,
        basis_weight_ref,
        path_weight_ref,
        value_weight_ref,
        latent_weight_ref,
        out_weight_ref,
        keep_ref,
        send_ref,
    ) = refs[2 * kind - 2 :]
    height, width = here_ref.shape
    owned = OWN_CELLS * SITES
    center_sides = 2 if kind == 2 else 1
    kept_sides = 1 if kind == 2 else kind
    own_pairs = owned * nbr
    pairs = center_sides * own_pairs
    centers = center_sides * owned
    radial = basis_weight_ref.shape[0]
    span = GROUP * nbr
    groups = centers // GROUP
    sites = SITES
    root_count = math.sqrt(nbr)
    root_three = math.sqrt(3.0)
    root_fifteen = math.sqrt(15.0)
    root_five = math.sqrt(5.0)
    far = next_z_ref[...]
    mains = [here_ref[...], last_x_ref[...], far[:height], far[height : 2 * height]]
    near_sides = [ref[...] for ref in near_side_refs]
    far_sides = far[2 * height :]
    far_sides = [far_sides[i * height : (i + 1) * height] for i in range(2 * kind - 2)]
    blocks_in = [
        [mains[0], *near_sides[0::2]],
        [mains[1], *near_sides[1::2]],
        [mains[2], *far_sides[0::2]],
        [mains[3], *far_sides[1::2]],
    ]
    feats = jnp.concatenate([side[:owned] for block in blocks_in for side in block], axis=0)
    known = feats.shape[0]
    center_feats = []
    center_coords = []
    coords = []
    scales = []
    codes = []
    cell_row = lax.broadcasted_iota(jnp.int32, (kind * OWN_CELLS, 128), 0) % OWN_CELLS
    tile_lane = lax.broadcasted_iota(jnp.int32, (kind * OWN_CELLS, 128), 1)
    for g, block in enumerate(blocks_in):
        behind_x, ahead_z = g % 2, g // 2
        rows = jnp.concatenate([side[owned : owned + OWN_CELLS] for side in block], axis=0)
        corner_x = (cell_row // 2 + 2 - 2 * behind_x).astype(F32) * CELL_SIDE
        corner_z = (cell_row % 2 + 2 * ahead_z).astype(F32) * CELL_SIDE
        corner = jnp.where(
            tile_lane < sites, corner_x, jnp.where(tile_lane < 2 * sites, 0.0, corner_z)
        )
        coords.append(rows + corner)
    for c in range(center_sides):
        for g, block in enumerate(blocks_in):
            cell = g % 2 * 2 + 1 - g // 2
            row = c * OWN_CELLS + cell
            center_feats.append(block[c][cell * sites : (cell + 1) * sites])
            scales.append(block[c][owned + cell : owned + cell + 1])
            center_coords.append(coords[g][row : row + 1])
            start = owned + OWN_CELLS + (1 - g // 2) * span // 128
            codes.extend(block[c][start + r : start + r + 1] for r in range(span // 128))
    center_feats = jnp.concatenate(center_feats, axis=0)
    coords = jnp.concatenate(coords, axis=0)
    code = jnp.concatenate(codes, axis=1).astype(jnp.int32)
    live = code > 0
    code = jnp.maximum(code - 1, 0)
    side_y = ((code >> 10) - 1).astype(F32)
    near_row = code & 1023
    if center_sides == 2:
        pair_lane = lax.broadcasted_iota(jnp.int32, (1, pairs), 1)
        near_row = jnp.where(pair_lane < own_pairs, near_row, near_row ^ owned)
    near_row = jnp.where(live, near_row, known)

    def place_rows(cell_rows):
        count = cell_rows.shape[0] * sites
        spread = jnp.broadcast_to(cell_rows[:, None, :], (cell_rows.shape[0], sites, 128))
        spread = spread.reshape(count, 128)
        lane = lax.broadcasted_iota(jnp.int32, (count, 128), 1)
        row = lax.broadcasted_iota(jnp.int32, (count, 128), 0)
        keep = (lane % sites == row % sites) & (lane < 3 * sites)
        spread = jnp.transpose(jnp.where(keep, spread, 0.0))
        return jnp.concatenate(split3(spread[: 3 * sites]), axis=0)

    place_parts = place_rows(coords)
    center_parts = place_rows(jnp.concatenate(center_coords, axis=0))

    value_rows = stacked(*split(jnp.transpose(value_weight_ref[...])))
    latent_high_t, latent_low_t = split(0.5 * jnp.transpose(latent_weight_ref[...]))
    latent_both_t = jnp.concatenate([latent_high_t, latent_low_t], axis=0)
    latent_rows = stacked(*split(latent_weight_ref[...] * out_weight_ref[...]))
    value_high, value_low = split(value_weight_ref[...])
    value_both = jnp.concatenate([value_high, value_low], axis=0)
    basis_t = jnp.transpose(basis_weight_ref[...])
    basis_high_t, basis_low_t = split(0.5 * basis_t)
    basis_rows = stacked(*split(basis_weight_ref[...]))

    def project(weight, rows):
        weight = stacked(*split(jnp.transpose(weight)))
        return folded(mm_nt(weight, jnp.concatenate(split(rows), axis=1)))

    near_t = project(near_weight_ref[...], feats)
    own_t = project(center_weight_ref[...], center_feats)
    near_high, near_low = split(0.5 * near_t)
    own_high, own_low = split(0.5 * own_t)
    near_lookup = jnp.concatenate([near_high, near_low], axis=0)
    rest_lookup = jnp.concatenate(
        [own_high, own_low, basis_high_t, basis_high_t, basis_low_t], axis=1
    )
    scale_rows = jnp.concatenate(scales, axis=0)
    scale_parts = jnp.concatenate(
        [*split3(scale_rows), jnp.zeros((-3 * groups % 16, 128), BF16)], axis=0
    )

    path_rows = jnp.concatenate(
        [jnp.broadcast_to(path_weight_ref[l : l + 1, :], (GROUP, width)) for l in LEVELS], axis=0
    ) * (1.0 / root_count)
    out_column = jnp.transpose(jnp.broadcast_to(out_weight_ref[...], (width, width)))
    out_column = jnp.concatenate([out_column] * (span // width), axis=1)

    site_ids = lax.broadcasted_iota(jnp.int32, (known, span), 0)
    slot_ids = lax.broadcasted_iota(jnp.int32, (centers, pairs), 0)
    slot_row = lax.broadcasted_iota(jnp.int32, (1, pairs), 1) // nbr
    group_lane = lax.broadcasted_iota(jnp.int32, (GROUP, pairs), 1) // nbr % GROUP
    group_mask = group_lane == lax.broadcasted_iota(jnp.int32, (GROUP, pairs), 0)
    group_mask = jnp.where(group_mask, 1.0, 0.0)
    tall = len(LEVELS) * GROUP
    order = lax.broadcasted_iota(jnp.int32, (radial, pairs), 0).astype(F32) + 1.0

    lanes = [slice(g * span, (g + 1) * span) for g in range(groups)]
    picks = [
        jnp.where(site_ids == near_row[:, cut], 1.0, 0.0).astype(BF16) for cut in lanes
    ]
    slot_half = jnp.where(slot_ids == slot_row, 1.0, 0.0).astype(BF16)

    moved = [mm(place_parts, pick) for pick in picks]
    moved = jnp.concatenate(moved, axis=1) - mm(center_parts, slot_half)
    moved = moved[: 3 * sites] + moved[3 * sites : 6 * sites] + moved[6 * sites :]
    dx = jnp.where(live, jnp.sum(moved[:sites], axis=0, keepdims=True), 6.0)
    dy = jnp.sum(moved[sites : 2 * sites], axis=0, keepdims=True) + CELL_SIDE * side_y
    dy = jnp.where(live, dy, 0.0)
    dz = jnp.where(live, jnp.sum(moved[2 * sites :], axis=0, keepdims=True), 0.0)
    length = jnp.sqrt(dx * dx + dy * dy + dz * dz)
    inverse = 1.0 / length
    ratio = length * (1.0 / CUTOFF)
    inside = live & (ratio < 1.0)
    r2 = ratio * ratio
    r5 = r2 * r2 * ratio
    r6 = r5 * ratio
    weight = jnp.where(inside, 1.0 - r6 * (28.0 - 48.0 * ratio + 21.0 * r2), 0.0)
    slope = jnp.where(inside, -168.0 * r5 * (1.0 - 2.0 * ratio + r2), 0.0)
    sine, cosine = sin_cos_pi(order * ratio)
    basis = (math.sqrt(2.0 / CUTOFF) * inverse) * sine
    basis_slope = (math.sqrt(2.0 / CUTOFF) * inverse) * (
        (math.pi / CUTOFF) * order * cosine - sine * inverse
    )
    ex = dx * inverse
    ey = dy * inverse
    ez = dz * inverse
    angular = jnp.concatenate(
        [
            jnp.ones_like(ex),
            root_three * ex,
            root_three * ey,
            root_three * ez,
            root_fifteen * ex * ey,
            root_fifteen * ey * ez,
            0.5 * root_five * (3.0 * ez * ez - 1.0),
            root_fifteen * ex * ez,
            0.5 * root_fifteen * (ex * ex - ey * ey),
        ],
        axis=0,
    )
    angular_high, angular_low = halves(angular)
    angular_low = angular_low.astype(BF16).astype(F32)
    block_high = [angular_high[m : m + 1] * group_mask for m in range(len(LEVELS))]
    block_low = [angular_low[m : m + 1] * group_mask for m in range(len(LEVELS))]
    blocks = jnp.concatenate(block_high + block_low + block_high, axis=0).astype(BF16)
    lane_ids = lax.broadcasted_iota(jnp.int32, (128, span), 0)
    lane_slot = lax.broadcasted_iota(jnp.int32, (128, span), 1) // nbr + 3 * sites
    scale = mm(scale_parts, jnp.where(lane_ids == lane_slot, 1.0, 0.0).astype(BF16))
    scale = scale[:groups] + scale[groups : 2 * groups] + scale[2 * groups : 3 * groups]
    scale = jnp.concatenate([scale[g : g + 1] for g in range(groups)], axis=1)
    scale = scale * (1.0 / root_count)
    pull = ROOT_HALF * scale

    basis_high, basis_low = halves(basis)
    basis_rest = jnp.concatenate([basis_high, basis_low, basis_high], axis=0).astype(BF16)
    rest = jnp.concatenate([slot_half, slot_half, basis_rest], axis=0)
    fall = 0.5 * pull * weight
    each = range(groups)

    gate, active, latent = [], [], []
    for g in each:
        cut = lanes[g]
        before = folded(mm(near_lookup, picks[g])) + mm(rest_lookup, rest[:, cut])
        gate.append(1.0 + jnp.tanh(before))
        active.append(before * gate[g])
        latent.append(split(weight[:, cut] * active[g]))

    values, env = [], []
    for g in each:
        mixed = folded(mm(value_rows, jnp.concatenate(latent[g], axis=0)))
        values.append(mixed[:width])
        env.append(split(mixed[width:]))

    def over_pairs(g, parts):
        quad = mm_nt(blocks[: 2 * tall, lanes[g]], jnp.concatenate(parts, axis=0))
        quad = quad[:tall, :width] + quad[tall:, :width] + quad[:tall, width:]
        return quad * path_rows

    def over_orders(g, table):
        high, low = halves(table)
        table = jnp.transpose(jnp.concatenate([high, high, low], axis=0)).astype(BF16)
        return mm(table, blocks[:, lanes[g]])

    weighted = [over_pairs(g, env[g]) for g in each]
    inner, scalars = [], []
    for g in each:
        inner.append(over_orders(g, weighted[g]))
        scalars.append(split(values[g] * inner[g]))

    update_sum, slope_z = [], []
    for g in each:
        z = full_depth(
            latent_both_t,
            latent_high_t,
            jnp.concatenate([latent[g][0], scalars[g][0]], axis=0),
            jnp.concatenate([latent[g][1], scalars[g][1]], axis=0),
        )
        z_gate = 1.0 + jnp.tanh(z)
        update = z * z_gate
        update_sum.append(jnp.sum(update * out_column, axis=0, keepdims=True))
        slope_z.append(split(fall[:, lanes[g]] * (z_gate + update * (2.0 - z_gate))))

    d_direct, d_values, d_inner = [], [], []
    for g in each:
        spread_back = folded(mm(latent_rows, jnp.concatenate(slope_z[g], axis=0)))
        d_direct.append(spread_back[:width] + pull[:, lanes[g]] * out_column)
        d_scalars = spread_back[width:]
        d_values.append(split(d_scalars * inner[g]))
        d_inner.append(split(d_scalars * values[g]))

    d_embed = [over_pairs(g, d_inner[g]) for g in each]
    d_env = [split(over_orders(g, d_embed[g])) for g in each]

    d_angular = []
    for g in each:
        sides_high, sides_low = halves(jnp.concatenate([weighted[g], d_embed[g]], axis=1))
        d_block = full_depth(
            jnp.concatenate([sides_high, sides_low], axis=0).astype(BF16),
            sides_high.astype(BF16),
            jnp.concatenate([d_inner[g][0], env[g][0]], axis=0),
            jnp.concatenate([d_inner[g][1], env[g][1]], axis=0),
        )
        d_block = d_block.reshape(len(LEVELS), GROUP, span) * group_mask[None, :, lanes[g]]
        d_angular.append(jnp.sum(d_block, axis=1))

    d_weight, d_basis = [], []
    for g in each:
        d_latent = d_direct[g] + full_depth(
            value_both,
            value_high,
            jnp.concatenate([d_values[g][0], d_env[g][0]], axis=0),
            jnp.concatenate([d_values[g][1], d_env[g][1]], axis=0),
        )
        d_weight.append(jnp.sum(d_latent * active[g], axis=0, keepdims=True))
        d_before = d_latent * (gate[g] + active[g] * (2.0 - gate[g]))
        d_basis.append(half_depth(basis_rows, d_before))

    active_sum = [
        jnp.sum(active[g] * out_column, axis=0, keepdims=True) for g in range(own_pairs // span)
    ]
    update_sum = jnp.concatenate(update_sum, axis=1)
    pair_energy = (jnp.concatenate(active_sum, axis=1) + update_sum[:, :own_pairs]) * (
        pull * weight
    )[:, :own_pairs]
    d_angular = jnp.concatenate(d_angular, axis=1)
    d_weight = jnp.concatenate(d_weight, axis=1) + pull * update_sum
    d_basis = jnp.concatenate(d_basis, axis=1) * (0.5 * weight)

    d_length = jnp.sum(d_basis * basis_slope, axis=0, keepdims=True) + d_weight * slope * (
        1.0 / CUTOFF
    )
    a1, a2, a3, a4, a5, a6, a7, a8 = [d_angular[m : m + 1] for m in range(1, 9)]
    ux = root_three * a1 + root_fifteen * (ey * a4 + ez * a7 + ex * a8)
    uy = root_three * a2 + root_fifteen * (ex * a4 + ez * a5 - ey * a8)
    uz = root_three * a3 + root_fifteen * (ey * a5 + ex * a7) + 3.0 * root_five * ez * a6
    along = ex * ux + ey * uy + ez * uz
    radial_part = d_length - along * inverse
    gx = ux * inverse + ex * radial_part
    gy = uy * inverse + ey * radial_part
    gz = uz * inverse + ez * radial_part
    hx = -0.5 * dx
    hy = -0.5 * dy
    hz = -0.5 * dz
    virial = [hx * gx, hx * gy, hx * gz, hy * gx, hy * gy, hy * gz, hz * gx, hz * gy, hz * gz]
    rest = [jnp.zeros((ORDERS - 13, pairs), F32)]
    near_terms = jnp.concatenate(
        [-gx, -gy, -gz, *virial, jnp.zeros_like(gx), *rest], axis=0
    )
    center_rows = [gx, gy, gz, *virial]
    center_rows = [r[:, :own_pairs] for r in center_rows] + [pair_energy]
    center_rows.append(jnp.zeros((ORDERS - 13, own_pairs), F32))
    center_terms = jnp.concatenate(center_rows, axis=0)
    terms_high, terms_low = split(near_terms)
    near_parts = jnp.concatenate([terms_high, terms_low], axis=0)
    near_sums = 0.0
    for g in each:
        reach = []
        for x, z, side in np.ndindex(2, 2, kept_sides):
            start = ((2 * z + x) * kind + side) * owned
            reach.append(picks[g][start : start + owned])
        near_sums = near_sums + mm_nt(near_parts[:, lanes[g]], jnp.concatenate(reach, axis=0))
    center_sums = mm_nt(
        jnp.concatenate(split(center_terms), axis=0), slot_half[:owned, :own_pairs]
    )
    center_sums = jnp.concatenate(
        [folded(center_sums), jnp.zeros((ORDERS, 128 - owned), F32)], axis=1
    )
    totals = folded(near_sums)
    lane = lax.broadcasted_iota(jnp.int32, (ORDERS, 128), 1)
    known = totals.shape[1]
    tiles = [totals[:, 128 * i : 128 * (i + 1)] for i in range(known // 128)]
    for g in range(owned // GROUP):
        cell = g % 2 * 2 + 1 - g // 2
        target = (g % 2 * 2 + g // 2) * kept_sides * owned + cell * sites
        turn = (target - g * GROUP) % 128
        piece = pltpu.roll(center_sums, turn, 1) if turn else center_sums
        begin = target % 128
        piece = jnp.where((lane >= begin) & (lane < begin + GROUP), piece, 0.0)
        tiles[target // 128] = tiles[target // 128] + piece
    totals = jnp.concatenate(tiles, axis=1)
    keep_ref[...] = totals[:, : known // 2]
    send_ref[...] = totals[:, known // 2 :]


def in_hbm(*arrays):
    return [pltpu.with_memory_space_constraint(array, pltpu.HBM) for array in arrays]


def joined(parts):
    total = sum(part.shape[0] for part in parts)
    start = 0
    pads = []
    for part in parts:
        end = start + part.shape[0]
        pads.append(jnp.pad(part, ((start, total - end), (0, 0))))
        start = end
    return functools.reduce(jnp.add, pads)


def local(
    positions,
    features,
    species,
    centers,
    neighbours,
    counts,
    species_scale,
    species_shift,
    center_weight,
    near_weight,
    basis_weight,
    path_weight,
    value_weight,
    latent_weight,
    out_weight,
):
    cells_x, cells_y, cells_z, sites, width = features.shape
    cell_count = cells_x * cells_y * cells_z
    owned = cell_count * sites
    assert (cells_x, cells_y, cells_z, sites) == (2, 1, 2, SITES)
    pairs = neighbours.size
    nbr = pairs // owned
    kind = min(3, lax.axis_size("gy"))

    def moved(array, steps):
        names = tuple(steps)
        sizes = [lax.axis_size(name) for name in names]
        route = []
        for at in np.ndindex(*sizes):
            to = [(p + steps[name]) % size for p, name, size in zip(at, names, sizes)]
            route.append(
                (int(np.ravel_multi_index(at, sizes)), int(np.ravel_multi_index(to, sizes)))
            )
        return lax.ppermute(array, names, route)

    vmem = pl.BlockSpec(memory_space=pltpu.VMEM)
    hbm = pl.BlockSpec(memory_space=pltpu.HBM)
    listed = centers.reshape(1, owned)
    payload = jax.ShapeDtypeStruct((owned + OWN_CELLS + pairs // 256, width), F32)
    low, high = pl.pallas_call(
        functools.partial(pack_kernel, kind),
        out_shape=(payload, payload),
        in_specs=[hbm] * 6,
        out_specs=(vmem, vmem),
        scratch_shapes=[
            pltpu.VMEM((owned, 128), F32),
            pltpu.VMEM(positions.shape, F32),
            pltpu.VMEM(species.shape, jnp.int32),
            pltpu.VMEM(listed.shape, jnp.int32),
            pltpu.VMEM(neighbours.shape, jnp.int32),
            pltpu.SMEM(species_scale.shape, F32),
            pltpu.SemaphoreType.DMA((6,)),
        ],
        compiler_params=pltpu.CompilerParams(vmem_limit_bytes=8 * 1024 * 1024),
        name="pack_payload",
    )(
        *in_hbm(
            positions,
            features.reshape(owned, width),
            species,
            listed,
            neighbours,
            species_scale,
        )
    )
    weights = (
        center_weight,
        near_weight,
        basis_weight,
        path_weight,
        value_weight,
        latent_weight,
        out_weight.reshape(1, width),
    )
    *weights, shift_row = pl.pallas_call(
        fetch_kernel,
        out_shape=(
            *(jax.ShapeDtypeStruct(w.shape, F32) for w in weights),
            jax.ShapeDtypeStruct((1, owned), F32),
        ),
        in_specs=[hbm] * (3 + len(weights)),
        out_specs=(vmem,) * (1 + len(weights)),
        scratch_shapes=[
            pltpu.VMEM(species.shape, jnp.int32),
            pltpu.VMEM(listed.shape, jnp.int32),
            pltpu.SMEM(species_shift.shape, F32),
            pltpu.SemaphoreType.DMA((3 + len(weights),)),
        ],
        compiler_params=pltpu.CompilerParams(vmem_limit_bytes=8 * 1024 * 1024),
        name="fetch_weights",
    )(*in_hbm(species, listed, species_shift, *weights))
    last_x = moved(high, {"gx": 1})
    sides = []
    for step in (-1, 1)[: kind - 1]:
        sides.append(moved(high, {"gx": 1, "gy": step}))
        sides.insert(-1, moved(low, {"gy": step}))
    next_z = moved(joined([low, last_x, *sides]), {"gz": -1})
    kept = 1 if kind == 2 else kind
    half = 2 * kept * owned
    keep, send = pl.pallas_call(
        functools.partial(force_kernel, kind, nbr),
        out_shape=(
            jax.ShapeDtypeStruct((ORDERS, half), F32),
            jax.ShapeDtypeStruct((ORDERS, half), F32),
        ),
        in_specs=[vmem] * (8 + 2 * kind),
        out_specs=(vmem, vmem),
        compiler_params=pltpu.CompilerParams(vmem_limit_bytes=44 * 1024 * 1024),
        name="pair_forces",
    )(
        low,
        last_x,
        *sides,
        next_z,
        *weights,
    )
    totals = keep + moved(send, {"gx": -1})

    def part(index):
        return totals[:, index * owned : (index + 1) * owned]

    back = [moved(part(kept), {"gz": 1})]
    for i, step in enumerate((1, -1)[: kept - 1]):
        back.append(moved(part(kept + 1 + i), {"gy": step, "gz": 1}))
        back.append(moved(part(1 + i), {"gy": step}))
    site_energy, forces, virial = pl.pallas_call(
        finish_kernel,
        out_shape=(
            jax.ShapeDtypeStruct(species.shape, F32),
            jax.ShapeDtypeStruct(positions.shape, F32),
            jax.ShapeDtypeStruct((*species.shape, 9), F32),
        ),
        in_specs=[vmem] * (2 + len(back)),
        out_specs=(vmem, vmem, vmem),
        compiler_params=pltpu.CompilerParams(vmem_limit_bytes=8 * 1024 * 1024),
        name="write_outputs",
    )(totals, shift_row, *back)
    return (site_energy, forces, jnp.transpose(virial, (4, 0, 1, 2, 3)))


def solution(mesh):
    placed = (
        P(None, "gx", "gy", "gz", None),
        P("gx", "gy", "gz", None, None),
        P("gx", "gy", "gz", None),
        P(("gx", "gy", "gz")),
        P(("gx", "gy", "gz"), None),
        P(("gx", "gy", "gz")),
        P(),
        P(),
        P(),
        P(),
        P(),
        P(),
        P(),
        P(),
        P(),
    )
    return jax.shard_map(
        local,
        mesh=mesh,
        in_specs=placed,
        out_specs=(
            P("gx", "gy", "gz", None),
            P(None, "gx", "gy", "gz", None),
            P(None, "gx", "gy", "gz", None),
        ),
        check_vma=False,
    )
```

```python
import functools
import math

import jax
import jax.numpy as jnp
import numpy as np
from jax import lax
from jax.experimental import pallas as pl
from jax.experimental.pallas import tpu as pltpu
from jax.sharding import PartitionSpec as P

EXACT_DOT = lax.Precision.HIGHEST
CUTOFF = 5.0
CELL_SIDE = 4.6
ROOT_HALF = 0.7071067811865476
GROUP = 8
TEAM = 16
ORDERS = 16
LEVELS = (0, 1, 1, 1, 2, 2, 2, 2, 2)
SITES = 8
OWN_CELLS = 4
FRAME_CELLS = 48
F32 = jnp.float32
BF16 = jnp.bfloat16


def split(value):
    high = value.astype(BF16)
    low = (value - high.astype(F32)).astype(BF16)
    return high, low


def split3(value):
    high = value.astype(BF16)
    rest = value - high.astype(F32)
    middle = rest.astype(BF16)
    low = (rest - middle.astype(F32)).astype(BF16)
    return high, middle, low


def halves(value):
    high = value.astype(BF16).astype(F32)
    return high, value - high


def mm(a, b):
    return lax.dot_general(a, b, (((1,), (0,)), ((), ())), preferred_element_type=F32)


def mm_nt(a, b):
    return lax.dot_general(a, b, (((1,), (1,)), ((), ())), preferred_element_type=F32)


def stacked(high, low):
    top = jnp.concatenate([high, high], axis=1)
    bottom = jnp.concatenate([low, jnp.zeros_like(low)], axis=1)
    return jnp.concatenate([top, bottom], axis=0)


def folded(product):
    half = product.shape[0] // 2
    return product[:half] + product[half:]


def half_depth(weights, value):
    return folded(mm(weights, jnp.concatenate(split(value), axis=0)))


def full_depth(both, high, value_high, value_low):
    return folded(mm(both, value_high)) + mm(high, value_low)


def sin_cos_pi(turns):
    near = turns - 2.0 * jnp.round(turns * 0.5)
    quarter = jnp.round(near * 2.0)
    v = (near - 0.5 * quarter) * math.pi
    v2 = v * v
    s = v * (
        1.0
        + v2
        * (-1.0 / 6 + v2 * (1.0 / 120 + v2 * (-1.0 / 5040 + v2 * (1.0 / 362880 - v2 / 39916800))))
    )
    c = 1.0 + v2 * (
        -0.5
        + v2
        * (1.0 / 24 + v2 * (-1.0 / 720 + v2 * (1.0 / 40320 + v2 * (-1.0 / 3628800 + v2 / 479001600))))
    )
    odd = jnp.abs(quarter) == 1.0
    sine = jnp.where(odd, quarter * c, jnp.where(quarter == 0.0, s, -s))
    cosine = jnp.where(odd, -quarter * s, jnp.where(quarter == 0.0, c, -c))
    return sine, cosine


def lane_row(piece, offset):
    row = jnp.concatenate([piece, jnp.zeros((1, 128 - piece.shape[1]), piece.dtype)], axis=1)
    return pltpu.roll(row, offset, 1) if offset else row


def pack_kernel(
    kind,
    positions_hbm,
    features_hbm,
    species_hbm,
    centers_hbm,
    neighbours_hbm,
    scale_hbm,
    low_ref,
    high_ref,
    wide_ref,
    positions_ref,
    species_ref,
    centers_ref,
    neighbours_ref,
    scale_ref,
    sems,
):
    owned, nbr = neighbours_ref.shape
    per_row = 128 // nbr
    pairs_in = (
        (features_hbm, low_ref.at[pl.ds(0, owned), :]),
        (neighbours_hbm, neighbours_ref),
        (centers_hbm, centers_ref),
        (positions_hbm, positions_ref),
        (species_hbm, species_ref),
        (scale_hbm, scale_ref),
    )
    copies = [
        pltpu.make_async_copy(source, target, sems.at[i])
        for i, (source, target) in enumerate(pairs_in)
    ]
    for copy in copies:
        copy.start()
    for copy in copies:
        copy.wait()
    for cell in range(OWN_CELLS):
        x, z = cell // 2, cell % 2
        species = species_ref[x, 0, z : z + 1, :]
        scale = jnp.zeros(species.shape, F32)
        for s in range(scale_ref.shape[0]):
            scale = jnp.where(species == s, scale_ref[s], scale)
        row = lane_row(scale, 3 * SITES)
        for c in range(3):
            row = row + lane_row(positions_ref[c, x, 0, z : z + 1, :], c * SITES)
        low_ref[owned + cell : owned + cell + 1] = row

    chosen = lax.broadcasted_iota(jnp.int32, (owned, owned), 0) == centers_ref[...]
    chosen = jnp.where(chosen, 1.0, 0.0)
    occupied = jnp.sum(chosen, axis=1, keepdims=True) > 0.5
    chosen = chosen.astype(BF16)
    rows = neighbours_ref[...]
    upper = mm(chosen, (rows >> 4).astype(F32).astype(BF16))
    lower = mm(chosen, (rows & 15).astype(F32).astype(BF16))
    rows = (upper * 16.0 + lower).astype(jnp.int32)
    live = occupied & (rows < FRAME_CELLS * SITES)
    slot = lax.broadcasted_iota(jnp.int32, (owned, nbr), 0)
    cell = slot >> 3
    site = rows & 7
    place = rows >> 3
    near_z = (place & 3) + 1 - 2 * (cell & 1)
    column = place >> 2
    frame_x = (column * 11) >> 5
    frame_y = column - 3 * frame_x
    near_x = frame_x + 1 - 2 * (cell >> 1)
    side = jnp.where(frame_y == 1, 0, jnp.where(frame_y == 2, 1, kind - 1))
    block = (near_z >> 1) * 2 + 1 - (near_x >> 1)
    where = (block * kind + side) * owned + (near_x & 1) * 16 + (near_z & 1) * 8 + site
    code = jnp.where(live, 1 + where + (frame_y << 10), 0).astype(F32)
    wide_ref[...] = jnp.concatenate([code, jnp.zeros((owned, 128 - nbr), F32)], axis=1)
    codes = wide_ref[pl.ds(0, owned // per_row, stride=per_row), :]
    for j in range(1, per_row):
        more = wide_ref[pl.ds(j, owned // per_row, stride=per_row), :]
        codes = codes + pltpu.roll(more, j * nbr, 1)
    tile = owned + OWN_CELLS
    low_ref[tile:] = codes[: codes.shape[0] // 2]
    high_ref[:tile] = low_ref[:tile]
    high_ref[tile:] = codes[codes.shape[0] // 2 :]


def fetch_kernel(species_hbm, centers_hbm, shift_hbm, *refs):
    *refs, shift_row_ref, species_ref, centers_ref, shift_ref, sems = refs
    count = len(refs) // 2
    pairs_in = [
        (species_hbm, species_ref),
        (centers_hbm, centers_ref),
        (shift_hbm, shift_ref),
        *zip(refs[:count], refs[count:]),
    ]
    copies = [
        pltpu.make_async_copy(source, target, sems.at[i])
        for i, (source, target) in enumerate(pairs_in)
    ]
    for copy in copies:
        copy.start()
    for copy in copies:
        copy.wait()
    owned = centers_ref.shape[1]
    shift_row = jnp.zeros((1, 128), F32)
    for cell in range(OWN_CELLS):
        species = species_ref[cell // 2, 0, cell % 2 : cell % 2 + 1, :]
        shift = jnp.zeros(species.shape, F32)
        for s in range(shift_ref.shape[0]):
            shift = jnp.where(species == s, shift_ref[s], shift)
        shift_row = shift_row + lane_row(shift, cell * SITES)
    chosen = lax.broadcasted_iota(jnp.int32, (owned, owned), 0) == centers_ref[...]
    occupied = jnp.sum(jnp.where(chosen, 1.0, 0.0), axis=1, keepdims=True) > 0.5
    column = jnp.where(occupied, jnp.ones((owned, 128), F32), 0.0)
    shift_row_ref[...] = shift_row[:, :owned] * jnp.transpose(column)[0:1]


def finish_kernel(mine_ref, shift_row_ref, *refs):
    *near_refs, energy_ref, forces_ref, virial_ref = refs
    owned = near_refs[0].shape[1]
    total = mine_ref[:, :owned]
    for near_ref in near_refs:
        total = total + near_ref[...]
    energy = total[12:13] + shift_row_ref[...]
    columns = jnp.transpose(jnp.concatenate([total, jnp.zeros((ORDERS, 128 - owned), F32)], axis=1))
    for cell in range(OWN_CELLS):
        x, z = cell // 2, cell % 2
        lanes = slice(cell * SITES, (cell + 1) * SITES)
        energy_ref[x, 0, z : z + 1, :] = energy[:, lanes]
        for c in range(3):
            forces_ref[c, x, 0, z : z + 1, :] = total[c : c + 1, lanes]
        virial_ref[x, 0, z] = columns[lanes, 3:12]


def force_kernel(kind, nbr, here_ref, last_x_ref, *refs):
    near_side_refs = refs[: 2 * kind - 2]
    (
        next_z_ref,
        center_weight_ref,
        near_weight_ref,
        basis_weight_ref,
        path_weight_ref,
        value_weight_ref,
        latent_weight_ref,
        out_weight_ref,
        keep_ref,
        send_ref,
    ) = refs[2 * kind - 2 :]
    height, width = here_ref.shape
    owned = OWN_CELLS * SITES
    center_sides = 2 if kind == 2 else 1
    kept_sides = 1 if kind == 2 else kind
    own_pairs = owned * nbr
    pairs = center_sides * own_pairs
    centers = center_sides * owned
    radial = basis_weight_ref.shape[0]
    span = GROUP * nbr
    groups = centers // GROUP
    sites = SITES
    root_count = math.sqrt(nbr)
    root_three = math.sqrt(3.0)
    root_fifteen = math.sqrt(15.0)
    root_five = math.sqrt(5.0)
    far = next_z_ref[...]
    mains = [here_ref[...], last_x_ref[...], far[:height], far[height : 2 * height]]
    near_sides = [ref[...] for ref in near_side_refs]
    far_sides = far[2 * height :]
    far_sides = [far_sides[i * height : (i + 1) * height] for i in range(2 * kind - 2)]
    blocks_in = [
        [mains[0], *near_sides[0::2]],
        [mains[1], *near_sides[1::2]],
        [mains[2], *far_sides[0::2]],
        [mains[3], *far_sides[1::2]],
    ]
    feats = jnp.concatenate([side[:owned] for block in blocks_in for side in block], axis=0)
    known = feats.shape[0]
    center_feats = []
    center_coords = []
    coords = []
    scales = []
    codes = []
    cell_row = lax.broadcasted_iota(jnp.int32, (kind * OWN_CELLS, 128), 0) % OWN_CELLS
    tile_lane = lax.broadcasted_iota(jnp.int32, (kind * OWN_CELLS, 128), 1)
    for g, block in enumerate(blocks_in):
        behind_x, ahead_z = g % 2, g // 2
        rows = jnp.concatenate([side[owned : owned + OWN_CELLS] for side in block], axis=0)
        corner_x = (cell_row // 2 + 2 - 2 * behind_x).astype(F32) * CELL_SIDE
        corner_z = (cell_row % 2 + 2 * ahead_z).astype(F32) * CELL_SIDE
        corner = jnp.where(
            tile_lane < sites, corner_x, jnp.where(tile_lane < 2 * sites, 0.0, corner_z)
        )
        coords.append(rows + corner)
    for c in range(center_sides):
        for g, block in enumerate(blocks_in):
            cell = g % 2 * 2 + 1 - g // 2
            row = c * OWN_CELLS + cell
            center_feats.append(block[c][cell * sites : (cell + 1) * sites])
            scales.append(block[c][owned + cell : owned + cell + 1])
            center_coords.append(coords[g][row : row + 1])
            start = owned + OWN_CELLS + (1 - g // 2) * span // 128
            codes.extend(block[c][start + r : start + r + 1] for r in range(span // 128))
    center_feats = jnp.concatenate(center_feats, axis=0)
    coords = jnp.concatenate(coords, axis=0)
    code = jnp.concatenate(codes, axis=1).astype(jnp.int32)
    live = code > 0
    code = jnp.maximum(code - 1, 0)
    side_y = ((code >> 10) - 1).astype(F32)
    near_row = code & 1023
    if center_sides == 2:
        pair_lane = lax.broadcasted_iota(jnp.int32, (1, pairs), 1)
        near_row = jnp.where(pair_lane < own_pairs, near_row, near_row ^ owned)
    near_row = jnp.where(live, near_row, known)

    def place_rows(cell_rows):
        count = cell_rows.shape[0] * sites
        spread = jnp.broadcast_to(cell_rows[:, None, :], (cell_rows.shape[0], sites, 128))
        spread = spread.reshape(count, 128)
        lane = lax.broadcasted_iota(jnp.int32, (count, 128), 1)
        row = lax.broadcasted_iota(jnp.int32, (count, 128), 0)
        keep = (lane % sites == row % sites) & (lane < 3 * sites)
        spread = jnp.transpose(jnp.where(keep, spread, 0.0))
        return jnp.concatenate(split3(spread[: 3 * sites]), axis=0)

    place_parts = place_rows(coords)
    center_parts = place_rows(jnp.concatenate(center_coords, axis=0))

    value_rows = stacked(*split(jnp.transpose(value_weight_ref[...])))
    latent_high_t, latent_low_t = split(0.5 * jnp.transpose(latent_weight_ref[...]))
    latent_both_t = jnp.concatenate([latent_high_t, latent_low_t], axis=0)
    latent_rows = stacked(*split(latent_weight_ref[...] * out_weight_ref[...]))
    value_high, value_low = split(value_weight_ref[...])
    value_both = jnp.concatenate([value_high, value_low], axis=0)
    basis_t = jnp.transpose(basis_weight_ref[...])
    basis_high_t, basis_low_t = split(0.5 * basis_t)
    basis_rows = stacked(*split(basis_weight_ref[...]))

    def project(weight, rows):
        weight = stacked(*split(jnp.transpose(weight)))
        return folded(mm_nt(weight, jnp.concatenate(split(rows), axis=1)))

    near_t = project(near_weight_ref[...], feats)
    own_t = project(center_weight_ref[...], center_feats)
    near_high, near_low = split(0.5 * near_t)
    own_high, own_low = split(0.5 * own_t)
    near_lookup = jnp.concatenate([near_high, near_low], axis=0)
    rest_lookup = jnp.concatenate(
        [own_high, own_low, basis_high_t, basis_high_t, basis_low_t], axis=1
    )
    scale_rows = jnp.concatenate(scales, axis=0)
    scale_parts = jnp.concatenate(
        [*split3(scale_rows), jnp.zeros((-3 * groups % 16, 128), BF16)], axis=0
    )

    path_rows = jnp.concatenate(
        [jnp.broadcast_to(path_weight_ref[l : l + 1, :], (TEAM, width)) for l in LEVELS], axis=0
    ) * (1.0 / root_count)
    out_column = jnp.transpose(jnp.broadcast_to(out_weight_ref[...], (width, width)))
    out_column = jnp.concatenate([out_column] * (pairs // width), axis=1)

    site_ids = lax.broadcasted_iota(jnp.int32, (known, pairs), 0)
    slot_ids = lax.broadcasted_iota(jnp.int32, (centers, pairs), 0)
    slot_row = lax.broadcasted_iota(jnp.int32, (1, pairs), 1) // nbr
    group_lane = lax.broadcasted_iota(jnp.int32, (TEAM, pairs), 1) // nbr % TEAM
    group_mask = group_lane == lax.broadcasted_iota(jnp.int32, (TEAM, pairs), 0)
    group_mask = jnp.where(group_mask, 1.0, 0.0)
    tall = len(LEVELS) * TEAM
    reach = TEAM * nbr
    order = lax.broadcasted_iota(jnp.int32, (radial, pairs), 0).astype(F32) + 1.0
    lanes = [slice(i, i + reach) for i in range(0, pairs, reach)]

    pick = jnp.where(site_ids == near_row, 1.0, 0.0)
    pick_half = pick.astype(BF16)
    slot_half = jnp.where(slot_ids == slot_row, 1.0, 0.0).astype(BF16)

    moved = mm(place_parts, pick_half) - mm(center_parts, slot_half)
    moved = moved[: 3 * sites] + moved[3 * sites : 6 * sites] + moved[6 * sites :]
    dx = jnp.where(live, jnp.sum(moved[:sites], axis=0, keepdims=True), 6.0)
    dy = jnp.sum(moved[sites : 2 * sites], axis=0, keepdims=True) + CELL_SIDE * side_y
    dy = jnp.where(live, dy, 0.0)
    dz = jnp.where(live, jnp.sum(moved[2 * sites :], axis=0, keepdims=True), 0.0)
    length = jnp.sqrt(dx * dx + dy * dy + dz * dz)
    inverse = 1.0 / length
    ratio = length * (1.0 / CUTOFF)
    inside = live & (ratio < 1.0)
    r2 = ratio * ratio
    r5 = r2 * r2 * ratio
    r6 = r5 * ratio
    weight = jnp.where(inside, 1.0 - r6 * (28.0 - 48.0 * ratio + 21.0 * r2), 0.0)
    slope = jnp.where(inside, -168.0 * r5 * (1.0 - 2.0 * ratio + r2), 0.0)
    sine, cosine = sin_cos_pi(order * ratio)
    basis = (math.sqrt(2.0 / CUTOFF) * inverse) * sine
    basis_slope = (math.sqrt(2.0 / CUTOFF) * inverse) * (
        (math.pi / CUTOFF) * order * cosine - sine * inverse
    )
    ex = dx * inverse
    ey = dy * inverse
    ez = dz * inverse
    angular = jnp.concatenate(
        [
            jnp.ones_like(ex),
            root_three * ex,
            root_three * ey,
            root_three * ez,
            root_fifteen * ex * ey,
            root_fifteen * ey * ez,
            0.5 * root_five * (3.0 * ez * ez - 1.0),
            root_fifteen * ex * ez,
            0.5 * root_fifteen * (ex * ex - ey * ey),
        ],
        axis=0,
    )
    angular_high, angular_low = halves(angular)
    angular_low = angular_low.astype(BF16).astype(F32)
    block_high = [angular_high[m : m + 1] * group_mask for m in range(len(LEVELS))]
    block_low = [angular_low[m : m + 1] * group_mask for m in range(len(LEVELS))]
    blocks = jnp.concatenate(block_high + block_low + block_high, axis=0).astype(BF16)
    lane_ids = lax.broadcasted_iota(jnp.int32, (128, span), 0)
    lane_slot = lax.broadcasted_iota(jnp.int32, (128, span), 1) // nbr + 3 * sites
    scale = mm(scale_parts, jnp.where(lane_ids == lane_slot, 1.0, 0.0).astype(BF16))
    scale = scale[:groups] + scale[groups : 2 * groups] + scale[2 * groups : 3 * groups]
    scale = jnp.concatenate([scale[g : g + 1] for g in range(groups)], axis=1)
    scale = scale * (1.0 / root_count)
    pull = ROOT_HALF * scale

    basis_high, basis_low = halves(basis)
    basis_rest = jnp.concatenate([basis_high, basis_low, basis_high], axis=0).astype(BF16)
    before = folded(mm(near_lookup, pick_half)) + mm(
        rest_lookup, jnp.concatenate([slot_half, slot_half, basis_rest], axis=0)
    )
    gate = 1.0 + jnp.tanh(before)
    active = before * gate
    latent = weight * active
    latent_high, latent_low = split(latent)
    mixed = folded(mm(value_rows, jnp.concatenate([latent_high, latent_low], axis=0)))
    values = mixed[:width]
    env_high, env_low = split(mixed[width:])

    def over_pairs(high, low):
        sums = []
        for cut in lanes:
            both = jnp.concatenate([high[:, cut], low[:, cut]], axis=0)
            quad = mm_nt(blocks[: 2 * tall, cut], both)
            quad = quad[:tall, :width] + quad[tall:, :width] + quad[:tall, width:]
            sums.append(quad * path_rows)
        return sums

    def over_orders(tables):
        parts = []
        for table, cut in zip(tables, lanes):
            high, low = halves(table)
            table = jnp.transpose(jnp.concatenate([high, high, low], axis=0)).astype(BF16)
            parts.append(mm(table, blocks[:, cut]))
        return jnp.concatenate(parts, axis=1)

    weighted = over_pairs(env_high, env_low)
    inner = over_orders(weighted)
    scalars = values * inner
    scalars_high, scalars_low = split(scalars)
    z = full_depth(
        latent_both_t,
        latent_high_t,
        jnp.concatenate([latent_high, scalars_high], axis=0),
        jnp.concatenate([latent_low, scalars_low], axis=0),
    )
    z_gate = 1.0 + jnp.tanh(z)
    update = z * z_gate
    update_sum = jnp.sum(update * out_column, axis=0, keepdims=True)
    active_sum = jnp.sum(
        active[:, :own_pairs] * out_column[:, :own_pairs], axis=0, keepdims=True
    )
    pair_energy = (active_sum + update_sum[:, :own_pairs]) * (pull * weight)[:, :own_pairs]
    d_z = (0.5 * pull * weight) * (z_gate + update * (2.0 - z_gate))
    spread_back = half_depth(latent_rows, d_z)
    d_scalars = spread_back[width:]
    d_values = d_scalars * inner
    dinner_high, dinner_low = split(d_scalars * values)
    d_embed = over_pairs(dinner_high, dinner_low)
    d_env = over_orders(d_embed)

    d_angular = []
    for g, cut in enumerate(lanes):
        sides_high, sides_low = halves(jnp.concatenate([weighted[g], d_embed[g]], axis=1))
        d_block = full_depth(
            jnp.concatenate([sides_high, sides_low], axis=0).astype(BF16),
            sides_high.astype(BF16),
            jnp.concatenate([dinner_high[:, cut], env_high[:, cut]], axis=0),
            jnp.concatenate([dinner_low[:, cut], env_low[:, cut]], axis=0),
        )
        d_block = d_block.reshape(len(LEVELS), TEAM, reach) * group_mask[None, :, cut]
        d_angular.append(jnp.sum(d_block, axis=1))
    d_angular = jnp.concatenate(d_angular, axis=1)

    mixed_high, mixed_low = split(jnp.concatenate([d_values, d_env], axis=0))
    d_latent = (
        full_depth(value_both, value_high, mixed_high, mixed_low)
        + spread_back[:width]
        + pull * out_column
    )
    d_weight = jnp.sum(d_latent * active, axis=0, keepdims=True) + pull * update_sum
    d_before = d_latent * (gate + active * (2.0 - gate))
    d_basis = half_depth(basis_rows, d_before) * (0.5 * weight)

    d_length = jnp.sum(d_basis * basis_slope, axis=0, keepdims=True) + d_weight * slope * (
        1.0 / CUTOFF
    )
    a1, a2, a3, a4, a5, a6, a7, a8 = [d_angular[m : m + 1] for m in range(1, 9)]
    ux = root_three * a1 + root_fifteen * (ey * a4 + ez * a7 + ex * a8)
    uy = root_three * a2 + root_fifteen * (ex * a4 + ez * a5 - ey * a8)
    uz = root_three * a3 + root_fifteen * (ey * a5 + ex * a7) + 3.0 * root_five * ez * a6
    along = ex * ux + ey * uy + ez * uz
    radial_part = d_length - along * inverse
    gx = ux * inverse + ex * radial_part
    gy = uy * inverse + ey * radial_part
    gz = uz * inverse + ez * radial_part
    hx = -0.5 * dx
    hy = -0.5 * dy
    hz = -0.5 * dz
    virial = [hx * gx, hx * gy, hx * gz, hy * gx, hy * gy, hy * gz, hz * gx, hz * gy, hz * gz]
    rest = [jnp.zeros((ORDERS - 13, pairs), F32)]
    near_terms = jnp.concatenate(
        [-gx, -gy, -gz, *virial, jnp.zeros_like(gx), *rest], axis=0
    )
    center_rows = [gx, gy, gz, *virial]
    center_rows = [r[:, :own_pairs] for r in center_rows] + [pair_energy]
    center_rows.append(jnp.zeros((ORDERS - 13, own_pairs), F32))
    center_terms = jnp.concatenate(center_rows, axis=0)
    rows = []
    for x, z, side in np.ndindex(2, 2, kept_sides):
        start = ((2 * z + x) * kind + side) * owned
        rows.append(pick_half[start : start + owned])
    rows = jnp.concatenate(rows, axis=0)
    near_sums = mm_nt(jnp.concatenate(split(near_terms), axis=0), rows)
    center_sums = mm_nt(
        jnp.concatenate(split(center_terms), axis=0), slot_half[:owned, :own_pairs]
    )
    center_sums = jnp.concatenate(
        [folded(center_sums), jnp.zeros((ORDERS, 128 - owned), F32)], axis=1
    )
    totals = folded(near_sums)
    lane = lax.broadcasted_iota(jnp.int32, (ORDERS, 128), 1)
    known = totals.shape[1]
    tiles = [totals[:, 128 * i : 128 * (i + 1)] for i in range(known // 128)]
    for g in range(owned // GROUP):
        cell = g % 2 * 2 + 1 - g // 2
        target = (g % 2 * 2 + g // 2) * kept_sides * owned + cell * sites
        turn = (target - g * GROUP) % 128
        piece = pltpu.roll(center_sums, turn, 1) if turn else center_sums
        begin = target % 128
        piece = jnp.where((lane >= begin) & (lane < begin + GROUP), piece, 0.0)
        tiles[target // 128] = tiles[target // 128] + piece
    totals = jnp.concatenate(tiles, axis=1)
    keep_ref[...] = totals[:, : known // 2]
    send_ref[...] = totals[:, known // 2 :]


def in_hbm(*arrays):
    return [pltpu.with_memory_space_constraint(array, pltpu.HBM) for array in arrays]


def joined(parts):
    total = sum(part.shape[0] for part in parts)
    start = 0
    pads = []
    for part in parts:
        end = start + part.shape[0]
        pads.append(jnp.pad(part, ((start, total - end), (0, 0))))
        start = end
    return functools.reduce(jnp.add, pads)


def local(
    positions,
    features,
    species,
    centers,
    neighbours,
    counts,
    species_scale,
    species_shift,
    center_weight,
    near_weight,
    basis_weight,
    path_weight,
    value_weight,
    latent_weight,
    out_weight,
):
    cells_x, cells_y, cells_z, sites, width = features.shape
    cell_count = cells_x * cells_y * cells_z
    owned = cell_count * sites
    assert (cells_x, cells_y, cells_z, sites) == (2, 1, 2, SITES)
    pairs = neighbours.size
    nbr = pairs // owned
    kind = min(3, lax.axis_size("gy"))

    def moved(array, steps):
        names = tuple(steps)
        sizes = [lax.axis_size(name) for name in names]
        route = []
        for at in np.ndindex(*sizes):
            to = [(p + steps[name]) % size for p, name, size in zip(at, names, sizes)]
            route.append(
                (int(np.ravel_multi_index(at, sizes)), int(np.ravel_multi_index(to, sizes)))
            )
        return lax.ppermute(array, names, route)

    vmem = pl.BlockSpec(memory_space=pltpu.VMEM)
    hbm = pl.BlockSpec(memory_space=pltpu.HBM)
    listed = centers.reshape(1, owned)
    payload = jax.ShapeDtypeStruct((owned + OWN_CELLS + pairs // 256, width), F32)
    low, high = pl.pallas_call(
        functools.partial(pack_kernel, kind),
        out_shape=(payload, payload),
        in_specs=[hbm] * 6,
        out_specs=(vmem, vmem),
        scratch_shapes=[
            pltpu.VMEM((owned, 128), F32),
            pltpu.VMEM(positions.shape, F32),
            pltpu.VMEM(species.shape, jnp.int32),
            pltpu.VMEM(listed.shape, jnp.int32),
            pltpu.VMEM(neighbours.shape, jnp.int32),
            pltpu.SMEM(species_scale.shape, F32),
            pltpu.SemaphoreType.DMA((6,)),
        ],
        compiler_params=pltpu.CompilerParams(vmem_limit_bytes=8 * 1024 * 1024),
        name="pack_payload",
    )(
        *in_hbm(
            positions,
            features.reshape(owned, width),
            species,
            listed,
            neighbours,
            species_scale,
        )
    )
    weights = (
        center_weight,
        near_weight,
        basis_weight,
        path_weight,
        value_weight,
        latent_weight,
        out_weight.reshape(1, width),
    )
    *weights, shift_row = pl.pallas_call(
        fetch_kernel,
        out_shape=(
            *(jax.ShapeDtypeStruct(w.shape, F32) for w in weights),
            jax.ShapeDtypeStruct((1, owned), F32),
        ),
        in_specs=[hbm] * (3 + len(weights)),
        out_specs=(vmem,) * (1 + len(weights)),
        scratch_shapes=[
            pltpu.VMEM(species.shape, jnp.int32),
            pltpu.VMEM(listed.shape, jnp.int32),
            pltpu.SMEM(species_shift.shape, F32),
            pltpu.SemaphoreType.DMA((3 + len(weights),)),
        ],
        compiler_params=pltpu.CompilerParams(vmem_limit_bytes=8 * 1024 * 1024),
        name="fetch_weights",
    )(*in_hbm(species, listed, species_shift, *weights))
    last_x = moved(high, {"gx": 1})
    sides = []
    for step in (-1, 1)[: kind - 1]:
        sides.append(moved(high, {"gx": 1, "gy": step}))
        sides.insert(-1, moved(low, {"gy": step}))
    next_z = moved(joined([low, last_x, *sides]), {"gz": -1})
    kept = 1 if kind == 2 else kind
    half = 2 * kept * owned
    keep, send = pl.pallas_call(
        functools.partial(force_kernel, kind, nbr),
        out_shape=(
            jax.ShapeDtypeStruct((ORDERS, half), F32),
            jax.ShapeDtypeStruct((ORDERS, half), F32),
        ),
        in_specs=[vmem] * (8 + 2 * kind),
        out_specs=(vmem, vmem),
        compiler_params=pltpu.CompilerParams(vmem_limit_bytes=44 * 1024 * 1024),
        name="pair_forces",
    )(
        low,
        last_x,
        *sides,
        next_z,
        *weights,
    )
    totals = keep + moved(send, {"gx": -1})

    def part(index):
        return totals[:, index * owned : (index + 1) * owned]

    back = [moved(part(kept), {"gz": 1})]
    for i, step in enumerate((1, -1)[: kept - 1]):
        back.append(moved(part(kept + 1 + i), {"gy": step, "gz": 1}))
        back.append(moved(part(1 + i), {"gy": step}))
    site_energy, forces, virial = pl.pallas_call(
        finish_kernel,
        out_shape=(
            jax.ShapeDtypeStruct(species.shape, F32),
            jax.ShapeDtypeStruct(positions.shape, F32),
            jax.ShapeDtypeStruct((*species.shape, 9), F32),
        ),
        in_specs=[vmem] * (2 + len(back)),
        out_specs=(vmem, vmem, vmem),
        compiler_params=pltpu.CompilerParams(vmem_limit_bytes=8 * 1024 * 1024),
        name="write_outputs",
    )(totals, shift_row, *back)
    return (site_energy, forces, jnp.transpose(virial, (4, 0, 1, 2, 3)))


def solution(mesh):
    placed = (
        P(None, "gx", "gy", "gz", None),
        P("gx", "gy", "gz", None, None),
        P("gx", "gy", "gz", None),
        P(("gx", "gy", "gz")),
        P(("gx", "gy", "gz"), None),
        P(("gx", "gy", "gz")),
        P(),
        P(),
        P(),
        P(),
        P(),
        P(),
        P(),
        P(),
        P(),
    )
    return jax.shard_map(
        local,
        mesh=mesh,
        in_specs=placed,
        out_specs=(
            P("gx", "gy", "gz", None),
            P(None, "gx", "gy", "gz", None),
            P(None, "gx", "gy", "gz", None),
        ),
        check_vma=False,
    )
```

```python
import functools
import math

import jax
import jax.numpy as jnp
import numpy as np
from jax import lax
from jax.experimental import pallas as pl
from jax.experimental.pallas import tpu as pltpu
from jax.sharding import PartitionSpec as P

EXACT_DOT = lax.Precision.HIGHEST
CUTOFF = 5.0
CELL_SIDE = 4.6
ROOT_HALF = 0.7071067811865476
GROUP = 8
ORDERS = 16
LEVELS = (0, 1, 1, 1, 2, 2, 2, 2, 2)
SITES = 8
OWN_CELLS = 4
FRAME_CELLS = 48
F32 = jnp.float32
BF16 = jnp.bfloat16


def split(value):
    high = value.astype(BF16)
    low = (value - high.astype(F32)).astype(BF16)
    return high, low


def split3(value):
    high = value.astype(BF16)
    rest = value - high.astype(F32)
    middle = rest.astype(BF16)
    low = (rest - middle.astype(F32)).astype(BF16)
    return high, middle, low


def halves(value):
    high = value.astype(BF16).astype(F32)
    return high, value - high


def mm(a, b):
    return lax.dot_general(a, b, (((1,), (0,)), ((), ())), preferred_element_type=F32)


def mm_nt(a, b):
    return lax.dot_general(a, b, (((1,), (1,)), ((), ())), preferred_element_type=F32)


def stacked(high, low):
    top = jnp.concatenate([high, high], axis=1)
    bottom = jnp.concatenate([low, jnp.zeros_like(low)], axis=1)
    return jnp.concatenate([top, bottom], axis=0)


def folded(product):
    half = product.shape[0] // 2
    return product[:half] + product[half:]


def three(high, low):
    return jnp.concatenate([high, low, high], axis=1)


def deep(weights, value_high, value_low):
    return mm(weights, jnp.concatenate([value_high, value_high, value_low], axis=0))


def sin_cos_pi(turns):
    near = turns - 2.0 * jnp.round(turns * 0.5)
    quarter = jnp.round(near * 2.0)
    v = (near - 0.5 * quarter) * math.pi
    v2 = v * v
    s = v * (
        1.0
        + v2
        * (-1.0 / 6 + v2 * (1.0 / 120 + v2 * (-1.0 / 5040 + v2 * (1.0 / 362880 - v2 / 39916800))))
    )
    c = 1.0 + v2 * (
        -0.5
        + v2
        * (1.0 / 24 + v2 * (-1.0 / 720 + v2 * (1.0 / 40320 + v2 * (-1.0 / 3628800 + v2 / 479001600))))
    )
    odd = jnp.abs(quarter) == 1.0
    sine = jnp.where(odd, quarter * c, jnp.where(quarter == 0.0, s, -s))
    cosine = jnp.where(odd, -quarter * s, jnp.where(quarter == 0.0, c, -c))
    return sine, cosine


def lane_row(piece, offset):
    row = jnp.concatenate([piece, jnp.zeros((1, 128 - piece.shape[1]), piece.dtype)], axis=1)
    return pltpu.roll(row, offset, 1) if offset else row


def pack_kernel(
    kind,
    positions_hbm,
    features_hbm,
    species_hbm,
    centers_hbm,
    neighbours_hbm,
    scale_hbm,
    low_ref,
    high_ref,
    wide_ref,
    positions_ref,
    species_ref,
    centers_ref,
    neighbours_ref,
    scale_ref,
    sems,
):
    owned, nbr = neighbours_ref.shape
    per_row = 128 // nbr
    pairs_in = (
        (features_hbm, low_ref.at[pl.ds(0, owned), :]),
        (neighbours_hbm, neighbours_ref),
        (centers_hbm, centers_ref),
        (positions_hbm, positions_ref),
        (species_hbm, species_ref),
        (scale_hbm, scale_ref),
    )
    copies = [
        pltpu.make_async_copy(source, target, sems.at[i])
        for i, (source, target) in enumerate(pairs_in)
    ]
    for copy in copies:
        copy.start()
    for copy in copies:
        copy.wait()
    for cell in range(OWN_CELLS):
        x, z = cell // 2, cell % 2
        species = species_ref[x, 0, z : z + 1, :]
        scale = jnp.zeros(species.shape, F32)
        for s in range(scale_ref.shape[0]):
            scale = jnp.where(species == s, scale_ref[s], scale)
        row = lane_row(scale, 3 * SITES)
        for c in range(3):
            row = row + lane_row(positions_ref[c, x, 0, z : z + 1, :], c * SITES)
        low_ref[owned + cell : owned + cell + 1] = row

    chosen = lax.broadcasted_iota(jnp.int32, (owned, owned), 0) == centers_ref[...]
    chosen = jnp.where(chosen, 1.0, 0.0)
    occupied = jnp.sum(chosen, axis=1, keepdims=True) > 0.5
    chosen = chosen.astype(BF16)
    rows = neighbours_ref[...]
    upper = mm(chosen, (rows >> 4).astype(F32).astype(BF16))
    lower = mm(chosen, (rows & 15).astype(F32).astype(BF16))
    rows = (upper * 16.0 + lower).astype(jnp.int32)
    live = occupied & (rows < FRAME_CELLS * SITES)
    slot = lax.broadcasted_iota(jnp.int32, (owned, nbr), 0)
    cell = slot >> 3
    site = rows & 7
    place = rows >> 3
    near_z = (place & 3) + 1 - 2 * (cell & 1)
    column = place >> 2
    frame_x = (column * 11) >> 5
    frame_y = column - 3 * frame_x
    near_x = frame_x + 1 - 2 * (cell >> 1)
    side = jnp.where(frame_y == 1, 0, jnp.where(frame_y == 2, 1, kind - 1))
    block = (near_z >> 1) * 2 + 1 - (near_x >> 1)
    where = (block * kind + side) * owned + (near_x & 1) * 16 + (near_z & 1) * 8 + site
    code = jnp.where(live, 1 + where + (frame_y << 10), 0).astype(F32)
    wide_ref[...] = jnp.concatenate([code, jnp.zeros((owned, 128 - nbr), F32)], axis=1)
    codes = wide_ref[pl.ds(0, owned // per_row, stride=per_row), :]
    for j in range(1, per_row):
        more = wide_ref[pl.ds(j, owned // per_row, stride=per_row), :]
        codes = codes + pltpu.roll(more, j * nbr, 1)
    tile = owned + OWN_CELLS
    low_ref[tile:] = codes[: codes.shape[0] // 2]
    high_ref[:tile] = low_ref[:tile]
    high_ref[tile:] = codes[codes.shape[0] // 2 :]


def fetch_kernel(species_hbm, centers_hbm, shift_hbm, *refs):
    *refs, shift_row_ref, species_ref, centers_ref, shift_ref, sems = refs
    count = len(refs) // 2
    pairs_in = [
        (species_hbm, species_ref),
        (centers_hbm, centers_ref),
        (shift_hbm, shift_ref),
        *zip(refs[:count], refs[count:]),
    ]
    copies = [
        pltpu.make_async_copy(source, target, sems.at[i])
        for i, (source, target) in enumerate(pairs_in)
    ]
    for copy in copies:
        copy.start()
    for copy in copies:
        copy.wait()
    owned = centers_ref.shape[1]
    shift_row = jnp.zeros((1, 128), F32)
    for cell in range(OWN_CELLS):
        species = species_ref[cell // 2, 0, cell % 2 : cell % 2 + 1, :]
        shift = jnp.zeros(species.shape, F32)
        for s in range(shift_ref.shape[0]):
            shift = jnp.where(species == s, shift_ref[s], shift)
        shift_row = shift_row + lane_row(shift, cell * SITES)
    chosen = lax.broadcasted_iota(jnp.int32, (owned, owned), 0) == centers_ref[...]
    occupied = jnp.sum(jnp.where(chosen, 1.0, 0.0), axis=1, keepdims=True) > 0.5
    column = jnp.where(occupied, jnp.ones((owned, 128), F32), 0.0)
    shift_row_ref[...] = shift_row[:, :owned] * jnp.transpose(column)[0:1]


def finish_kernel(mine_ref, shift_row_ref, *refs):
    *near_refs, energy_ref, forces_ref, virial_ref = refs
    owned = near_refs[0].shape[1]
    total = mine_ref[:, :owned]
    for near_ref in near_refs:
        total = total + near_ref[...]
    energy = total[12:13] + shift_row_ref[...]
    columns = jnp.transpose(jnp.concatenate([total, jnp.zeros((ORDERS, 128 - owned), F32)], axis=1))
    for cell in range(OWN_CELLS):
        x, z = cell // 2, cell % 2
        lanes = slice(cell * SITES, (cell + 1) * SITES)
        energy_ref[x, 0, z : z + 1, :] = energy[:, lanes]
        for c in range(3):
            forces_ref[c, x, 0, z : z + 1, :] = total[c : c + 1, lanes]
        virial_ref[x, 0, z] = columns[lanes, 3:12]


def force_kernel(kind, nbr, here_ref, last_x_ref, *refs):
    near_side_refs = refs[: 2 * kind - 2]
    (
        next_z_ref,
        center_weight_ref,
        near_weight_ref,
        basis_weight_ref,
        path_weight_ref,
        value_weight_ref,
        latent_weight_ref,
        out_weight_ref,
        keep_ref,
        send_ref,
    ) = refs[2 * kind - 2 :]
    height, width = here_ref.shape
    owned = OWN_CELLS * SITES
    center_sides = 2 if kind == 2 else 1
    kept_sides = 1 if kind == 2 else kind
    own_pairs = owned * nbr
    pairs = center_sides * own_pairs
    centers = center_sides * owned
    radial = basis_weight_ref.shape[0]
    span = GROUP * nbr
    groups = centers // GROUP
    sites = SITES
    root_count = math.sqrt(nbr)
    root_three = math.sqrt(3.0)
    root_fifteen = math.sqrt(15.0)
    root_five = math.sqrt(5.0)
    far = next_z_ref[...]
    mains = [here_ref[...], last_x_ref[...], far[:height], far[height : 2 * height]]
    near_sides = [ref[...] for ref in near_side_refs]
    far_sides = far[2 * height :]
    far_sides = [far_sides[i * height : (i + 1) * height] for i in range(2 * kind - 2)]
    blocks_in = [
        [mains[0], *near_sides[0::2]],
        [mains[1], *near_sides[1::2]],
        [mains[2], *far_sides[0::2]],
        [mains[3], *far_sides[1::2]],
    ]
    feats = jnp.concatenate([side[:owned] for block in blocks_in for side in block], axis=0)
    known = feats.shape[0]
    center_feats = []
    center_coords = []
    coords = []
    scales = []
    codes = []
    cell_row = lax.broadcasted_iota(jnp.int32, (kind * OWN_CELLS, 128), 0) % OWN_CELLS
    tile_lane = lax.broadcasted_iota(jnp.int32, (kind * OWN_CELLS, 128), 1)
    for g, block in enumerate(blocks_in):
        behind_x, ahead_z = g % 2, g // 2
        rows = jnp.concatenate([side[owned : owned + OWN_CELLS] for side in block], axis=0)
        corner_x = (cell_row // 2 + 2 - 2 * behind_x).astype(F32) * CELL_SIDE
        corner_z = (cell_row % 2 + 2 * ahead_z).astype(F32) * CELL_SIDE
        corner = jnp.where(
            tile_lane < sites, corner_x, jnp.where(tile_lane < 2 * sites, 0.0, corner_z)
        )
        coords.append(rows + corner)
    for c in range(center_sides):
        for g, block in enumerate(blocks_in):
            cell = g % 2 * 2 + 1 - g // 2
            row = c * OWN_CELLS + cell
            center_feats.append(block[c][cell * sites : (cell + 1) * sites])
            scales.append(block[c][owned + cell : owned + cell + 1])
            center_coords.append(coords[g][row : row + 1])
            start = owned + OWN_CELLS + (1 - g // 2) * span // 128
            codes.extend(block[c][start + r : start + r + 1] for r in range(span // 128))
    center_feats = jnp.concatenate(center_feats, axis=0)
    coords = jnp.concatenate(coords, axis=0)
    code = jnp.concatenate(codes, axis=1).astype(jnp.int32)
    live = code > 0
    code = jnp.maximum(code - 1, 0)
    side_y = ((code >> 10) - 1).astype(F32)
    near_row = code & 1023
    if center_sides == 2:
        pair_lane = lax.broadcasted_iota(jnp.int32, (1, pairs), 1)
        near_row = jnp.where(pair_lane < own_pairs, near_row, near_row ^ owned)
    near_row = jnp.where(live, near_row, known)

    def place_rows(cell_rows):
        count = cell_rows.shape[0] * sites
        spread = jnp.broadcast_to(cell_rows[:, None, :], (cell_rows.shape[0], sites, 128))
        spread = spread.reshape(count, 128)
        lane = lax.broadcasted_iota(jnp.int32, (count, 128), 1)
        row = lax.broadcasted_iota(jnp.int32, (count, 128), 0)
        keep = (lane % sites == row % sites) & (lane < 3 * sites)
        spread = jnp.transpose(jnp.where(keep, spread, 0.0))
        return jnp.concatenate(split3(spread[: 3 * sites]), axis=0)

    place_parts = place_rows(coords)
    center_parts = place_rows(jnp.concatenate(center_coords, axis=0))

    value_rows = three(*split(jnp.transpose(value_weight_ref[...])))
    latent_t = three(*split(0.5 * jnp.transpose(latent_weight_ref[...])))
    latent_rows = three(*split(latent_weight_ref[...] * out_weight_ref[...]))
    value_plain = three(*split(value_weight_ref[...]))
    basis_t = jnp.transpose(basis_weight_ref[...])
    basis_high_t, basis_low_t = split(0.5 * basis_t)
    basis_rows = three(*split(basis_weight_ref[...]))

    def project(weight, rows):
        weight = stacked(*split(jnp.transpose(weight)))
        return folded(mm_nt(weight, jnp.concatenate(split(rows), axis=1)))

    near_t = project(near_weight_ref[...], feats)
    own_t = project(center_weight_ref[...], center_feats)
    near_high, near_low = split(0.5 * near_t)
    own_high, own_low = split(0.5 * own_t)
    lookup = jnp.concatenate(
        [near_high, near_low, own_high, own_low, basis_high_t, basis_high_t, basis_low_t], axis=1
    )
    scale_rows = jnp.concatenate(scales, axis=0)
    scale_parts = jnp.concatenate(
        [*split3(scale_rows), jnp.zeros((-3 * groups % 16, 128), BF16)], axis=0
    )

    path_rows = jnp.concatenate(
        [jnp.broadcast_to(path_weight_ref[l : l + 1, :], (GROUP, width)) for l in LEVELS], axis=0
    ) * (1.0 / root_count)
    out_column = jnp.transpose(jnp.broadcast_to(out_weight_ref[...], (width, width)))
    out_column = jnp.concatenate([out_column] * (pairs // width), axis=1)

    site_ids = lax.broadcasted_iota(jnp.int32, (known, pairs), 0)
    slot_ids = lax.broadcasted_iota(jnp.int32, (centers, pairs), 0)
    slot_row = lax.broadcasted_iota(jnp.int32, (1, pairs), 1) // nbr
    group_lane = lax.broadcasted_iota(jnp.int32, (GROUP, pairs), 1) // nbr % GROUP
    group_mask = group_lane == lax.broadcasted_iota(jnp.int32, (GROUP, pairs), 0)
    group_mask = jnp.where(group_mask, 1.0, 0.0)
    tall = len(LEVELS) * GROUP
    order = lax.broadcasted_iota(jnp.int32, (radial, pairs), 0).astype(F32) + 1.0
    lanes = [slice(g * span, (g + 1) * span) for g in range(groups)]

    pick = jnp.where(site_ids == near_row, 1.0, 0.0)
    pick_half = pick.astype(BF16)
    slot_half = jnp.where(slot_ids == slot_row, 1.0, 0.0).astype(BF16)

    moved = mm(
        jnp.concatenate([place_parts, -center_parts], axis=1),
        jnp.concatenate([pick_half, slot_half], axis=0),
    )
    moved = moved[: 3 * sites] + moved[3 * sites : 6 * sites] + moved[6 * sites :]
    dx = jnp.where(live, jnp.sum(moved[:sites], axis=0, keepdims=True), 6.0)
    dy = jnp.sum(moved[sites : 2 * sites], axis=0, keepdims=True) + CELL_SIDE * side_y
    dy = jnp.where(live, dy, 0.0)
    dz = jnp.where(live, jnp.sum(moved[2 * sites :], axis=0, keepdims=True), 0.0)
    length = jnp.sqrt(dx * dx + dy * dy + dz * dz)
    inverse = 1.0 / length
    ratio = length * (1.0 / CUTOFF)
    inside = live & (ratio < 1.0)
    r2 = ratio * ratio
    r5 = r2 * r2 * ratio
    r6 = r5 * ratio
    weight = jnp.where(inside, 1.0 - r6 * (28.0 - 48.0 * ratio + 21.0 * r2), 0.0)
    slope = jnp.where(inside, -168.0 * r5 * (1.0 - 2.0 * ratio + r2), 0.0)
    sine, cosine = sin_cos_pi(order * ratio)
    basis = (math.sqrt(2.0 / CUTOFF) * inverse) * sine
    basis_slope = (math.sqrt(2.0 / CUTOFF) * inverse) * (
        (math.pi / CUTOFF) * order * cosine - sine * inverse
    )
    ex = dx * inverse
    ey = dy * inverse
    ez = dz * inverse
    angular = jnp.concatenate(
        [
            jnp.ones_like(ex),
            root_three * ex,
            root_three * ey,
            root_three * ez,
            root_fifteen * ex * ey,
            root_fifteen * ey * ez,
            0.5 * root_five * (3.0 * ez * ez - 1.0),
            root_fifteen * ex * ez,
            0.5 * root_fifteen * (ex * ex - ey * ey),
        ],
        axis=0,
    )
    angular_high, angular_low = halves(angular)
    angular_low = angular_low.astype(BF16).astype(F32)
    block_high = [angular_high[m : m + 1] * group_mask for m in range(len(LEVELS))]
    block_low = [angular_low[m : m + 1] * group_mask for m in range(len(LEVELS))]
    blocks = jnp.concatenate(block_high + block_low + block_high, axis=0).astype(BF16)
    lane_ids = lax.broadcasted_iota(jnp.int32, (128, span), 0)
    lane_slot = lax.broadcasted_iota(jnp.int32, (128, span), 1) // nbr + 3 * sites
    scale = mm(scale_parts, jnp.where(lane_ids == lane_slot, 1.0, 0.0).astype(BF16))
    scale = scale[:groups] + scale[groups : 2 * groups] + scale[2 * groups : 3 * groups]
    scale = jnp.concatenate([scale[g : g + 1] for g in range(groups)], axis=1)
    scale = scale * (1.0 / root_count)
    pull = ROOT_HALF * scale

    basis_high, basis_low = halves(basis)
    basis_rest = jnp.concatenate([basis_high, basis_low, basis_high], axis=0).astype(BF16)
    before = mm(
        lookup,
        jnp.concatenate([pick_half, pick_half, slot_half, slot_half, basis_rest], axis=0),
    )
    gate = 1.0 + jnp.tanh(before)
    active = before * gate
    latent = weight * active
    latent_high, latent_low = split(latent)
    mixed = deep(value_rows, latent_high, latent_low)
    values = mixed[:width]
    env_high, env_low = split(mixed[width:])

    def over_pairs(high, low):
        sums = []
        for cut in lanes:
            both = jnp.concatenate([high[:, cut], low[:, cut]], axis=0)
            quad = mm_nt(blocks[: 2 * tall, cut], both)
            quad = quad[:tall, :width] + quad[tall:, :width] + quad[:tall, width:]
            sums.append(quad * path_rows)
        return sums

    def over_orders(tables):
        parts = []
        for table, cut in zip(tables, lanes):
            high, low = halves(table)
            table = jnp.transpose(jnp.concatenate([high, high, low], axis=0)).astype(BF16)
            parts.append(mm(table, blocks[:, cut]))
        return jnp.concatenate(parts, axis=1)

    weighted = over_pairs(env_high, env_low)
    inner = over_orders(weighted)
    scalars = values * inner
    scalars_high, scalars_low = split(scalars)
    z = deep(
        latent_t,
        jnp.concatenate([latent_high, scalars_high], axis=0),
        jnp.concatenate([latent_low, scalars_low], axis=0),
    )
    z_gate = 1.0 + jnp.tanh(z)
    update = z * z_gate
    update_sum = jnp.sum(update * out_column, axis=0, keepdims=True)
    active_sum = jnp.sum(
        active[:, :own_pairs] * out_column[:, :own_pairs], axis=0, keepdims=True
    )
    pair_energy = (active_sum + update_sum[:, :own_pairs]) * (pull * weight)[:, :own_pairs]
    d_z = (0.5 * pull * weight) * (z_gate + update * (2.0 - z_gate))
    spread_back = deep(latent_rows, *split(d_z))
    d_scalars = spread_back[width:]
    d_values = d_scalars * inner
    dinner_high, dinner_low = split(d_scalars * values)
    d_embed = over_pairs(dinner_high, dinner_low)
    d_env = over_orders(d_embed)

    d_angular = []
    for g, cut in enumerate(lanes):
        sides_high, sides_low = halves(jnp.concatenate([weighted[g], d_embed[g]], axis=1))
        d_block = deep(
            three(sides_high.astype(BF16), sides_low.astype(BF16)),
            jnp.concatenate([dinner_high[:, cut], env_high[:, cut]], axis=0),
            jnp.concatenate([dinner_low[:, cut], env_low[:, cut]], axis=0),
        )
        d_block = d_block.reshape(len(LEVELS), GROUP, span) * group_mask[None, :, cut]
        d_angular.append(jnp.sum(d_block, axis=1))
    d_angular = jnp.concatenate(d_angular, axis=1)

    mixed_high, mixed_low = split(jnp.concatenate([d_values, d_env], axis=0))
    d_latent = (
        deep(value_plain, mixed_high, mixed_low)
        + spread_back[:width]
        + pull * out_column
    )
    d_weight = jnp.sum(d_latent * active, axis=0, keepdims=True) + pull * update_sum
    d_before = d_latent * (gate + active * (2.0 - gate))
    d_basis = deep(basis_rows, *split(d_before)) * (0.5 * weight)

    d_length = jnp.sum(d_basis * basis_slope, axis=0, keepdims=True) + d_weight * slope * (
        1.0 / CUTOFF
    )
    a1, a2, a3, a4, a5, a6, a7, a8 = [d_angular[m : m + 1] for m in range(1, 9)]
    ux = root_three * a1 + root_fifteen * (ey * a4 + ez * a7 + ex * a8)
    uy = root_three * a2 + root_fifteen * (ex * a4 + ez * a5 - ey * a8)
    uz = root_three * a3 + root_fifteen * (ey * a5 + ex * a7) + 3.0 * root_five * ez * a6
    along = ex * ux + ey * uy + ez * uz
    radial_part = d_length - along * inverse
    gx = ux * inverse + ex * radial_part
    gy = uy * inverse + ey * radial_part
    gz = uz * inverse + ez * radial_part
    hx = -0.5 * dx
    hy = -0.5 * dy
    hz = -0.5 * dz
    virial = [hx * gx, hx * gy, hx * gz, hy * gx, hy * gy, hy * gz, hz * gx, hz * gy, hz * gz]
    rest = [jnp.zeros((ORDERS - 13, pairs), F32)]
    near_terms = jnp.concatenate(
        [-gx, -gy, -gz, *virial, jnp.zeros_like(gx), *rest], axis=0
    )
    center_rows = [gx, gy, gz, *virial]
    center_rows = [r[:, :own_pairs] for r in center_rows] + [pair_energy]
    center_rows.append(jnp.zeros((ORDERS - 13, own_pairs), F32))
    center_terms = jnp.concatenate(center_rows, axis=0)
    reach = []
    for x, z, side in np.ndindex(2, 2, kept_sides):
        start = ((2 * z + x) * kind + side) * owned
        reach.append(pick_half[start : start + owned])
    reach = jnp.concatenate(reach, axis=0)
    near_sums = mm_nt(jnp.concatenate(split(near_terms), axis=0), reach)
    center_sums = mm_nt(
        jnp.concatenate(split(center_terms), axis=0), slot_half[:owned, :own_pairs]
    )
    center_sums = jnp.concatenate(
        [folded(center_sums), jnp.zeros((ORDERS, 128 - owned), F32)], axis=1
    )
    totals = folded(near_sums)
    lane = lax.broadcasted_iota(jnp.int32, (ORDERS, 128), 1)
    known = totals.shape[1]
    tiles = [totals[:, 128 * i : 128 * (i + 1)] for i in range(known // 128)]
    for g in range(owned // GROUP):
        cell = g % 2 * 2 + 1 - g // 2
        target = (g % 2 * 2 + g // 2) * kept_sides * owned + cell * sites
        turn = (target - g * GROUP) % 128
        piece = pltpu.roll(center_sums, turn, 1) if turn else center_sums
        begin = target % 128
        piece = jnp.where((lane >= begin) & (lane < begin + GROUP), piece, 0.0)
        tiles[target // 128] = tiles[target // 128] + piece
    totals = jnp.concatenate(tiles, axis=1)
    keep_ref[...] = totals[:, : known // 2]
    send_ref[...] = totals[:, known // 2 :]


def in_hbm(*arrays):
    return [pltpu.with_memory_space_constraint(array, pltpu.HBM) for array in arrays]


def joined(parts):
    total = sum(part.shape[0] for part in parts)
    start = 0
    pads = []
    for part in parts:
        end = start + part.shape[0]
        pads.append(jnp.pad(part, ((start, total - end), (0, 0))))
        start = end
    return functools.reduce(jnp.add, pads)


def local(
    positions,
    features,
    species,
    centers,
    neighbours,
    counts,
    species_scale,
    species_shift,
    center_weight,
    near_weight,
    basis_weight,
    path_weight,
    value_weight,
    latent_weight,
    out_weight,
):
    cells_x, cells_y, cells_z, sites, width = features.shape
    cell_count = cells_x * cells_y * cells_z
    owned = cell_count * sites
    assert (cells_x, cells_y, cells_z, sites) == (2, 1, 2, SITES)
    pairs = neighbours.size
    nbr = pairs // owned
    kind = min(3, lax.axis_size("gy"))

    def moved(array, steps):
        names = tuple(steps)
        sizes = [lax.axis_size(name) for name in names]
        route = []
        for at in np.ndindex(*sizes):
            to = [(p + steps[name]) % size for p, name, size in zip(at, names, sizes)]
            route.append(
                (int(np.ravel_multi_index(at, sizes)), int(np.ravel_multi_index(to, sizes)))
            )
        return lax.ppermute(array, names, route)

    vmem = pl.BlockSpec(memory_space=pltpu.VMEM)
    hbm = pl.BlockSpec(memory_space=pltpu.HBM)
    listed = centers.reshape(1, owned)
    payload = jax.ShapeDtypeStruct((owned + OWN_CELLS + pairs // 256, width), F32)
    low, high = pl.pallas_call(
        functools.partial(pack_kernel, kind),
        out_shape=(payload, payload),
        in_specs=[hbm] * 6,
        out_specs=(vmem, vmem),
        scratch_shapes=[
            pltpu.VMEM((owned, 128), F32),
            pltpu.VMEM(positions.shape, F32),
            pltpu.VMEM(species.shape, jnp.int32),
            pltpu.VMEM(listed.shape, jnp.int32),
            pltpu.VMEM(neighbours.shape, jnp.int32),
            pltpu.SMEM(species_scale.shape, F32),
            pltpu.SemaphoreType.DMA((6,)),
        ],
        compiler_params=pltpu.CompilerParams(vmem_limit_bytes=8 * 1024 * 1024),
        name="pack_payload",
    )(
        *in_hbm(
            positions,
            features.reshape(owned, width),
            species,
            listed,
            neighbours,
            species_scale,
        )
    )
    weights = (
        center_weight,
        near_weight,
        basis_weight,
        path_weight,
        value_weight,
        latent_weight,
        out_weight.reshape(1, width),
    )
    *weights, shift_row = pl.pallas_call(
        fetch_kernel,
        out_shape=(
            *(jax.ShapeDtypeStruct(w.shape, F32) for w in weights),
            jax.ShapeDtypeStruct((1, owned), F32),
        ),
        in_specs=[hbm] * (3 + len(weights)),
        out_specs=(vmem,) * (1 + len(weights)),
        scratch_shapes=[
            pltpu.VMEM(species.shape, jnp.int32),
            pltpu.VMEM(listed.shape, jnp.int32),
            pltpu.SMEM(species_shift.shape, F32),
            pltpu.SemaphoreType.DMA((3 + len(weights),)),
        ],
        compiler_params=pltpu.CompilerParams(vmem_limit_bytes=8 * 1024 * 1024),
        name="fetch_weights",
    )(*in_hbm(species, listed, species_shift, *weights))
    last_x = moved(high, {"gx": 1})
    sides = []
    for step in (-1, 1)[: kind - 1]:
        sides.append(moved(high, {"gx": 1, "gy": step}))
        sides.insert(-1, moved(low, {"gy": step}))
    next_z = moved(joined([low, last_x, *sides]), {"gz": -1})
    kept = 1 if kind == 2 else kind
    half = 2 * kept * owned
    keep, send = pl.pallas_call(
        functools.partial(force_kernel, kind, nbr),
        out_shape=(
            jax.ShapeDtypeStruct((ORDERS, half), F32),
            jax.ShapeDtypeStruct((ORDERS, half), F32),
        ),
        in_specs=[vmem] * (8 + 2 * kind),
        out_specs=(vmem, vmem),
        compiler_params=pltpu.CompilerParams(vmem_limit_bytes=44 * 1024 * 1024),
        name="pair_forces",
    )(
        low,
        last_x,
        *sides,
        next_z,
        *weights,
    )
    totals = keep + moved(send, {"gx": -1})

    def part(index):
        return totals[:, index * owned : (index + 1) * owned]

    back = [moved(part(kept), {"gz": 1})]
    for i, step in enumerate((1, -1)[: kept - 1]):
        back.append(moved(part(kept + 1 + i), {"gy": step, "gz": 1}))
        back.append(moved(part(1 + i), {"gy": step}))
    site_energy, forces, virial = pl.pallas_call(
        finish_kernel,
        out_shape=(
            jax.ShapeDtypeStruct(species.shape, F32),
            jax.ShapeDtypeStruct(positions.shape, F32),
            jax.ShapeDtypeStruct((*species.shape, 9), F32),
        ),
        in_specs=[vmem] * (2 + len(back)),
        out_specs=(vmem, vmem, vmem),
        compiler_params=pltpu.CompilerParams(vmem_limit_bytes=8 * 1024 * 1024),
        name="write_outputs",
    )(totals, shift_row, *back)
    return (site_energy, forces, jnp.transpose(virial, (4, 0, 1, 2, 3)))


def solution(mesh):
    placed = (
        P(None, "gx", "gy", "gz", None),
        P("gx", "gy", "gz", None, None),
        P("gx", "gy", "gz", None),
        P(("gx", "gy", "gz")),
        P(("gx", "gy", "gz"), None),
        P(("gx", "gy", "gz")),
        P(),
        P(),
        P(),
        P(),
        P(),
        P(),
        P(),
        P(),
        P(),
    )
    return jax.shard_map(
        local,
        mesh=mesh,
        in_specs=placed,
        out_specs=(
            P("gx", "gy", "gz", None),
            P(None, "gx", "gy", "gz", None),
            P(None, "gx", "gy", "gz", None),
        ),
        check_vma=False,
    )
```

```python
import functools
import math

import jax
import jax.numpy as jnp
import numpy as np
from jax import lax
from jax.experimental import pallas as pl
from jax.experimental.pallas import tpu as pltpu
from jax.sharding import PartitionSpec as P

EXACT_DOT = lax.Precision.HIGHEST
CUTOFF = 5.0
CELL_SIDE = 4.6
ROOT_HALF = 0.7071067811865476
GROUP = 8
ORDERS = 16
LEVELS = (0, 1, 1, 1, 2, 2, 2, 2, 2)
SITES = 8
OWN_CELLS = 4
FRAME_CELLS = 48
F32 = jnp.float32
BF16 = jnp.bfloat16


def split(value):
    high = value.astype(BF16)
    low = (value - high.astype(F32)).astype(BF16)
    return high, low


def split3(value):
    high = value.astype(BF16)
    rest = value - high.astype(F32)
    middle = rest.astype(BF16)
    low = (rest - middle.astype(F32)).astype(BF16)
    return high, middle, low


def halves(value):
    high = value.astype(BF16).astype(F32)
    return high, value - high


def mm(a, b):
    return lax.dot_general(a, b, (((1,), (0,)), ((), ())), preferred_element_type=F32)


def mm_nt(a, b):
    return lax.dot_general(a, b, (((1,), (1,)), ((), ())), preferred_element_type=F32)


def stacked(high, low):
    top = jnp.concatenate([high, high], axis=1)
    bottom = jnp.concatenate([low, jnp.zeros_like(low)], axis=1)
    return jnp.concatenate([top, bottom], axis=0)


def folded(product):
    half = product.shape[0] // 2
    return product[:half] + product[half:]


def three(high, low):
    return jnp.concatenate([high, low, high], axis=1)


def deep(weights, value_high, value_low):
    return mm(weights, jnp.concatenate([value_high, value_high, value_low], axis=0))


def sin_cos_pi(turns):
    near = turns - 2.0 * jnp.round(turns * 0.5)
    quarter = jnp.round(near * 2.0)
    v = (near - 0.5 * quarter) * math.pi
    v2 = v * v
    s = v * (
        1.0
        + v2
        * (-1.0 / 6 + v2 * (1.0 / 120 + v2 * (-1.0 / 5040 + v2 * (1.0 / 362880 - v2 / 39916800))))
    )
    c = 1.0 + v2 * (
        -0.5
        + v2
        * (1.0 / 24 + v2 * (-1.0 / 720 + v2 * (1.0 / 40320 + v2 * (-1.0 / 3628800 + v2 / 479001600))))
    )
    odd = jnp.abs(quarter) == 1.0
    sine = jnp.where(odd, quarter * c, jnp.where(quarter == 0.0, s, -s))
    cosine = jnp.where(odd, -quarter * s, jnp.where(quarter == 0.0, c, -c))
    return sine, cosine


def lane_row(piece, offset):
    row = jnp.concatenate([piece, jnp.zeros((1, 128 - piece.shape[1]), piece.dtype)], axis=1)
    return pltpu.roll(row, offset, 1) if offset else row


def pack_kernel(
    kind,
    positions_hbm,
    features_hbm,
    species_hbm,
    centers_hbm,
    neighbours_hbm,
    scale_hbm,
    low_ref,
    high_ref,
    wide_ref,
    positions_ref,
    species_ref,
    centers_ref,
    neighbours_ref,
    scale_ref,
    features_ref,
    sems,
):
    owned, nbr = neighbours_ref.shape
    per_row = 128 // nbr
    pairs_in = (
        (centers_hbm, centers_ref),
        (neighbours_hbm, neighbours_ref),
        (positions_hbm, positions_ref),
        (species_hbm, species_ref),
        (scale_hbm, scale_ref),
        (features_hbm, features_ref),
    )
    copies = [
        pltpu.make_async_copy(source, target, sems.at[i])
        for i, (source, target) in enumerate(pairs_in)
    ]
    for copy in copies:
        copy.start()
    for copy in copies[:2]:
        copy.wait()
    chosen = lax.broadcasted_iota(jnp.int32, (owned, owned), 0) == centers_ref[...]
    chosen = jnp.where(chosen, 1.0, 0.0)
    occupied = jnp.sum(chosen, axis=1, keepdims=True) > 0.5
    chosen = chosen.astype(BF16)
    rows = neighbours_ref[...]
    upper = mm(chosen, (rows >> 4).astype(F32).astype(BF16))
    lower = mm(chosen, (rows & 15).astype(F32).astype(BF16))
    rows = (upper * 16.0 + lower).astype(jnp.int32)
    live = occupied & (rows < FRAME_CELLS * SITES)
    slot = lax.broadcasted_iota(jnp.int32, (owned, nbr), 0)
    cell = slot >> 3
    site = rows & 7
    place = rows >> 3
    near_z = (place & 3) + 1 - 2 * (cell & 1)
    column = place >> 2
    frame_x = (column * 11) >> 5
    frame_y = column - 3 * frame_x
    near_x = frame_x + 1 - 2 * (cell >> 1)
    side = jnp.where(frame_y == 1, 0, jnp.where(frame_y == 2, 1, kind - 1))
    block = (near_z >> 1) * 2 + 1 - (near_x >> 1)
    where = (block * kind + side) * owned + (near_x & 1) * 16 + (near_z & 1) * 8 + site
    code = jnp.where(live, 1 + where + (frame_y << 10), 0).astype(F32)
    wide_ref[...] = jnp.concatenate([code, jnp.zeros((owned, 128 - nbr), F32)], axis=1)
    codes = wide_ref[pl.ds(0, owned // per_row, stride=per_row), :]
    for j in range(1, per_row):
        more = wide_ref[pl.ds(j, owned // per_row, stride=per_row), :]
        codes = codes + pltpu.roll(more, j * nbr, 1)
    tile = owned + OWN_CELLS
    low_ref[tile:] = codes[: codes.shape[0] // 2]
    high_ref[tile:] = codes[codes.shape[0] // 2 :]
    for copy in copies[2:]:
        copy.wait()
    for cell in range(OWN_CELLS):
        x, z = cell // 2, cell % 2
        species = species_ref[x, 0, z : z + 1, :]
        scale = jnp.zeros(species.shape, F32)
        for s in range(scale_ref.shape[0]):
            scale = jnp.where(species == s, scale_ref[s], scale)
        row = lane_row(scale, 3 * SITES)
        for c in range(3):
            row = row + lane_row(positions_ref[c, x, 0, z : z + 1, :], c * SITES)
        low_ref[owned + cell : owned + cell + 1] = row
        high_ref[owned + cell : owned + cell + 1] = row

    low_ref[:owned] = features_ref[...]
    high_ref[:owned] = features_ref[...]


def fetch_kernel(nbr, *refs):
    sources = refs[:9]
    (
        near_ref,
        center_ref,
        path_rows_ref,
        value_rows_ref,
        value_plain_ref,
        latent_t_ref,
        latent_rows_ref,
        out_column_ref,
        shift_row_ref,
    ) = refs[9:18]
    targets = refs[18:27]
    sems = refs[27]
    copies = [
        pltpu.make_async_copy(source, target, sems.at[i])
        for i, (source, target) in enumerate(zip(sources, targets))
    ]
    for copy in copies:
        copy.start()
    for copy in copies:
        copy.wait()
    species_ref, centers_ref, shift_ref, *weights = targets
    center_weight, near_weight, path_weight, value_weight, latent_weight, out_weight = [
        ref[...] for ref in weights
    ]
    width = near_weight.shape[0]
    near_ref[...] = stacked(*split(jnp.transpose(near_weight)))
    center_ref[...] = stacked(*split(jnp.transpose(center_weight)))
    path_rows_ref[...] = jnp.concatenate(
        [jnp.broadcast_to(path_weight[l : l + 1, :], (GROUP, width)) for l in LEVELS], axis=0
    ) * (1.0 / math.sqrt(nbr))
    value_rows_ref[...] = three(*split(jnp.transpose(value_weight)))
    value_plain_ref[...] = three(*split(value_weight))
    latent_t_ref[...] = three(*split(0.5 * jnp.transpose(latent_weight)))
    latent_rows_ref[...] = three(*split(latent_weight * out_weight))
    out_column_ref[...] = jnp.transpose(jnp.broadcast_to(out_weight, (width, width)))
    owned = centers_ref.shape[1]
    shift_row = jnp.zeros((1, 128), F32)
    for cell in range(OWN_CELLS):
        species = species_ref[cell // 2, 0, cell % 2 : cell % 2 + 1, :]
        shift = jnp.zeros(species.shape, F32)
        for s in range(shift_ref.shape[0]):
            shift = jnp.where(species == s, shift_ref[s], shift)
        shift_row = shift_row + lane_row(shift, cell * SITES)
    chosen = lax.broadcasted_iota(jnp.int32, (owned, owned), 0) == centers_ref[...]
    occupied = jnp.sum(jnp.where(chosen, 1.0, 0.0), axis=1, keepdims=True) > 0.5
    column = jnp.where(occupied, jnp.ones((owned, 128), F32), 0.0)
    shift_row_ref[...] = shift_row[:, :owned] * jnp.transpose(column)[0:1]


def finish_kernel(mine_ref, shift_row_ref, *refs):
    *near_refs, energy_ref, forces_ref, virial_ref = refs
    owned = shift_row_ref.shape[1]
    total = mine_ref[:, :owned]
    for near_ref in near_refs:
        start = near_ref.shape[1] - owned
        total = total + near_ref[:, start : start + owned]
    energy = total[12:13] + shift_row_ref[...]
    columns = jnp.transpose(jnp.concatenate([total, jnp.zeros((ORDERS, 128 - owned), F32)], axis=1))
    for cell in range(OWN_CELLS):
        x, z = cell // 2, cell % 2
        lanes = slice(cell * SITES, (cell + 1) * SITES)
        energy_ref[x, 0, z : z + 1, :] = energy[:, lanes]
        for c in range(3):
            forces_ref[c, x, 0, z : z + 1, :] = total[c : c + 1, lanes]
        virial_ref[x, 0, z] = columns[lanes, 3:12]


def force_kernel(kind, nbr, here_ref, last_x_ref, *refs):
    near_side_refs = refs[: 2 * kind - 2]
    (
        next_z_ref,
        near_stack_ref,
        center_stack_ref,
        path_rows_ref,
        value_rows_ref,
        value_plain_ref,
        latent_t_ref,
        latent_rows_ref,
        out_column_ref,
        basis_weight_ref,
        keep_ref,
        send_ref,
    ) = refs[2 * kind - 2 :]
    height, width = here_ref.shape
    owned = OWN_CELLS * SITES
    center_sides = 2 if kind == 2 else 1
    kept_sides = 1 if kind == 2 else kind
    own_pairs = owned * nbr
    pairs = center_sides * own_pairs
    centers = center_sides * owned
    radial = basis_weight_ref.shape[0]
    span = GROUP * nbr
    groups = centers // GROUP
    sites = SITES
    root_count = math.sqrt(nbr)
    root_three = math.sqrt(3.0)
    root_fifteen = math.sqrt(15.0)
    root_five = math.sqrt(5.0)
    far = next_z_ref[...]
    mains = [here_ref[...], last_x_ref[...], far[:height], far[height : 2 * height]]
    near_sides = [ref[...] for ref in near_side_refs]
    far_sides = far[2 * height :]
    far_sides = [far_sides[i * height : (i + 1) * height] for i in range(2 * kind - 2)]
    blocks_in = [
        [mains[0], *near_sides[0::2]],
        [mains[1], *near_sides[1::2]],
        [mains[2], *far_sides[0::2]],
        [mains[3], *far_sides[1::2]],
    ]
    feats = jnp.concatenate([side[:owned] for block in blocks_in for side in block], axis=0)
    known = feats.shape[0]
    center_feats = []
    center_coords = []
    coords = []
    scales = []
    codes = []
    cell_row = lax.broadcasted_iota(jnp.int32, (kind * OWN_CELLS, 128), 0) % OWN_CELLS
    tile_lane = lax.broadcasted_iota(jnp.int32, (kind * OWN_CELLS, 128), 1)
    for g, block in enumerate(blocks_in):
        behind_x, ahead_z = g % 2, g // 2
        rows = jnp.concatenate([side[owned : owned + OWN_CELLS] for side in block], axis=0)
        corner_x = (cell_row // 2 + 2 - 2 * behind_x).astype(F32) * CELL_SIDE
        corner_z = (cell_row % 2 + 2 * ahead_z).astype(F32) * CELL_SIDE
        corner = jnp.where(
            tile_lane < sites, corner_x, jnp.where(tile_lane < 2 * sites, 0.0, corner_z)
        )
        coords.append(rows + corner)
    for c in range(center_sides):
        for g, block in enumerate(blocks_in):
            cell = g % 2 * 2 + 1 - g // 2
            row = c * OWN_CELLS + cell
            center_feats.append(block[c][cell * sites : (cell + 1) * sites])
            scales.append(block[c][owned + cell : owned + cell + 1])
            center_coords.append(coords[g][row : row + 1])
            start = owned + OWN_CELLS + (1 - g // 2) * span // 128
            codes.extend(block[c][start + r : start + r + 1] for r in range(span // 128))
    center_feats = jnp.concatenate(center_feats, axis=0)
    coords = jnp.concatenate(coords, axis=0)
    code = jnp.concatenate(codes, axis=1).astype(jnp.int32)
    live = code > 0
    code = jnp.maximum(code - 1, 0)
    side_y = ((code >> 10) - 1).astype(F32)
    near_row = code & 1023
    if center_sides == 2:
        pair_lane = lax.broadcasted_iota(jnp.int32, (1, pairs), 1)
        near_row = jnp.where(pair_lane < own_pairs, near_row, near_row ^ owned)
    near_row = jnp.where(live, near_row, known)

    def place_rows(cell_rows):
        count = cell_rows.shape[0] * sites
        spread = jnp.broadcast_to(cell_rows[:, None, :], (cell_rows.shape[0], sites, 128))
        spread = spread.reshape(count, 128)
        lane = lax.broadcasted_iota(jnp.int32, (count, 128), 1)
        row = lax.broadcasted_iota(jnp.int32, (count, 128), 0)
        keep = (lane % sites == row % sites) & (lane < 3 * sites)
        spread = jnp.transpose(jnp.where(keep, spread, 0.0))
        return jnp.concatenate(split3(spread[: 3 * sites]), axis=0)

    place_parts = place_rows(coords)
    center_parts = place_rows(jnp.concatenate(center_coords, axis=0))

    value_rows = value_rows_ref[...]
    value_plain = value_plain_ref[...]
    latent_t = latent_t_ref[...]
    latent_rows = latent_rows_ref[...]
    path_rows = path_rows_ref[...]
    basis_t = jnp.transpose(basis_weight_ref[...])
    basis_high_t, basis_low_t = split(0.5 * basis_t)
    basis_rows = three(*split(basis_weight_ref[...]))

    def project(weight, rows):
        return folded(mm_nt(weight, jnp.concatenate(split(rows), axis=1)))

    near_t = project(near_stack_ref[...], feats)
    own_t = project(center_stack_ref[...], center_feats)
    near_high, near_low = split(0.5 * near_t)
    own_high, own_low = split(0.5 * own_t)
    lookup = jnp.concatenate(
        [near_high, near_low, own_high, own_low, basis_high_t, basis_high_t, basis_low_t], axis=1
    )
    scale_rows = jnp.concatenate(scales, axis=0)
    scale_parts = jnp.concatenate(
        [*split3(scale_rows), jnp.zeros((-3 * groups % 16, 128), BF16)], axis=0
    )

    out_column = jnp.concatenate([out_column_ref[...]] * (pairs // width), axis=1)

    site_ids = lax.broadcasted_iota(jnp.int32, (known, pairs), 0)
    slot_ids = lax.broadcasted_iota(jnp.int32, (centers, pairs), 0)
    slot_row = lax.broadcasted_iota(jnp.int32, (1, pairs), 1) // nbr
    group_lane = lax.broadcasted_iota(jnp.int32, (GROUP, pairs), 1) // nbr % GROUP
    group_mask = group_lane == lax.broadcasted_iota(jnp.int32, (GROUP, pairs), 0)
    group_mask = jnp.where(group_mask, 1.0, 0.0)
    tall = len(LEVELS) * GROUP
    order = lax.broadcasted_iota(jnp.int32, (radial, pairs), 0).astype(F32) + 1.0
    lanes = [slice(g * span, (g + 1) * span) for g in range(groups)]

    pick = jnp.where(site_ids == near_row, 1.0, 0.0)
    pick_half = pick.astype(BF16)
    slot_half = jnp.where(slot_ids == slot_row, 1.0, 0.0).astype(BF16)

    moved = mm(
        jnp.concatenate([place_parts, -center_parts], axis=1),
        jnp.concatenate([pick_half, slot_half], axis=0),
    )
    moved = moved[: 3 * sites] + moved[3 * sites : 6 * sites] + moved[6 * sites :]
    dx = jnp.where(live, jnp.sum(moved[:sites], axis=0, keepdims=True), 6.0)
    dy = jnp.sum(moved[sites : 2 * sites], axis=0, keepdims=True) + CELL_SIDE * side_y
    dy = jnp.where(live, dy, 0.0)
    dz = jnp.where(live, jnp.sum(moved[2 * sites :], axis=0, keepdims=True), 0.0)
    length = jnp.sqrt(dx * dx + dy * dy + dz * dz)
    inverse = 1.0 / length
    ratio = length * (1.0 / CUTOFF)
    inside = live & (ratio < 1.0)
    r2 = ratio * ratio
    r5 = r2 * r2 * ratio
    r6 = r5 * ratio
    weight = jnp.where(inside, 1.0 - r6 * (28.0 - 48.0 * ratio + 21.0 * r2), 0.0)
    slope = jnp.where(inside, -168.0 * r5 * (1.0 - 2.0 * ratio + r2), 0.0)
    sine, cosine = sin_cos_pi(order * ratio)
    basis = (math.sqrt(2.0 / CUTOFF) * inverse) * sine
    basis_slope = (math.sqrt(2.0 / CUTOFF) * inverse) * (
        (math.pi / CUTOFF) * order * cosine - sine * inverse
    )
    ex = dx * inverse
    ey = dy * inverse
    ez = dz * inverse
    angular = jnp.concatenate(
        [
            jnp.ones_like(ex),
            root_three * ex,
            root_three * ey,
            root_three * ez,
            root_fifteen * ex * ey,
            root_fifteen * ey * ez,
            0.5 * root_five * (3.0 * ez * ez - 1.0),
            root_fifteen * ex * ez,
            0.5 * root_fifteen * (ex * ex - ey * ey),
        ],
        axis=0,
    )
    angular_high, angular_low = halves(angular)
    angular_low = angular_low.astype(BF16).astype(F32)
    block_high = [angular_high[m : m + 1] * group_mask for m in range(len(LEVELS))]
    block_low = [angular_low[m : m + 1] * group_mask for m in range(len(LEVELS))]
    blocks = jnp.concatenate(block_high + block_low + block_high, axis=0).astype(BF16)
    lane_ids = lax.broadcasted_iota(jnp.int32, (128, span), 0)
    lane_slot = lax.broadcasted_iota(jnp.int32, (128, span), 1) // nbr + 3 * sites
    scale = mm(scale_parts, jnp.where(lane_ids == lane_slot, 1.0, 0.0).astype(BF16))
    scale = scale[:groups] + scale[groups : 2 * groups] + scale[2 * groups : 3 * groups]
    scale = jnp.concatenate([scale[g : g + 1] for g in range(groups)], axis=1)
    scale = scale * (1.0 / root_count)
    pull = ROOT_HALF * scale

    basis_high, basis_low = halves(basis)
    basis_rest = jnp.concatenate([basis_high, basis_low, basis_high], axis=0).astype(BF16)
    before = mm(
        lookup,
        jnp.concatenate([pick_half, pick_half, slot_half, slot_half, basis_rest], axis=0),
    )
    gate = 1.0 + jnp.tanh(before)
    active = before * gate
    latent = weight * active
    latent_high, latent_low = split(latent)
    mixed = deep(value_rows, latent_high, latent_low)
    values = mixed[:width]
    env_high, env_low = split(mixed[width:])

    def over_pairs(high, low):
        sums = []
        for cut in lanes:
            both = jnp.concatenate([high[:, cut], low[:, cut]], axis=0)
            quad = mm_nt(blocks[: 2 * tall, cut], both)
            quad = quad[:tall, :width] + quad[tall:, :width] + quad[:tall, width:]
            sums.append(quad * path_rows)
        return sums

    def over_orders(tables):
        parts = []
        for table, cut in zip(tables, lanes):
            high, low = halves(table)
            table = jnp.transpose(jnp.concatenate([high, high, low], axis=0)).astype(BF16)
            parts.append(mm(table, blocks[:, cut]))
        return jnp.concatenate(parts, axis=1)

    weighted = over_pairs(env_high, env_low)
    inner = over_orders(weighted)
    scalars = values * inner
    scalars_high, scalars_low = split(scalars)
    z = deep(
        latent_t,
        jnp.concatenate([latent_high, scalars_high], axis=0),
        jnp.concatenate([latent_low, scalars_low], axis=0),
    )
    z_gate = 1.0 + jnp.tanh(z)
    update = z * z_gate
    update_sum = jnp.sum(update * out_column, axis=0, keepdims=True)
    active_sum = jnp.sum(
        active[:, :own_pairs] * out_column[:, :own_pairs], axis=0, keepdims=True
    )
    pair_energy = (active_sum + update_sum[:, :own_pairs]) * (pull * weight)[:, :own_pairs]
    d_z = (0.5 * pull * weight) * (z_gate + update * (2.0 - z_gate))
    spread_back = deep(latent_rows, *split(d_z))
    d_scalars = spread_back[width:]
    d_values = d_scalars * inner
    dinner_high, dinner_low = split(d_scalars * values)
    d_embed = over_pairs(dinner_high, dinner_low)
    d_env = over_orders(d_embed)

    d_angular = []
    for g, cut in enumerate(lanes):
        sides_high, sides_low = halves(jnp.concatenate([weighted[g], d_embed[g]], axis=1))
        d_block = deep(
            three(sides_high.astype(BF16), sides_low.astype(BF16)),
            jnp.concatenate([dinner_high[:, cut], env_high[:, cut]], axis=0),
            jnp.concatenate([dinner_low[:, cut], env_low[:, cut]], axis=0),
        )
        d_block = d_block.reshape(len(LEVELS), GROUP, span) * group_mask[None, :, cut]
        d_angular.append(jnp.sum(d_block, axis=1))
    d_angular = jnp.concatenate(d_angular, axis=1)

    mixed_high, mixed_low = split(jnp.concatenate([d_values, d_env], axis=0))
    d_latent = (
        deep(value_plain, mixed_high, mixed_low)
        + spread_back[:width]
        + pull * out_column
    )
    d_weight = jnp.sum(d_latent * active, axis=0, keepdims=True) + pull * update_sum
    d_before = d_latent * (gate + active * (2.0 - gate))
    d_basis = deep(basis_rows, *split(d_before)) * (0.5 * weight)

    d_length = jnp.sum(d_basis * basis_slope, axis=0, keepdims=True) + d_weight * slope * (
        1.0 / CUTOFF
    )
    a1, a2, a3, a4, a5, a6, a7, a8 = [d_angular[m : m + 1] for m in range(1, 9)]
    ux = root_three * a1 + root_fifteen * (ey * a4 + ez * a7 + ex * a8)
    uy = root_three * a2 + root_fifteen * (ex * a4 + ez * a5 - ey * a8)
    uz = root_three * a3 + root_fifteen * (ey * a5 + ex * a7) + 3.0 * root_five * ez * a6
    along = ex * ux + ey * uy + ez * uz
    radial_part = d_length - along * inverse
    gx = ux * inverse + ex * radial_part
    gy = uy * inverse + ey * radial_part
    gz = uz * inverse + ez * radial_part
    hx = -0.5 * dx
    hy = -0.5 * dy
    hz = -0.5 * dz
    virial = [hx * gx, hx * gy, hx * gz, hy * gx, hy * gy, hy * gz, hz * gx, hz * gy, hz * gz]
    rest = [jnp.zeros((ORDERS - 13, pairs), F32)]
    near_terms = jnp.concatenate(
        [-gx, -gy, -gz, *virial, jnp.zeros_like(gx), *rest], axis=0
    )
    center_rows = [gx, gy, gz, *virial]
    center_rows = [r[:, :own_pairs] for r in center_rows] + [pair_energy]
    center_rows.append(jnp.zeros((ORDERS - 13, own_pairs), F32))
    center_terms = jnp.concatenate(center_rows, axis=0)
    reach = []
    for x, z, side in np.ndindex(2, 2, kept_sides):
        start = ((2 * z + x) * kind + side) * owned
        reach.append(pick_half[start : start + owned])
    reach = jnp.concatenate(reach, axis=0)
    near_sums = mm_nt(jnp.concatenate(split(near_terms), axis=0), reach)
    center_sums = mm_nt(
        jnp.concatenate(split(center_terms), axis=0), slot_half[:owned, :own_pairs]
    )
    center_sums = jnp.concatenate(
        [folded(center_sums), jnp.zeros((ORDERS, 128 - owned), F32)], axis=1
    )
    totals = folded(near_sums)
    lane = lax.broadcasted_iota(jnp.int32, (ORDERS, 128), 1)
    known = totals.shape[1]
    tiles = [totals[:, 128 * i : 128 * (i + 1)] for i in range(known // 128)]
    for g in range(owned // GROUP):
        cell = g % 2 * 2 + 1 - g // 2
        target = (g % 2 * 2 + g // 2) * kept_sides * owned + cell * sites
        turn = (target - g * GROUP) % 128
        piece = pltpu.roll(center_sums, turn, 1) if turn else center_sums
        begin = target % 128
        piece = jnp.where((lane >= begin) & (lane < begin + GROUP), piece, 0.0)
        tiles[target // 128] = tiles[target // 128] + piece
    totals = jnp.concatenate(tiles, axis=1)
    keep_ref[...] = totals[:, : known // 2]
    send_ref[...] = totals[:, known // 2 :]


def in_hbm(*arrays):
    return [pltpu.with_memory_space_constraint(array, pltpu.HBM) for array in arrays]


def joined(parts):
    total = sum(part.shape[0] for part in parts)
    start = 0
    pads = []
    for part in parts:
        end = start + part.shape[0]
        pads.append(jnp.pad(part, ((start, total - end), (0, 0))))
        start = end
    return functools.reduce(jnp.add, pads)


def local(
    positions,
    features,
    species,
    centers,
    neighbours,
    counts,
    species_scale,
    species_shift,
    center_weight,
    near_weight,
    basis_weight,
    path_weight,
    value_weight,
    latent_weight,
    out_weight,
):
    cells_x, cells_y, cells_z, sites, width = features.shape
    cell_count = cells_x * cells_y * cells_z
    owned = cell_count * sites
    assert (cells_x, cells_y, cells_z, sites) == (2, 1, 2, SITES)
    pairs = neighbours.size
    nbr = pairs // owned
    kind = min(3, lax.axis_size("gy"))

    def moved(array, steps):
        names = tuple(steps)
        sizes = [lax.axis_size(name) for name in names]
        route = []
        for at in np.ndindex(*sizes):
            to = [(p + steps[name]) % size for p, name, size in zip(at, names, sizes)]
            route.append(
                (int(np.ravel_multi_index(at, sizes)), int(np.ravel_multi_index(to, sizes)))
            )
        return lax.ppermute(array, names, route)

    vmem = pl.BlockSpec(memory_space=pltpu.VMEM)
    hbm = pl.BlockSpec(memory_space=pltpu.HBM)
    listed = centers.reshape(1, owned)
    payload = jax.ShapeDtypeStruct((owned + OWN_CELLS + pairs // 256, width), F32)
    low, high = pl.pallas_call(
        functools.partial(pack_kernel, kind),
        out_shape=(payload, payload),
        in_specs=[hbm] * 6,
        out_specs=(vmem, vmem),
        scratch_shapes=[
            pltpu.VMEM((owned, 128), F32),
            pltpu.VMEM(positions.shape, F32),
            pltpu.VMEM(species.shape, jnp.int32),
            pltpu.VMEM(listed.shape, jnp.int32),
            pltpu.VMEM(neighbours.shape, jnp.int32),
            pltpu.SMEM(species_scale.shape, F32),
            pltpu.VMEM((owned, width), F32),
            pltpu.SemaphoreType.DMA((6,)),
        ],
        compiler_params=pltpu.CompilerParams(vmem_limit_bytes=8 * 1024 * 1024),
        name="pack_payload",
    )(
        *in_hbm(
            positions,
            features.reshape(owned, width),
            species,
            listed,
            neighbours,
            species_scale,
        )
    )
    fetched = (
        species,
        listed,
        species_shift,
        center_weight,
        near_weight,
        path_weight,
        value_weight,
        latent_weight,
        out_weight.reshape(1, width),
    )
    smem_at = 2
    *weights, shift_row = pl.pallas_call(
        functools.partial(fetch_kernel, nbr),
        out_shape=(
            jax.ShapeDtypeStruct((2 * width, 2 * width), BF16),
            jax.ShapeDtypeStruct((2 * width, 2 * width), BF16),
            jax.ShapeDtypeStruct((len(LEVELS) * GROUP, width), F32),
            jax.ShapeDtypeStruct((2 * width, 3 * width), BF16),
            jax.ShapeDtypeStruct((width, 6 * width), BF16),
            jax.ShapeDtypeStruct((width, 6 * width), BF16),
            jax.ShapeDtypeStruct((2 * width, 3 * width), BF16),
            jax.ShapeDtypeStruct((width, width), F32),
            jax.ShapeDtypeStruct((1, owned), F32),
        ),
        in_specs=[hbm] * len(fetched),
        out_specs=(vmem,) * 9,
        scratch_shapes=[
            (pltpu.SMEM if i == smem_at else pltpu.VMEM)(a.shape, a.dtype)
            for i, a in enumerate(fetched)
        ]
        + [pltpu.SemaphoreType.DMA((len(fetched),))],
        compiler_params=pltpu.CompilerParams(vmem_limit_bytes=8 * 1024 * 1024),
        name="fetch_weights",
    )(*in_hbm(*fetched))
    last_x = moved(high, {"gx": 1})
    sides = []
    for step in (-1, 1)[: kind - 1]:
        sides.append(moved(high, {"gx": 1, "gy": step}))
        sides.insert(-1, moved(low, {"gy": step}))
    next_z = moved(joined([low, last_x, *sides]), {"gz": -1})
    kept = 1 if kind == 2 else kind
    half = 2 * kept * owned
    keep, send = pl.pallas_call(
        functools.partial(force_kernel, kind, nbr),
        out_shape=(
            jax.ShapeDtypeStruct((ORDERS, half), F32),
            jax.ShapeDtypeStruct((ORDERS, half), F32),
        ),
        in_specs=[vmem] * (10 + 2 * kind),
        out_specs=(vmem, vmem),
        compiler_params=pltpu.CompilerParams(vmem_limit_bytes=44 * 1024 * 1024),
        name="pair_forces",
    )(
        low,
        last_x,
        *sides,
        next_z,
        *weights,
        basis_weight,
    )
    totals = keep + moved(send, {"gx": -1})

    def part(index):
        return totals[:, index * owned : (index + 1) * owned]

    back = [moved(totals, {"gz": 1}) if kept == 1 else moved(part(kept), {"gz": 1})]
    for i, step in enumerate((1, -1)[: kept - 1]):
        back.append(moved(part(kept + 1 + i), {"gy": step, "gz": 1}))
        back.append(moved(part(1 + i), {"gy": step}))
    site_energy, forces, virial = pl.pallas_call(
        finish_kernel,
        out_shape=(
            jax.ShapeDtypeStruct(species.shape, F32),
            jax.ShapeDtypeStruct(positions.shape, F32),
            jax.ShapeDtypeStruct((*species.shape, 9), F32),
        ),
        in_specs=[vmem] * (2 + len(back)),
        out_specs=(vmem, vmem, vmem),
        compiler_params=pltpu.CompilerParams(vmem_limit_bytes=8 * 1024 * 1024),
        name="write_outputs",
    )(totals, shift_row, *back)
    return (site_energy, forces, jnp.transpose(virial, (4, 0, 1, 2, 3)))


def solution(mesh):
    placed = (
        P(None, "gx", "gy", "gz", None),
        P("gx", "gy", "gz", None, None),
        P("gx", "gy", "gz", None),
        P(("gx", "gy", "gz")),
        P(("gx", "gy", "gz"), None),
        P(("gx", "gy", "gz")),
        P(),
        P(),
        P(),
        P(),
        P(),
        P(),
        P(),
        P(),
        P(),
    )
    return jax.shard_map(
        local,
        mesh=mesh,
        in_specs=placed,
        out_specs=(
            P("gx", "gy", "gz", None),
            P(None, "gx", "gy", "gz", None),
            P(None, "gx", "gy", "gz", None),
        ),
        check_vma=False,
    )
```

```python
import functools
import math

import jax
import jax.numpy as jnp
import numpy as np
from jax import lax
from jax.experimental import pallas as pl
from jax.experimental.pallas import tpu as pltpu
from jax.sharding import PartitionSpec as P

EXACT_DOT = lax.Precision.HIGHEST
CUTOFF = 5.0
CELL_SIDE = 4.6
ROOT_HALF = 0.7071067811865476
GROUP = 8
ORDERS = 16
LEVELS = (0, 1, 1, 1, 2, 2, 2, 2, 2)
SITES = 8
OWN_CELLS = 4
FRAME_CELLS = 48
F32 = jnp.float32
BF16 = jnp.bfloat16


def split(value):
    high = value.astype(BF16)
    low = (value - high.astype(F32)).astype(BF16)
    return high, low


def split3(value):
    high = value.astype(BF16)
    rest = value - high.astype(F32)
    middle = rest.astype(BF16)
    low = (rest - middle.astype(F32)).astype(BF16)
    return high, middle, low


def halves(value):
    high = value.astype(BF16).astype(F32)
    return high, value - high


def mm(a, b):
    return lax.dot_general(a, b, (((1,), (0,)), ((), ())), preferred_element_type=F32)


def mm_nt(a, b):
    return lax.dot_general(a, b, (((1,), (1,)), ((), ())), preferred_element_type=F32)


def stacked(high, low):
    top = jnp.concatenate([high, high], axis=1)
    bottom = jnp.concatenate([low, jnp.zeros_like(low)], axis=1)
    return jnp.concatenate([top, bottom], axis=0)


def folded(product):
    half = product.shape[0] // 2
    return product[:half] + product[half:]


def three(high, low):
    return jnp.concatenate([high, low, high], axis=1)


def deep(weights, value_high, value_low):
    return mm(weights, jnp.concatenate([value_high, value_high, value_low], axis=0))


def sin_cos_pi(turns):
    near = turns - 2.0 * jnp.round(turns * 0.5)
    quarter = jnp.round(near * 2.0)
    v = (near - 0.5 * quarter) * math.pi
    v2 = v * v
    s = v * (
        1.0
        + v2
        * (-1.0 / 6 + v2 * (1.0 / 120 + v2 * (-1.0 / 5040 + v2 * (1.0 / 362880 - v2 / 39916800))))
    )
    c = 1.0 + v2 * (
        -0.5
        + v2
        * (1.0 / 24 + v2 * (-1.0 / 720 + v2 * (1.0 / 40320 + v2 * (-1.0 / 3628800 + v2 / 479001600))))
    )
    odd = jnp.abs(quarter) == 1.0
    sine = jnp.where(odd, quarter * c, jnp.where(quarter == 0.0, s, -s))
    cosine = jnp.where(odd, -quarter * s, jnp.where(quarter == 0.0, c, -c))
    return sine, cosine


def lane_row(piece, offset):
    row = jnp.concatenate([piece, jnp.zeros((1, 128 - piece.shape[1]), piece.dtype)], axis=1)
    return pltpu.roll(row, offset, 1) if offset else row


def pack_kernel(
    kind,
    positions_hbm,
    features_hbm,
    species_hbm,
    centers_hbm,
    neighbours_hbm,
    scale_hbm,
    low_ref,
    high_ref,
    wide_ref,
    positions_ref,
    species_ref,
    centers_ref,
    neighbours_ref,
    scale_ref,
    sems,
):
    owned, nbr = neighbours_ref.shape
    per_row = 128 // nbr
    pairs_in = (
        (features_hbm, low_ref.at[pl.ds(0, owned), :]),
        (neighbours_hbm, neighbours_ref),
        (centers_hbm, centers_ref),
        (positions_hbm, positions_ref),
        (species_hbm, species_ref),
        (scale_hbm, scale_ref),
    )
    copies = [
        pltpu.make_async_copy(source, target, sems.at[i])
        for i, (source, target) in enumerate(pairs_in)
    ]
    for copy in copies:
        copy.start()
    for copy in copies:
        copy.wait()
    for cell in range(OWN_CELLS):
        x, z = cell // 2, cell % 2
        species = species_ref[x, 0, z : z + 1, :]
        scale = jnp.zeros(species.shape, F32)
        for s in range(scale_ref.shape[0]):
            scale = jnp.where(species == s, scale_ref[s], scale)
        row = lane_row(scale, 3 * SITES)
        for c in range(3):
            row = row + lane_row(positions_ref[c, x, 0, z : z + 1, :], c * SITES)
        low_ref[owned + cell : owned + cell + 1] = row

    chosen = lax.broadcasted_iota(jnp.int32, (owned, owned), 0) == centers_ref[...]
    chosen = jnp.where(chosen, 1.0, 0.0)
    occupied = jnp.sum(chosen, axis=1, keepdims=True) > 0.5
    chosen = chosen.astype(BF16)
    rows = neighbours_ref[...]
    upper = mm(chosen, (rows >> 4).astype(F32).astype(BF16))
    lower = mm(chosen, (rows & 15).astype(F32).astype(BF16))
    rows = (upper * 16.0 + lower).astype(jnp.int32)
    live = occupied & (rows < FRAME_CELLS * SITES)
    slot = lax.broadcasted_iota(jnp.int32, (owned, nbr), 0)
    cell = slot >> 3
    site = rows & 7
    place = rows >> 3
    near_z = (place & 3) + 1 - 2 * (cell & 1)
    column = place >> 2
    frame_x = (column * 11) >> 5
    frame_y = column - 3 * frame_x
    near_x = frame_x + 1 - 2 * (cell >> 1)
    side = jnp.where(frame_y == 1, 0, jnp.where(frame_y == 2, 1, kind - 1))
    block = (near_z >> 1) * 2 + 1 - (near_x >> 1)
    where = (block * kind + side) * owned + (near_x & 1) * 16 + (near_z & 1) * 8 + site
    code = jnp.where(live, 1 + where + (frame_y << 10), 0).astype(F32)
    wide_ref[...] = jnp.concatenate([code, jnp.zeros((owned, 128 - nbr), F32)], axis=1)
    codes = wide_ref[pl.ds(0, owned // per_row, stride=per_row), :]
    for j in range(1, per_row):
        more = wide_ref[pl.ds(j, owned // per_row, stride=per_row), :]
        codes = codes + pltpu.roll(more, j * nbr, 1)
    tile = owned + OWN_CELLS
    low_ref[tile:] = codes[: codes.shape[0] // 2]
    high_ref[:tile] = low_ref[:tile]
    high_ref[tile:] = codes[codes.shape[0] // 2 :]


def fetch_kernel(species_hbm, centers_hbm, shift_hbm, *refs):
    *refs, shift_row_ref, species_ref, centers_ref, shift_ref, sems = refs
    count = len(refs) // 2
    pairs_in = [
        (species_hbm, species_ref),
        (centers_hbm, centers_ref),
        (shift_hbm, shift_ref),
        *zip(refs[:count], refs[count:]),
    ]
    copies = [
        pltpu.make_async_copy(source, target, sems.at[i])
        for i, (source, target) in enumerate(pairs_in)
    ]
    for copy in copies:
        copy.start()
    for copy in copies:
        copy.wait()
    owned = centers_ref.shape[1]
    shift_row = jnp.zeros((1, 128), F32)
    for cell in range(OWN_CELLS):
        species = species_ref[cell // 2, 0, cell % 2 : cell % 2 + 1, :]
        shift = jnp.zeros(species.shape, F32)
        for s in range(shift_ref.shape[0]):
            shift = jnp.where(species == s, shift_ref[s], shift)
        shift_row = shift_row + lane_row(shift, cell * SITES)
    chosen = lax.broadcasted_iota(jnp.int32, (owned, owned), 0) == centers_ref[...]
    occupied = jnp.sum(jnp.where(chosen, 1.0, 0.0), axis=1, keepdims=True) > 0.5
    column = jnp.where(occupied, jnp.ones((owned, 128), F32), 0.0)
    shift_row_ref[...] = shift_row[:, :owned] * jnp.transpose(column)[0:1]


def finish_kernel(mine_ref, shift_row_ref, *refs):
    *near_refs, energy_ref, forces_ref, virial_ref = refs
    owned = shift_row_ref.shape[1]
    total = mine_ref[:, :owned]
    for near_ref in near_refs:
        start = near_ref.shape[1] - owned
        total = total + near_ref[:, start : start + owned]
    energy = total[12:13] + shift_row_ref[...]
    columns = jnp.transpose(jnp.concatenate([total, jnp.zeros((ORDERS, 128 - owned), F32)], axis=1))
    for cell in range(OWN_CELLS):
        x, z = cell // 2, cell % 2
        lanes = slice(cell * SITES, (cell + 1) * SITES)
        energy_ref[x, 0, z : z + 1, :] = energy[:, lanes]
        for c in range(3):
            forces_ref[c, x, 0, z : z + 1, :] = total[c : c + 1, lanes]
        virial_ref[x, 0, z] = columns[lanes, 3:12]


def force_kernel(kind, nbr, here_ref, last_x_ref, *refs):
    near_side_refs = refs[: 2 * kind - 2]
    (
        next_z_ref,
        center_weight_ref,
        near_weight_ref,
        basis_weight_ref,
        path_weight_ref,
        value_weight_ref,
        latent_weight_ref,
        out_weight_ref,
        keep_ref,
        send_ref,
    ) = refs[2 * kind - 2 :]
    height, width = here_ref.shape
    owned = OWN_CELLS * SITES
    center_sides = 2 if kind == 2 else 1
    kept_sides = 1 if kind == 2 else kind
    own_pairs = owned * nbr
    pairs = center_sides * own_pairs
    centers = center_sides * owned
    radial = basis_weight_ref.shape[0]
    span = GROUP * nbr
    groups = centers // GROUP
    sites = SITES
    root_count = math.sqrt(nbr)
    root_three = math.sqrt(3.0)
    root_fifteen = math.sqrt(15.0)
    root_five = math.sqrt(5.0)
    far = next_z_ref[...]
    mains = [here_ref[...], last_x_ref[...], far[:height], far[height : 2 * height]]
    near_sides = [ref[...] for ref in near_side_refs]
    far_sides = far[2 * height :]
    far_sides = [far_sides[i * height : (i + 1) * height] for i in range(2 * kind - 2)]
    blocks_in = [
        [mains[0], *near_sides[0::2]],
        [mains[1], *near_sides[1::2]],
        [mains[2], *far_sides[0::2]],
        [mains[3], *far_sides[1::2]],
    ]
    feats = jnp.concatenate([side[:owned] for block in blocks_in for side in block], axis=0)
    known = feats.shape[0]
    center_feats = []
    center_coords = []
    coords = []
    scales = []
    codes = []
    cell_row = lax.broadcasted_iota(jnp.int32, (kind * OWN_CELLS, 128), 0) % OWN_CELLS
    tile_lane = lax.broadcasted_iota(jnp.int32, (kind * OWN_CELLS, 128), 1)
    for g, block in enumerate(blocks_in):
        behind_x, ahead_z = g % 2, g // 2
        rows = jnp.concatenate([side[owned : owned + OWN_CELLS] for side in block], axis=0)
        corner_x = (cell_row // 2 + 2 - 2 * behind_x).astype(F32) * CELL_SIDE
        corner_z = (cell_row % 2 + 2 * ahead_z).astype(F32) * CELL_SIDE
        corner = jnp.where(
            tile_lane < sites, corner_x, jnp.where(tile_lane < 2 * sites, 0.0, corner_z)
        )
        coords.append(rows + corner)
    for c in range(center_sides):
        for g, block in enumerate(blocks_in):
            cell = g % 2 * 2 + 1 - g // 2
            row = c * OWN_CELLS + cell
            center_feats.append(block[c][cell * sites : (cell + 1) * sites])
            scales.append(block[c][owned + cell : owned + cell + 1])
            center_coords.append(coords[g][row : row + 1])
            start = owned + OWN_CELLS + (1 - g // 2) * span // 128
            codes.extend(block[c][start + r : start + r + 1] for r in range(span // 128))
    center_feats = jnp.concatenate(center_feats, axis=0)
    coords = jnp.concatenate(coords, axis=0)
    code = jnp.concatenate(codes, axis=1).astype(jnp.int32)
    live = code > 0
    code = jnp.maximum(code - 1, 0)
    side_y = ((code >> 10) - 1).astype(F32)
    near_row = code & 1023
    if center_sides == 2:
        pair_lane = lax.broadcasted_iota(jnp.int32, (1, pairs), 1)
        near_row = jnp.where(pair_lane < own_pairs, near_row, near_row ^ owned)
    near_row = jnp.where(live, near_row, known)

    def place_rows(cell_rows):
        count = cell_rows.shape[0] * sites
        spread = jnp.broadcast_to(cell_rows[:, None, :], (cell_rows.shape[0], sites, 128))
        spread = spread.reshape(count, 128)
        lane = lax.broadcasted_iota(jnp.int32, (count, 128), 1)
        row = lax.broadcasted_iota(jnp.int32, (count, 128), 0)
        keep = (lane % sites == row % sites) & (lane < 3 * sites)
        spread = jnp.transpose(jnp.where(keep, spread, 0.0))
        return jnp.concatenate(split3(spread[: 3 * sites]), axis=0)

    place_parts = place_rows(coords)
    center_parts = place_rows(jnp.concatenate(center_coords, axis=0))

    value_rows = three(*split(jnp.transpose(value_weight_ref[...])))
    latent_t = three(*split(0.5 * jnp.transpose(latent_weight_ref[...])))
    latent_rows = three(*split(latent_weight_ref[...] * out_weight_ref[...]))
    value_plain = three(*split(value_weight_ref[...]))
    basis_t = jnp.transpose(basis_weight_ref[...])
    basis_high_t, basis_low_t = split(0.5 * basis_t)
    basis_rows = three(*split(basis_weight_ref[...]))

    def project(weight, rows):
        weight = stacked(*split(jnp.transpose(weight)))
        return folded(mm_nt(weight, jnp.concatenate(split(rows), axis=1)))

    near_t = project(near_weight_ref[...], feats)
    own_t = project(center_weight_ref[...], center_feats)
    near_high, near_low = split(0.5 * near_t)
    own_high, own_low = split(0.5 * own_t)
    lookup = jnp.concatenate(
        [near_high, near_low, own_high, own_low, basis_high_t, basis_high_t, basis_low_t], axis=1
    )
    scale_rows = jnp.concatenate(scales, axis=0)
    scale_parts = jnp.concatenate(
        [*split3(scale_rows), jnp.zeros((-3 * groups % 16, 128), BF16)], axis=0
    )

    path_rows = jnp.concatenate(
        [jnp.broadcast_to(path_weight_ref[l : l + 1, :], (GROUP, width)) for l in LEVELS], axis=0
    ) * (1.0 / root_count)
    out_column = jnp.transpose(jnp.broadcast_to(out_weight_ref[...], (width, width)))
    out_column = jnp.concatenate([out_column] * (pairs // width), axis=1)

    slot_ids = lax.broadcasted_iota(jnp.int32, (centers, pairs), 0)
    slot_row = lax.broadcasted_iota(jnp.int32, (1, pairs), 1) // nbr
    group_lane = lax.broadcasted_iota(jnp.int32, (GROUP, pairs), 1) // nbr % GROUP
    group_mask = group_lane == lax.broadcasted_iota(jnp.int32, (GROUP, pairs), 0)
    group_mask = jnp.where(group_mask, 1.0, 0.0)
    tall = len(LEVELS) * GROUP
    order = lax.broadcasted_iota(jnp.int32, (radial, pairs), 0).astype(F32) + 1.0
    lanes = [slice(g * span, (g + 1) * span) for g in range(groups)]

    site_ids = lax.broadcasted_iota(jnp.int32, (known, 128), 0)
    if known <= 256:
        site_ids = site_ids.astype(F32).astype(BF16)
        wanted = jnp.broadcast_to(near_row.astype(F32), (16, pairs)).astype(BF16)
        wanted = jnp.concatenate([wanted] * (known // 16), axis=0)
        one, zero = jnp.ones((), BF16), jnp.zeros((), BF16)
    else:
        wanted = near_row
        one, zero = 1.0, 0.0
    site_ids = jnp.concatenate([site_ids] * (pairs // 128), axis=1)
    pick_half = jnp.where(site_ids == wanted, one, zero).astype(BF16)
    slot_half = jnp.where(slot_ids == slot_row, 1.0, 0.0).astype(BF16)

    moved = mm(
        jnp.concatenate([place_parts, -center_parts], axis=1),
        jnp.concatenate([pick_half, slot_half], axis=0),
    )
    moved = moved[: 3 * sites] + moved[3 * sites : 6 * sites] + moved[6 * sites :]
    dx = jnp.where(live, jnp.sum(moved[:sites], axis=0, keepdims=True), 6.0)
    dy = jnp.sum(moved[sites : 2 * sites], axis=0, keepdims=True) + CELL_SIDE * side_y
    dy = jnp.where(live, dy, 0.0)
    dz = jnp.where(live, jnp.sum(moved[2 * sites :], axis=0, keepdims=True), 0.0)
    length = jnp.sqrt(dx * dx + dy * dy + dz * dz)
    inverse = 1.0 / length
    ratio = length * (1.0 / CUTOFF)
    inside = live & (ratio < 1.0)
    r2 = ratio * ratio
    r5 = r2 * r2 * ratio
    r6 = r5 * ratio
    weight = jnp.where(inside, 1.0 - r6 * (28.0 - 48.0 * ratio + 21.0 * r2), 0.0)
    slope = jnp.where(inside, -168.0 * r5 * (1.0 - 2.0 * ratio + r2), 0.0)
    sine, cosine = sin_cos_pi(order * ratio)
    basis = (math.sqrt(2.0 / CUTOFF) * inverse) * sine
    basis_slope = (math.sqrt(2.0 / CUTOFF) * inverse) * (
        (math.pi / CUTOFF) * order * cosine - sine * inverse
    )
    ex = dx * inverse
    ey = dy * inverse
    ez = dz * inverse
    angular = jnp.concatenate(
        [
            jnp.ones_like(ex),
            root_three * ex,
            root_three * ey,
            root_three * ez,
            root_fifteen * ex * ey,
            root_fifteen * ey * ez,
            0.5 * root_five * (3.0 * ez * ez - 1.0),
            root_fifteen * ex * ez,
            0.5 * root_fifteen * (ex * ex - ey * ey),
        ],
        axis=0,
    )
    angular_high, angular_low = halves(angular)
    angular_low = angular_low.astype(BF16).astype(F32)
    block_high = [angular_high[m : m + 1] * group_mask for m in range(len(LEVELS))]
    block_low = [angular_low[m : m + 1] * group_mask for m in range(len(LEVELS))]
    blocks = jnp.concatenate(block_high + block_low + block_high, axis=0).astype(BF16)
    lane_ids = lax.broadcasted_iota(jnp.int32, (128, span), 0)
    lane_slot = lax.broadcasted_iota(jnp.int32, (128, span), 1) // nbr + 3 * sites
    scale = mm(scale_parts, jnp.where(lane_ids == lane_slot, 1.0, 0.0).astype(BF16))
    scale = scale[:groups] + scale[groups : 2 * groups] + scale[2 * groups : 3 * groups]
    scale = jnp.concatenate([scale[g : g + 1] for g in range(groups)], axis=1)
    scale = scale * (1.0 / root_count)
    pull = ROOT_HALF * scale

    basis_high, basis_low = halves(basis)
    basis_rest = jnp.concatenate([basis_high, basis_low, basis_high], axis=0).astype(BF16)
    before = mm(
        lookup,
        jnp.concatenate([pick_half, pick_half, slot_half, slot_half, basis_rest], axis=0),
    )
    gate = 1.0 + jnp.tanh(before)
    active = before * gate
    latent = weight * active
    latent_high, latent_low = split(latent)
    mixed = deep(value_rows, latent_high, latent_low)
    values = mixed[:width]
    env_high, env_low = split(mixed[width:])

    def over_pairs(high, low):
        sums = []
        for cut in lanes:
            both = jnp.concatenate([high[:, cut], low[:, cut]], axis=0)
            quad = mm_nt(blocks[: 2 * tall, cut], both)
            quad = quad[:tall, :width] + quad[tall:, :width] + quad[:tall, width:]
            sums.append(quad * path_rows)
        return sums

    def over_orders(tables):
        parts = []
        for table, cut in zip(tables, lanes):
            high, low = halves(table)
            table = jnp.transpose(jnp.concatenate([high, high, low], axis=0)).astype(BF16)
            parts.append(mm(table, blocks[:, cut]))
        return jnp.concatenate(parts, axis=1)

    weighted = over_pairs(env_high, env_low)
    inner = over_orders(weighted)
    scalars = values * inner
    scalars_high, scalars_low = split(scalars)
    z = deep(
        latent_t,
        jnp.concatenate([latent_high, scalars_high], axis=0),
        jnp.concatenate([latent_low, scalars_low], axis=0),
    )
    z_gate = 1.0 + jnp.tanh(z)
    update = z * z_gate
    update_sum = jnp.sum(update * out_column, axis=0, keepdims=True)
    active_sum = jnp.sum(
        active[:, :own_pairs] * out_column[:, :own_pairs], axis=0, keepdims=True
    )
    pair_energy = (active_sum + update_sum[:, :own_pairs]) * (pull * weight)[:, :own_pairs]
    d_z = (0.5 * pull * weight) * (z_gate + update * (2.0 - z_gate))
    spread_back = deep(latent_rows, *split(d_z))
    d_scalars = spread_back[width:]
    d_values = d_scalars * inner
    dinner_high, dinner_low = split(d_scalars * values)
    d_embed = over_pairs(dinner_high, dinner_low)
    d_env = over_orders(d_embed)

    d_angular = []
    for g, cut in enumerate(lanes):
        sides_high, sides_low = halves(jnp.concatenate([weighted[g], d_embed[g]], axis=1))
        d_block = deep(
            three(sides_high.astype(BF16), sides_low.astype(BF16)),
            jnp.concatenate([dinner_high[:, cut], env_high[:, cut]], axis=0),
            jnp.concatenate([dinner_low[:, cut], env_low[:, cut]], axis=0),
        )
        d_block = d_block.reshape(len(LEVELS), GROUP, span) * group_mask[None, :, cut]
        d_angular.append(jnp.sum(d_block, axis=1))
    d_angular = jnp.concatenate(d_angular, axis=1)

    mixed_high, mixed_low = split(jnp.concatenate([d_values, d_env], axis=0))
    d_latent = (
        deep(value_plain, mixed_high, mixed_low)
        + spread_back[:width]
        + pull * out_column
    )
    d_weight = jnp.sum(d_latent * active, axis=0, keepdims=True) + pull * update_sum
    d_before = d_latent * (gate + active * (2.0 - gate))
    d_basis = deep(basis_rows, *split(d_before)) * (0.5 * weight)

    d_length = jnp.sum(d_basis * basis_slope, axis=0, keepdims=True) + d_weight * slope * (
        1.0 / CUTOFF
    )
    a1, a2, a3, a4, a5, a6, a7, a8 = [d_angular[m : m + 1] for m in range(1, 9)]
    ux = root_three * a1 + root_fifteen * (ey * a4 + ez * a7 + ex * a8)
    uy = root_three * a2 + root_fifteen * (ex * a4 + ez * a5 - ey * a8)
    uz = root_three * a3 + root_fifteen * (ey * a5 + ex * a7) + 3.0 * root_five * ez * a6
    along = ex * ux + ey * uy + ez * uz
    radial_part = d_length - along * inverse
    gx = ux * inverse + ex * radial_part
    gy = uy * inverse + ey * radial_part
    gz = uz * inverse + ez * radial_part
    hx = -0.5 * dx
    hy = -0.5 * dy
    hz = -0.5 * dz
    virial = [hx * gx, hx * gy, hx * gz, hy * gx, hy * gy, hy * gz, hz * gx, hz * gy, hz * gz]
    rest = [jnp.zeros((ORDERS - 13, pairs), F32)]
    near_terms = jnp.concatenate(
        [-gx, -gy, -gz, *virial, jnp.zeros_like(gx), *rest], axis=0
    )
    center_rows = [gx, gy, gz, *virial]
    center_rows = [r[:, :own_pairs] for r in center_rows] + [pair_energy]
    center_rows.append(jnp.zeros((ORDERS - 13, own_pairs), F32))
    center_terms = jnp.concatenate(center_rows, axis=0)
    reach = []
    for x, z, side in np.ndindex(2, 2, kept_sides):
        start = ((2 * z + x) * kind + side) * owned
        reach.append(pick_half[start : start + owned])
    reach = jnp.concatenate(reach, axis=0)
    near_sums = mm_nt(jnp.concatenate(split(near_terms), axis=0), reach)
    center_sums = mm_nt(
        jnp.concatenate(split(center_terms), axis=0), slot_half[:owned, :own_pairs]
    )
    center_sums = jnp.concatenate(
        [folded(center_sums), jnp.zeros((ORDERS, 128 - owned), F32)], axis=1
    )
    totals = folded(near_sums)
    lane = lax.broadcasted_iota(jnp.int32, (ORDERS, 128), 1)
    known = totals.shape[1]
    tiles = [totals[:, 128 * i : 128 * (i + 1)] for i in range(known // 128)]
    for g in range(owned // GROUP):
        cell = g % 2 * 2 + 1 - g // 2
        target = (g % 2 * 2 + g // 2) * kept_sides * owned + cell * sites
        turn = (target - g * GROUP) % 128
        piece = pltpu.roll(center_sums, turn, 1) if turn else center_sums
        begin = target % 128
        piece = jnp.where((lane >= begin) & (lane < begin + GROUP), piece, 0.0)
        tiles[target // 128] = tiles[target // 128] + piece
    totals = jnp.concatenate(tiles, axis=1)
    keep_ref[...] = totals[:, : known // 2]
    send_ref[...] = totals[:, known // 2 :]


def in_hbm(*arrays):
    return [pltpu.with_memory_space_constraint(array, pltpu.HBM) for array in arrays]


def joined(parts):
    total = sum(part.shape[0] for part in parts)
    start = 0
    pads = []
    for part in parts:
        end = start + part.shape[0]
        pads.append(jnp.pad(part, ((start, total - end), (0, 0))))
        start = end
    return functools.reduce(jnp.add, pads)


def local(
    positions,
    features,
    species,
    centers,
    neighbours,
    counts,
    species_scale,
    species_shift,
    center_weight,
    near_weight,
    basis_weight,
    path_weight,
    value_weight,
    latent_weight,
    out_weight,
):
    cells_x, cells_y, cells_z, sites, width = features.shape
    cell_count = cells_x * cells_y * cells_z
    owned = cell_count * sites
    assert (cells_x, cells_y, cells_z, sites) == (2, 1, 2, SITES)
    pairs = neighbours.size
    nbr = pairs // owned
    kind = min(3, lax.axis_size("gy"))

    def moved(array, steps):
        names = tuple(steps)
        sizes = [lax.axis_size(name) for name in names]
        route = []
        for at in np.ndindex(*sizes):
            to = [(p + steps[name]) % size for p, name, size in zip(at, names, sizes)]
            route.append(
                (int(np.ravel_multi_index(at, sizes)), int(np.ravel_multi_index(to, sizes)))
            )
        return lax.ppermute(array, names, route)

    vmem = pl.BlockSpec(memory_space=pltpu.VMEM)
    hbm = pl.BlockSpec(memory_space=pltpu.HBM)
    listed = centers.reshape(1, owned)
    payload = jax.ShapeDtypeStruct((owned + OWN_CELLS + pairs // 256, width), F32)
    low, high = pl.pallas_call(
        functools.partial(pack_kernel, kind),
        out_shape=(payload, payload),
        in_specs=[hbm] * 6,
        out_specs=(vmem, vmem),
        scratch_shapes=[
            pltpu.VMEM((owned, 128), F32),
            pltpu.VMEM(positions.shape, F32),
            pltpu.VMEM(species.shape, jnp.int32),
            pltpu.VMEM(listed.shape, jnp.int32),
            pltpu.VMEM(neighbours.shape, jnp.int32),
            pltpu.SMEM(species_scale.shape, F32),
            pltpu.SemaphoreType.DMA((6,)),
        ],
        compiler_params=pltpu.CompilerParams(vmem_limit_bytes=8 * 1024 * 1024),
        name="pack_payload",
    )(
        *in_hbm(
            positions,
            features.reshape(owned, width),
            species,
            listed,
            neighbours,
            species_scale,
        )
    )
    weights = (
        center_weight,
        near_weight,
        basis_weight,
        path_weight,
        value_weight,
        latent_weight,
        out_weight.reshape(1, width),
    )
    *weights, shift_row = pl.pallas_call(
        fetch_kernel,
        out_shape=(
            *(jax.ShapeDtypeStruct(w.shape, F32) for w in weights),
            jax.ShapeDtypeStruct((1, owned), F32),
        ),
        in_specs=[hbm] * (3 + len(weights)),
        out_specs=(vmem,) * (1 + len(weights)),
        scratch_shapes=[
            pltpu.VMEM(species.shape, jnp.int32),
            pltpu.VMEM(listed.shape, jnp.int32),
            pltpu.SMEM(species_shift.shape, F32),
            pltpu.SemaphoreType.DMA((3 + len(weights),)),
        ],
        compiler_params=pltpu.CompilerParams(vmem_limit_bytes=8 * 1024 * 1024),
        name="fetch_weights",
    )(*in_hbm(species, listed, species_shift, *weights))
    last_x = moved(high, {"gx": 1})
    sides = []
    for step in (-1, 1)[: kind - 1]:
        sides.append(moved(high, {"gx": 1, "gy": step}))
        sides.insert(-1, moved(low, {"gy": step}))
    next_z = moved(joined([low, last_x, *sides]), {"gz": -1})
    kept = 1 if kind == 2 else kind
    half = 2 * kept * owned
    keep, send = pl.pallas_call(
        functools.partial(force_kernel, kind, nbr),
        out_shape=(
            jax.ShapeDtypeStruct((ORDERS, half), F32),
            jax.ShapeDtypeStruct((ORDERS, half), F32),
        ),
        in_specs=[vmem] * (8 + 2 * kind),
        out_specs=(vmem, vmem),
        compiler_params=pltpu.CompilerParams(vmem_limit_bytes=44 * 1024 * 1024),
        name="pair_forces",
    )(
        low,
        last_x,
        *sides,
        next_z,
        *weights,
    )
    totals = keep + moved(send, {"gx": -1})

    def part(index):
        return totals[:, index * owned : (index + 1) * owned]

    back = [moved(totals, {"gz": 1}) if kept == 1 else moved(part(kept), {"gz": 1})]
    for i, step in enumerate((1, -1)[: kept - 1]):
        back.append(moved(part(kept + 1 + i), {"gy": step, "gz": 1}))
        back.append(moved(part(1 + i), {"gy": step}))
    site_energy, forces, virial = pl.pallas_call(
        finish_kernel,
        out_shape=(
            jax.ShapeDtypeStruct(species.shape, F32),
            jax.ShapeDtypeStruct(positions.shape, F32),
            jax.ShapeDtypeStruct((*species.shape, 9), F32),
        ),
        in_specs=[vmem] * (2 + len(back)),
        out_specs=(vmem, vmem, vmem),
        compiler_params=pltpu.CompilerParams(vmem_limit_bytes=8 * 1024 * 1024),
        name="write_outputs",
    )(totals, shift_row, *back)
    return (site_energy, forces, jnp.transpose(virial, (4, 0, 1, 2, 3)))


def solution(mesh):
    placed = (
        P(None, "gx", "gy", "gz", None),
        P("gx", "gy", "gz", None, None),
        P("gx", "gy", "gz", None),
        P(("gx", "gy", "gz")),
        P(("gx", "gy", "gz"), None),
        P(("gx", "gy", "gz")),
        P(),
        P(),
        P(),
        P(),
        P(),
        P(),
        P(),
        P(),
        P(),
    )
    return jax.shard_map(
        local,
        mesh=mesh,
        in_specs=placed,
        out_specs=(
            P("gx", "gy", "gz", None),
            P(None, "gx", "gy", "gz", None),
            P(None, "gx", "gy", "gz", None),
        ),
        check_vma=False,
    )
```

```python
import functools
import math

import jax
import jax.numpy as jnp
import numpy as np
from jax import lax
from jax.experimental import pallas as pl
from jax.experimental.pallas import tpu as pltpu
from jax.sharding import PartitionSpec as P

EXACT_DOT = lax.Precision.HIGHEST
CUTOFF = 5.0
CELL_SIDE = 4.6
ROOT_HALF = 0.7071067811865476
GROUP = 8
ORDERS = 16
LEVELS = (0, 1, 1, 1, 2, 2, 2, 2, 2)
SITES = 8
OWN_CELLS = 4
FRAME_CELLS = 48
F32 = jnp.float32
BF16 = jnp.bfloat16


def split(value):
    high = value.astype(BF16)
    low = (value - high.astype(F32)).astype(BF16)
    return high, low


def split3(value):
    high = value.astype(BF16)
    rest = value - high.astype(F32)
    middle = rest.astype(BF16)
    low = (rest - middle.astype(F32)).astype(BF16)
    return high, middle, low


def halves(value):
    high = value.astype(BF16).astype(F32)
    return high, value - high


def mm(a, b):
    return lax.dot_general(a, b, (((1,), (0,)), ((), ())), preferred_element_type=F32)


def mm_nt(a, b):
    return lax.dot_general(a, b, (((1,), (1,)), ((), ())), preferred_element_type=F32)


def stacked(high, low):
    top = jnp.concatenate([high, high], axis=1)
    bottom = jnp.concatenate([low, jnp.zeros_like(low)], axis=1)
    return jnp.concatenate([top, bottom], axis=0)


def folded(product):
    half = product.shape[0] // 2
    return product[:half] + product[half:]


def three(high, low):
    return jnp.concatenate([high, low, high], axis=1)


def deep(weights, value_high, value_low):
    return mm(weights, jnp.concatenate([value_high, value_high, value_low], axis=0))


def sin_cos_pi(turns):
    near = turns - 2.0 * jnp.round(turns * 0.5)
    quarter = jnp.round(near * 2.0)
    v = (near - 0.5 * quarter) * math.pi
    v2 = v * v
    s = v * (
        1.0
        + v2
        * (-1.0 / 6 + v2 * (1.0 / 120 + v2 * (-1.0 / 5040 + v2 * (1.0 / 362880 - v2 / 39916800))))
    )
    c = 1.0 + v2 * (
        -0.5
        + v2
        * (1.0 / 24 + v2 * (-1.0 / 720 + v2 * (1.0 / 40320 + v2 * (-1.0 / 3628800 + v2 / 479001600))))
    )
    odd = jnp.abs(quarter) == 1.0
    sine = jnp.where(odd, quarter * c, jnp.where(quarter == 0.0, s, -s))
    cosine = jnp.where(odd, -quarter * s, jnp.where(quarter == 0.0, c, -c))
    return sine, cosine


def lane_row(piece, offset):
    row = jnp.concatenate([piece, jnp.zeros((1, 128 - piece.shape[1]), piece.dtype)], axis=1)
    return pltpu.roll(row, offset, 1) if offset else row


def pack_kernel(
    kind,
    positions_hbm,
    features_hbm,
    species_hbm,
    centers_hbm,
    neighbours_hbm,
    scale_hbm,
    low_ref,
    high_ref,
    wide_ref,
    positions_ref,
    species_ref,
    centers_ref,
    neighbours_ref,
    scale_ref,
    sems,
):
    owned, nbr = neighbours_ref.shape
    per_row = 128 // nbr
    pairs_in = (
        (features_hbm, low_ref.at[pl.ds(0, owned), :]),
        (neighbours_hbm, neighbours_ref),
        (centers_hbm, centers_ref),
        (positions_hbm, positions_ref),
        (species_hbm, species_ref),
        (scale_hbm, scale_ref),
    )
    copies = [
        pltpu.make_async_copy(source, target, sems.at[i])
        for i, (source, target) in enumerate(pairs_in)
    ]
    for copy in copies:
        copy.start()
    for copy in copies:
        copy.wait()
    for cell in range(OWN_CELLS):
        x, z = cell // 2, cell % 2
        species = species_ref[x, 0, z : z + 1, :]
        scale = jnp.zeros(species.shape, F32)
        for s in range(scale_ref.shape[0]):
            scale = jnp.where(species == s, scale_ref[s], scale)
        row = lane_row(scale, 3 * SITES)
        for c in range(3):
            row = row + lane_row(positions_ref[c, x, 0, z : z + 1, :], c * SITES)
        low_ref[owned + cell : owned + cell + 1] = row

    chosen = lax.broadcasted_iota(jnp.int32, (owned, owned), 0) == centers_ref[...]
    chosen = jnp.where(chosen, 1.0, 0.0)
    occupied = jnp.sum(chosen, axis=1, keepdims=True) > 0.5
    chosen = chosen.astype(BF16)
    rows = neighbours_ref[...]
    upper = mm(chosen, (rows >> 4).astype(F32).astype(BF16))
    lower = mm(chosen, (rows & 15).astype(F32).astype(BF16))
    rows = (upper * 16.0 + lower).astype(jnp.int32)
    live = occupied & (rows < FRAME_CELLS * SITES)
    slot = lax.broadcasted_iota(jnp.int32, (owned, nbr), 0)
    cell = slot >> 3
    site = rows & 7
    place = rows >> 3
    near_z = (place & 3) + 1 - 2 * (cell & 1)
    column = place >> 2
    frame_x = (column * 11) >> 5
    frame_y = column - 3 * frame_x
    near_x = frame_x + 1 - 2 * (cell >> 1)
    side = jnp.where(frame_y == 1, 0, jnp.where(frame_y == 2, 1, kind - 1))
    block = (near_z >> 1) * 2 + 1 - (near_x >> 1)
    where = (block * kind + side) * owned + (near_x & 1) * 16 + (near_z & 1) * 8 + site
    code = jnp.where(live, 1 + where + (frame_y << 10), 0).astype(F32)
    wide_ref[...] = jnp.concatenate([code, jnp.zeros((owned, 128 - nbr), F32)], axis=1)
    codes = wide_ref[pl.ds(0, owned // per_row, stride=per_row), :]
    for j in range(1, per_row):
        more = wide_ref[pl.ds(j, owned // per_row, stride=per_row), :]
        codes = codes + pltpu.roll(more, j * nbr, 1)
    tile = owned + OWN_CELLS
    low_ref[tile:] = codes[: codes.shape[0] // 2]
    high_ref[:tile] = low_ref[:tile]
    high_ref[tile:] = codes[codes.shape[0] // 2 :]


def fetch_kernel(species_hbm, centers_hbm, shift_hbm, *refs):
    *refs, shift_row_ref, species_ref, centers_ref, shift_ref, sems = refs
    count = len(refs) // 2
    pairs_in = [
        (species_hbm, species_ref),
        (centers_hbm, centers_ref),
        (shift_hbm, shift_ref),
        *zip(refs[:count], refs[count:]),
    ]
    copies = [
        pltpu.make_async_copy(source, target, sems.at[i])
        for i, (source, target) in enumerate(pairs_in)
    ]
    for copy in copies:
        copy.start()
    for copy in copies:
        copy.wait()
    owned = centers_ref.shape[1]
    shift_row = jnp.zeros((1, 128), F32)
    for cell in range(OWN_CELLS):
        species = species_ref[cell // 2, 0, cell % 2 : cell % 2 + 1, :]
        shift = jnp.zeros(species.shape, F32)
        for s in range(shift_ref.shape[0]):
            shift = jnp.where(species == s, shift_ref[s], shift)
        shift_row = shift_row + lane_row(shift, cell * SITES)
    chosen = lax.broadcasted_iota(jnp.int32, (owned, owned), 0) == centers_ref[...]
    occupied = jnp.sum(jnp.where(chosen, 1.0, 0.0), axis=1, keepdims=True) > 0.5
    column = jnp.where(occupied, jnp.ones((owned, 128), F32), 0.0)
    shift_row_ref[...] = shift_row[:, :owned] * jnp.transpose(column)[0:1]


def finish_kernel(mine_ref, shift_row_ref, *refs):
    *near_refs, energy_ref, forces_ref, virial_ref = refs
    owned = shift_row_ref.shape[1]
    total = mine_ref[:, :owned]
    for near_ref in near_refs:
        start = near_ref.shape[1] - owned
        total = total + near_ref[:, start : start + owned]
    energy = total[12:13] + shift_row_ref[...]
    columns = jnp.transpose(jnp.concatenate([total, jnp.zeros((ORDERS, 128 - owned), F32)], axis=1))
    for cell in range(OWN_CELLS):
        x, z = cell // 2, cell % 2
        lanes = slice(cell * SITES, (cell + 1) * SITES)
        energy_ref[x, 0, z : z + 1, :] = energy[:, lanes]
        for c in range(3):
            forces_ref[c, x, 0, z : z + 1, :] = total[c : c + 1, lanes]
        virial_ref[x, 0, z] = columns[lanes, 3:12]


def force_kernel(kind, nbr, here_ref, last_x_ref, *refs):
    near_side_refs = refs[: 2 * kind - 2]
    (
        next_z_ref,
        center_weight_ref,
        near_weight_ref,
        basis_weight_ref,
        path_weight_ref,
        value_weight_ref,
        latent_weight_ref,
        out_weight_ref,
        keep_ref,
        send_ref,
    ) = refs[2 * kind - 2 :]
    height, width = here_ref.shape
    owned = OWN_CELLS * SITES
    center_sides = 2 if kind == 2 else 1
    kept_sides = 1 if kind == 2 else kind
    own_pairs = owned * nbr
    pairs = center_sides * own_pairs
    centers = center_sides * owned
    radial = basis_weight_ref.shape[0]
    span = GROUP * nbr
    groups = centers // GROUP
    sites = SITES
    root_count = math.sqrt(nbr)
    root_three = math.sqrt(3.0)
    root_fifteen = math.sqrt(15.0)
    root_five = math.sqrt(5.0)
    far = next_z_ref[...]
    mains = [here_ref[...], last_x_ref[...], far[:height], far[height : 2 * height]]
    near_sides = [ref[...] for ref in near_side_refs]
    far_sides = far[2 * height :]
    far_sides = [far_sides[i * height : (i + 1) * height] for i in range(2 * kind - 2)]
    blocks_in = [
        [mains[0], *near_sides[0::2]],
        [mains[1], *near_sides[1::2]],
        [mains[2], *far_sides[0::2]],
        [mains[3], *far_sides[1::2]],
    ]
    feats = jnp.concatenate([side[:owned] for block in blocks_in for side in block], axis=0)
    known = feats.shape[0]
    center_feats = []
    center_coords = []
    coords = []
    scales = []
    codes = []
    cell_row = lax.broadcasted_iota(jnp.int32, (kind * OWN_CELLS, 128), 0) % OWN_CELLS
    tile_lane = lax.broadcasted_iota(jnp.int32, (kind * OWN_CELLS, 128), 1)
    for g, block in enumerate(blocks_in):
        behind_x, ahead_z = g % 2, g // 2
        rows = jnp.concatenate([side[owned : owned + OWN_CELLS] for side in block], axis=0)
        corner_x = (cell_row // 2 + 2 - 2 * behind_x).astype(F32) * CELL_SIDE
        corner_z = (cell_row % 2 + 2 * ahead_z).astype(F32) * CELL_SIDE
        corner = jnp.where(
            tile_lane < sites, corner_x, jnp.where(tile_lane < 2 * sites, 0.0, corner_z)
        )
        coords.append(rows + corner)
    for c in range(center_sides):
        for g, block in enumerate(blocks_in):
            cell = g % 2 * 2 + 1 - g // 2
            row = c * OWN_CELLS + cell
            center_feats.append(block[c][cell * sites : (cell + 1) * sites])
            scales.append(block[c][owned + cell : owned + cell + 1])
            center_coords.append(coords[g][row : row + 1])
            start = owned + OWN_CELLS + (1 - g // 2) * span // 128
            codes.extend(block[c][start + r : start + r + 1] for r in range(span // 128))
    center_feats = jnp.concatenate(center_feats, axis=0)
    coords = jnp.concatenate(coords, axis=0)
    code = jnp.concatenate(codes, axis=1).astype(jnp.int32)
    live = code > 0
    code = jnp.maximum(code - 1, 0)
    side_y = ((code >> 10) - 1).astype(F32)
    near_row = code & 1023
    if center_sides == 2:
        pair_lane = lax.broadcasted_iota(jnp.int32, (1, pairs), 1)
        near_row = jnp.where(pair_lane < own_pairs, near_row, near_row ^ owned)
    near_row = jnp.where(live, near_row, known)

    def place_rows(cell_rows):
        count = cell_rows.shape[0] * sites
        spread = jnp.broadcast_to(cell_rows[:, None, :], (cell_rows.shape[0], sites, 128))
        spread = spread.reshape(count, 128)
        lane = lax.broadcasted_iota(jnp.int32, (count, 128), 1)
        row = lax.broadcasted_iota(jnp.int32, (count, 128), 0)
        keep = (lane % sites == row % sites) & (lane < 3 * sites)
        spread = jnp.transpose(jnp.where(keep, spread, 0.0))
        return jnp.concatenate(split3(spread[: 3 * sites]), axis=0)

    place_parts = place_rows(coords)
    center_parts = place_rows(jnp.concatenate(center_coords, axis=0))

    value_rows = three(*split(jnp.transpose(value_weight_ref[...])))
    latent_t = three(*split(0.5 * jnp.transpose(latent_weight_ref[...])))
    latent_rows = three(*split(latent_weight_ref[...] * out_weight_ref[...]))
    value_plain = three(*split(value_weight_ref[...]))
    basis_t = jnp.transpose(basis_weight_ref[...])
    basis_high_t, basis_low_t = split(0.5 * basis_t)
    basis_rows = three(*split(basis_weight_ref[...]))

    def project(weight, rows):
        weight = stacked(*split(jnp.transpose(weight)))
        return folded(mm_nt(weight, jnp.concatenate(split(rows), axis=1)))

    near_t = project(near_weight_ref[...], feats)
    own_t = project(center_weight_ref[...], center_feats)
    near_high, near_low = split(0.5 * near_t)
    own_high, own_low = split(0.5 * own_t)
    lookup = jnp.concatenate(
        [near_high, near_low, own_high, own_low, basis_high_t, basis_high_t, basis_low_t], axis=1
    )
    scale_rows = jnp.concatenate(scales, axis=0)
    scale_parts = jnp.concatenate(
        [*split3(scale_rows), jnp.zeros((-3 * groups % 16, 128), BF16)], axis=0
    )

    path_rows = jnp.concatenate(
        [jnp.broadcast_to(path_weight_ref[l : l + 1, :], (GROUP, width)) for l in LEVELS], axis=0
    ) * (1.0 / root_count)
    out_column = jnp.transpose(jnp.broadcast_to(out_weight_ref[...], (width, width)))
    out_column = jnp.concatenate([out_column] * (pairs // width), axis=1)

    slot_ids = lax.broadcasted_iota(jnp.int32, (centers, pairs), 0)
    slot_row = lax.broadcasted_iota(jnp.int32, (1, pairs), 1) // nbr
    group_lane = lax.broadcasted_iota(jnp.int32, (GROUP, pairs), 1) // nbr % GROUP
    group_mask = group_lane == lax.broadcasted_iota(jnp.int32, (GROUP, pairs), 0)
    group_mask = jnp.where(group_mask, 1.0, 0.0)
    tall = len(LEVELS) * GROUP
    order = lax.broadcasted_iota(jnp.int32, (radial, pairs), 0).astype(F32) + 1.0
    lanes = [slice(g * span, (g + 1) * span) for g in range(groups)]

    site_ids = lax.broadcasted_iota(jnp.int32, (known, 128), 0)
    if known <= 256:
        site_ids = site_ids.astype(F32).astype(BF16)
        wanted = jnp.broadcast_to(near_row.astype(F32), (16, pairs)).astype(BF16)
        wanted = jnp.concatenate([wanted] * (known // 16), axis=0)
        one, zero = jnp.ones((), BF16), jnp.zeros((), BF16)
    else:
        wanted = near_row
        one, zero = 1.0, 0.0
    site_ids = jnp.concatenate([site_ids] * (pairs // 128), axis=1)
    pick_half = jnp.where(site_ids == wanted, one, zero).astype(BF16)
    slot_half = jnp.where(slot_ids == slot_row, 1.0, 0.0).astype(BF16)

    moved = mm(
        jnp.concatenate([place_parts, -center_parts], axis=1),
        jnp.concatenate([pick_half, slot_half], axis=0),
    )
    moved = moved[: 3 * sites] + moved[3 * sites : 6 * sites] + moved[6 * sites :]
    dx = jnp.where(live, jnp.sum(moved[:sites], axis=0, keepdims=True), 6.0)
    dy = jnp.sum(moved[sites : 2 * sites], axis=0, keepdims=True) + CELL_SIDE * side_y
    dy = jnp.where(live, dy, 0.0)
    dz = jnp.where(live, jnp.sum(moved[2 * sites :], axis=0, keepdims=True), 0.0)
    length = jnp.sqrt(dx * dx + dy * dy + dz * dz)
    inverse = 1.0 / length
    ratio = length * (1.0 / CUTOFF)
    inside = live & (ratio < 1.0)
    r2 = ratio * ratio
    r5 = r2 * r2 * ratio
    r6 = r5 * ratio
    weight = jnp.where(inside, 1.0 - r6 * (28.0 - 48.0 * ratio + 21.0 * r2), 0.0)
    slope = jnp.where(inside, -168.0 * r5 * (1.0 - 2.0 * ratio + r2), 0.0)
    sine, cosine = sin_cos_pi(order * ratio)
    basis = (math.sqrt(2.0 / CUTOFF) * inverse) * sine
    basis_slope = (math.sqrt(2.0 / CUTOFF) * inverse) * (
        (math.pi / CUTOFF) * order * cosine - sine * inverse
    )
    ex = dx * inverse
    ey = dy * inverse
    ez = dz * inverse
    angular = jnp.concatenate(
        [
            jnp.ones_like(ex),
            root_three * ex,
            root_three * ey,
            root_three * ez,
            root_fifteen * ex * ey,
            root_fifteen * ey * ez,
            0.5 * root_five * (3.0 * ez * ez - 1.0),
            root_fifteen * ex * ez,
            0.5 * root_fifteen * (ex * ex - ey * ey),
        ],
        axis=0,
    )
    angular_high, angular_low = halves(angular)
    angular_low = angular_low.astype(BF16).astype(F32)
    block_high = [angular_high[m : m + 1] * group_mask for m in range(len(LEVELS))]
    block_low = [angular_low[m : m + 1] * group_mask for m in range(len(LEVELS))]
    blocks = jnp.concatenate(block_high + block_low + block_high, axis=0).astype(BF16)
    lane_ids = lax.broadcasted_iota(jnp.int32, (128, span), 0)
    lane_slot = lax.broadcasted_iota(jnp.int32, (128, span), 1) // nbr + 3 * sites
    scale = mm(scale_parts, jnp.where(lane_ids == lane_slot, 1.0, 0.0).astype(BF16))
    scale = scale[:groups] + scale[groups : 2 * groups] + scale[2 * groups : 3 * groups]
    scale = jnp.concatenate([scale[g : g + 1] for g in range(groups)], axis=1)
    scale = scale * (1.0 / root_count)
    pull = ROOT_HALF * scale

    basis_high, basis_low = halves(basis)
    basis_rest = jnp.concatenate([basis_high, basis_low, basis_high], axis=0).astype(BF16)
    before = mm(
        lookup,
        jnp.concatenate([pick_half, pick_half, slot_half, slot_half, basis_rest], axis=0),
    )
    gate = 1.0 + jnp.tanh(before)
    active = before * gate
    latent = weight * active
    latent_high, latent_low = split(latent)
    mixed = deep(value_rows, latent_high, latent_low)
    values = mixed[:width]
    env_high, env_low = split(mixed[width:])

    def over_pairs(high, low):
        sums = []
        for cut in lanes:
            both = jnp.concatenate([high[:, cut], low[:, cut]], axis=0)
            quad = mm_nt(blocks[: 2 * tall, cut], both)
            quad = quad[:tall, :width] + quad[tall:, :width] + quad[:tall, width:]
            sums.append(quad * path_rows)
        return sums

    def over_orders(tables):
        parts = []
        for table, cut in zip(tables, lanes):
            high, low = halves(table)
            table = jnp.concatenate([high, high, low], axis=0).astype(BF16)
            table = jnp.transpose(table)
            parts.append(mm(table, blocks[:, cut]))
        return jnp.concatenate(parts, axis=1)

    weighted = over_pairs(env_high, env_low)
    inner = over_orders(weighted)
    scalars = values * inner
    scalars_high, scalars_low = split(scalars)
    z = deep(
        latent_t,
        jnp.concatenate([latent_high, scalars_high], axis=0),
        jnp.concatenate([latent_low, scalars_low], axis=0),
    )
    z_gate = 1.0 + jnp.tanh(z)
    update = z * z_gate
    update_sum = jnp.sum(update * out_column, axis=0, keepdims=True)
    active_sum = jnp.sum(
        active[:, :own_pairs] * out_column[:, :own_pairs], axis=0, keepdims=True
    )
    pair_energy = (active_sum + update_sum[:, :own_pairs]) * (pull * weight)[:, :own_pairs]
    d_z = (0.5 * pull * weight) * (z_gate + update * (2.0 - z_gate))
    spread_back = deep(latent_rows, *split(d_z))
    d_scalars = spread_back[width:]
    d_values = d_scalars * inner
    dinner_high, dinner_low = split(d_scalars * values)
    d_embed = over_pairs(dinner_high, dinner_low)
    d_env = over_orders(d_embed)

    d_angular = []
    for g, cut in enumerate(lanes):
        sides_high, sides_low = halves(jnp.concatenate([weighted[g], d_embed[g]], axis=1))
        d_block = deep(
            three(sides_high.astype(BF16), sides_low.astype(BF16)),
            jnp.concatenate([dinner_high[:, cut], env_high[:, cut]], axis=0),
            jnp.concatenate([dinner_low[:, cut], env_low[:, cut]], axis=0),
        )
        d_block = d_block.reshape(len(LEVELS), GROUP, span) * group_mask[None, :, cut]
        d_angular.append(jnp.sum(d_block, axis=1))
    d_angular = jnp.concatenate(d_angular, axis=1)

    mixed_high, mixed_low = split(jnp.concatenate([d_values, d_env], axis=0))
    d_latent = (
        deep(value_plain, mixed_high, mixed_low)
        + spread_back[:width]
        + pull * out_column
    )
    d_weight = jnp.sum(d_latent * active, axis=0, keepdims=True) + pull * update_sum
    d_before = d_latent * (gate + active * (2.0 - gate))
    d_basis = deep(basis_rows, *split(d_before)) * (0.5 * weight)

    d_length = jnp.sum(d_basis * basis_slope, axis=0, keepdims=True) + d_weight * slope * (
        1.0 / CUTOFF
    )
    a1, a2, a3, a4, a5, a6, a7, a8 = [d_angular[m : m + 1] for m in range(1, 9)]
    ux = root_three * a1 + root_fifteen * (ey * a4 + ez * a7 + ex * a8)
    uy = root_three * a2 + root_fifteen * (ex * a4 + ez * a5 - ey * a8)
    uz = root_three * a3 + root_fifteen * (ey * a5 + ex * a7) + 3.0 * root_five * ez * a6
    along = ex * ux + ey * uy + ez * uz
    radial_part = d_length - along * inverse
    gx = ux * inverse + ex * radial_part
    gy = uy * inverse + ey * radial_part
    gz = uz * inverse + ez * radial_part
    hx = -0.5 * dx
    hy = -0.5 * dy
    hz = -0.5 * dz
    virial = [hx * gx, hx * gy, hx * gz, hy * gx, hy * gy, hy * gz, hz * gx, hz * gy, hz * gz]
    rest = [jnp.zeros((ORDERS - 13, pairs), F32)]
    near_terms = jnp.concatenate(
        [-gx, -gy, -gz, *virial, jnp.zeros_like(gx), *rest], axis=0
    )
    center_rows = [gx, gy, gz, *virial]
    center_rows = [r[:, :own_pairs] for r in center_rows] + [pair_energy]
    center_rows.append(jnp.zeros((ORDERS - 13, own_pairs), F32))
    center_terms = jnp.concatenate(center_rows, axis=0)
    reach = []
    for x, z, side in np.ndindex(2, 2, kept_sides):
        start = ((2 * z + x) * kind + side) * owned
        reach.append(pick_half[start : start + owned])
    reach = jnp.concatenate(reach, axis=0)
    near_sums = mm_nt(jnp.concatenate(split(near_terms), axis=0), reach)
    center_sums = mm_nt(
        jnp.concatenate(split(center_terms), axis=0), slot_half[:owned, :own_pairs]
    )
    center_sums = jnp.concatenate(
        [folded(center_sums), jnp.zeros((ORDERS, 128 - owned), F32)], axis=1
    )
    totals = folded(near_sums)
    lane = lax.broadcasted_iota(jnp.int32, (ORDERS, 128), 1)
    known = totals.shape[1]
    tiles = [totals[:, 128 * i : 128 * (i + 1)] for i in range(known // 128)]
    for g in range(owned // GROUP):
        cell = g % 2 * 2 + 1 - g // 2
        target = (g % 2 * 2 + g // 2) * kept_sides * owned + cell * sites
        turn = (target - g * GROUP) % 128
        piece = pltpu.roll(center_sums, turn, 1) if turn else center_sums
        begin = target % 128
        piece = jnp.where((lane >= begin) & (lane < begin + GROUP), piece, 0.0)
        tiles[target // 128] = tiles[target // 128] + piece
    totals = jnp.concatenate(tiles, axis=1)
    keep_ref[...] = totals[:, : known // 2]
    send_ref[...] = totals[:, known // 2 :]


def in_hbm(*arrays):
    return [pltpu.with_memory_space_constraint(array, pltpu.HBM) for array in arrays]


def joined(parts):
    total = sum(part.shape[0] for part in parts)
    start = 0
    pads = []
    for part in parts:
        end = start + part.shape[0]
        pads.append(jnp.pad(part, ((start, total - end), (0, 0))))
        start = end
    return functools.reduce(jnp.add, pads)


def local(
    positions,
    features,
    species,
    centers,
    neighbours,
    counts,
    species_scale,
    species_shift,
    center_weight,
    near_weight,
    basis_weight,
    path_weight,
    value_weight,
    latent_weight,
    out_weight,
):
    cells_x, cells_y, cells_z, sites, width = features.shape
    cell_count = cells_x * cells_y * cells_z
    owned = cell_count * sites
    assert (cells_x, cells_y, cells_z, sites) == (2, 1, 2, SITES)
    pairs = neighbours.size
    nbr = pairs // owned
    kind = min(3, lax.axis_size("gy"))

    def moved(array, steps):
        names = tuple(steps)
        sizes = [lax.axis_size(name) for name in names]
        route = []
        for at in np.ndindex(*sizes):
            to = [(p + steps[name]) % size for p, name, size in zip(at, names, sizes)]
            route.append(
                (int(np.ravel_multi_index(at, sizes)), int(np.ravel_multi_index(to, sizes)))
            )
        return lax.ppermute(array, names, route)

    vmem = pl.BlockSpec(memory_space=pltpu.VMEM)
    hbm = pl.BlockSpec(memory_space=pltpu.HBM)
    listed = centers.reshape(1, owned)
    payload = jax.ShapeDtypeStruct((owned + OWN_CELLS + pairs // 256, width), F32)
    low, high = pl.pallas_call(
        functools.partial(pack_kernel, kind),
        out_shape=(payload, payload),
        in_specs=[hbm] * 6,
        out_specs=(vmem, vmem),
        scratch_shapes=[
            pltpu.VMEM((owned, 128), F32),
            pltpu.VMEM(positions.shape, F32),
            pltpu.VMEM(species.shape, jnp.int32),
            pltpu.VMEM(listed.shape, jnp.int32),
            pltpu.VMEM(neighbours.shape, jnp.int32),
            pltpu.SMEM(species_scale.shape, F32),
            pltpu.SemaphoreType.DMA((6,)),
        ],
        compiler_params=pltpu.CompilerParams(vmem_limit_bytes=8 * 1024 * 1024),
        name="pack_payload",
    )(
        *in_hbm(
            positions,
            features.reshape(owned, width),
            species,
            listed,
            neighbours,
            species_scale,
        )
    )
    weights = (
        center_weight,
        near_weight,
        basis_weight,
        path_weight,
        value_weight,
        latent_weight,
        out_weight.reshape(1, width),
    )
    *weights, shift_row = pl.pallas_call(
        fetch_kernel,
        out_shape=(
            *(jax.ShapeDtypeStruct(w.shape, F32) for w in weights),
            jax.ShapeDtypeStruct((1, owned), F32),
        ),
        in_specs=[hbm] * (3 + len(weights)),
        out_specs=(vmem,) * (1 + len(weights)),
        scratch_shapes=[
            pltpu.VMEM(species.shape, jnp.int32),
            pltpu.VMEM(listed.shape, jnp.int32),
            pltpu.SMEM(species_shift.shape, F32),
            pltpu.SemaphoreType.DMA((3 + len(weights),)),
        ],
        compiler_params=pltpu.CompilerParams(vmem_limit_bytes=8 * 1024 * 1024),
        name="fetch_weights",
    )(*in_hbm(species, listed, species_shift, *weights))
    last_x = moved(high, {"gx": 1})
    sides = []
    for step in (-1, 1)[: kind - 1]:
        sides.append(moved(high, {"gx": 1, "gy": step}))
        sides.insert(-1, moved(low, {"gy": step}))
    next_z = moved(joined([low, last_x, *sides]), {"gz": -1})
    kept = 1 if kind == 2 else kind
    half = 2 * kept * owned
    keep, send = pl.pallas_call(
        functools.partial(force_kernel, kind, nbr),
        out_shape=(
            jax.ShapeDtypeStruct((ORDERS, half), F32),
            jax.ShapeDtypeStruct((ORDERS, half), F32),
        ),
        in_specs=[vmem] * (8 + 2 * kind),
        out_specs=(vmem, vmem),
        compiler_params=pltpu.CompilerParams(vmem_limit_bytes=44 * 1024 * 1024),
        name="pair_forces",
    )(
        low,
        last_x,
        *sides,
        next_z,
        *weights,
    )
    totals = keep + moved(send, {"gx": -1})

    def part(index):
        return totals[:, index * owned : (index + 1) * owned]

    back = [moved(totals, {"gz": 1}) if kept == 1 else moved(part(kept), {"gz": 1})]
    for i, step in enumerate((1, -1)[: kept - 1]):
        back.append(moved(part(kept + 1 + i), {"gy": step, "gz": 1}))
        back.append(moved(part(1 + i), {"gy": step}))
    site_energy, forces, virial = pl.pallas_call(
        finish_kernel,
        out_shape=(
            jax.ShapeDtypeStruct(species.shape, F32),
            jax.ShapeDtypeStruct(positions.shape, F32),
            jax.ShapeDtypeStruct((*species.shape, 9), F32),
        ),
        in_specs=[vmem] * (2 + len(back)),
        out_specs=(vmem, vmem, vmem),
        compiler_params=pltpu.CompilerParams(vmem_limit_bytes=8 * 1024 * 1024),
        name="write_outputs",
    )(totals, shift_row, *back)
    return (site_energy, forces, jnp.transpose(virial, (4, 0, 1, 2, 3)))


def solution(mesh):
    placed = (
        P(None, "gx", "gy", "gz", None),
        P("gx", "gy", "gz", None, None),
        P("gx", "gy", "gz", None),
        P(("gx", "gy", "gz")),
        P(("gx", "gy", "gz"), None),
        P(("gx", "gy", "gz")),
        P(),
        P(),
        P(),
        P(),
        P(),
        P(),
        P(),
        P(),
        P(),
    )
    return jax.shard_map(
        local,
        mesh=mesh,
        in_specs=placed,
        out_specs=(
            P("gx", "gy", "gz", None),
            P(None, "gx", "gy", "gz", None),
            P(None, "gx", "gy", "gz", None),
        ),
        check_vma=False,
    )
```

```python
import functools
import math

import jax
import jax.numpy as jnp
import numpy as np
from jax import lax
from jax.experimental import pallas as pl
from jax.experimental.pallas import tpu as pltpu
from jax.sharding import PartitionSpec as P

EXACT_DOT = lax.Precision.HIGHEST
CUTOFF = 5.0
CELL_SIDE = 4.6
ROOT_HALF = 0.7071067811865476
GROUP = 8
ORDERS = 16
LEVELS = (0, 1, 1, 1, 2, 2, 2, 2, 2)
SITES = 8
OWN_CELLS = 4
FRAME_CELLS = 48
F32 = jnp.float32
BF16 = jnp.bfloat16


def split(value):
    high = value.astype(BF16)
    low = (value - high.astype(F32)).astype(BF16)
    return high, low


def split3(value):
    high = value.astype(BF16)
    rest = value - high.astype(F32)
    middle = rest.astype(BF16)
    low = (rest - middle.astype(F32)).astype(BF16)
    return high, middle, low


def halves(value):
    high = value.astype(BF16).astype(F32)
    return high, value - high


def mm(a, b):
    return lax.dot_general(a, b, (((1,), (0,)), ((), ())), preferred_element_type=F32)


def mm_nt(a, b):
    return lax.dot_general(a, b, (((1,), (1,)), ((), ())), preferred_element_type=F32)


def stacked(high, low):
    top = jnp.concatenate([high, high], axis=1)
    bottom = jnp.concatenate([low, jnp.zeros_like(low)], axis=1)
    return jnp.concatenate([top, bottom], axis=0)


def folded(product):
    half = product.shape[0] // 2
    return product[:half] + product[half:]


def three(high, low):
    return jnp.concatenate([high, low, high], axis=1)


def tall_product(weights, value_high, value_low):
    return folded(mm(weights, jnp.concatenate([value_high, value_low], axis=0)))


def deep(weights, value_high, value_low):
    return mm(weights, jnp.concatenate([value_high, value_high, value_low], axis=0))


def sin_cos_pi(turns):
    near = turns - 2.0 * jnp.round(turns * 0.5)
    quarter = jnp.round(near * 2.0)
    v = (near - 0.5 * quarter) * math.pi
    v2 = v * v
    s = v * (
        1.0
        + v2
        * (-1.0 / 6 + v2 * (1.0 / 120 + v2 * (-1.0 / 5040 + v2 * (1.0 / 362880 - v2 / 39916800))))
    )
    c = 1.0 + v2 * (
        -0.5
        + v2
        * (1.0 / 24 + v2 * (-1.0 / 720 + v2 * (1.0 / 40320 + v2 * (-1.0 / 3628800 + v2 / 479001600))))
    )
    odd = jnp.abs(quarter) == 1.0
    sine = jnp.where(odd, quarter * c, jnp.where(quarter == 0.0, s, -s))
    cosine = jnp.where(odd, -quarter * s, jnp.where(quarter == 0.0, c, -c))
    return sine, cosine


def lane_row(piece, offset):
    row = jnp.concatenate([piece, jnp.zeros((1, 128 - piece.shape[1]), piece.dtype)], axis=1)
    return pltpu.roll(row, offset, 1) if offset else row


def pack_kernel(
    kind,
    positions_hbm,
    features_hbm,
    species_hbm,
    centers_hbm,
    neighbours_hbm,
    scale_hbm,
    low_ref,
    high_ref,
    wide_ref,
    positions_ref,
    species_ref,
    centers_ref,
    neighbours_ref,
    scale_ref,
    sems,
):
    owned, nbr = neighbours_ref.shape
    per_row = 128 // nbr
    pairs_in = (
        (features_hbm, low_ref.at[pl.ds(0, owned), :]),
        (neighbours_hbm, neighbours_ref),
        (centers_hbm, centers_ref),
        (positions_hbm, positions_ref),
        (species_hbm, species_ref),
        (scale_hbm, scale_ref),
    )
    copies = [
        pltpu.make_async_copy(source, target, sems.at[i])
        for i, (source, target) in enumerate(pairs_in)
    ]
    for copy in copies:
        copy.start()
    for copy in copies:
        copy.wait()
    for cell in range(OWN_CELLS):
        x, z = cell // 2, cell % 2
        species = species_ref[x, 0, z : z + 1, :]
        scale = jnp.zeros(species.shape, F32)
        for s in range(scale_ref.shape[0]):
            scale = jnp.where(species == s, scale_ref[s], scale)
        row = lane_row(scale, 3 * SITES)
        for c in range(3):
            row = row + lane_row(positions_ref[c, x, 0, z : z + 1, :], c * SITES)
        low_ref[owned + cell : owned + cell + 1] = row

    chosen = lax.broadcasted_iota(jnp.int32, (owned, owned), 0) == centers_ref[...]
    chosen = jnp.where(chosen, 1.0, 0.0)
    occupied = jnp.sum(chosen, axis=1, keepdims=True) > 0.5
    chosen = chosen.astype(BF16)
    rows = neighbours_ref[...]
    upper = mm(chosen, (rows >> 4).astype(F32).astype(BF16))
    lower = mm(chosen, (rows & 15).astype(F32).astype(BF16))
    rows = (upper * 16.0 + lower).astype(jnp.int32)
    live = occupied & (rows < FRAME_CELLS * SITES)
    slot = lax.broadcasted_iota(jnp.int32, (owned, nbr), 0)
    cell = slot >> 3
    site = rows & 7
    place = rows >> 3
    near_z = (place & 3) + 1 - 2 * (cell & 1)
    column = place >> 2
    frame_x = (column * 11) >> 5
    frame_y = column - 3 * frame_x
    near_x = frame_x + 1 - 2 * (cell >> 1)
    side = jnp.where(frame_y == 1, 0, jnp.where(frame_y == 2, 1, kind - 1))
    block = (near_z >> 1) * 2 + 1 - (near_x >> 1)
    where = (block * kind + side) * owned + (near_x & 1) * 16 + (near_z & 1) * 8 + site
    code = jnp.where(live, 1 + where + (frame_y << 10), 0).astype(F32)
    wide_ref[...] = jnp.concatenate([code, jnp.zeros((owned, 128 - nbr), F32)], axis=1)
    codes = wide_ref[pl.ds(0, owned // per_row, stride=per_row), :]
    for j in range(1, per_row):
        more = wide_ref[pl.ds(j, owned // per_row, stride=per_row), :]
        codes = codes + pltpu.roll(more, j * nbr, 1)
    tile = owned + OWN_CELLS
    low_ref[tile:] = codes[: codes.shape[0] // 2]
    high_ref[:tile] = low_ref[:tile]
    high_ref[tile:] = codes[codes.shape[0] // 2 :]


def fetch_kernel(species_hbm, centers_hbm, shift_hbm, *refs):
    *refs, shift_row_ref, species_ref, centers_ref, shift_ref, sems = refs
    count = len(refs) // 2
    pairs_in = [
        (species_hbm, species_ref),
        (centers_hbm, centers_ref),
        (shift_hbm, shift_ref),
        *zip(refs[:count], refs[count:]),
    ]
    copies = [
        pltpu.make_async_copy(source, target, sems.at[i])
        for i, (source, target) in enumerate(pairs_in)
    ]
    for copy in copies:
        copy.start()
    for copy in copies:
        copy.wait()
    owned = centers_ref.shape[1]
    shift_row = jnp.zeros((1, 128), F32)
    for cell in range(OWN_CELLS):
        species = species_ref[cell // 2, 0, cell % 2 : cell % 2 + 1, :]
        shift = jnp.zeros(species.shape, F32)
        for s in range(shift_ref.shape[0]):
            shift = jnp.where(species == s, shift_ref[s], shift)
        shift_row = shift_row + lane_row(shift, cell * SITES)
    chosen = lax.broadcasted_iota(jnp.int32, (owned, owned), 0) == centers_ref[...]
    occupied = jnp.sum(jnp.where(chosen, 1.0, 0.0), axis=1, keepdims=True) > 0.5
    column = jnp.where(occupied, jnp.ones((owned, 128), F32), 0.0)
    shift_row_ref[...] = shift_row[:, :owned] * jnp.transpose(column)[0:1]


def finish_kernel(mine_ref, shift_row_ref, *refs):
    *near_refs, energy_ref, forces_ref, virial_ref = refs
    owned = shift_row_ref.shape[1]
    total = mine_ref[:, :owned]
    for near_ref in near_refs:
        start = near_ref.shape[1] - owned
        total = total + near_ref[:, start : start + owned]
    energy = total[12:13] + shift_row_ref[...]
    columns = jnp.transpose(jnp.concatenate([total, jnp.zeros((ORDERS, 128 - owned), F32)], axis=1))
    for cell in range(OWN_CELLS):
        x, z = cell // 2, cell % 2
        lanes = slice(cell * SITES, (cell + 1) * SITES)
        energy_ref[x, 0, z : z + 1, :] = energy[:, lanes]
        for c in range(3):
            forces_ref[c, x, 0, z : z + 1, :] = total[c : c + 1, lanes]
        virial_ref[x, 0, z] = columns[lanes, 3:12]


def force_kernel(kind, nbr, here_ref, last_x_ref, *refs):
    near_side_refs = refs[: 2 * kind - 2]
    (
        next_z_ref,
        center_weight_ref,
        near_weight_ref,
        basis_weight_ref,
        path_weight_ref,
        value_weight_ref,
        latent_weight_ref,
        out_weight_ref,
        keep_ref,
        send_ref,
    ) = refs[2 * kind - 2 :]
    height, width = here_ref.shape
    owned = OWN_CELLS * SITES
    center_sides = 2 if kind == 2 else 1
    kept_sides = 1 if kind == 2 else kind
    own_pairs = owned * nbr
    pairs = center_sides * own_pairs
    centers = center_sides * owned
    radial = basis_weight_ref.shape[0]
    span = GROUP * nbr
    groups = centers // GROUP
    sites = SITES
    root_count = math.sqrt(nbr)
    root_three = math.sqrt(3.0)
    root_fifteen = math.sqrt(15.0)
    root_five = math.sqrt(5.0)
    far = next_z_ref[...]
    mains = [here_ref[...], last_x_ref[...], far[:height], far[height : 2 * height]]
    near_sides = [ref[...] for ref in near_side_refs]
    far_sides = far[2 * height :]
    far_sides = [far_sides[i * height : (i + 1) * height] for i in range(2 * kind - 2)]
    blocks_in = [
        [mains[0], *near_sides[0::2]],
        [mains[1], *near_sides[1::2]],
        [mains[2], *far_sides[0::2]],
        [mains[3], *far_sides[1::2]],
    ]
    feats = jnp.concatenate([side[:owned] for block in blocks_in for side in block], axis=0)
    known = feats.shape[0]
    center_feats = []
    center_coords = []
    coords = []
    scales = []
    codes = []
    cell_row = lax.broadcasted_iota(jnp.int32, (kind * OWN_CELLS, 128), 0) % OWN_CELLS
    tile_lane = lax.broadcasted_iota(jnp.int32, (kind * OWN_CELLS, 128), 1)
    for g, block in enumerate(blocks_in):
        behind_x, ahead_z = g % 2, g // 2
        rows = jnp.concatenate([side[owned : owned + OWN_CELLS] for side in block], axis=0)
        corner_x = (cell_row // 2 + 2 - 2 * behind_x).astype(F32) * CELL_SIDE
        corner_z = (cell_row % 2 + 2 * ahead_z).astype(F32) * CELL_SIDE
        corner = jnp.where(
            tile_lane < sites, corner_x, jnp.where(tile_lane < 2 * sites, 0.0, corner_z)
        )
        coords.append(rows + corner)
    for c in range(center_sides):
        for g, block in enumerate(blocks_in):
            cell = g % 2 * 2 + 1 - g // 2
            row = c * OWN_CELLS + cell
            center_feats.append(block[c][cell * sites : (cell + 1) * sites])
            scales.append(block[c][owned + cell : owned + cell + 1])
            center_coords.append(coords[g][row : row + 1])
            start = owned + OWN_CELLS + (1 - g // 2) * span // 128
            codes.extend(block[c][start + r : start + r + 1] for r in range(span // 128))
    center_feats = jnp.concatenate(center_feats, axis=0)
    coords = jnp.concatenate(coords, axis=0)
    code = jnp.concatenate(codes, axis=1).astype(jnp.int32)
    live = code > 0
    code = jnp.maximum(code - 1, 0)
    side_y = ((code >> 10) - 1).astype(F32)
    near_row = code & 1023
    if center_sides == 2:
        pair_lane = lax.broadcasted_iota(jnp.int32, (1, pairs), 1)
        near_row = jnp.where(pair_lane < own_pairs, near_row, near_row ^ owned)
    near_row = jnp.where(live, near_row, known)

    def place_rows(cell_rows):
        count = cell_rows.shape[0] * sites
        spread = jnp.broadcast_to(cell_rows[:, None, :], (cell_rows.shape[0], sites, 128))
        spread = spread.reshape(count, 128)
        lane = lax.broadcasted_iota(jnp.int32, (count, 128), 1)
        row = lax.broadcasted_iota(jnp.int32, (count, 128), 0)
        keep = (lane % sites == row % sites) & (lane < 3 * sites)
        spread = jnp.transpose(jnp.where(keep, spread, 0.0))
        return jnp.concatenate(split3(spread[: 3 * sites]), axis=0)

    place_parts = place_rows(coords)
    center_parts = place_rows(jnp.concatenate(center_coords, axis=0))

    value_rows = stacked(*split(jnp.transpose(value_weight_ref[...])))
    latent_t = three(*split(0.5 * jnp.transpose(latent_weight_ref[...])))
    latent_rows = stacked(*split(latent_weight_ref[...] * out_weight_ref[...]))
    value_plain = three(*split(value_weight_ref[...]))
    basis_t = jnp.transpose(basis_weight_ref[...])
    basis_high_t, basis_low_t = split(0.5 * basis_t)
    basis_rows = stacked(*split(basis_weight_ref[...]))

    def project(weight, rows):
        weight = stacked(*split(jnp.transpose(weight)))
        return folded(mm_nt(weight, jnp.concatenate(split(rows), axis=1)))

    near_t = project(near_weight_ref[...], feats)
    own_t = project(center_weight_ref[...], center_feats)
    near_high, near_low = split(0.5 * near_t)
    own_high, own_low = split(0.5 * own_t)
    lookup = jnp.concatenate(
        [near_high, near_low, own_high, own_low, basis_high_t, basis_high_t, basis_low_t], axis=1
    )
    scale_rows = jnp.concatenate(scales, axis=0)
    scale_parts = jnp.concatenate(
        [*split3(scale_rows), jnp.zeros((-3 * groups % 16, 128), BF16)], axis=0
    )

    path_rows = jnp.concatenate(
        [jnp.broadcast_to(path_weight_ref[l : l + 1, :], (GROUP, width)) for l in LEVELS], axis=0
    ) * (1.0 / root_count)
    out_column = jnp.transpose(jnp.broadcast_to(out_weight_ref[...], (width, width)))
    out_column = jnp.concatenate([out_column] * (pairs // width), axis=1)

    slot_ids = lax.broadcasted_iota(jnp.int32, (centers, pairs), 0)
    slot_row = lax.broadcasted_iota(jnp.int32, (1, pairs), 1) // nbr
    group_lane = lax.broadcasted_iota(jnp.int32, (GROUP, pairs), 1) // nbr % GROUP
    group_mask = group_lane == lax.broadcasted_iota(jnp.int32, (GROUP, pairs), 0)
    group_mask = jnp.where(group_mask, 1.0, 0.0)
    tall = len(LEVELS) * GROUP
    order = lax.broadcasted_iota(jnp.int32, (radial, pairs), 0).astype(F32) + 1.0
    lanes = [slice(g * span, (g + 1) * span) for g in range(groups)]

    site_ids = lax.broadcasted_iota(jnp.int32, (known, 128), 0)
    if known <= 256:
        site_ids = site_ids.astype(F32).astype(BF16)
        wanted = jnp.broadcast_to(near_row.astype(F32), (16, pairs)).astype(BF16)
        wanted = jnp.concatenate([wanted] * (known // 16), axis=0)
        one, zero = jnp.ones((), BF16), jnp.zeros((), BF16)
    else:
        wanted = near_row
        one, zero = 1.0, 0.0
    site_ids = jnp.concatenate([site_ids] * (pairs // 128), axis=1)
    pick_half = jnp.where(site_ids == wanted, one, zero).astype(BF16)
    slot_half = jnp.where(slot_ids == slot_row, 1.0, 0.0).astype(BF16)

    moved = mm(
        jnp.concatenate([place_parts, -center_parts], axis=1),
        jnp.concatenate([pick_half, slot_half], axis=0),
    )
    moved = moved[: 3 * sites] + moved[3 * sites : 6 * sites] + moved[6 * sites :]
    dx = jnp.where(live, jnp.sum(moved[:sites], axis=0, keepdims=True), 6.0)
    dy = jnp.sum(moved[sites : 2 * sites], axis=0, keepdims=True) + CELL_SIDE * side_y
    dy = jnp.where(live, dy, 0.0)
    dz = jnp.where(live, jnp.sum(moved[2 * sites :], axis=0, keepdims=True), 0.0)
    length = jnp.sqrt(dx * dx + dy * dy + dz * dz)
    inverse = 1.0 / length
    ratio = length * (1.0 / CUTOFF)
    inside = live & (ratio < 1.0)
    r2 = ratio * ratio
    r5 = r2 * r2 * ratio
    r6 = r5 * ratio
    weight = jnp.where(inside, 1.0 - r6 * (28.0 - 48.0 * ratio + 21.0 * r2), 0.0)
    slope = jnp.where(inside, -168.0 * r5 * (1.0 - 2.0 * ratio + r2), 0.0)
    sine, cosine = sin_cos_pi(order * ratio)
    basis = (math.sqrt(2.0 / CUTOFF) * inverse) * sine
    basis_slope = (math.sqrt(2.0 / CUTOFF) * inverse) * (
        (math.pi / CUTOFF) * order * cosine - sine * inverse
    )
    ex = dx * inverse
    ey = dy * inverse
    ez = dz * inverse
    angular = jnp.concatenate(
        [
            jnp.ones_like(ex),
            root_three * ex,
            root_three * ey,
            root_three * ez,
            root_fifteen * ex * ey,
            root_fifteen * ey * ez,
            0.5 * root_five * (3.0 * ez * ez - 1.0),
            root_fifteen * ex * ez,
            0.5 * root_fifteen * (ex * ex - ey * ey),
        ],
        axis=0,
    )
    angular_high, angular_low = halves(angular)
    angular_low = angular_low.astype(BF16).astype(F32)
    block_high = [angular_high[m : m + 1] * group_mask for m in range(len(LEVELS))]
    block_low = [angular_low[m : m + 1] * group_mask for m in range(len(LEVELS))]
    blocks = jnp.concatenate(block_high + block_low + block_high, axis=0).astype(BF16)
    lane_ids = lax.broadcasted_iota(jnp.int32, (128, span), 0)
    lane_slot = lax.broadcasted_iota(jnp.int32, (128, span), 1) // nbr + 3 * sites
    scale = mm(scale_parts, jnp.where(lane_ids == lane_slot, 1.0, 0.0).astype(BF16))
    scale = scale[:groups] + scale[groups : 2 * groups] + scale[2 * groups : 3 * groups]
    scale = jnp.concatenate([scale[g : g + 1] for g in range(groups)], axis=1)
    scale = scale * (1.0 / root_count)
    pull = ROOT_HALF * scale

    basis_high, basis_low = halves(basis)
    basis_rest = jnp.concatenate([basis_high, basis_low, basis_high], axis=0).astype(BF16)
    before = mm(
        lookup,
        jnp.concatenate([pick_half, pick_half, slot_half, slot_half, basis_rest], axis=0),
    )
    gate = 1.0 + jnp.tanh(before)
    active = before * gate
    latent = weight * active
    latent_high, latent_low = split(latent)
    mixed = tall_product(value_rows, latent_high, latent_low)
    values = mixed[:width]
    env_high, env_low = split(mixed[width:])

    def over_pairs(high, low):
        sums = []
        for cut in lanes:
            both = jnp.concatenate([high[:, cut], low[:, cut]], axis=0)
            quad = mm_nt(blocks[: 2 * tall, cut], both)
            quad = quad[:tall, :width] + quad[tall:, :width] + quad[:tall, width:]
            sums.append(quad * path_rows)
        return sums

    def over_orders(tables):
        parts = []
        for table, cut in zip(tables, lanes):
            high, low = halves(table)
            table = jnp.concatenate([high, high, low], axis=0).astype(BF16)
            table = jnp.transpose(table)
            parts.append(mm(table, blocks[:, cut]))
        return jnp.concatenate(parts, axis=1)

    weighted = over_pairs(env_high, env_low)
    inner = over_orders(weighted)
    scalars = values * inner
    scalars_high, scalars_low = split(scalars)
    z = deep(
        latent_t,
        jnp.concatenate([latent_high, scalars_high], axis=0),
        jnp.concatenate([latent_low, scalars_low], axis=0),
    )
    z_gate = 1.0 + jnp.tanh(z)
    update = z * z_gate
    update_sum = jnp.sum(update * out_column, axis=0, keepdims=True)
    active_sum = jnp.sum(
        active[:, :own_pairs] * out_column[:, :own_pairs], axis=0, keepdims=True
    )
    pair_energy = (active_sum + update_sum[:, :own_pairs]) * (pull * weight)[:, :own_pairs]
    d_z = (0.5 * pull * weight) * (z_gate + update * (2.0 - z_gate))
    spread_back = tall_product(latent_rows, *split(d_z))
    d_scalars = spread_back[width:]
    d_values = d_scalars * inner
    dinner_high, dinner_low = split(d_scalars * values)
    d_embed = over_pairs(dinner_high, dinner_low)
    d_env = over_orders(d_embed)

    d_angular = []
    for g, cut in enumerate(lanes):
        sides_high, sides_low = halves(jnp.concatenate([weighted[g], d_embed[g]], axis=1))
        d_block = deep(
            three(sides_high.astype(BF16), sides_low.astype(BF16)),
            jnp.concatenate([dinner_high[:, cut], env_high[:, cut]], axis=0),
            jnp.concatenate([dinner_low[:, cut], env_low[:, cut]], axis=0),
        )
        d_block = d_block.reshape(len(LEVELS), GROUP, span) * group_mask[None, :, cut]
        d_angular.append(jnp.sum(d_block, axis=1))
    d_angular = jnp.concatenate(d_angular, axis=1)

    mixed_high, mixed_low = split(jnp.concatenate([d_values, d_env], axis=0))
    d_latent = (
        deep(value_plain, mixed_high, mixed_low)
        + spread_back[:width]
        + pull * out_column
    )
    d_weight = jnp.sum(d_latent * active, axis=0, keepdims=True) + pull * update_sum
    d_before = d_latent * (gate + active * (2.0 - gate))
    d_basis = tall_product(basis_rows, *split(d_before)) * (0.5 * weight)

    d_length = jnp.sum(d_basis * basis_slope, axis=0, keepdims=True) + d_weight * slope * (
        1.0 / CUTOFF
    )
    a1, a2, a3, a4, a5, a6, a7, a8 = [d_angular[m : m + 1] for m in range(1, 9)]
    ux = root_three * a1 + root_fifteen * (ey * a4 + ez * a7 + ex * a8)
    uy = root_three * a2 + root_fifteen * (ex * a4 + ez * a5 - ey * a8)
    uz = root_three * a3 + root_fifteen * (ey * a5 + ex * a7) + 3.0 * root_five * ez * a6
    along = ex * ux + ey * uy + ez * uz
    radial_part = d_length - along * inverse
    gx = ux * inverse + ex * radial_part
    gy = uy * inverse + ey * radial_part
    gz = uz * inverse + ez * radial_part
    hx = -0.5 * dx
    hy = -0.5 * dy
    hz = -0.5 * dz
    virial = [hx * gx, hx * gy, hx * gz, hy * gx, hy * gy, hy * gz, hz * gx, hz * gy, hz * gz]
    rest = [jnp.zeros((ORDERS - 13, pairs), F32)]
    near_terms = jnp.concatenate(
        [-gx, -gy, -gz, *virial, jnp.zeros_like(gx), *rest], axis=0
    )
    center_rows = [gx, gy, gz, *virial]
    center_rows = [r[:, :own_pairs] for r in center_rows] + [pair_energy]
    center_rows.append(jnp.zeros((ORDERS - 13, own_pairs), F32))
    center_terms = jnp.concatenate(center_rows, axis=0)
    reach = []
    for x, z, side in np.ndindex(2, 2, kept_sides):
        start = ((2 * z + x) * kind + side) * owned
        reach.append(pick_half[start : start + owned])
    reach = jnp.concatenate(reach, axis=0)
    near_sums = mm_nt(jnp.concatenate(split(near_terms), axis=0), reach)
    center_sums = mm_nt(
        jnp.concatenate(split(center_terms), axis=0), slot_half[:owned, :own_pairs]
    )
    center_sums = jnp.concatenate(
        [folded(center_sums), jnp.zeros((ORDERS, 128 - owned), F32)], axis=1
    )
    totals = folded(near_sums)
    lane = lax.broadcasted_iota(jnp.int32, (ORDERS, 128), 1)
    known = totals.shape[1]
    tiles = [totals[:, 128 * i : 128 * (i + 1)] for i in range(known // 128)]
    for g in range(owned // GROUP):
        cell = g % 2 * 2 + 1 - g // 2
        target = (g % 2 * 2 + g // 2) * kept_sides * owned + cell * sites
        turn = (target - g * GROUP) % 128
        piece = pltpu.roll(center_sums, turn, 1) if turn else center_sums
        begin = target % 128
        piece = jnp.where((lane >= begin) & (lane < begin + GROUP), piece, 0.0)
        tiles[target // 128] = tiles[target // 128] + piece
    totals = jnp.concatenate(tiles, axis=1)
    keep_ref[...] = totals[:, : known // 2]
    send_ref[...] = totals[:, known // 2 :]


def in_hbm(*arrays):
    return [pltpu.with_memory_space_constraint(array, pltpu.HBM) for array in arrays]


def joined(parts):
    total = sum(part.shape[0] for part in parts)
    start = 0
    pads = []
    for part in parts:
        end = start + part.shape[0]
        pads.append(jnp.pad(part, ((start, total - end), (0, 0))))
        start = end
    return functools.reduce(jnp.add, pads)


def local(
    positions,
    features,
    species,
    centers,
    neighbours,
    counts,
    species_scale,
    species_shift,
    center_weight,
    near_weight,
    basis_weight,
    path_weight,
    value_weight,
    latent_weight,
    out_weight,
):
    cells_x, cells_y, cells_z, sites, width = features.shape
    cell_count = cells_x * cells_y * cells_z
    owned = cell_count * sites
    assert (cells_x, cells_y, cells_z, sites) == (2, 1, 2, SITES)
    pairs = neighbours.size
    nbr = pairs // owned
    kind = min(3, lax.axis_size("gy"))

    def moved(array, steps):
        names = tuple(steps)
        sizes = [lax.axis_size(name) for name in names]
        route = []
        for at in np.ndindex(*sizes):
            to = [(p + steps[name]) % size for p, name, size in zip(at, names, sizes)]
            route.append(
                (int(np.ravel_multi_index(at, sizes)), int(np.ravel_multi_index(to, sizes)))
            )
        return lax.ppermute(array, names, route)

    vmem = pl.BlockSpec(memory_space=pltpu.VMEM)
    hbm = pl.BlockSpec(memory_space=pltpu.HBM)
    listed = centers.reshape(1, owned)
    payload = jax.ShapeDtypeStruct((owned + OWN_CELLS + pairs // 256, width), F32)
    low, high = pl.pallas_call(
        functools.partial(pack_kernel, kind),
        out_shape=(payload, payload),
        in_specs=[hbm] * 6,
        out_specs=(vmem, vmem),
        scratch_shapes=[
            pltpu.VMEM((owned, 128), F32),
            pltpu.VMEM(positions.shape, F32),
            pltpu.VMEM(species.shape, jnp.int32),
            pltpu.VMEM(listed.shape, jnp.int32),
            pltpu.VMEM(neighbours.shape, jnp.int32),
            pltpu.SMEM(species_scale.shape, F32),
            pltpu.SemaphoreType.DMA((6,)),
        ],
        compiler_params=pltpu.CompilerParams(vmem_limit_bytes=8 * 1024 * 1024),
        name="pack_payload",
    )(
        *in_hbm(
            positions,
            features.reshape(owned, width),
            species,
            listed,
            neighbours,
            species_scale,
        )
    )
    weights = (
        center_weight,
        near_weight,
        basis_weight,
        path_weight,
        value_weight,
        latent_weight,
        out_weight.reshape(1, width),
    )
    *weights, shift_row = pl.pallas_call(
        fetch_kernel,
        out_shape=(
            *(jax.ShapeDtypeStruct(w.shape, F32) for w in weights),
            jax.ShapeDtypeStruct((1, owned), F32),
        ),
        in_specs=[hbm] * (3 + len(weights)),
        out_specs=(vmem,) * (1 + len(weights)),
        scratch_shapes=[
            pltpu.VMEM(species.shape, jnp.int32),
            pltpu.VMEM(listed.shape, jnp.int32),
            pltpu.SMEM(species_shift.shape, F32),
            pltpu.SemaphoreType.DMA((3 + len(weights),)),
        ],
        compiler_params=pltpu.CompilerParams(vmem_limit_bytes=8 * 1024 * 1024),
        name="fetch_weights",
    )(*in_hbm(species, listed, species_shift, *weights))
    last_x = moved(high, {"gx": 1})
    sides = []
    for step in (-1, 1)[: kind - 1]:
        sides.append(moved(high, {"gx": 1, "gy": step}))
        sides.insert(-1, moved(low, {"gy": step}))
    next_z = moved(joined([low, last_x, *sides]), {"gz": -1})
    kept = 1 if kind == 2 else kind
    half = 2 * kept * owned
    keep, send = pl.pallas_call(
        functools.partial(force_kernel, kind, nbr),
        out_shape=(
            jax.ShapeDtypeStruct((ORDERS, half), F32),
            jax.ShapeDtypeStruct((ORDERS, half), F32),
        ),
        in_specs=[vmem] * (8 + 2 * kind),
        out_specs=(vmem, vmem),
        compiler_params=pltpu.CompilerParams(vmem_limit_bytes=44 * 1024 * 1024),
        name="pair_forces",
    )(
        low,
        last_x,
        *sides,
        next_z,
        *weights,
    )
    totals = keep + moved(send, {"gx": -1})

    def part(index):
        return totals[:, index * owned : (index + 1) * owned]

    back = [moved(totals, {"gz": 1}) if kept == 1 else moved(part(kept), {"gz": 1})]
    for i, step in enumerate((1, -1)[: kept - 1]):
        back.append(moved(part(kept + 1 + i), {"gy": step, "gz": 1}))
        back.append(moved(part(1 + i), {"gy": step}))
    site_energy, forces, virial = pl.pallas_call(
        finish_kernel,
        out_shape=(
            jax.ShapeDtypeStruct(species.shape, F32),
            jax.ShapeDtypeStruct(positions.shape, F32),
            jax.ShapeDtypeStruct((*species.shape, 9), F32),
        ),
        in_specs=[vmem] * (2 + len(back)),
        out_specs=(vmem, vmem, vmem),
        compiler_params=pltpu.CompilerParams(vmem_limit_bytes=8 * 1024 * 1024),
        name="write_outputs",
    )(totals, shift_row, *back)
    return (site_energy, forces, jnp.transpose(virial, (4, 0, 1, 2, 3)))


def solution(mesh):
    placed = (
        P(None, "gx", "gy", "gz", None),
        P("gx", "gy", "gz", None, None),
        P("gx", "gy", "gz", None),
        P(("gx", "gy", "gz")),
        P(("gx", "gy", "gz"), None),
        P(("gx", "gy", "gz")),
        P(),
        P(),
        P(),
        P(),
        P(),
        P(),
        P(),
        P(),
        P(),
    )
    return jax.shard_map(
        local,
        mesh=mesh,
        in_specs=placed,
        out_specs=(
            P("gx", "gy", "gz", None),
            P(None, "gx", "gy", "gz", None),
            P(None, "gx", "gy", "gz", None),
        ),
        check_vma=False,
    )
```

```python
import functools
import math

import jax
import jax.numpy as jnp
import numpy as np
from jax import lax
from jax.experimental import pallas as pl
from jax.experimental.pallas import tpu as pltpu
from jax.sharding import PartitionSpec as P

EXACT_DOT = lax.Precision.HIGHEST
CUTOFF = 5.0
CELL_SIDE = 4.6
ROOT_HALF = 0.7071067811865476
GROUP = 8
ORDERS = 16
LEVELS = (0, 1, 1, 1, 2, 2, 2, 2, 2)
SITES = 8
OWN_CELLS = 4
FRAME_CELLS = 48
F32 = jnp.float32
BF16 = jnp.bfloat16


def split(value):
    high = value.astype(BF16)
    low = (value - high.astype(F32)).astype(BF16)
    return high, low


def split3(value):
    high = value.astype(BF16)
    rest = value - high.astype(F32)
    middle = rest.astype(BF16)
    low = (rest - middle.astype(F32)).astype(BF16)
    return high, middle, low


def halves(value):
    high = value.astype(BF16).astype(F32)
    return high, value - high


def mm(a, b):
    return lax.dot_general(a, b, (((1,), (0,)), ((), ())), preferred_element_type=F32)


def mm_nt(a, b):
    return lax.dot_general(a, b, (((1,), (1,)), ((), ())), preferred_element_type=F32)


def stacked(high, low):
    top = jnp.concatenate([high, high], axis=1)
    bottom = jnp.concatenate([low, jnp.zeros_like(low)], axis=1)
    return jnp.concatenate([top, bottom], axis=0)


def folded(product):
    half = product.shape[0] // 2
    return product[:half] + product[half:]


def three(high, low):
    return jnp.concatenate([high, low, high], axis=1)


def deep(weights, value_high, value_low):
    return mm(weights, jnp.concatenate([value_high, value_high, value_low], axis=0))


def sin_cos_pi(turns):
    near = turns - 2.0 * jnp.round(turns * 0.5)
    quarter = jnp.round(near * 2.0)
    v = (near - 0.5 * quarter) * math.pi
    v2 = v * v
    s = v * (
        1.0
        + v2
        * (-1.0 / 6 + v2 * (1.0 / 120 + v2 * (-1.0 / 5040 + v2 * (1.0 / 362880 - v2 / 39916800))))
    )
    c = 1.0 + v2 * (
        -0.5
        + v2
        * (1.0 / 24 + v2 * (-1.0 / 720 + v2 * (1.0 / 40320 + v2 * (-1.0 / 3628800 + v2 / 479001600))))
    )
    odd = jnp.abs(quarter) == 1.0
    sine = jnp.where(odd, quarter * c, jnp.where(quarter == 0.0, s, -s))
    cosine = jnp.where(odd, -quarter * s, jnp.where(quarter == 0.0, c, -c))
    return sine, cosine


def lane_row(piece, offset):
    row = jnp.concatenate([piece, jnp.zeros((1, 128 - piece.shape[1]), piece.dtype)], axis=1)
    return pltpu.roll(row, offset, 1) if offset else row


def pack_kernel(
    kind,
    positions_hbm,
    features_hbm,
    species_hbm,
    centers_hbm,
    neighbours_hbm,
    scale_hbm,
    low_ref,
    high_ref,
    wide_ref,
    positions_ref,
    species_ref,
    centers_ref,
    neighbours_ref,
    scale_ref,
    sems,
):
    owned, nbr = neighbours_ref.shape
    per_row = 128 // nbr
    pairs_in = (
        (features_hbm, low_ref.at[pl.ds(0, owned), :]),
        (neighbours_hbm, neighbours_ref),
        (centers_hbm, centers_ref),
        (positions_hbm, positions_ref),
        (species_hbm, species_ref),
        (scale_hbm, scale_ref),
    )
    copies = [
        pltpu.make_async_copy(source, target, sems.at[i])
        for i, (source, target) in enumerate(pairs_in)
    ]
    for copy in copies:
        copy.start()
    for copy in copies:
        copy.wait()
    for cell in range(OWN_CELLS):
        x, z = cell // 2, cell % 2
        species = species_ref[x, 0, z : z + 1, :]
        scale = jnp.zeros(species.shape, F32)
        for s in range(scale_ref.shape[0]):
            scale = jnp.where(species == s, scale_ref[s], scale)
        row = lane_row(scale, 3 * SITES)
        for c in range(3):
            row = row + lane_row(positions_ref[c, x, 0, z : z + 1, :], c * SITES)
        low_ref[owned + cell : owned + cell + 1] = row

    chosen = lax.broadcasted_iota(jnp.int32, (owned, owned), 0) == centers_ref[...]
    chosen = jnp.where(chosen, 1.0, 0.0)
    occupied = jnp.sum(chosen, axis=1, keepdims=True) > 0.5
    chosen = chosen.astype(BF16)
    rows = neighbours_ref[...]
    upper = mm(chosen, (rows >> 4).astype(F32).astype(BF16))
    lower = mm(chosen, (rows & 15).astype(F32).astype(BF16))
    rows = (upper * 16.0 + lower).astype(jnp.int32)
    live = occupied & (rows < FRAME_CELLS * SITES)
    slot = lax.broadcasted_iota(jnp.int32, (owned, nbr), 0)
    cell = slot >> 3
    site = rows & 7
    place = rows >> 3
    near_z = (place & 3) + 1 - 2 * (cell & 1)
    column = place >> 2
    frame_x = (column * 11) >> 5
    frame_y = column - 3 * frame_x
    near_x = frame_x + 1 - 2 * (cell >> 1)
    side = jnp.where(frame_y == 1, 0, jnp.where(frame_y == 2, 1, kind - 1))
    block = (near_z >> 1) * 2 + 1 - (near_x >> 1)
    where = (block * kind + side) * owned + (near_x & 1) * 16 + (near_z & 1) * 8 + site
    code = jnp.where(live, 1 + where + (frame_y << 10), 0).astype(F32)
    wide_ref[...] = jnp.concatenate([code, jnp.zeros((owned, 128 - nbr), F32)], axis=1)
    codes = wide_ref[pl.ds(0, owned // per_row, stride=per_row), :]
    for j in range(1, per_row):
        more = wide_ref[pl.ds(j, owned // per_row, stride=per_row), :]
        codes = codes + pltpu.roll(more, j * nbr, 1)
    tile = owned + OWN_CELLS
    low_ref[tile:] = codes[: codes.shape[0] // 2]
    high_ref[:tile] = low_ref[:tile]
    high_ref[tile:] = codes[codes.shape[0] // 2 :]


def fetch_kernel(species_hbm, centers_hbm, shift_hbm, *refs):
    *refs, shift_row_ref, species_ref, centers_ref, shift_ref, sems = refs
    count = len(refs) // 2
    pairs_in = [
        (species_hbm, species_ref),
        (centers_hbm, centers_ref),
        (shift_hbm, shift_ref),
        *zip(refs[:count], refs[count:]),
    ]
    copies = [
        pltpu.make_async_copy(source, target, sems.at[i])
        for i, (source, target) in enumerate(pairs_in)
    ]
    for copy in copies:
        copy.start()
    for copy in copies:
        copy.wait()
    owned = centers_ref.shape[1]
    shift_row = jnp.zeros((1, 128), F32)
    for cell in range(OWN_CELLS):
        species = species_ref[cell // 2, 0, cell % 2 : cell % 2 + 1, :]
        shift = jnp.zeros(species.shape, F32)
        for s in range(shift_ref.shape[0]):
            shift = jnp.where(species == s, shift_ref[s], shift)
        shift_row = shift_row + lane_row(shift, cell * SITES)
    chosen = lax.broadcasted_iota(jnp.int32, (owned, owned), 0) == centers_ref[...]
    occupied = jnp.sum(jnp.where(chosen, 1.0, 0.0), axis=1, keepdims=True) > 0.5
    column = jnp.where(occupied, jnp.ones((owned, 128), F32), 0.0)
    shift_row_ref[...] = shift_row[:, :owned] * jnp.transpose(column)[0:1]


def finish_kernel(mine_ref, shift_row_ref, *refs):
    *near_refs, energy_ref, forces_ref, virial_ref = refs
    owned = shift_row_ref.shape[1]
    total = mine_ref[:, :owned]
    for near_ref in near_refs:
        start = near_ref.shape[1] - owned
        total = total + near_ref[:, start : start + owned]
    energy = total[12:13] + shift_row_ref[...]
    columns = jnp.transpose(jnp.concatenate([total, jnp.zeros((ORDERS, 128 - owned), F32)], axis=1))
    for cell in range(OWN_CELLS):
        x, z = cell // 2, cell % 2
        lanes = slice(cell * SITES, (cell + 1) * SITES)
        energy_ref[x, 0, z : z + 1, :] = energy[:, lanes]
        for c in range(3):
            forces_ref[c, x, 0, z : z + 1, :] = total[c : c + 1, lanes]
        virial_ref[x, 0, z] = columns[lanes, 3:12]


def force_kernel(kind, nbr, here_ref, last_x_ref, *refs):
    near_side_refs = refs[: 2 * kind - 2]
    (
        next_z_ref,
        center_weight_ref,
        near_weight_ref,
        basis_weight_ref,
        path_weight_ref,
        value_weight_ref,
        latent_weight_ref,
        out_weight_ref,
        keep_ref,
        send_ref,
    ) = refs[2 * kind - 2 :]
    height, width = here_ref.shape
    owned = OWN_CELLS * SITES
    center_sides = 2 if kind == 2 else 1
    kept_sides = 1 if kind == 2 else kind
    own_pairs = owned * nbr
    pairs = center_sides * own_pairs
    centers = center_sides * owned
    radial = basis_weight_ref.shape[0]
    span = GROUP * nbr
    groups = centers // GROUP
    sites = SITES
    root_count = math.sqrt(nbr)
    root_three = math.sqrt(3.0)
    root_fifteen = math.sqrt(15.0)
    root_five = math.sqrt(5.0)
    far = next_z_ref[...]
    mains = [here_ref[...], last_x_ref[...], far[:height], far[height : 2 * height]]
    near_sides = [ref[...] for ref in near_side_refs]
    far_sides = far[2 * height :]
    far_sides = [far_sides[i * height : (i + 1) * height] for i in range(2 * kind - 2)]
    blocks_in = [
        [mains[0], *near_sides[0::2]],
        [mains[1], *near_sides[1::2]],
        [mains[2], *far_sides[0::2]],
        [mains[3], *far_sides[1::2]],
    ]
    feats = jnp.concatenate([side[:owned] for block in blocks_in for side in block], axis=0)
    known = feats.shape[0]
    center_feats = []
    center_coords = []
    coords = []
    scales = []
    codes = []
    cell_row = lax.broadcasted_iota(jnp.int32, (kind * OWN_CELLS, 128), 0) % OWN_CELLS
    tile_lane = lax.broadcasted_iota(jnp.int32, (kind * OWN_CELLS, 128), 1)
    for g, block in enumerate(blocks_in):
        behind_x, ahead_z = g % 2, g // 2
        rows = jnp.concatenate([side[owned : owned + OWN_CELLS] for side in block], axis=0)
        corner_x = (cell_row // 2 + 2 - 2 * behind_x).astype(F32) * CELL_SIDE
        corner_z = (cell_row % 2 + 2 * ahead_z).astype(F32) * CELL_SIDE
        corner = jnp.where(
            tile_lane < sites, corner_x, jnp.where(tile_lane < 2 * sites, 0.0, corner_z)
        )
        coords.append(rows + corner)
    for c in range(center_sides):
        for g, block in enumerate(blocks_in):
            cell = g % 2 * 2 + 1 - g // 2
            row = c * OWN_CELLS + cell
            center_feats.append(block[c][cell * sites : (cell + 1) * sites])
            scales.append(block[c][owned + cell : owned + cell + 1])
            center_coords.append(coords[g][row : row + 1])
            start = owned + OWN_CELLS + (1 - g // 2) * span // 128
            codes.extend(block[c][start + r : start + r + 1] for r in range(span // 128))
    center_feats = jnp.concatenate(center_feats, axis=0)
    coords = jnp.concatenate(coords, axis=0)
    code = jnp.concatenate(codes, axis=1).astype(jnp.int32)
    live = code > 0
    code = jnp.maximum(code - 1, 0)
    side_y = ((code >> 10) - 1).astype(F32)
    near_row = code & 1023
    if center_sides == 2:
        pair_lane = lax.broadcasted_iota(jnp.int32, (1, pairs), 1)
        near_row = jnp.where(pair_lane < own_pairs, near_row, near_row ^ owned)
    near_row = jnp.where(live, near_row, known)

    def place_rows(cell_rows):
        count = cell_rows.shape[0] * sites
        spread = jnp.broadcast_to(cell_rows[:, None, :], (cell_rows.shape[0], sites, 128))
        spread = spread.reshape(count, 128)
        lane = lax.broadcasted_iota(jnp.int32, (count, 128), 1)
        row = lax.broadcasted_iota(jnp.int32, (count, 128), 0)
        keep = (lane % sites == row % sites) & (lane < 3 * sites)
        spread = jnp.transpose(jnp.where(keep, spread, 0.0))
        return jnp.concatenate(split3(spread[: 3 * sites]), axis=0)

    place_parts = place_rows(coords)
    center_parts = place_rows(jnp.concatenate(center_coords, axis=0))

    value_rows = three(*split(jnp.transpose(value_weight_ref[...])))
    latent_t = three(*split(0.5 * jnp.transpose(latent_weight_ref[...])))
    latent_rows = three(*split(latent_weight_ref[...] * out_weight_ref[...]))
    value_plain = three(*split(value_weight_ref[...]))
    basis_t = jnp.transpose(basis_weight_ref[...])
    basis_high_t, basis_low_t = split(0.5 * basis_t)
    basis_rows = three(*split(basis_weight_ref[...]))

    def project(weight, rows):
        weight = stacked(*split(jnp.transpose(weight)))
        return folded(mm_nt(weight, jnp.concatenate(split(rows), axis=1)))

    near_t = project(near_weight_ref[...], feats)
    own_t = project(center_weight_ref[...], center_feats)
    near_high, near_low = split(0.5 * near_t)
    own_high, own_low = split(0.5 * own_t)
    lookup = jnp.concatenate(
        [near_high, near_low, own_high, own_low, basis_high_t, basis_high_t, basis_low_t], axis=1
    )
    scale_rows = jnp.concatenate(scales, axis=0)
    scale_parts = jnp.concatenate(
        [*split3(scale_rows), jnp.zeros((-3 * groups % 16, 128), BF16)], axis=0
    )

    path_rows = jnp.concatenate(
        [jnp.broadcast_to(path_weight_ref[l : l + 1, :], (GROUP, width)) for l in LEVELS], axis=0
    ) * (1.0 / root_count)
    out_column = jnp.transpose(jnp.broadcast_to(out_weight_ref[...], (width, width)))
    out_column = jnp.concatenate([out_column] * (pairs // width), axis=1)

    slot_ids = lax.broadcasted_iota(jnp.int32, (centers, 128), 0)
    slot_row = lax.broadcasted_iota(jnp.int32, (1, pairs), 1) // nbr
    group_lane = lax.broadcasted_iota(jnp.int32, (GROUP, pairs), 1) // nbr % GROUP
    group_mask = group_lane == lax.broadcasted_iota(jnp.int32, (GROUP, pairs), 0)
    group_mask = jnp.where(group_mask, 1.0, 0.0)
    tall = len(LEVELS) * GROUP
    order = lax.broadcasted_iota(jnp.int32, (radial, pairs), 0).astype(F32) + 1.0
    lanes = [slice(g * span, (g + 1) * span) for g in range(groups)]

    site_ids = lax.broadcasted_iota(jnp.int32, (known, 128), 0)
    if known <= 256:
        site_ids = site_ids.astype(F32).astype(BF16)
        wanted = jnp.broadcast_to(near_row.astype(F32), (16, pairs)).astype(BF16)
        wanted = jnp.concatenate([wanted] * (known // 16), axis=0)
        one, zero = jnp.ones((), BF16), jnp.zeros((), BF16)
    else:
        wanted = near_row
        one, zero = 1.0, 0.0
    site_ids = jnp.concatenate([site_ids] * (pairs // 128), axis=1)
    pick_half = jnp.where(site_ids == wanted, one, zero).astype(BF16)
    slot_ids = slot_ids.astype(F32).astype(BF16)
    slot_ids = jnp.concatenate([slot_ids] * (pairs // 128), axis=1)
    slot_row = jnp.broadcast_to(slot_row.astype(F32), (16, pairs)).astype(BF16)
    slot_row = jnp.concatenate([slot_row] * (centers // 16), axis=0)
    slot_half = jnp.where(slot_ids == slot_row, jnp.ones((), BF16), jnp.zeros((), BF16))

    moved = mm(
        jnp.concatenate([place_parts, -center_parts], axis=1),
        jnp.concatenate([pick_half, slot_half], axis=0),
    )
    moved = moved[: 3 * sites] + moved[3 * sites : 6 * sites] + moved[6 * sites :]
    dx = jnp.where(live, jnp.sum(moved[:sites], axis=0, keepdims=True), 6.0)
    dy = jnp.sum(moved[sites : 2 * sites], axis=0, keepdims=True) + CELL_SIDE * side_y
    dy = jnp.where(live, dy, 0.0)
    dz = jnp.where(live, jnp.sum(moved[2 * sites :], axis=0, keepdims=True), 0.0)
    length = jnp.sqrt(dx * dx + dy * dy + dz * dz)
    inverse = 1.0 / length
    ratio = length * (1.0 / CUTOFF)
    inside = live & (ratio < 1.0)
    r2 = ratio * ratio
    r5 = r2 * r2 * ratio
    r6 = r5 * ratio
    weight = jnp.where(inside, 1.0 - r6 * (28.0 - 48.0 * ratio + 21.0 * r2), 0.0)
    slope = jnp.where(inside, -168.0 * r5 * (1.0 - 2.0 * ratio + r2), 0.0)
    sine, cosine = sin_cos_pi(order * ratio)
    basis = (math.sqrt(2.0 / CUTOFF) * inverse) * sine
    basis_slope = (math.sqrt(2.0 / CUTOFF) * inverse) * (
        (math.pi / CUTOFF) * order * cosine - sine * inverse
    )
    ex = dx * inverse
    ey = dy * inverse
    ez = dz * inverse
    angular = jnp.concatenate(
        [
            jnp.ones_like(ex),
            root_three * ex,
            root_three * ey,
            root_three * ez,
            root_fifteen * ex * ey,
            root_fifteen * ey * ez,
            0.5 * root_five * (3.0 * ez * ez - 1.0),
            root_fifteen * ex * ez,
            0.5 * root_fifteen * (ex * ex - ey * ey),
        ],
        axis=0,
    )
    angular_high, angular_low = halves(angular)
    angular_low = angular_low.astype(BF16).astype(F32)
    block_high = [angular_high[m : m + 1] * group_mask for m in range(len(LEVELS))]
    block_low = [angular_low[m : m + 1] * group_mask for m in range(len(LEVELS))]
    blocks = jnp.concatenate(block_high + block_low, axis=0).astype(BF16)
    blocks = jnp.concatenate([blocks, blocks[:tall]], axis=0)
    lane_ids = lax.broadcasted_iota(jnp.int32, (128, span), 0)
    lane_slot = lax.broadcasted_iota(jnp.int32, (128, span), 1) // nbr + 3 * sites
    scale = mm(scale_parts, jnp.where(lane_ids == lane_slot, 1.0, 0.0).astype(BF16))
    scale = scale[:groups] + scale[groups : 2 * groups] + scale[2 * groups : 3 * groups]
    scale = jnp.concatenate([scale[g : g + 1] for g in range(groups)], axis=1)
    scale = scale * (1.0 / root_count)
    pull = ROOT_HALF * scale

    basis_high, basis_low = halves(basis)
    basis_rest = jnp.concatenate([basis_high, basis_low, basis_high], axis=0).astype(BF16)
    before = mm(
        lookup,
        jnp.concatenate([pick_half, pick_half, slot_half, slot_half, basis_rest], axis=0),
    )
    gate = 1.0 + jnp.tanh(before)
    active = before * gate
    latent = weight * active
    latent_high, latent_low = split(latent)
    mixed = deep(value_rows, latent_high, latent_low)
    values = mixed[:width]
    env_high, env_low = split(mixed[width:])

    def over_pairs(high, low):
        sums = []
        for cut in lanes:
            both = jnp.concatenate([high[:, cut], low[:, cut]], axis=0)
            quad = mm_nt(blocks[: 2 * tall, cut], both)
            quad = quad[:tall, :width] + quad[tall:, :width] + quad[:tall, width:]
            sums.append(quad * path_rows)
        return sums

    def over_orders(tables):
        parts = []
        for table, cut in zip(tables, lanes):
            high, low = halves(table)
            table = jnp.concatenate([high, high, low], axis=0).astype(BF16)
            table = jnp.transpose(table)
            parts.append(mm(table, blocks[:, cut]))
        return jnp.concatenate(parts, axis=1)

    weighted = over_pairs(env_high, env_low)
    inner = over_orders(weighted)
    scalars = values * inner
    scalars_high, scalars_low = split(scalars)
    z = deep(
        latent_t,
        jnp.concatenate([latent_high, scalars_high], axis=0),
        jnp.concatenate([latent_low, scalars_low], axis=0),
    )
    z_gate = 1.0 + jnp.tanh(z)
    update = z * z_gate
    update_sum = jnp.sum(update * out_column, axis=0, keepdims=True)
    active_sum = jnp.sum(
        active[:, :own_pairs] * out_column[:, :own_pairs], axis=0, keepdims=True
    )
    pair_energy = (active_sum + update_sum[:, :own_pairs]) * (pull * weight)[:, :own_pairs]
    d_z = (0.5 * pull * weight) * (z_gate + update * (2.0 - z_gate))
    spread_back = deep(latent_rows, *split(d_z))
    d_scalars = spread_back[width:]
    d_values = d_scalars * inner
    dinner_high, dinner_low = split(d_scalars * values)
    d_embed = over_pairs(dinner_high, dinner_low)
    d_env = over_orders(d_embed)

    d_angular = []
    for g, cut in enumerate(lanes):
        sides_high, sides_low = halves(jnp.concatenate([weighted[g], d_embed[g]], axis=1))
        d_block = deep(
            three(sides_high.astype(BF16), sides_low.astype(BF16)),
            jnp.concatenate([dinner_high[:, cut], env_high[:, cut]], axis=0),
            jnp.concatenate([dinner_low[:, cut], env_low[:, cut]], axis=0),
        )
        d_block = d_block.reshape(len(LEVELS), GROUP, span) * group_mask[None, :, cut]
        d_angular.append(jnp.sum(d_block, axis=1))
    d_angular = jnp.concatenate(d_angular, axis=1)

    mixed_high, mixed_low = split(jnp.concatenate([d_values, d_env], axis=0))
    d_latent = (
        deep(value_plain, mixed_high, mixed_low)
        + spread_back[:width]
        + pull * out_column
    )
    d_weight = jnp.sum(d_latent * active, axis=0, keepdims=True) + pull * update_sum
    d_before = d_latent * (gate + active * (2.0 - gate))
    d_basis = deep(basis_rows, *split(d_before)) * (0.5 * weight)

    d_length = jnp.sum(d_basis * basis_slope, axis=0, keepdims=True) + d_weight * slope * (
        1.0 / CUTOFF
    )
    a1, a2, a3, a4, a5, a6, a7, a8 = [d_angular[m : m + 1] for m in range(1, 9)]
    ux = root_three * a1 + root_fifteen * (ey * a4 + ez * a7 + ex * a8)
    uy = root_three * a2 + root_fifteen * (ex * a4 + ez * a5 - ey * a8)
    uz = root_three * a3 + root_fifteen * (ey * a5 + ex * a7) + 3.0 * root_five * ez * a6
    along = ex * ux + ey * uy + ez * uz
    radial_part = d_length - along * inverse
    gx = ux * inverse + ex * radial_part
    gy = uy * inverse + ey * radial_part
    gz = uz * inverse + ez * radial_part
    hx = -0.5 * dx
    hy = -0.5 * dy
    hz = -0.5 * dz
    virial = [hx * gx, hx * gy, hx * gz, hy * gx, hy * gy, hy * gz, hz * gx, hz * gy, hz * gz]
    rest = [jnp.zeros((ORDERS - 13, pairs), F32)]
    near_terms = jnp.concatenate(
        [-gx, -gy, -gz, *virial, jnp.zeros_like(gx), *rest], axis=0
    )
    center_rows = [gx, gy, gz, *virial]
    center_rows = [r[:, :own_pairs] for r in center_rows] + [pair_energy]
    center_rows.append(jnp.zeros((ORDERS - 13, own_pairs), F32))
    center_terms = jnp.concatenate(center_rows, axis=0)
    reach = []
    for x, z, side in np.ndindex(2, 2, kept_sides):
        start = ((2 * z + x) * kind + side) * owned
        reach.append(pick_half[start : start + owned])
    reach = jnp.concatenate(reach, axis=0)
    near_sums = mm_nt(jnp.concatenate(split(near_terms), axis=0), reach)
    center_sums = mm_nt(
        jnp.concatenate(split(center_terms), axis=0), slot_half[:owned, :own_pairs]
    )
    center_sums = jnp.concatenate(
        [folded(center_sums), jnp.zeros((ORDERS, 128 - owned), F32)], axis=1
    )
    totals = folded(near_sums)
    lane = lax.broadcasted_iota(jnp.int32, (ORDERS, 128), 1)
    known = totals.shape[1]
    tiles = [totals[:, 128 * i : 128 * (i + 1)] for i in range(known // 128)]
    for g in range(owned // GROUP):
        cell = g % 2 * 2 + 1 - g // 2
        target = (g % 2 * 2 + g // 2) * kept_sides * owned + cell * sites
        turn = (target - g * GROUP) % 128
        piece = pltpu.roll(center_sums, turn, 1) if turn else center_sums
        begin = target % 128
        piece = jnp.where((lane >= begin) & (lane < begin + GROUP), piece, 0.0)
        tiles[target // 128] = tiles[target // 128] + piece
    totals = jnp.concatenate(tiles, axis=1)
    keep_ref[...] = totals[:, : known // 2]
    send_ref[...] = totals[:, known // 2 :]


def in_hbm(*arrays):
    return [pltpu.with_memory_space_constraint(array, pltpu.HBM) for array in arrays]


def joined(parts):
    total = sum(part.shape[0] for part in parts)
    start = 0
    pads = []
    for part in parts:
        end = start + part.shape[0]
        pads.append(jnp.pad(part, ((start, total - end), (0, 0))))
        start = end
    return functools.reduce(jnp.add, pads)


def local(
    positions,
    features,
    species,
    centers,
    neighbours,
    counts,
    species_scale,
    species_shift,
    center_weight,
    near_weight,
    basis_weight,
    path_weight,
    value_weight,
    latent_weight,
    out_weight,
):
    cells_x, cells_y, cells_z, sites, width = features.shape
    cell_count = cells_x * cells_y * cells_z
    owned = cell_count * sites
    assert (cells_x, cells_y, cells_z, sites) == (2, 1, 2, SITES)
    pairs = neighbours.size
    nbr = pairs // owned
    kind = min(3, lax.axis_size("gy"))

    def moved(array, steps):
        names = tuple(steps)
        sizes = [lax.axis_size(name) for name in names]
        route = []
        for at in np.ndindex(*sizes):
            to = [(p + steps[name]) % size for p, name, size in zip(at, names, sizes)]
            route.append(
                (int(np.ravel_multi_index(at, sizes)), int(np.ravel_multi_index(to, sizes)))
            )
        return lax.ppermute(array, names, route)

    vmem = pl.BlockSpec(memory_space=pltpu.VMEM)
    hbm = pl.BlockSpec(memory_space=pltpu.HBM)
    listed = centers.reshape(1, owned)
    payload = jax.ShapeDtypeStruct((owned + OWN_CELLS + pairs // 256, width), F32)
    low, high = pl.pallas_call(
        functools.partial(pack_kernel, kind),
        out_shape=(payload, payload),
        in_specs=[hbm] * 6,
        out_specs=(vmem, vmem),
        scratch_shapes=[
            pltpu.VMEM((owned, 128), F32),
            pltpu.VMEM(positions.shape, F32),
            pltpu.VMEM(species.shape, jnp.int32),
            pltpu.VMEM(listed.shape, jnp.int32),
            pltpu.VMEM(neighbours.shape, jnp.int32),
            pltpu.SMEM(species_scale.shape, F32),
            pltpu.SemaphoreType.DMA((6,)),
        ],
        compiler_params=pltpu.CompilerParams(vmem_limit_bytes=8 * 1024 * 1024),
        name="pack_payload",
    )(
        *in_hbm(
            positions,
            features.reshape(owned, width),
            species,
            listed,
            neighbours,
            species_scale,
        )
    )
    weights = (
        center_weight,
        near_weight,
        basis_weight,
        path_weight,
        value_weight,
        latent_weight,
        out_weight.reshape(1, width),
    )
    *weights, shift_row = pl.pallas_call(
        fetch_kernel,
        out_shape=(
            *(jax.ShapeDtypeStruct(w.shape, F32) for w in weights),
            jax.ShapeDtypeStruct((1, owned), F32),
        ),
        in_specs=[hbm] * (3 + len(weights)),
        out_specs=(vmem,) * (1 + len(weights)),
        scratch_shapes=[
            pltpu.VMEM(species.shape, jnp.int32),
            pltpu.VMEM(listed.shape, jnp.int32),
            pltpu.SMEM(species_shift.shape, F32),
            pltpu.SemaphoreType.DMA((3 + len(weights),)),
        ],
        compiler_params=pltpu.CompilerParams(vmem_limit_bytes=8 * 1024 * 1024),
        name="fetch_weights",
    )(*in_hbm(species, listed, species_shift, *weights))
    last_x = moved(high, {"gx": 1})
    sides = []
    for step in (-1, 1)[: kind - 1]:
        sides.append(moved(high, {"gx": 1, "gy": step}))
        sides.insert(-1, moved(low, {"gy": step}))
    next_z = moved(joined([low, last_x, *sides]), {"gz": -1})
    kept = 1 if kind == 2 else kind
    half = 2 * kept * owned
    keep, send = pl.pallas_call(
        functools.partial(force_kernel, kind, nbr),
        out_shape=(
            jax.ShapeDtypeStruct((ORDERS, half), F32),
            jax.ShapeDtypeStruct((ORDERS, half), F32),
        ),
        in_specs=[vmem] * (8 + 2 * kind),
        out_specs=(vmem, vmem),
        compiler_params=pltpu.CompilerParams(vmem_limit_bytes=44 * 1024 * 1024),
        name="pair_forces",
    )(
        low,
        last_x,
        *sides,
        next_z,
        *weights,
    )
    totals = keep + moved(send, {"gx": -1})

    def part(index):
        return totals[:, index * owned : (index + 1) * owned]

    back = [moved(totals, {"gz": 1}) if kept == 1 else moved(part(kept), {"gz": 1})]
    for i, step in enumerate((1, -1)[: kept - 1]):
        back.append(moved(part(kept + 1 + i), {"gy": step, "gz": 1}))
        back.append(moved(part(1 + i), {"gy": step}))
    site_energy, forces, virial = pl.pallas_call(
        finish_kernel,
        out_shape=(
            jax.ShapeDtypeStruct(species.shape, F32),
            jax.ShapeDtypeStruct(positions.shape, F32),
            jax.ShapeDtypeStruct((*species.shape, 9), F32),
        ),
        in_specs=[vmem] * (2 + len(back)),
        out_specs=(vmem, vmem, vmem),
        compiler_params=pltpu.CompilerParams(vmem_limit_bytes=8 * 1024 * 1024),
        name="write_outputs",
    )(totals, shift_row, *back)
    return (site_energy, forces, jnp.transpose(virial, (4, 0, 1, 2, 3)))


def solution(mesh):
    placed = (
        P(None, "gx", "gy", "gz", None),
        P("gx", "gy", "gz", None, None),
        P("gx", "gy", "gz", None),
        P(("gx", "gy", "gz")),
        P(("gx", "gy", "gz"), None),
        P(("gx", "gy", "gz")),
        P(),
        P(),
        P(),
        P(),
        P(),
        P(),
        P(),
        P(),
        P(),
    )
    return jax.shard_map(
        local,
        mesh=mesh,
        in_specs=placed,
        out_specs=(
            P("gx", "gy", "gz", None),
            P(None, "gx", "gy", "gz", None),
            P(None, "gx", "gy", "gz", None),
        ),
        check_vma=False,
    )
```
